32 devices in a mesh: dp: 8 (over z, x), mp: 4 (over y, core).
Axes of the slice: x: 2, y: 2, z: 4, core: 2. Of those that a mesh axis runs over, the one named last changes fastest.
Arguments:
- tokens: bfloat16 [8192, 768], P(('dp', 'mp')), may hold values from -6 to 6
- norm_gain: float32 [768], replicated, may hold values from 0.5 to 1.5
- w_query: bfloat16 [768, 768], P('dp', 'mp'), may hold values from -0.21875 to 0.21875
- w_key: bfloat16 [768, 768], P('dp', 'mp'), may hold values from -0.21875 to 0.21875
- w_value: bfloat16 [768, 768], P('dp', 'mp'), may hold values from -0.21875 to 0.21875
- w_output: bfloat16 [768, 768], P('mp', 'dp'), may hold values from -1.75 to 1.75
- bias_table: float32 [32, 12], P(None, 'mp'), may hold values from -6 to 6
- ffn_gain: float32 [768], replicated, may hold values from 0.5 to 1.5
- w_router: bfloat16 [768, 8], replicated, may hold values from -0.15625 to 0.15625
- w_in: bfloat16 [8, 768, 3072], P('dp'), may hold values from -0.21875 to 0.21875
- w_out: bfloat16 [8, 3072, 768], P('dp'), may hold values from -2 to 2
- segments: int32 [8, 1024], P('dp'), may hold values from 0 to 3, never falling along the last dimension, each value on 1 to 512 neighbouring positions
- buckets: int32 [1024], replicated, may hold values from 0 to 31
- routes: int32 [8192, 2], P(('dp', 'mp')), may hold values from 0 to 7, all different within a row; in each aligned block of 256 rows (0 to 255, 256 to 511, ...) at most 128 rows name the same one
- cotangent: bfloat16 [8192, 768], P(('dp', 'mp')), may hold values from -6 to 6
Outputs:
- block_out: bfloat16 [8192, 768], P(('dp', 'mp'))
- tokens_grad: bfloat16 [8192, 768], P(('dp', 'mp'))
- norm_gain_grad: float32 [768], replicated
- w_query_grad: float32 [768, 768], P('dp', 'mp')
- w_key_grad: float32 [768, 768], P('dp', 'mp')
- w_value_grad: float32 [768, 768], P('dp', 'mp')
- w_output_grad: float32 [768, 768], P('mp', 'dp')
- bias_table_grad: float32 [32, 12], replicated
- ffn_gain_grad: float32 [768], replicated
- w_router_grad: float32 [768, 8], replicated
- w_in_grad: float32 [8, 768, 3072], P('dp', None, 'mp')
- w_out_grad: float32 [8, 3072, 768], P('dp', 'mp')
The draws below stay inside these ranges and needn't reach their ends.
Inputs may be any that keep to these rules, and one draw needn't show every extreme that they name: `routes`: in the rows of one device each expert is named at most 128 times, a bound that some block reaches; the two experts of a row differ. `segments`: within each sequence the numbers never fall; each document has at most 512 positions and one has exactly that many.
All inputs are finite; a program needn't handle non-finite values.
Results may differ from the reference program's by a relative error of at most 0.017.
Values may be sent and summed in bfloat16 or wider, within the bound.
No kernel may reach another device: no remote copies, remote signals or barrier semaphores. Data moves between devices by JAX's collectives and lax.ppermute only.
A program may use at most 192 MiB of HBM per device.

```python
import math
import jax
import jax.numpy as jnp
import numpy as np
from jax import lax

D = 768
HEADS = 12
HD = 64
FF = 3072
NB = 32
LEN = 1024
EXPERTS = 8
SEQS = 8
TOKENS = 8192
ROWS_DEV = 256
CAP = 128
N_DP = 8
N_MP = 4


def place_ends(drawn, key, least, largest):
    index_at = [jax.random.randint(jax.random.fold_in(key, axis), (), 0, length) for axis, length in enumerate(drawn.shape)]
    longest = drawn.shape.index(max(drawn.shape))
    next_to = index_at[:longest] + [(index_at[longest] + 1) % drawn.shape[longest]] + index_at[longest + 1:]
    return drawn.at[tuple(index_at)].set(least).at[tuple(next_to)].set(largest)


def spiked(array, key, source, target, blocks, factor):
    owner, partner = [(jnp.arange(array.shape[axis_at]) // (array.shape[axis_at] // blocks)).reshape([-1 if axis == axis_at else 1 for axis in range(array.ndim)]) for axis_at in (source, target)]
    chosen = jax.random.permutation(key, blocks)[partner]
    strong = (owner == chosen) | (owner == (partner + blocks // 2) % blocks)
    return jnp.where(strong, factor * array, array)


def level_of(own_key, dims, split, low, top_value):
    def one(dim, shards_of):
        steps = jax.random.uniform(jax.random.fold_in(jax.random.fold_in(own_key, 6), dim), (shards_of,), jnp.float32, low / len(split), top_value / len(split))
        return jnp.repeat(jnp.exp(steps), dims[dim] // shards_of).reshape((-1,) + (1,) * (len(dims) - dim - 1))

    loudness = one(*split[0])
    for cut in split[1:]:
        loudness = loudness * one(*cut)
    return loudness


def split_up(count, total, reach, skew):
    portions = [(1 << 20) // math.isqrt(rank ** skew) + 1 for rank in range(2, count + 1)]
    spare, given = total - reach - (count - 1), [1] * (count - 1)
    while spare > 0:
        movable = [i for i in range(count - 1) if given[i] < reach]
        whole, left = sum([portions[i] for i in movable]), spare
        for i in movable:
            addition = min(reach - given[i], max(1, left * portions[i] // whole), spare)
            given[i] = given[i] + addition
            spare = spare - addition
    return np.array([reach] + given)


def ragged(own_key, amount, total, bound, skew):
    if amount == 2:
        one = jax.random.randint(own_key, (), max(1, total - bound), min(bound, total - 1) + 1)
        return jnp.stack([one, total - one])
    lengths = jnp.asarray(split_up(amount, total, bound, skew), jnp.int32)
    twos = (amount - 1) // 2
    source_of, receiver = lengths[1:1 + 2 * twos:2], lengths[2:2 + 2 * twos:2]
    room = jnp.minimum(source_of - 1, bound - receiver)
    moved = jax.random.randint(jax.random.fold_in(own_key, 1), (twos,), 0, 1 << 20) % (room + 1)
    lengths = lengths.at[1:1 + 2 * twos:2].set(source_of - moved).at[2:2 + 2 * twos:2].set(receiver + moved)
    return lengths[jax.random.permutation(jax.random.fold_in(own_key, 2), amount)]


def shared_out(own_key, own, number, rows, number_of, top, reach, skew):
    sequence = jax.random.permutation(own_key, number_of)
    packed, usual = shares(number_of, rows * top, reach, skew, True), shares(number_of, rows * top, reach, skew, False)
    places = jnp.arange(number_of)

    def named(lengths, rotation):
        used = int((lengths > 0).sum())
        fixed = max(1, used // 4)
        moved = fixed + (places - fixed + rotation * (used - fixed)) % max(1, number_of - fixed)
        return jnp.zeros((number_of,), jnp.int32).at[sequence[jnp.where(places < fixed, places, moved)]].set(jnp.asarray(lengths, jnp.int32))

    lengths = jnp.where(number % 4 == 0, named(packed, number // 4), named(usual, number - number // 4 - 1))
    mixed = jax.random.permutation(jax.random.fold_in(own, 3), number_of)
    donor, taker = mixed[0:number_of // 2 * 2:2], mixed[1:number_of // 2 * 2:2]
    room = jnp.minimum(lengths[donor] - 1, reach - lengths[taker]) // 2
    room = jnp.where((donor == sequence[0]) | (taker == sequence[0]) | (lengths[taker] == 0), 0, jnp.maximum(room, 0))
    moved = jax.random.randint(jax.random.fold_in(own, 4), (number_of // 2,), 0, 1 << 20) % (room + 1)
    lengths = lengths.at[donor].add(-moved).at[taker].add(moved)
    items = jnp.searchsorted(jnp.cumsum(lengths), jnp.arange(rows * top), side="right").astype(jnp.int32)
    listing = items.reshape(top, rows).T
    listing = listing[jax.random.permutation(jax.random.fold_in(own, 1), rows)]
    rotation = jax.random.randint(jax.random.fold_in(own, 2), (rows, 1), 0, top)
    return jnp.take_along_axis(listing, (jnp.arange(top)[None, :] + rotation) % top, axis=1)


def shares(number_of, total, limit, lean, full):
    weights = [(1 << 20) // math.isqrt(standing ** lean) + 1 for standing in range(1, number_of + 1)]
    largest = limit if full else min(limit, max(-(-total // number_of), total * weights[0] // sum(weights)))
    least = 1 if total - largest >= number_of - 1 else 0
    given, spare = [largest] + [least] * (number_of - 1), total - largest - least * (number_of - 1)
    while spare > 0:
        free = [i for i in range(1, number_of) if given[i] < largest] or [i for i in range(1, number_of) if given[i] < limit]
        mass, left = sum([weights[i] for i in free]), spare
        for i in free:
            extra = min(limit - given[i], max(1, left * weights[i] // mass), spare)
            given[i] = given[i] + extra
            spare = spare - extra
    return np.array(given)


def normal_values(rng, extent, scale, limit, cuts=(), held_as=jnp.bfloat16):
    entries = jax.random.normal(rng, extent, jnp.float32) * scale
    if len(cuts) > 0:
        entries = level_of(rng, extent, cuts, -0.22, 0.18) * entries
    return jnp.clip(entries, min=-limit, max=limit).astype(held_as)


def gaussian_with(key, shape, spread, bound, shards, heavy, held_as=jnp.bfloat16):
    array = spread * jax.random.normal(key, shape, jnp.float32)
    if shards:
        array = array * level_of(key, shape, shards, -0.22, 0.18)
    return jnp.clip(spiked(array, jax.random.fold_in(key, 3), *heavy), -bound, bound).astype(held_as)


def setup_inputs(seed: int = 0) -> dict:
    splits = jax.random.split(jax.random.key(seed), 16)
    tokens = normal_values(splits[0], (TOKENS, D), 1.0, 6.0, ((0, 32),))
    norm_gain = jnp.clip(1.0 + 0.1 * jax.random.normal(splits[1], (D,), jnp.float32), 0.5, 1.5)
    w_query = normal_values(splits[2], (D, D), D ** -0.5, 0.21875, ((0, 8), (1, 4)))
    w_key = normal_values(splits[3], (D, D), D ** -0.5, 0.21875, ((0, 8), (1, 4)))
    w_value = normal_values(splits[4], (D, D), D ** -0.5, 0.21875, ((0, 8), (1, 4)))
    w_output = normal_values(splits[5], (D, D), (D // 64) ** -0.5, 1.75, ((0, 4), (1, 8)))
    bias_table = normal_values(splits[6], (NB, HEADS), 1.0, 6.0, ((1, 4),), jnp.float32)
    ffn_gain = jnp.clip(1.0 + 0.1 * jax.random.normal(splits[7], (D,), jnp.float32), 0.5, 1.5)
    w_router = normal_values(splits[8], (D, EXPERTS), (2 * D) ** -0.5, 0.15625)
    w_in = normal_values(splits[9], (EXPERTS, D, FF), D ** -0.5, 0.21875, ((0, 8),))
    w_out = normal_values(splits[10], (EXPERTS, FF, D), (EXPERTS * 0.017), 2.0, ((0, 8),))
    segments = jax.vmap(lambda own: jnp.searchsorted(jnp.cumsum(ragged(own, 4, LEN, LEN // 2, 0)), jnp.arange(LEN), side="right"))(jax.random.split(splits[11], SEQS)).reshape((SEQS, LEN)).astype(jnp.int32)
    buckets = place_ends(jax.random.randint(splits[12], (LEN,), 0, NB), jax.random.fold_in(splits[12], 1), 0, NB - 1).astype(jnp.int32)
    routes_keys = jax.random.split(jax.random.fold_in(splits[13], 1), TOKENS // ROWS_DEV)
    routes_turns = jax.random.permutation(jax.random.fold_in(splits[13], 3), TOKENS // ROWS_DEV)
    routes = jax.vmap(lambda own, number: shared_out(jax.random.fold_in(splits[13], 2), own, number, ROWS_DEV, EXPERTS, 2, CAP, 2))(routes_keys, routes_turns).reshape((TOKENS, 2))
    cotangent = gaussian_with(splits[14], (TOKENS, D), 1.0, 6.0, ((0, 32),), (0, 1, 32, 2.75))
    return dict(tokens=tokens, norm_gain=norm_gain, w_query=w_query, w_key=w_key, w_value=w_value, w_output=w_output, bias_table=bias_table, ffn_gain=ffn_gain, w_router=w_router, w_in=w_in, w_out=w_out, segments=segments, buckets=buckets, routes=routes, cotangent=cotangent)


eps = 1e-06
highest = lax.Precision.HIGHEST

@jax.custom_vjp
def low(v):
    return lax.optimization_barrier(v.astype(jnp.bfloat16)).astype(jnp.float32)

@jax.custom_vjp
def low_back(v):
    return v

def low_keep(v):
    return (low(v), None)

def low_pass(kept, grad):
    return (grad,)

def back_keep(v):
    return (v, None)

def back_low(kept, grad):
    return (low(grad),)
low.defvjp(low_keep, low_pass)
low_back.defvjp(back_keep, back_low)

def matmul(left, right):
    return jnp.dot(left, right, precision=highest)

def rms_norm(values, gain):
    return values * lax.rsqrt(lax.optimization_barrier(jnp.mean(values * values, axis=-1, keepdims=True)) + eps) * gain

def gelu(values):
    return 0.5 * values * (1.0 + lax.erf(values * math.sqrt(0.5)))

def one_hot(values, count):
    return (values[:, None] == jnp.arange(count, dtype=jnp.int32)[None, :]).astype(jnp.float32)

def softmax_rows(scores):
    shifted = scores - lax.optimization_barrier(jnp.max(scores, axis=-1, keepdims=True))
    powers = jnp.exp(shifted)
    return powers / lax.optimization_barrier(jnp.sum(powers, axis=-1, keepdims=True))

def attend_sequence(query, key, value, seg_ids, bias_rows):
    block = min(512, LEN)
    scale = HD ** (-0.5)

    def one_block(start):
        part_q = lax.dynamic_slice_in_dim(query, start, block, 0)
        raw = jnp.einsum('qhd,khd->hqk', part_q, key, precision=highest) * scale
        place = start + jnp.arange(block, dtype=jnp.int32)
        distance = place[:, None] - jnp.arange(LEN, dtype=jnp.int32)[None, :]
        bias = jnp.take(bias_rows, jnp.clip(distance, 0, LEN - 1), axis=1)
        seg_q = lax.dynamic_slice_in_dim(seg_ids, start, block, 0)
        allowed = (distance >= 0) & (seg_q[:, None] == seg_ids[None, :])
        scores = low_back(raw + bias)
        scores = jnp.where(allowed[None], scores, -1e+30)
        probs = softmax_rows(scores)
        return jnp.einsum('hqk,khd->qhd', low(probs), value, precision=highest)
    starts = jnp.arange(LEN // block, dtype=jnp.int32) * block
    result = lax.map(jax.checkpoint(one_block), starts)
    return result.reshape(LEN, HEADS, HD)

def slot_tables(routes):
    devices = N_DP * N_MP
    flat_routes = routes.reshape(devices, ROWS_DEV * 2)
    hits = (flat_routes[:, :, None] == jnp.arange(EXPERTS, dtype=jnp.int32)[None, None, :]).astype(jnp.int32)
    ranks = lax.optimization_barrier(jnp.sum((jnp.cumsum(hits, axis=1).astype(jnp.int32) - 1) * hits, axis=2)).astype(jnp.int32)
    column = (jnp.arange(devices, dtype=jnp.int32)[:, None] * CAP + ranks).astype(jnp.int32)
    number = jnp.arange(devices * ROWS_DEV * 2, dtype=jnp.int32).reshape(devices, ROWS_DEV * 2) + 1
    slot_asg = jnp.zeros((EXPERTS, devices * CAP), jnp.int32).at[flat_routes, column].set(number)
    slot_tok = jnp.where(slot_asg > 0, (slot_asg - 1) // 2 + 1, 0).astype(jnp.int32)
    return (slot_tok, slot_asg)

def reference(tokens, norm_gain, w_query, w_key, w_value, w_output, bias_table, ffn_gain, w_router, w_in, w_out, segments, buckets, routes, cotangent):
    slot_tok, slot_asg = slot_tables(routes)

    def forward(resid, gain_one, weight_q, weight_k, weight_v, weight_o, table, gain_two, weight_r, weight_in, weight_out):
        normed = low(rms_norm(resid, gain_one))

        def project(weight):
            return low_back(low(matmul(normed, weight))).reshape(SEQS, LEN, HEADS, HD)
        query, key, value = (project(weight_q), project(weight_k), project(weight_v))
        bias_rows = matmul(one_hot(buckets, NB), table).T

        def one_sequence(items):
            return attend_sequence(items[0], items[1], items[2], items[3], bias_rows)
        mixed = lax.map(one_sequence, (query, key, value, segments))
        mixed = low_back(low(mixed.reshape(TOKENS, D)))
        hidden = resid + low_back(matmul(mixed, weight_o))
        ffn_input = low(rms_norm(hidden, gain_two))
        router_probs = softmax_rows(matmul(ffn_input, weight_r))
        gates = jnp.take_along_axis(router_probs, routes, axis=1).reshape(-1)
        rows_pad = jnp.concatenate([jnp.zeros((1, D), jnp.float32), ffn_input], axis=0)
        gates_pad = jnp.concatenate([jnp.zeros((1,), jnp.float32), gates])

        def one_expert(items):
            expert_in, expert_out, token_ids = items
            rows_now = low_back(jnp.take(rows_pad, token_ids, axis=0))
            pre_act = low_back(matmul(rows_now, expert_in))
            active = low(gelu(pre_act))
            return low_back(low(matmul(active, expert_out)))
        results = lax.map(jax.checkpoint(one_expert), (weight_in, weight_out, slot_tok))
        weighted = jnp.take(gates_pad, slot_asg)[:, :, None] * results
        total = jnp.zeros((TOKENS + 1, D), jnp.float32).at[slot_tok.reshape(-1)].add(weighted.reshape(-1, D))
        return hidden + total[1:]
    inputs = [tokens, norm_gain, w_query, w_key, w_value, w_output, bias_table, ffn_gain, w_router, w_in, w_out]
    inputs = [item.astype(jnp.float32) for item in inputs]
    block_out, pull = jax.vjp(forward, *inputs)
    grads = pull(cotangent.astype(jnp.float32))
    return (block_out.astype(jnp.bfloat16), grads[0].astype(jnp.bfloat16), grads[1], grads[2], grads[3], grads[4], grads[5], grads[6], grads[7], grads[8], grads[9], grads[10])
```

```python
import functools
import math

import jax
import jax.numpy as jnp
from jax import lax
from jax.experimental import pallas as pl
from jax.experimental.pallas import tpu as pltpu
from jax.sharding import PartitionSpec as P

eps = 1e-06
highest = lax.Precision.HIGHEST
f32, bf16 = jnp.float32, jnp.bfloat16
excluded = -1e30
reach = 512
tile = 128


def normalize(values, gain):
    inverse = lax.rsqrt(jnp.mean(values * values, axis=-1, keepdims=True) + eps)
    return (values * inverse * gain, inverse)


def dot(left, right, left_dim, right_dim, precision=None):
    return lax.dot_general(
        left,
        right,
        (((left_dim,), (right_dim,)), ((), ())),
        precision=precision,
        preferred_element_type=f32,
    )


def swap(values, axis, step):
    count = lax.axis_size(axis)
    return lax.ppermute(values, axis, [(i, i ^ step) for i in range(count)])


def call(kernel, name, operands, outs, scratch=(), flops=0, limit=32, scalars=None):
    vmem = pl.BlockSpec(memory_space=pltpu.VMEM)
    in_specs = [vmem] * len(operands)
    if scalars is not None:
        operands = [scalars] + list(operands)
        in_specs = [pl.BlockSpec(memory_space=pltpu.SMEM)] + in_specs
    moved = sum(math.prod(o.shape) * o.dtype.itemsize for o in operands)
    moved += sum(math.prod(o.shape) * o.dtype.itemsize for o in outs)
    return pl.pallas_call(
        kernel,
        name=name,
        in_specs=in_specs,
        out_specs=[vmem] * len(outs),
        out_shape=outs,
        scratch_shapes=list(scratch),
        compiler_params=pltpu.CompilerParams(vmem_limit_bytes=limit * 1024 * 1024),
        cost_estimate=pl.CostEstimate(
            flops=int(flops), bytes_accessed=int(moved), transcendentals=0
        ),
    )(*operands)


def shape(dims, dtype):
    return jax.ShapeDtypeStruct(tuple(dims), dtype)


def fill_skew(line_ref, skew, heads):
    window = reach + tile
    row = lax.broadcasted_iota(jnp.int32, (tile, window), 0)
    column = lax.broadcasted_iota(jnp.int32, (tile, window), 1)
    usable = (column - row <= reach) & (column - row >= 1)
    for head in range(heads):
        line = jnp.broadcast_to(line_ref[head : head + 1, :], (tile, window))
        rolled = pltpu.roll(line, 0, 1, stride=1, stride_axis=0)
        skew[head * tile : (head + 1) * tile, :] = jnp.where(usable, rolled, excluded)


def fill_window(source_ref, padded):
    padded[:reach, :] = jnp.zeros((reach, padded.shape[1]), bf16)
    padded[reach:, :] = source_ref[...]


def spread_heads(values, heads, scale):
    span = values.shape[1]
    size = span // heads
    lane = lax.broadcasted_iota(jnp.int32, (tile, span), 1)
    wide = values.astype(f32) * scale
    parts = [
        jnp.where((lane >= head * size) & (lane < (head + 1) * size), wide, 0.0)
        for head in range(heads)
    ]
    return jnp.concatenate(parts, axis=0).astype(bf16)


def collect_heads(stacked, heads):
    span = stacked.shape[1]
    size = span // heads
    lane = lax.broadcasted_iota(jnp.int32, (tile, span), 1)
    total = stacked[:tile, :]
    for head in range(1, heads):
        total = jnp.where(lane < head * size, total, stacked[head * tile : (head + 1) * tile, :])
    return total


def window_powers(q_all, keys, skew, seg_q_ref, seg_k_ref, start, heads):
    window = reach + tile
    seg_q = jnp.concatenate([seg_q_ref[pl.ds(start, tile), :]] * heads, axis=0)
    seg_k = seg_k_ref[:, pl.ds(start, window)]
    scores = dot(q_all, keys, 1, 1) + skew[...]
    scores = jnp.where(seg_q == seg_k, scores, excluded)
    powers = jnp.exp(scores - jnp.max(scores, axis=-1, keepdims=True))
    return powers, 1.0 / jnp.sum(powers, axis=-1, keepdims=True)


def attend_kernel(heads, place, q_ref, k_ref, v_ref, seg_q_ref, seg_k_ref, line_ref, *rest):
    *out_refs, mixed, k_pad, v_pad, skew = rest
    window = reach + tile
    scale = (q_ref.shape[1] // heads) ** (-0.5)
    fill_skew(line_ref, skew, heads)
    fill_window(k_ref, k_pad)
    fill_window(v_ref, v_pad)

    def step(index, carry):
        start = pl.multiple_of(index * tile, tile)
        q_all = spread_heads(q_ref[pl.ds(start, tile), :], heads, scale)
        powers, inverse = window_powers(
            q_all, k_pad[pl.ds(start, window), :], skew, seg_q_ref, seg_k_ref, start, heads
        )
        probs = (powers * inverse).astype(bf16)
        part = dot(probs, v_pad[pl.ds(start, window), :], 1, 0)
        mixed[pl.ds(start, tile), :] = collect_heads(part, heads).astype(bf16)
        return carry

    lax.fori_loop(0, q_ref.shape[0] // tile, step, 0)
    rows = out_refs[0].shape[0]
    for r, out_ref in enumerate(out_refs):
        out_ref[...] = mixed[pl.ds(pl.multiple_of((place[1] ^ r) * rows, rows), rows), :]


def attend(place, query, key_rows, value_rows, seg_q, seg_k, line, heads, members):
    seq_len, span = query.shape
    window = reach + tile

    def kernel(place_ref, *refs):
        attend_kernel(heads, place_ref, *refs)

    return call(
        kernel,
        "attend",
        [query, key_rows, value_rows, seg_q, seg_k, line],
        [shape((seq_len // members, span), bf16)] * members,
        scratch=[
            pltpu.VMEM((seq_len, span), bf16),
            pltpu.VMEM((seq_len + reach, span), bf16),
            pltpu.VMEM((seq_len + reach, span), bf16),
            pltpu.VMEM((heads * tile, window), f32),
        ],
        flops=4 * seq_len * window * heads * 256,
        scalars=place,
    )


def attend_back_kernel(heads, members, place, *refs):
    q_ref, k_ref, v_ref, seg_q_ref, seg_k_ref, line_ref = refs[:6]
    g_refs = refs[6 : 6 + members]
    dq_ref, dk_ref, dv_ref, line_grad_ref = refs[6 + members : 10 + members]
    grad, k_pad, v_pad, skew, dk_sum, dv_sum, bias_sum = refs[10 + members :]
    window = reach + tile
    scale = (q_ref.shape[1] // heads) ** (-0.5)
    rows = g_refs[0].shape[0]
    fill_skew(line_ref, skew, heads)
    fill_window(k_ref, k_pad)
    fill_window(v_ref, v_pad)
    dk_sum[...] = jnp.zeros_like(dk_sum)
    dv_sum[...] = jnp.zeros_like(dv_sum)
    bias_sum[...] = jnp.zeros_like(bias_sum)
    for r, g_ref in enumerate(g_refs):
        grad[pl.ds(pl.multiple_of((place[1] ^ r) * rows, rows), rows), :] = g_ref[...]

    def step(index, carry):
        start = pl.multiple_of(index * tile, tile)
        keys = k_pad[pl.ds(start, window), :]
        values = v_pad[pl.ds(start, window), :]
        q_all = spread_heads(q_ref[pl.ds(start, tile), :], heads, scale)
        g_all = spread_heads(grad[pl.ds(start, tile), :], heads, 1.0)
        powers, inverse = window_powers(q_all, keys, skew, seg_q_ref, seg_k_ref, start, heads)
        probs = powers * inverse
        dot_grad = dot(g_all, values, 1, 1)
        inner = jnp.sum(probs * dot_grad, axis=-1, keepdims=True)
        score_grad = (probs * (dot_grad - inner)).astype(bf16)
        bias_sum[...] += score_grad.astype(f32)
        part = collect_heads(dot(score_grad, keys, 1, 0), heads) * scale
        dq_ref[pl.ds(start, tile), :] = part.astype(bf16)
        dk_sum[pl.ds(start, window), :] += dot(score_grad, q_all, 0, 0)
        dv_sum[pl.ds(start, window), :] += dot(probs.astype(bf16), g_all, 0, 0)
        return carry

    lax.fori_loop(0, q_ref.shape[0] // tile, step, 0)
    dk_ref[...] = dk_sum[reach:, :].astype(bf16)
    dv_ref[...] = dv_sum[reach:, :].astype(bf16)
    line_grad_ref[...] = jnp.zeros_like(line_grad_ref)
    row = lax.broadcasted_iota(jnp.int32, (tile, tile), 0)
    column = lax.broadcasted_iota(jnp.int32, (tile, tile), 1)
    mirror = (row + column == tile - 1).astype(f32)
    for head in range(heads):
        part = bias_sum[head * tile : (head + 1) * tile, :]
        turned = dot(mirror, part, 1, 0, highest)
        straight = pltpu.roll(turned, window - tile + 1, 1, stride=1, stride_axis=0)
        line_grad_ref[head : head + 1, :] = jnp.sum(straight, axis=0, keepdims=True)


def attend_back(place, query, key_rows, value_rows, seg_q, seg_k, line, grads, heads):
    seq_len, span = query.shape
    window = reach + tile

    def kernel(place_ref, *refs):
        attend_back_kernel(heads, len(grads), place_ref, *refs)

    return call(
        kernel,
        "attend_back",
        [query, key_rows, value_rows, seg_q, seg_k, line] + grads,
        [shape((seq_len, span), bf16)] * 3 + [shape((8, window), f32)],
        scratch=[
            pltpu.VMEM((seq_len, span), bf16),
            pltpu.VMEM((seq_len + reach, span), bf16),
            pltpu.VMEM((seq_len + reach, span), bf16),
            pltpu.VMEM((heads * tile, window), f32),
            pltpu.VMEM((seq_len + reach, span), f32),
            pltpu.VMEM((seq_len + reach, span), f32),
            pltpu.VMEM((heads * tile, window), f32),
        ],
        flops=10 * seq_len * window * heads * 256,
        limit=48,
        scalars=place,
    )


def project(place, token_blocks, pack_blocks, gain, cotangent, span):
    rows, width = token_blocks[0].shape
    members = len(token_blocks)
    seq_len = rows * members
    parts = sum(len(held) for _, held in pack_blocks)
    part = width // parts

    def kernel(place_ref, gain_ref, cot_ref, *refs):
        token_refs = refs[:members]
        pack_refs = refs[members : members + len(pack_blocks)]
        (normed_ref, q_ref, k_ref, v_ref, wq_ref, wk_ref, wv_ref, wo_ref, late_ref, pack) = refs[
            members + len(pack_blocks) :
        ]
        for (_, held), ref in zip(pack_blocks, pack_refs):
            for i, r in enumerate(held):
                at = pl.multiple_of((place_ref[0] ^ r) * part, part) if parts > 1 else 0
                pack[pl.ds(at, part), :] = ref[i * part : (i + 1) * part, :]
        for at, ref in enumerate((wq_ref, wk_ref, wv_ref)):
            ref[...] = pack[:, at * span : (at + 1) * span]
        wo_ref[...] = pack[:, 3 * span :].astype(f32).T.astype(bf16)
        for r, ref in enumerate(token_refs):
            normed, _ = normalize(ref[...].astype(f32), gain_ref[...])
            normed = normed.astype(bf16)
            at = pl.ds(pl.multiple_of((place_ref[1] ^ r) * rows, rows), rows)
            normed_ref[at, :] = normed
            q_ref[at, :] = dot(normed, wq_ref[...], 1, 0).astype(bf16)
            k_ref[at, :] = dot(normed, wk_ref[...], 1, 0).astype(bf16)
            v_ref[at, :] = dot(normed, wv_ref[...], 1, 0).astype(bf16)
        late_ref[...] = cot_ref[...]

    return call(
        kernel,
        "project",
        [gain, cotangent] + list(token_blocks) + [array for array, _ in pack_blocks],
        [shape((seq_len, width), bf16)]
        + [shape((seq_len, span), bf16)] * 3
        + [shape((width, span), bf16)] * 3
        + [shape((span, width), bf16), shape((rows, width), bf16)],
        scratch=[pltpu.VMEM((width, width), bf16)],
        flops=2 * seq_len * width * 4 * span,
        scalars=place,
    )


def hot(slots_ref, first, count):
    tokens = slots_ref.shape[1]
    slot = lax.broadcasted_iota(jnp.int32, (count, tokens), 0) + first
    taken = (slot == slots_ref[0:1, :]) | (slot == slots_ref[1:2, :])
    return jnp.where(taken, 1.0, 0.0).astype(bf16)


def to_slots(name, sets, blocks, size):
    width = sets[0][0].shape[1]

    def kernel(*refs):
        out_refs = refs[2 * len(sets) :]
        for at in range(len(sets)):
            rows_ref, slots_ref = refs[2 * at], refs[2 * at + 1]
            for b, out_ref in enumerate(out_refs):
                part = dot(hot(slots_ref, b * size, size), rows_ref[...], 1, 0)
                out_ref[at * size : (at + 1) * size, :] = part.astype(bf16)

    operands = [item for pair in sets for item in pair]
    return call(
        kernel,
        name,
        operands,
        [shape((size * len(sets), width), bf16)] * blocks,
        flops=2 * len(sets) * blocks * size * sets[0][0].shape[0] * width,
    )


def from_slots(name, blocks, slots, size, dtypes):
    count, sets = len(blocks), len(slots)
    width = blocks[0].shape[1]
    rows = slots[0].shape[1]

    def kernel(*refs):
        block_refs, slot_refs, out_refs = refs[:count], refs[count : count + sets], refs[count + sets :]
        for at in range(sets):
            total = None
            for b, ref in enumerate(block_refs):
                held = ref[at * size : (at + 1) * size, :]
                part = dot(hot(slot_refs[at], b * size, size), held, 0, 0)
                total = part if total is None else total + part
            out_refs[at][...] = total.astype(out_refs[at].dtype)

    return call(
        kernel,
        name,
        list(blocks) + list(slots),
        [shape((rows, width), dtype) for dtype in dtypes],
        flops=2 * sets * count * size * rows * width,
    )


def router_softmax(values, w_router, experts):
    logits = dot(values, w_router, 1, 0)
    lane = lax.broadcasted_iota(jnp.int32, logits.shape, 1)
    logits = jnp.where(lane < experts, logits, excluded)
    powers = jnp.exp(logits - jnp.max(logits, axis=-1, keepdims=True))
    return powers / jnp.sum(powers, axis=-1, keepdims=True)


def middle(tokens, mixed, weight_o, gain, w_router, slots, experts, blocks, size):
    rows, width = tokens.shape
    members = len(mixed)

    def kernel(*refs):
        token_ref, gain_ref, router_ref, slots_ref = refs[:4]
        mixed_refs, weight_refs = refs[4 : 4 + members], refs[4 + members : 4 + 2 * members]
        hidden_ref, input_ref, probs_ref, *send_refs = refs[4 + 2 * members :]
        hidden = token_ref[...].astype(f32)
        for left, right in zip(mixed_refs, weight_refs):
            hidden = hidden + dot(left[...], right[...], 1, 0)
        hidden_ref[...] = hidden
        normed, _ = normalize(hidden, gain_ref[...])
        normed = normed.astype(bf16)
        input_ref[...] = normed
        for b, ref in enumerate(send_refs):
            ref[...] = dot(hot(slots_ref, b * size, size), normed, 1, 0).astype(bf16)
        probs_ref[...] = router_softmax(normed, router_ref[...], experts)

    return call(
        kernel,
        "middle",
        [tokens, gain, w_router, slots] + mixed + weight_o,
        [shape((rows, width), f32), shape((rows, width), bf16), shape((rows, 128), f32)]
        + [shape((size, width), bf16)] * blocks,
        flops=2 * rows * width * (width + blocks * size),
    )


def experts_kernel(count, grads, experts, me_ref, w_in_ref, w_out_ref, router_ref, *refs):
    x_refs, g_refs = refs[:count], refs[count : count + grads]
    refs = refs[count + grads :]
    back_refs, result_refs = refs[:count], refs[count : count + grads]
    active_ref, pre_grad_ref, x_all, s_all = refs[count + grads : count + grads + 4]
    gates, result_sum, back_sum = refs[count + grads + 4 :]
    step = pl.program_id(0)
    total, width = x_all.shape
    size = total // count
    chunk = min(256, total)

    def grad_rows():
        return jnp.concatenate([ref[...] for ref in g_refs], axis=0)

    @pl.when(step == 0)
    def _():
        for b, ref in enumerate(x_refs):
            x_all[b * size : (b + 1) * size, :] = ref[...]
        probs = router_softmax(x_all[...], router_ref[...], experts)
        lane = lax.broadcasted_iota(jnp.int32, probs.shape, 1)
        own = jnp.sum(jnp.where(lane == me_ref[0], probs, 0.0), axis=1, keepdims=True)
        gates[...] = jnp.broadcast_to(own, gates.shape)
        s_all[...] = (own * grad_rows().astype(f32)).astype(bf16)
        result_sum[...] = jnp.zeros_like(result_sum)
        back_sum[...] = jnp.zeros_like(back_sum)

    for c in range(total // chunk):
        at = slice(c * chunk, (c + 1) * chunk)
        pre_act = dot(x_all[at, :], w_in_ref[...], 1, 0)
        active_grad = dot(s_all[at, :], w_out_ref[...], 1, 1)
        below = 0.5 + 0.5 * lax.erf(pre_act * math.sqrt(0.5))
        active = (pre_act * below).astype(bf16)
        bell = jnp.exp(-0.5 * pre_act * pre_act) * (1.0 / math.sqrt(2.0 * math.pi))
        pre_grad = (active_grad * (below + pre_act * bell)).astype(bf16)
        active_ref[at, :] = active
        pre_grad_ref[at, :] = pre_grad
        result_sum[at, :] += dot(active, w_out_ref[...], 1, 0)
        back_sum[at, :] += dot(pre_grad, w_in_ref[...], 1, 1)

    @pl.when(step == pl.num_programs(0) - 1)
    def _():
        result = result_sum[...].astype(bf16).astype(f32)
        gate_grad = jnp.sum(grad_rows().astype(f32) * result, axis=1, keepdims=True)
        upper = gate_grad.astype(bf16).astype(f32)
        lane = lax.broadcasted_iota(jnp.int32, (total, 128), 1)
        columns = jnp.where(
            lane == me_ref[0], upper, jnp.where(lane == me_ref[0] + 64, gate_grad - upper, 0.0)
        ).astype(bf16)
        back = back_sum[...].astype(bf16)
        for b, ref in enumerate(back_refs):
            ref[:, :width] = back[b * size : (b + 1) * size, :]
            ref[:, width:] = columns[b * size : (b + 1) * size, :]
        gated = (gates[:, 0:1] * result).astype(bf16)
        each = total // grads
        for b, ref in enumerate(result_refs):
            ref[...] = gated[b * each : (b + 1) * each, :]


def run_experts(place, w_in, w_out, w_router, x_blocks, g_blocks, experts):
    width, units = w_in.shape
    count, grads = len(x_blocks), len(g_blocks)
    size, each = x_blocks[0].shape[0], g_blocks[0].shape[0]
    total = size * count
    piece = 512

    def whole(dims):
        return pl.BlockSpec(tuple(dims), lambda i: (0, 0))

    columns = pl.BlockSpec((total, piece), lambda i: (0, i))
    outs = (
        [shape((size, width + 128), bf16)] * count
        + [shape((each, width), bf16)] * grads
        + [shape((total, units), bf16)] * 2
        + [shape((total, width), bf16)] * 2
    )
    flat = pl.pallas_call(
        functools.partial(experts_kernel, count, grads, experts),
        name="run_experts",
        grid=(units // piece,),
        in_specs=[
            pl.BlockSpec(memory_space=pltpu.SMEM),
            pl.BlockSpec((width, piece), lambda i: (0, i)),
            pl.BlockSpec((piece, width), lambda i: (i, 0)),
            whole(w_router.shape),
        ]
        + [whole((size, width))] * count
        + [whole((each, width))] * grads,
        out_specs=[whole((size, width + 128))] * count
        + [whole((each, width))] * grads
        + [columns] * 2
        + [whole((total, width))] * 2,
        out_shape=outs,
        scratch_shapes=[
            pltpu.VMEM((total, 128), f32),
            pltpu.VMEM((total, width), f32),
            pltpu.VMEM((total, width), f32),
        ],
        compiler_params=pltpu.CompilerParams(vmem_limit_bytes=56 * 1024 * 1024),
        cost_estimate=pl.CostEstimate(
            flops=8 * total * width * units,
            bytes_accessed=4 * width * units + 4 * total * units,
            transcendentals=2 * total * units,
        ),
    )(place, w_in, w_out, w_router, *x_blocks, *g_blocks)
    return (
        flat[:count],
        flat[count : count + grads],
        *flat[count + grads :],
    )


def home(own_back, far_sum, slots, hidden, probs, cotangent, gain, w_router, weight_o, size):
    rows, width = hidden.shape
    count, members = len(own_back), len(weight_o)
    span = weight_o[0].shape[0]
    far = [] if far_sum is None else [far_sum]

    def kernel(*refs):
        slots_ref, hidden_ref, probs_ref, cot_ref, gain_ref, router_ref = refs[:6]
        back_refs = refs[6 : 6 + count]
        far_refs = refs[6 + count : 6 + count + len(far)]
        weight_refs = refs[6 + count + len(far) : 6 + count + len(far) + members]
        outs = refs[6 + count + len(far) + members :]
        grad_refs = outs[:members]
        attn_ref, hidden_grad_ref, gain_grad_ref, logit_ref = outs[members:]
        total = None
        for b, ref in enumerate(back_refs):
            part = dot(hot(slots_ref, b * size, size), ref[...], 0, 0)
            total = part if total is None else total + part
        for ref in far_refs:
            total = total + ref[...].astype(f32)
        columns = total[:, width:]
        lane = lax.broadcasted_iota(jnp.int32, columns.shape, 1)
        prob_grad = jnp.where(lane < 64, columns + pltpu.roll(columns, 64, 1), 0.0)
        router_probs = probs_ref[...]
        logit_grad = router_probs * (
            prob_grad - jnp.sum(router_probs * prob_grad, axis=-1, keepdims=True)
        )
        logit_ref[...] = logit_grad
        grad = total[:, :width] + dot(logit_grad, router_ref[...].astype(f32), 1, 1, highest)
        hidden_now = hidden_ref[...]
        inverse = lax.rsqrt(jnp.mean(hidden_now * hidden_now, axis=-1, keepdims=True) + eps)
        scaled = grad * gain_ref[...]
        gain_grad_ref[...] = jnp.sum(grad * hidden_now * inverse, axis=0, keepdims=True)
        inner = jnp.mean(scaled * hidden_now, axis=-1, keepdims=True)
        hidden_grad = (
            cot_ref[...].astype(f32)
            + inverse * scaled
            - hidden_now * inverse * inverse * inverse * inner
        )
        hidden_grad_ref[...] = hidden_grad
        attn_grad = hidden_grad.astype(bf16)
        attn_ref[...] = attn_grad
        for ref, weight in zip(grad_refs, weight_refs):
            ref[...] = dot(attn_grad, weight[...], 1, 1).astype(bf16)

    return call(
        kernel,
        "home",
        [slots, hidden, probs, cotangent, gain, w_router] + list(own_back) + far + weight_o,
        [shape((rows, span), bf16)] * members
        + [
            shape((rows, width), bf16),
            shape((rows, width), f32),
            shape((1, width), f32),
            shape((rows, 128), f32),
        ],
        flops=2 * rows * width * (width + size * count),
    )


def input_grads(place, proj_grads, normed, weights, output_sum, gain, members, owners):
    seq_len, width = normed.shape
    span = weights[0].shape[1]
    rows = seq_len // members
    part = width // owners
    few = owners == 8

    def kernel(place_ref, *refs):
        dq_ref, dk_ref, dv_ref, normed_ref, wq_ref, wk_ref, wv_ref, out_ref, gain_ref = refs[:9]
        near_ref, base_ref, gain_grad_ref, *weight_refs, sums = refs[9:]
        for at, ref in enumerate((dq_ref, dk_ref, dv_ref)):
            sums[:, at * span : (at + 1) * span] = dot(normed_ref[...], ref[...], 0, 0)
        sums[:, 3 * span :] = out_ref[...]
        if few:
            for r, ref in enumerate(weight_refs):
                for i, far in enumerate((0, 4)):
                    at = pl.multiple_of((place_ref[0] ^ r ^ far) * part, part)
                    ref[i * part : (i + 1) * part, :] = sums[pl.ds(at, part), :].astype(ref.dtype)
        else:
            weight_refs[0][...] = sums[...]
        gain_grad = jnp.zeros((1, width), f32)
        for r, (ref, first) in enumerate(
            ((base_ref, 0), (near_ref, 0), (base_ref, rows), (near_ref, rows))
        ):
            at = pl.ds(pl.multiple_of((place_ref[1] ^ r) * rows, rows), rows)
            grad = (
                dot(dq_ref[at, :], wq_ref[...], 1, 1)
                + dot(dk_ref[at, :], wk_ref[...], 1, 1)
                + dot(dv_ref[at, :], wv_ref[...], 1, 1)
            )
            gain_grad = gain_grad + jnp.sum(
                grad * normed_ref[at, :].astype(f32), axis=0, keepdims=True
            )
            ref[first : first + rows, :] = grad.astype(ref.dtype)
        gain_grad_ref[...] = gain_grad / gain_ref[...]

    if few:
        weight_outs = [shape((2 * part, 4 * span), f32)] + [shape((2 * part, 4 * span), bf16)] * 3
    else:
        weight_outs = [shape((width, 4 * span), f32)]
    return call(
        kernel,
        "input_grads",
        list(proj_grads) + [normed] + list(weights) + [output_sum, gain],
        [shape((2 * rows, width), bf16), shape((2 * rows, width), f32), shape((1, width), f32)]
        + weight_outs,
        scratch=[pltpu.VMEM((width, 4 * span), f32)],
        flops=4 * seq_len * width * 3 * span,
        limit=48,
        scalars=place,
    )


def gather_mp(values):
    across = swap(values, "mp", 2)
    return [values, swap(values, "mp", 1), across, swap(across, "mp", 1)]


def scatter_sum_mp(blocks):
    near = swap(jnp.concatenate([blocks[1], blocks[3]], axis=0).astype(bf16), "mp", 1)
    size = blocks[0].shape[0]
    far = blocks[2].astype(f32) + near[size:].astype(f32)
    far = swap(far.astype(bf16), "mp", 2)
    return blocks[0].astype(f32) + near[:size].astype(f32) + far.astype(f32)


def sum_all(values):
    for axis in ("mp", "dp"):
        step = 1
        while step < lax.axis_size(axis):
            values = values + swap(values, axis, step)
            step = 2 * step
    return values


def all_to_all_dp(values):
    return lax.all_to_all(values, "dp", split_axis=0, concat_axis=0, tiled=True)


def slots_of(routes, place, capacity, experts, limit):
    rows = routes.shape[0]
    expert_ids = jnp.arange(experts, dtype=jnp.int32)[None, :]
    hits = (routes[:, 0:1] == expert_ids) | (routes[:, 1:2] == expert_ids)
    earlier = jnp.arange(rows)[:, None] > jnp.arange(rows)[None, :]
    ranks = jnp.dot(earlier.astype(bf16), hits.astype(bf16), preferred_element_type=f32)
    lines = []
    for k in (0, 1):
        rank = jnp.sum(jnp.where(routes[:, k : k + 1] == expert_ids, ranks, 0.0), axis=1)
        block = routes[:, k] ^ place
        lines.append(jnp.where(block < limit, block * capacity + rank.astype(jnp.int32), -1))
    return jnp.pad(jnp.stack(lines), ((0, 6), (0, 0)), constant_values=-1)


def on_device(
    tokens,
    norm_gain,
    w_query,
    w_key,
    w_value,
    w_output,
    bias_table,
    ffn_gain,
    w_router,
    w_in,
    w_out,
    segments,
    buckets,
    routes,
    cotangent,
):
    rows, width = tokens.shape
    heads = bias_table.shape[1]
    seq_len = buckets.shape[0]
    experts = w_router.shape[1]
    owners, members = lax.axis_size("dp"), lax.axis_size("mp")
    me, member = lax.axis_index("dp"), lax.axis_index("mp")
    place = jnp.stack([me, member]).astype(jnp.int32)
    capacity = 4 * rows // experts
    span = w_query.shape[1]
    window = reach + tile
    few = owners == 8

    token_blocks = gather_mp(tokens)
    pack = jnp.concatenate([w_query, w_key, w_value, w_output.T], axis=1)
    if few:
        both = jnp.concatenate([pack, swap(pack, "dp", 4)], axis=0)
        pack_blocks = [(both, (0, 4))] + [(swap(both, "dp", r), (r, r ^ 4)) for r in (1, 2, 3)]
    else:
        pack_blocks = [(lax.all_gather(pack, "dp", axis=0, tiled=True), (0,))]
    gain_one, gain_two = norm_gain.reshape(1, width), ffn_gain.reshape(1, width)
    normed, query, key_rows, value_rows, weight_q, weight_k, weight_v, w_o, late_cotangent = (
        project(place, token_blocks, pack_blocks, gain_one, cotangent, span)
    )
    weight_o = gather_mp(w_o)

    if few:
        blocks, size = 4, capacity
        slots = [slots_of(routes, me, capacity, experts, 4)]
        slots.append(slots_of(swap(routes, "dp", 4), me, capacity, experts, 4))
    else:
        blocks, size = 1, experts * capacity
        slots = [slots_of(routes, 0, capacity, experts, experts)]

    if few:
        far_cotangent = swap(late_cotangent, "dp", 4)
        held = to_slots(
            "grads_to_slots",
            [(late_cotangent, slots[0]), (far_cotangent, slots[1])],
            blocks,
            size,
        )
        g_blocks = [held[0]] + [swap(held[r], "dp", r) for r in (1, 2, 3)]
    else:
        held = to_slots("grads_to_slots", [(late_cotangent, slots[0])], blocks, size)
        g_blocks = [all_to_all_dp(held[0])]

    line_buckets = jnp.pad(jnp.flip(buckets[: reach + 1]), (0, window - reach - 1))
    bucket_hot = (
        line_buckets[:, None] == jnp.arange(bias_table.shape[0], dtype=jnp.int32)[None, :]
    ).astype(f32)
    line = jnp.dot(bias_table.T, bucket_hot.T, precision=highest)
    line = jnp.pad(line, ((0, 8 - heads), (0, 0)))
    seg_q = segments.reshape(seq_len, 1)
    seg_k = jnp.pad(segments.reshape(1, seq_len), ((0, 0), (reach, 0)), constant_values=-1)
    mixed_out = attend(place, query, key_rows, value_rows, seg_q, seg_k, line, heads, members)
    mixed_in = [mixed_out[0]] + [swap(mixed_out[r], "mp", r) for r in range(1, members)]

    router_wide = jnp.pad(w_router, ((0, 0), (0, 128 - experts)))
    hidden, ffn_input, router_probs, *send = middle(
        tokens, mixed_in, weight_o, gain_two, router_wide, slots[0], experts, blocks, size
    )
    if few:
        far_input = swap(ffn_input, "dp", 4)
        own = [send[0]] + [swap(send[r], "dp", r) for r in (1, 2, 3)]
        far = to_slots("far_to_slots", [(far_input, slots[1])], blocks, size)
        far = [far[0]] + [swap(far[r], "dp", r) for r in (1, 2, 3)]
        x_blocks = [item for pair in zip(own, far) for item in pair]
    else:
        x_blocks = [all_to_all_dp(send[0])]

    back, result, active, pre_grad, arrived, slot_grad = run_experts(
        place, w_in[0], w_out[0], router_wide, x_blocks, g_blocks, experts
    )
    if few:
        far_back = [back[1]] + [swap(back[2 * r + 1], "dp", r) for r in (1, 2, 3)]
        (far_total,) = from_slots("back_from_slots", far_back, [slots[1]], size, [bf16])
        far_sum = swap(far_total, "dp", 4)
        own_back = [back[0]] + [swap(back[2 * r], "dp", r) for r in (1, 2, 3)]
    else:
        own_back, far_sum = [all_to_all_dp(back[0])], None

    *grad_out, attn_grad, hidden_grad, ffn_gain_grad, logit_grad = home(
        own_back,
        far_sum,
        slots[0],
        hidden,
        router_probs,
        cotangent,
        gain_two,
        router_wide,
        weight_o,
        size,
    )
    grad_in = [grad_out[0]] + [swap(grad_out[r], "mp", r) for r in range(1, members)]

    *proj_grads, line_grad = attend_back(
        place, query, key_rows, value_rows, seg_q, seg_k, line, grad_in, heads
    )
    output_sum = scatter_sum_mp([dot(attn_grad, part, 0, 0) for part in mixed_in])
    near, base, gain_part, *weight_sums = input_grads(
        place,
        proj_grads,
        normed,
        (weight_q, weight_k, weight_v),
        output_sum,
        gain_one,
        members,
        owners,
    )
    if few:
        total = weight_sums[0]
        for r in (1, 2, 3):
            total = total + swap(weight_sums[r], "dp", r).astype(f32)
        part = width // owners
        far_part = swap(total[part:].astype(bf16), "dp", 4)
        joined_grad = total[:part] + far_part.astype(f32)
    else:
        joined_grad = lax.psum_scatter(weight_sums[0], "dp", scatter_dimension=0, tiled=True)
    near = base + swap(near, "mp", 1).astype(f32)
    normed_grad = near[:rows] + swap(near[rows:].astype(bf16), "mp", 2).astype(f32)
    resid = tokens.astype(f32)
    _, inverse_one = normalize(resid, norm_gain)
    scaled = normed_grad * norm_gain
    inner = jnp.mean(scaled * resid, axis=-1, keepdims=True)
    tokens_grad = (
        hidden_grad + inverse_one * scaled - resid * inverse_one * inverse_one * inverse_one * inner
    ).astype(bf16)

    if few:
        result_in = [result[0]] + [swap(result[r], "dp", r) for r in (1, 2, 3)]
        own_result, far_result = from_slots(
            "result_from_slots", result_in, slots, size, [f32, bf16]
        )
        block_out = hidden + own_result + swap(far_result, "dp", 4).astype(f32)
    else:
        (own_result,) = from_slots(
            "result_from_slots", [all_to_all_dp(result[0])], slots, size, [f32]
        )
        block_out = hidden + own_result
    block_out = block_out.astype(bf16)

    piece = w_in.shape[2] // members

    def hidden_cut(values, axis):
        return [
            lax.dynamic_slice_in_dim(values, (member ^ r) * piece, piece, axis)
            for r in range(members)
        ]

    w_in_grad = scatter_sum_mp([dot(arrived, part, 0, 0) for part in hidden_cut(pre_grad, 1)])
    w_out_grad = scatter_sum_mp([dot(part, slot_grad, 0, 0) for part in hidden_cut(active, 1)])

    router_grad = jnp.dot(ffn_input.astype(f32).T, logit_grad[:, :experts], precision=highest)
    table_local = jnp.dot(bucket_hot.T, line_grad[:heads].T, precision=highest)
    table_full = jnp.zeros((bias_table.shape[0], heads * members), f32)
    table_full = lax.dynamic_update_slice_in_dim(table_full, table_local, member * heads, 1)
    pieces = [router_grad, table_full, gain_part, ffn_gain_grad]
    sums = sum_all(jnp.concatenate([item.reshape(-1) for item in pieces]))
    ends = [0]
    for item in pieces:
        ends.append(ends[-1] + item.size)
    router_sum, table_sum, gain_sum, ffn_gain_sum = [
        sums[ends[i] : ends[i + 1]].reshape(pieces[i].shape) for i in range(4)
    ]
    return (
        block_out,
        tokens_grad,
        gain_sum.reshape(width),
        joined_grad[:, :span],
        joined_grad[:, span : 2 * span],
        joined_grad[:, 2 * span : 3 * span],
        joined_grad[:, 3 * span :].T,
        table_sum,
        ffn_gain_sum.reshape(width),
        router_sum,
        w_in_grad[None],
        w_out_grad[None],
    )


def solution(mesh):
    return jax.shard_map(
        on_device,
        mesh=mesh,
        in_specs=(
            P(("dp", "mp"), None),
            P(),
            P("dp", "mp"),
            P("dp", "mp"),
            P("dp", "mp"),
            P("mp", "dp"),
            P(None, "mp"),
            P(),
            P(),
            P("dp", None, None),
            P("dp", None, None),
            P("dp", None),
            P(),
            P(("dp", "mp"), None),
            P(("dp", "mp"), None),
        ),
        out_specs=(
            P(("dp", "mp"), None),
            P(("dp", "mp"), None),
            P(),
            P("dp", "mp"),
            P("dp", "mp"),
            P("dp", "mp"),
            P("mp", "dp"),
            P(),
            P(),
            P(),
            P("dp", None, "mp"),
            P("dp", "mp", None),
        ),
        check_vma=False,
    )
```

```python
import functools
import math

import jax
import jax.numpy as jnp
from jax import lax
from jax.experimental import pallas as pl
from jax.experimental.pallas import tpu as pltpu
from jax.sharding import PartitionSpec as P

eps = 1e-06
highest = lax.Precision.HIGHEST
f32, bf16 = jnp.float32, jnp.bfloat16
excluded = -1e30
reach = 512
tile = 128


def normalize(values, gain):
    inverse = lax.rsqrt(jnp.mean(values * values, axis=-1, keepdims=True) + eps)
    return (values * inverse * gain, inverse)


def dot(left, right, left_dim, right_dim, precision=None):
    return lax.dot_general(
        left,
        right,
        (((left_dim,), (right_dim,)), ((), ())),
        precision=precision,
        preferred_element_type=f32,
    )


def swap(values, axis, step):
    count = lax.axis_size(axis)
    return lax.ppermute(values, axis, [(i, i ^ step) for i in range(count)])


def whole(dims):
    return pl.BlockSpec(tuple(dims), lambda *_: (0,) * len(dims), pipeline_mode=pl.Buffered(1))


def call(
    kernel, name, operands, outs, scratch=(), flops=0, limit=32, scalars=None, after=(), through=()
):
    operands, outs = list(operands), list(outs)
    moved = sum(math.prod(o.shape) * o.dtype.itemsize for o in operands + outs)
    in_specs = [whole(o.shape) for o in operands]
    out_specs = [whole(o.shape) for o in outs]
    if scalars is not None:
        operands = [scalars] + operands
        in_specs = [pl.BlockSpec(memory_space=pltpu.SMEM)] + in_specs
    count, results = len(operands), len(outs)
    extra = list(through) + list(after)

    def body(*refs):
        rest = refs[count + len(extra) :]
        kernel(*refs[:count], *rest[:results], *rest[results + len(through) :])

    return pl.pallas_call(
        body,
        name=name,
        grid=(1,),
        in_specs=in_specs + [pl.BlockSpec(memory_space=pl.ANY)] * len(extra),
        out_specs=out_specs + [pl.BlockSpec(memory_space=pl.ANY)] * len(through),
        out_shape=outs + [shape(o.shape, o.dtype) for o in through],
        input_output_aliases={count + i: results + i for i in range(len(through))},
        scratch_shapes=list(scratch),
        compiler_params=pltpu.CompilerParams(vmem_limit_bytes=limit * 1024 * 1024),
        cost_estimate=pl.CostEstimate(
            flops=int(flops), bytes_accessed=int(moved), transcendentals=0
        ),
    )(*operands, *extra)


def shape(dims, dtype):
    return jax.ShapeDtypeStruct(tuple(dims), dtype)


def fill_skew(line_ref, skew, heads):
    window = reach + tile
    row = lax.broadcasted_iota(jnp.int32, (tile, window), 0)
    column = lax.broadcasted_iota(jnp.int32, (tile, window), 1)
    usable = (column - row <= reach) & (column - row >= 1)
    for head in range(heads):
        line = jnp.broadcast_to(line_ref[head : head + 1, :], (tile, window))
        rolled = pltpu.roll(line, 0, 1, stride=1, stride_axis=0)
        skew[head * tile : (head + 1) * tile, :] = jnp.where(usable, rolled, excluded)


def fill_window(source_ref, padded):
    padded[:reach, :] = jnp.zeros((reach, padded.shape[1]), bf16)
    padded[reach:, :] = source_ref[...]


def spread_heads(values, heads, scale):
    span = values.shape[1]
    size = span // heads
    lane = lax.broadcasted_iota(jnp.int32, (tile, span), 1)
    wide = values.astype(f32) * scale
    parts = [
        jnp.where((lane >= head * size) & (lane < (head + 1) * size), wide, 0.0)
        for head in range(heads)
    ]
    return jnp.concatenate(parts, axis=0).astype(bf16)


def collect_heads(stacked, heads):
    span = stacked.shape[1]
    size = span // heads
    lane = lax.broadcasted_iota(jnp.int32, (tile, span), 1)
    total = stacked[:tile, :]
    for head in range(1, heads):
        total = jnp.where(lane < head * size, total, stacked[head * tile : (head + 1) * tile, :])
    return total


def window_powers(q_all, keys, skew, seg_q_ref, seg_k_ref, start, heads):
    window = reach + tile
    seg_q = jnp.concatenate([seg_q_ref[pl.ds(start, tile), :]] * heads, axis=0)
    seg_k = seg_k_ref[:, pl.ds(start, window)]
    scores = dot(q_all, keys, 1, 1) + skew[...]
    scores = jnp.where(seg_q == seg_k, scores, excluded)
    powers = jnp.exp(scores - jnp.max(scores, axis=-1, keepdims=True))
    return powers, 1.0 / jnp.sum(powers, axis=-1, keepdims=True)


def attend_kernel(heads, place, q_ref, k_ref, v_ref, seg_q_ref, seg_k_ref, line_ref, *rest):
    *out_refs, mixed, k_pad, v_pad, skew = rest
    window = reach + tile
    scale = (q_ref.shape[1] // heads) ** (-0.5)
    fill_skew(line_ref, skew, heads)
    fill_window(k_ref, k_pad)
    fill_window(v_ref, v_pad)

    def step(index, carry):
        start = pl.multiple_of(index * tile, tile)
        q_all = spread_heads(q_ref[pl.ds(start, tile), :], heads, scale)
        powers, inverse = window_powers(
            q_all, k_pad[pl.ds(start, window), :], skew, seg_q_ref, seg_k_ref, start, heads
        )
        probs = (powers * inverse).astype(bf16)
        part = dot(probs, v_pad[pl.ds(start, window), :], 1, 0)
        mixed[pl.ds(start, tile), :] = collect_heads(part, heads).astype(bf16)
        return carry

    lax.fori_loop(0, q_ref.shape[0] // tile, step, 0)
    rows = out_refs[0].shape[0]
    for r, out_ref in enumerate(out_refs):
        out_ref[...] = mixed[pl.ds(pl.multiple_of((place[1] ^ r) * rows, rows), rows), :]


def attend(place, query, key_rows, value_rows, seg_q, seg_k, line, heads, members, after):
    seq_len, span = query.shape
    window = reach + tile

    def kernel(place_ref, *refs):
        attend_kernel(heads, place_ref, *refs)

    return call(
        kernel,
        "attend",
        [query, key_rows, value_rows, seg_q, seg_k, line],
        [shape((seq_len // members, span), bf16)] * members,
        scratch=[
            pltpu.VMEM((seq_len, span), bf16),
            pltpu.VMEM((seq_len + reach, span), bf16),
            pltpu.VMEM((seq_len + reach, span), bf16),
            pltpu.VMEM((heads * tile, window), f32),
        ],
        flops=4 * seq_len * window * heads * 256,
        scalars=place,
        after=after,
    )


def attend_back_kernel(heads, members, place, *refs):
    q_ref, k_ref, v_ref, seg_q_ref, seg_k_ref, line_ref = refs[:6]
    g_refs = refs[6 : 6 + members]
    dq_ref, dk_ref, dv_ref, line_grad_ref = refs[6 + members : 10 + members]
    grad, k_pad, v_pad, skew, dk_sum, dv_sum, bias_sum = refs[10 + members :]
    window = reach + tile
    scale = (q_ref.shape[1] // heads) ** (-0.5)
    rows = g_refs[0].shape[0]
    fill_skew(line_ref, skew, heads)
    fill_window(k_ref, k_pad)
    fill_window(v_ref, v_pad)
    dk_sum[...] = jnp.zeros_like(dk_sum)
    dv_sum[...] = jnp.zeros_like(dv_sum)
    bias_sum[...] = jnp.zeros_like(bias_sum)
    for r, g_ref in enumerate(g_refs):
        grad[pl.ds(pl.multiple_of((place[1] ^ r) * rows, rows), rows), :] = g_ref[...]

    def step(index, carry):
        start = pl.multiple_of(index * tile, tile)
        keys = k_pad[pl.ds(start, window), :]
        values = v_pad[pl.ds(start, window), :]
        q_all = spread_heads(q_ref[pl.ds(start, tile), :], heads, scale)
        g_all = spread_heads(grad[pl.ds(start, tile), :], heads, 1.0)
        powers, inverse = window_powers(q_all, keys, skew, seg_q_ref, seg_k_ref, start, heads)
        probs = powers * inverse
        dot_grad = dot(g_all, values, 1, 1)
        inner = jnp.sum(probs * dot_grad, axis=-1, keepdims=True)
        score_grad = (probs * (dot_grad - inner)).astype(bf16)
        bias_sum[...] += score_grad.astype(f32)
        part = collect_heads(dot(score_grad, keys, 1, 0), heads) * scale
        dq_ref[pl.ds(start, tile), :] = part.astype(bf16)
        dk_sum[pl.ds(start, window), :] += dot(score_grad, q_all, 0, 0)
        dv_sum[pl.ds(start, window), :] += dot(probs.astype(bf16), g_all, 0, 0)
        return carry

    lax.fori_loop(0, q_ref.shape[0] // tile, step, 0)
    dk_ref[...] = dk_sum[reach:, :].astype(bf16)
    dv_ref[...] = dv_sum[reach:, :].astype(bf16)
    line_grad_ref[...] = jnp.zeros_like(line_grad_ref)
    row = lax.broadcasted_iota(jnp.int32, (tile, tile), 0)
    column = lax.broadcasted_iota(jnp.int32, (tile, tile), 1)
    mirror = (row + column == tile - 1).astype(f32)
    for head in range(heads):
        part = bias_sum[head * tile : (head + 1) * tile, :]
        turned = dot(mirror, part, 1, 0, highest)
        straight = pltpu.roll(turned, window - tile + 1, 1, stride=1, stride_axis=0)
        line_grad_ref[head : head + 1, :] = jnp.sum(straight, axis=0, keepdims=True)


def attend_back(place, query, key_rows, value_rows, seg_q, seg_k, line, grads, heads, after):
    seq_len, span = query.shape
    window = reach + tile

    def kernel(place_ref, *refs):
        attend_back_kernel(heads, len(grads), place_ref, *refs)

    return call(
        kernel,
        "attend_back",
        [query, key_rows, value_rows, seg_q, seg_k, line] + grads,
        [shape((seq_len, span), bf16)] * 3 + [shape((8, window), f32)],
        scratch=[
            pltpu.VMEM((seq_len, span), bf16),
            pltpu.VMEM((seq_len + reach, span), bf16),
            pltpu.VMEM((seq_len + reach, span), bf16),
            pltpu.VMEM((heads * tile, window), f32),
            pltpu.VMEM((seq_len + reach, span), f32),
            pltpu.VMEM((seq_len + reach, span), f32),
            pltpu.VMEM((heads * tile, window), f32),
        ],
        flops=10 * seq_len * window * heads * 256,
        limit=48,
        scalars=place,
        after=after,
    )


def pack_weights(w_query, w_key, w_value, w_output):
    part, span = w_query.shape

    def kernel(q_ref, k_ref, v_ref, o_ref, pack_ref):
        for at, ref in enumerate((q_ref, k_ref, v_ref)):
            pack_ref[:, at * span : (at + 1) * span] = ref[...]
        pack_ref[:, 3 * span :] = o_ref[...].astype(f32).T.astype(bf16)

    (pack,) = call(
        kernel, "pack_weights", [w_query, w_key, w_value, w_output], [shape((part, 4 * span), bf16)]
    )
    return pack


def pair_up(pack, far, cotangent):
    part = pack.shape[0]

    def kernel(near_ref, far_ref, both_ref):
        both_ref[:part, :] = near_ref[...]
        both_ref[part:, :] = far_ref[...]

    return call(
        kernel,
        "pair_up",
        [pack, far],
        [shape((2 * part, pack.shape[1]), bf16)],
        through=[cotangent],
    )


def project(place, token_blocks, pack_blocks, gain, span):
    rows, width = token_blocks[0].shape
    members = len(token_blocks)
    seq_len = rows * members
    parts = sum(len(held) for _, held in pack_blocks)
    part = width // parts

    def kernel(place_ref, gain_ref, *refs):
        token_refs = refs[:members]
        pack_refs = refs[members : members + len(pack_blocks)]
        (normed_ref, q_ref, k_ref, v_ref, wq_ref, wk_ref, wv_ref, wo_ref, pack) = refs[
            members + len(pack_blocks) :
        ]
        for (_, held), ref in zip(pack_blocks, pack_refs):
            for i, r in enumerate(held):
                at = pl.multiple_of((place_ref[0] ^ r) * part, part) if parts > 1 else 0
                pack[pl.ds(at, part), :] = ref[i * part : (i + 1) * part, :]
        for at, ref in enumerate((wq_ref, wk_ref, wv_ref)):
            ref[...] = pack[:, at * span : (at + 1) * span]
        wo_ref[...] = pack[:, 3 * span :].astype(f32).T.astype(bf16)
        for r, ref in enumerate(token_refs):
            normed, _ = normalize(ref[...].astype(f32), gain_ref[...])
            normed = normed.astype(bf16)
            at = pl.ds(pl.multiple_of((place_ref[1] ^ r) * rows, rows), rows)
            normed_ref[at, :] = normed
            q_ref[at, :] = dot(normed, wq_ref[...], 1, 0).astype(bf16)
            k_ref[at, :] = dot(normed, wk_ref[...], 1, 0).astype(bf16)
            v_ref[at, :] = dot(normed, wv_ref[...], 1, 0).astype(bf16)

    return call(
        kernel,
        "project",
        [gain] + list(token_blocks) + [array for array, _ in pack_blocks],
        [shape((seq_len, width), bf16)]
        + [shape((seq_len, span), bf16)] * 3
        + [shape((width, span), bf16)] * 3
        + [shape((span, width), bf16)],
        scratch=[pltpu.VMEM((width, width), bf16)],
        flops=2 * seq_len * width * 4 * span,
        scalars=place,
    )


def hot(slots_ref, first, count):
    tokens = slots_ref.shape[1]
    slot = lax.broadcasted_iota(jnp.int32, (count, tokens), 0) + first
    taken = (slot == slots_ref[0:1, :]) | (slot == slots_ref[1:2, :])
    return jnp.where(taken, 1.0, 0.0).astype(bf16)


def to_slots(name, sets, blocks, size):
    width = sets[0][0].shape[1]

    def kernel(*refs):
        out_refs = refs[2 * len(sets) :]
        for at in range(len(sets)):
            rows_ref, slots_ref = refs[2 * at], refs[2 * at + 1]
            for b, out_ref in enumerate(out_refs):
                part = dot(hot(slots_ref, b * size, size), rows_ref[...], 1, 0)
                out_ref[at * size : (at + 1) * size, :] = part.astype(bf16)

    operands = [item for pair in sets for item in pair]
    return call(
        kernel,
        name,
        operands,
        [shape((size * len(sets), width), bf16)] * blocks,
        flops=2 * len(sets) * blocks * size * sets[0][0].shape[0] * width,
    )


def from_slots(name, blocks, slots, size, dtypes, after=(), through=()):
    count, sets = len(blocks), len(slots)
    width = blocks[0].shape[1]
    rows = slots[0].shape[1]

    def kernel(*refs):
        block_refs, slot_refs, out_refs = refs[:count], refs[count : count + sets], refs[count + sets :]
        for at in range(sets):
            total = None
            for b, ref in enumerate(block_refs):
                held = ref[at * size : (at + 1) * size, :]
                part = dot(hot(slot_refs[at], b * size, size), held, 0, 0)
                total = part if total is None else total + part
            out_refs[at][...] = total.astype(out_refs[at].dtype)

    return call(
        kernel,
        name,
        list(blocks) + list(slots),
        [shape((rows, width), dtype) for dtype in dtypes],
        flops=2 * sets * count * size * rows * width,
        after=after,
        through=through,
    )


def router_softmax(values, w_router, experts):
    logits = dot(values, w_router, 1, 0)
    lane = lax.broadcasted_iota(jnp.int32, logits.shape, 1)
    logits = jnp.where(lane < experts, logits, excluded)
    powers = jnp.exp(logits - jnp.max(logits, axis=-1, keepdims=True))
    return powers / jnp.sum(powers, axis=-1, keepdims=True)


def middle(tokens, mixed, weight_o, gain, w_router, slots, experts, blocks, size, after):
    rows, width = tokens.shape
    members = len(mixed)

    def kernel(*refs):
        token_ref, gain_ref, router_ref, slots_ref = refs[:4]
        mixed_refs, weight_refs = refs[4 : 4 + members], refs[4 + members : 4 + 2 * members]
        hidden_ref, input_ref, probs_ref, *send_refs = refs[4 + 2 * members :]
        hidden = token_ref[...].astype(f32)
        for left, right in zip(mixed_refs, weight_refs):
            hidden = hidden + dot(left[...], right[...], 1, 0)
        hidden_ref[...] = hidden
        normed, _ = normalize(hidden, gain_ref[...])
        normed = normed.astype(bf16)
        input_ref[...] = normed
        for b, ref in enumerate(send_refs):
            ref[...] = dot(hot(slots_ref, b * size, size), normed, 1, 0).astype(bf16)
        probs_ref[...] = router_softmax(normed, router_ref[...], experts)

    return call(
        kernel,
        "middle",
        [tokens, gain, w_router, slots] + mixed + weight_o,
        [shape((rows, width), f32), shape((rows, width), bf16), shape((rows, 128), f32)]
        + [shape((size, width), bf16)] * blocks,
        flops=2 * rows * width * (width + blocks * size),
        after=after,
    )


def experts_kernel(count, grads, experts, me_ref, w_in_ref, w_out_ref, router_ref, *refs):
    x_refs, g_refs = refs[:count], refs[count : count + grads]
    refs = refs[count + grads :]
    back_refs, result_refs = refs[:count], refs[count : count + grads]
    active_ref, pre_grad_ref, x_all, s_all = refs[count + grads : count + grads + 4]
    gates, result_sum, back_sum = refs[count + grads + 4 :]
    step = pl.program_id(0)
    total, width = x_all.shape
    size = total // count
    chunk = min(256, total)

    def grad_rows():
        return jnp.concatenate([ref[...] for ref in g_refs], axis=0)

    @pl.when(step == 0)
    def _():
        for b, ref in enumerate(x_refs):
            x_all[b * size : (b + 1) * size, :] = ref[...]
        probs = router_softmax(x_all[...], router_ref[...], experts)
        lane = lax.broadcasted_iota(jnp.int32, probs.shape, 1)
        own = jnp.sum(jnp.where(lane == me_ref[0], probs, 0.0), axis=1, keepdims=True)
        gates[...] = jnp.broadcast_to(own, gates.shape)
        s_all[...] = (own * grad_rows().astype(f32)).astype(bf16)
        result_sum[...] = jnp.zeros_like(result_sum)
        back_sum[...] = jnp.zeros_like(back_sum)

    for c in range(total // chunk):
        at = slice(c * chunk, (c + 1) * chunk)
        pre_act = dot(x_all[at, :], w_in_ref[...], 1, 0)
        active_grad = dot(s_all[at, :], w_out_ref[...], 1, 1)
        below = 0.5 + 0.5 * lax.erf(pre_act * math.sqrt(0.5))
        active = (pre_act * below).astype(bf16)
        bell = jnp.exp(-0.5 * pre_act * pre_act) * (1.0 / math.sqrt(2.0 * math.pi))
        pre_grad = (active_grad * (below + pre_act * bell)).astype(bf16)
        active_ref[at, :] = active
        pre_grad_ref[at, :] = pre_grad
        result_sum[at, :] += dot(active, w_out_ref[...], 1, 0)
        back_sum[at, :] += dot(pre_grad, w_in_ref[...], 1, 1)

    @pl.when(step == pl.num_programs(0) - 1)
    def _():
        result = result_sum[...].astype(bf16).astype(f32)
        gate_grad = jnp.sum(grad_rows().astype(f32) * result, axis=1, keepdims=True)
        upper = gate_grad.astype(bf16).astype(f32)
        lane = lax.broadcasted_iota(jnp.int32, (total, 128), 1)
        columns = jnp.where(
            lane == me_ref[0], upper, jnp.where(lane == me_ref[0] + 64, gate_grad - upper, 0.0)
        ).astype(bf16)
        back = back_sum[...].astype(bf16)
        for b, ref in enumerate(back_refs):
            ref[:, :width] = back[b * size : (b + 1) * size, :]
            ref[:, width:] = columns[b * size : (b + 1) * size, :]
        gated = (gates[:, 0:1] * result).astype(bf16)
        each = total // grads
        for b, ref in enumerate(result_refs):
            ref[...] = gated[b * each : (b + 1) * each, :]


def run_experts(place, w_in, w_out, w_router, x_blocks, g_blocks, experts):
    width, units = w_in.shape
    count, grads = len(x_blocks), len(g_blocks)
    size, each = x_blocks[0].shape[0], g_blocks[0].shape[0]
    total = size * count
    piece = 512

    columns = pl.BlockSpec((total, piece), lambda i: (0, i))
    outs = (
        [shape((size, width + 128), bf16)] * count
        + [shape((each, width), bf16)] * grads
        + [shape((total, units), bf16)] * 2
        + [shape((total, width), bf16)] * 2
    )
    flat = pl.pallas_call(
        functools.partial(experts_kernel, count, grads, experts),
        name="run_experts",
        grid=(units // piece,),
        in_specs=[
            pl.BlockSpec(memory_space=pltpu.SMEM),
            pl.BlockSpec((width, piece), lambda i: (0, i)),
            pl.BlockSpec((piece, width), lambda i: (i, 0)),
            whole(w_router.shape),
        ]
        + [whole((size, width))] * count
        + [whole((each, width))] * grads,
        out_specs=[whole((size, width + 128))] * count
        + [whole((each, width))] * grads
        + [columns] * 2
        + [whole((total, width))] * 2,
        out_shape=outs,
        scratch_shapes=[
            pltpu.VMEM((total, 128), f32),
            pltpu.VMEM((total, width), f32),
            pltpu.VMEM((total, width), f32),
        ],
        compiler_params=pltpu.CompilerParams(vmem_limit_bytes=56 * 1024 * 1024),
        cost_estimate=pl.CostEstimate(
            flops=8 * total * width * units,
            bytes_accessed=4 * width * units + 4 * total * units,
            transcendentals=2 * total * units,
        ),
    )(place, w_in, w_out, w_router, *x_blocks, *g_blocks)
    return (
        flat[:count],
        flat[count : count + grads],
        *flat[count + grads :],
    )


def home(
    own_back,
    far_sum,
    slots,
    hidden,
    probs,
    cotangent,
    gain,
    w_router,
    ffn_input,
    weight_o,
    mixed,
    size,
    experts,
    after,
):
    rows, width = hidden.shape
    count, members = len(own_back), len(weight_o)
    span = weight_o[0].shape[0]
    far = [] if far_sum is None else [far_sum]

    def kernel(*refs):
        slots_ref, hidden_ref, probs_ref, cot_ref, gain_ref, router_ref, input_ref = refs[:7]
        refs = refs[7:]
        back_refs, refs = refs[:count], refs[count:]
        far_refs, refs = refs[: len(far)], refs[len(far) :]
        weight_refs, mixed_refs, refs = refs[:members], refs[members : 2 * members], refs[2 * members :]
        grad_refs = refs[:members]
        hidden_grad_ref, gain_grad_ref, router_grad_ref, near_ref, base_ref = refs[members:]
        total = None
        for b, ref in enumerate(back_refs):
            part = dot(hot(slots_ref, b * size, size), ref[...], 0, 0)
            total = part if total is None else total + part
        for ref in far_refs:
            total = total + ref[...].astype(f32)
        columns = total[:, width:]
        lane = lax.broadcasted_iota(jnp.int32, columns.shape, 1)
        prob_grad = jnp.where(lane < 64, columns + pltpu.roll(columns, 64, 1), 0.0)
        router_probs = probs_ref[...]
        logit_grad = router_probs * (
            prob_grad - jnp.sum(router_probs * prob_grad, axis=-1, keepdims=True)
        )
        router_grad_ref[...] = dot(logit_grad, input_ref[...].astype(f32), 0, 0, highest)[:experts, :]
        grad = total[:, :width] + dot(logit_grad, router_ref[...].astype(f32), 1, 1, highest)
        hidden_now = hidden_ref[...]
        inverse = lax.rsqrt(jnp.mean(hidden_now * hidden_now, axis=-1, keepdims=True) + eps)
        scaled = grad * gain_ref[...]
        gain_grad_ref[...] = jnp.sum(grad * hidden_now * inverse, axis=0, keepdims=True)
        inner = jnp.mean(scaled * hidden_now, axis=-1, keepdims=True)
        hidden_grad = (
            cot_ref[...].astype(f32)
            + inverse * scaled
            - hidden_now * inverse * inverse * inverse * inner
        )
        hidden_grad_ref[...] = hidden_grad
        attn_grad = hidden_grad.astype(bf16)
        for ref, weight in zip(grad_refs, weight_refs):
            ref[...] = dot(attn_grad, weight[...], 1, 1).astype(bf16)
        for r, (ref, first) in enumerate(
            ((base_ref, 0), (near_ref, 0), (base_ref, span), (near_ref, span))
        ):
            part = dot(attn_grad, mixed_refs[r][...], 0, 0)
            ref[:, first : first + span] = part.astype(ref.dtype)

    return call(
        kernel,
        "home",
        [slots, hidden, probs, cotangent, gain, w_router, ffn_input]
        + list(own_back)
        + far
        + weight_o
        + mixed,
        [shape((rows, span), bf16)] * members
        + [
            shape((rows, width), f32),
            shape((1, width), f32),
            shape((experts, width), f32),
            shape((width, 2 * span), bf16),
            shape((width, 2 * span), f32),
        ],
        flops=2 * rows * width * (2 * width + size * count),
        after=after,
    )


def expert_weight_grads(name, place, fixed, cut, cut_left, members):
    total, width = fixed.shape
    piece = cut.shape[1] // members
    dims = (piece, width) if cut_left else (width, piece)

    def kernel(place_ref, fixed_ref, cut_ref, near_ref, base_ref):
        pair = (cut_ref, fixed_ref) if cut_left else (fixed_ref, cut_ref)
        part = dot(pair[0][...], pair[1][...], 0, 0)

        @pl.when(pl.program_id(0) < 2)
        def _():
            near_ref[...] = part.astype(bf16)

        @pl.when(pl.program_id(0) >= 2)
        def _():
            base_ref[...] = part

    def cut_map(i, place_ref):
        return (0, place_ref[1] ^ jnp.where(i < 2, 2 * i + 1, 2 * i - 4))

    return pl.pallas_call(
        kernel,
        name=name,
        grid_spec=pltpu.PrefetchScalarGridSpec(
            num_scalar_prefetch=1,
            grid=(4,),
            in_specs=[
                pl.BlockSpec((total, width), lambda i, p: (0, 0)),
                pl.BlockSpec((total, piece), cut_map),
            ],
            out_specs=[
                pl.BlockSpec(dims, lambda i, p: (jnp.minimum(i, 1), 0)),
                pl.BlockSpec(dims, lambda i, p: (jnp.maximum(i - 2, 0), 0)),
            ],
        ),
        out_shape=[shape((2 * dims[0], dims[1]), bf16), shape((2 * dims[0], dims[1]), f32)],
        compiler_params=pltpu.CompilerParams(vmem_limit_bytes=40 * 1024 * 1024),
        cost_estimate=pl.CostEstimate(
            flops=8 * total * width * piece,
            bytes_accessed=2 * total * (width + 4 * piece) + 12 * width * piece,
            transcendentals=0,
        ),
    )(place, fixed, cut)


def input_grads(
    place,
    proj_grads,
    normed,
    weights,
    output_sum,
    gain,
    line_grad,
    bucket_hot,
    ffn_gain_grad,
    router_grad,
    members,
    owners,
    heads,
    after,
):
    seq_len, width = normed.shape
    span = weights[0].shape[1]
    rows = seq_len // members
    part = width // owners
    few = owners == 8
    experts = router_grad.shape[0]

    def kernel(place_ref, *refs):
        dq_ref, dk_ref, dv_ref, normed_ref, wq_ref, wk_ref, wv_ref, out_ref, gain_ref = refs[:9]
        line_ref, hot_ref, ffn_gain_ref, router_ref = refs[9:13]
        near_ref, base_ref, far_ref, small_ref, *weight_refs, sums = refs[13:]
        for at, ref in enumerate((dq_ref, dk_ref, dv_ref)):
            sums[:, at * span : (at + 1) * span] = dot(normed_ref[...], ref[...], 0, 0)
        sums[:, 3 * span :] = out_ref[...]
        if few:
            for r, ref in enumerate(weight_refs):
                for i, far in enumerate((0, 4)):
                    at = pl.multiple_of((place_ref[0] ^ r ^ far) * part, part)
                    ref[i * part : (i + 1) * part, :] = sums[pl.ds(at, part), :].astype(ref.dtype)
        else:
            weight_refs[0][...] = sums[...]
        gain_grad = jnp.zeros((1, width), f32)
        for r, (ref, first) in enumerate(
            ((base_ref, 0), (near_ref, 0), (far_ref, 0), (near_ref, rows))
        ):
            at = pl.ds(pl.multiple_of((place_ref[1] ^ r) * rows, rows), rows)
            grad = (
                dot(dq_ref[at, :], wq_ref[...], 1, 1)
                + dot(dk_ref[at, :], wk_ref[...], 1, 1)
                + dot(dv_ref[at, :], wv_ref[...], 1, 1)
            )
            gain_grad = gain_grad + jnp.sum(
                grad * normed_ref[at, :].astype(f32), axis=0, keepdims=True
            )
            ref[first : first + rows, :] = grad.astype(ref.dtype)
        small_ref[...] = jnp.zeros_like(small_ref)
        small_ref[0:1, :] = gain_grad / gain_ref[...]
        small_ref[1:2, :] = ffn_gain_ref[...]
        table = dot(line_ref[...], hot_ref[...], 1, 0, highest)
        for m in range(members):
            own = jnp.where(place_ref[1] == m, table[:heads, :], 0.0)
            small_ref[2 + m * heads : 2 + (m + 1) * heads, :128] = own
        small_ref[16:, :] = router_ref[...]

    if few:
        weight_outs = [shape((2 * part, 4 * span), f32)] + [shape((2 * part, 4 * span), bf16)] * 3
    else:
        weight_outs = [shape((width, 4 * span), f32)]
    return call(
        kernel,
        "input_grads",
        list(proj_grads)
        + [normed]
        + list(weights)
        + [output_sum, gain, line_grad, bucket_hot, ffn_gain_grad, router_grad],
        [
            shape((2 * rows, width), bf16),
            shape((rows, width), f32),
            shape((rows, width), f32),
            shape((16 + experts, width), f32),
        ]
        + weight_outs,
        scratch=[pltpu.VMEM((width, 4 * span), f32)],
        flops=4 * seq_len * width * 3 * span,
        limit=48,
        scalars=place,
        after=after,
    )


def fold_weights(base, arrived):
    part, width = base.shape[0] // 2, base.shape[1]

    def kernel(base_ref, *refs):
        own_ref, far_ref = refs[-2:]
        total = base_ref[...]
        for ref in refs[:-2]:
            total = total + ref[...].astype(f32)
        own_ref[...] = total[:part, :]
        far_ref[...] = total[part:, :].astype(bf16)

    return call(
        kernel,
        "fold_weights",
        [base] + arrived,
        [shape((part, width), f32), shape((part, width), bf16)],
    )


def split_weights(parts, span):
    part = parts[0].shape[0]

    def kernel(*refs):
        q_ref, k_ref, v_ref, o_ref = refs[-4:]
        total = refs[0][...]
        for ref in refs[1:-4]:
            total = total + ref[...].astype(f32)
        for at, ref in enumerate((q_ref, k_ref, v_ref)):
            ref[...] = total[:, at * span : (at + 1) * span]
        o_ref[...] = total[:, 3 * span :].T

    return call(
        kernel,
        "split_weights",
        parts,
        [shape((part, span), f32)] * 3 + [shape((span, part), f32)],
    )


def gather_mp(values):
    across = swap(values, "mp", 2)
    return [values, swap(values, "mp", 1), across, swap(across, "mp", 1)]


def scatter_near(near, base, axis):
    size = base.shape[axis] // 2
    near = swap(near, "mp", 1)
    own, far = [
        lax.slice_in_dim(base, i * size, (i + 1) * size, axis=axis)
        + lax.slice_in_dim(near, i * size, (i + 1) * size, axis=axis).astype(f32)
        for i in (0, 1)
    ]
    return own, far.astype(bf16)


def sum_all(values):
    for axis in ("mp", "dp"):
        step = 1
        while step < lax.axis_size(axis):
            values = values + swap(values, axis, step)
            step = 2 * step
    return values


def all_to_all_dp(values):
    return lax.all_to_all(values, "dp", split_axis=0, concat_axis=0, tiled=True)


def slots_of(routes, place, capacity, experts, limit):
    rows = routes.shape[0]
    expert_ids = jnp.arange(experts, dtype=jnp.int32)[None, :]
    hits = (routes[:, 0:1] == expert_ids) | (routes[:, 1:2] == expert_ids)
    earlier = jnp.arange(rows)[:, None] > jnp.arange(rows)[None, :]
    ranks = jnp.dot(earlier.astype(bf16), hits.astype(bf16), preferred_element_type=f32)
    lines = []
    for k in (0, 1):
        rank = jnp.sum(jnp.where(routes[:, k : k + 1] == expert_ids, ranks, 0.0), axis=1)
        block = routes[:, k] ^ place
        lines.append(jnp.where(block < limit, block * capacity + rank.astype(jnp.int32), -1))
    return jnp.pad(jnp.stack(lines), ((0, 6), (0, 0)), constant_values=-1)


def on_device(
    tokens,
    norm_gain,
    w_query,
    w_key,
    w_value,
    w_output,
    bias_table,
    ffn_gain,
    w_router,
    w_in,
    w_out,
    segments,
    buckets,
    routes,
    cotangent,
):
    rows, width = tokens.shape
    heads = bias_table.shape[1]
    seq_len = buckets.shape[0]
    experts = w_router.shape[1]
    owners, members = lax.axis_size("dp"), lax.axis_size("mp")
    me, member = lax.axis_index("dp"), lax.axis_index("mp")
    place = jnp.stack([me, member]).astype(jnp.int32)
    capacity = 4 * rows // experts
    span = w_query.shape[1]
    window = reach + tile
    few = owners == 8

    token_blocks = gather_mp(tokens)
    pack = pack_weights(w_query, w_key, w_value, w_output)
    if few:
        both, late_cotangent = pair_up(pack, swap(pack, "dp", 4), cotangent)
        pack_blocks = [(both, (0, 4))] + [(swap(both, "dp", r), (r, r ^ 4)) for r in (1, 2, 3)]
    else:
        late_cotangent = cotangent
        pack_blocks = [(lax.all_gather(pack, "dp", axis=0, tiled=True), (0,))]
    gain_one, gain_two = norm_gain.reshape(1, width), ffn_gain.reshape(1, width)
    normed, query, key_rows, value_rows, weight_q, weight_k, weight_v, w_o = project(
        place, token_blocks, pack_blocks, gain_one, span
    )
    weight_o = gather_mp(w_o)

    if few:
        blocks, size = 4, capacity
        slots = [slots_of(routes, me, capacity, experts, 4)]
        slots.append(slots_of(swap(routes, "dp", 4), me, capacity, experts, 4))
    else:
        blocks, size = 1, experts * capacity
        slots = [slots_of(routes, 0, capacity, experts, experts)]

    if few:
        far_cotangent = swap(late_cotangent, "dp", 4)
        held = to_slots(
            "grads_to_slots",
            [(late_cotangent, slots[0]), (far_cotangent, slots[1])],
            blocks,
            size,
        )
        g_blocks = [held[0]] + [swap(held[r], "dp", r) for r in (1, 2, 3)]
    else:
        held = to_slots("grads_to_slots", [(late_cotangent, slots[0])], blocks, size)
        g_blocks = [all_to_all_dp(held[0])]

    line_buckets = jnp.pad(jnp.flip(buckets[: reach + 1]), (0, window - reach - 1))
    bucket_hot = (
        line_buckets[:, None] == jnp.arange(128, dtype=jnp.int32)[None, :]
    ).astype(f32)
    buckets_all = bias_table.shape[0]
    table = jnp.pad(bias_table.T, ((0, 8 - heads), (0, 128 - buckets_all)))
    line = jnp.dot(table, bucket_hot.T, precision=highest)
    seg_q = segments.reshape(seq_len, 1)
    seg_k = jnp.pad(segments.reshape(1, seq_len), ((0, 0), (reach, 0)), constant_values=-1)
    mixed_out = attend(
        place, query, key_rows, value_rows, seg_q, seg_k, line, heads, members, held[:1]
    )
    mixed_in = [mixed_out[0]] + [swap(mixed_out[r], "mp", r) for r in range(1, members)]

    router_wide = jnp.pad(w_router, ((0, 0), (0, 128 - experts)))
    hidden, ffn_input, router_probs, *send = middle(
        tokens,
        mixed_in,
        weight_o,
        gain_two,
        router_wide,
        slots[0],
        experts,
        blocks,
        size,
        g_blocks[1:],
    )
    if few:
        far_input = swap(ffn_input, "dp", 4)
        own = [send[0]] + [swap(send[r], "dp", r) for r in (1, 2, 3)]
        far = to_slots("far_to_slots", [(far_input, slots[1])], blocks, size)
        far = [far[0]] + [swap(far[r], "dp", r) for r in (1, 2, 3)]
        x_blocks = [item for pair in zip(own, far) for item in pair]
    else:
        x_blocks = [all_to_all_dp(send[0])]

    back, result, active, pre_grad, arrived, slot_grad = run_experts(
        place, w_in[0], w_out[0], router_wide, x_blocks, g_blocks, experts
    )
    near_in, base_in = expert_weight_grads(
        "w_in_grads", place, arrived, pre_grad, False, members
    )
    near_out, base_out = expert_weight_grads(
        "w_out_grads", place, slot_grad, active, True, members
    )
    if few:
        far_back = [back[1]] + [swap(back[2 * r + 1], "dp", r) for r in (1, 2, 3)]
        far_total, *own_back = from_slots(
            "back_from_slots",
            far_back,
            [slots[1]],
            size,
            [bf16],
            after=[near_in],
            through=back[2::2],
        )
        far_sum = swap(far_total, "dp", 4)
        own_back = [back[0]] + [swap(own_back[r - 1], "dp", r) for r in (1, 2, 3)]
    else:
        own_back, far_sum = [all_to_all_dp(back[0])], None

    *grad_out, hidden_grad, ffn_gain_grad, router_grad, near_o, base_o = home(
        own_back,
        far_sum,
        slots[0],
        hidden,
        router_probs,
        cotangent,
        gain_two,
        router_wide,
        ffn_input,
        weight_o,
        mixed_in,
        size,
        experts,
        [near_out],
    )
    grad_in = [grad_out[0]] + [swap(grad_out[r], "mp", r) for r in range(1, members)]
    own_in, far_in = scatter_near(near_in, base_in, 0)
    own_out, far_out = scatter_near(near_out, base_out, 0)
    own_o, far_o = scatter_near(near_o, base_o, 1)

    *proj_grads, line_grad = attend_back(
        place,
        query,
        key_rows,
        value_rows,
        seg_q,
        seg_k,
        line,
        grad_in,
        heads,
        [far_in, far_out],
    )
    output_sum = own_o + swap(far_o, "mp", 2).astype(f32)
    far_in = swap(far_in, "mp", 2)
    far_out = swap(far_out, "mp", 2)
    if few:
        result_in = [result[0]] + [swap(result[r], "dp", r) for r in (1, 2, 3)]
        own_result, far_result = from_slots(
            "result_from_slots", result_in, slots, size, [f32, bf16]
        )
    else:
        (own_result,) = from_slots(
            "result_from_slots", [all_to_all_dp(result[0])], slots, size, [f32]
        )
    near, base, base_far, small, *weight_sums = input_grads(
        place,
        proj_grads,
        normed,
        (weight_q, weight_k, weight_v),
        output_sum,
        gain_one,
        line_grad,
        bucket_hot,
        ffn_gain_grad,
        router_grad,
        members,
        owners,
        heads,
        [far_in, own_result],
    )
    if few:
        arrived_sums = [swap(weight_sums[r], "dp", r) for r in (1, 2, 3)]
        own_sum, far_part = fold_weights(weight_sums[0], arrived_sums)
        weight_grads = split_weights([own_sum, swap(far_part, "dp", 4)], span)
    else:
        joined_grad = lax.psum_scatter(weight_sums[0], "dp", scatter_dimension=0, tiled=True)
        weight_grads = split_weights([joined_grad], span)
    near = swap(near, "mp", 1)
    far_normed = swap((base_far + near[rows:].astype(f32)).astype(bf16), "mp", 2)
    normed_grad = base + near[:rows].astype(f32) + far_normed.astype(f32)
    resid = tokens.astype(f32)
    _, inverse_one = normalize(resid, norm_gain)
    scaled = normed_grad * norm_gain
    inner = jnp.mean(scaled * resid, axis=-1, keepdims=True)
    tokens_grad = (
        hidden_grad + inverse_one * scaled - resid * inverse_one * inverse_one * inverse_one * inner
    ).astype(bf16)

    block_out = hidden + own_result
    if few:
        block_out = block_out + swap(far_result, "dp", 4).astype(f32)
    block_out = block_out.astype(bf16)
    w_in_grad = own_in + far_in.astype(f32)
    w_out_grad = own_out + far_out.astype(f32)
    small = sum_all(small)
    return (
        block_out,
        tokens_grad,
        small[0],
        *weight_grads,
        small[2 : 2 + heads * members, :buckets_all].T,
        small[1],
        small[16:].T,
        w_in_grad[None],
        w_out_grad[None],
    )


def solution(mesh):
    return jax.shard_map(
        on_device,
        mesh=mesh,
        in_specs=(
            P(("dp", "mp"), None),
            P(),
            P("dp", "mp"),
            P("dp", "mp"),
            P("dp", "mp"),
            P("mp", "dp"),
            P(None, "mp"),
            P(),
            P(),
            P("dp", None, None),
            P("dp", None, None),
            P("dp", None),
            P(),
            P(("dp", "mp"), None),
            P(("dp", "mp"), None),
        ),
        out_specs=(
            P(("dp", "mp"), None),
            P(("dp", "mp"), None),
            P(),
            P("dp", "mp"),
            P("dp", "mp"),
            P("dp", "mp"),
            P("mp", "dp"),
            P(),
            P(),
            P(),
            P("dp", None, "mp"),
            P("dp", "mp", None),
        ),
        check_vma=False,
    )
```

```python
import functools
import math

import jax
import jax.numpy as jnp
from jax import lax
from jax.experimental import pallas as pl
from jax.experimental.pallas import tpu as pltpu
from jax.sharding import PartitionSpec as P

eps = 1e-06
highest = lax.Precision.HIGHEST
f32, bf16 = jnp.float32, jnp.bfloat16
excluded = -1e30
reach = 512
tile = 128
params = pltpu.CompilerParams(vmem_limit_bytes=64 * 1024 * 1024)
brief = pl.CostEstimate(flops=10**9, bytes_accessed=10**6, transcendentals=0)
long = pl.CostEstimate(flops=2 * 10**10, bytes_accessed=10**7, transcendentals=0)


def normalize(values, gain):
    inverse = lax.rsqrt(jnp.mean(values * values, axis=-1, keepdims=True) + eps)
    return (values * inverse * gain, inverse)


def dot(left, right, left_dim, right_dim, precision=None):
    return lax.dot_general(
        left,
        right,
        (((left_dim,), (right_dim,)), ((), ())),
        precision=precision,
        preferred_element_type=f32,
    )


def swap(values, axis, step):
    count = lax.axis_size(axis)
    return lax.ppermute(values, axis, [(i, i ^ step) for i in range(count)])


def whole(dims):
    return pl.BlockSpec(tuple(dims), lambda *_: (0,) * len(dims), pipeline_mode=pl.Buffered(1))


def call(
    kernel, name, operands, outs, scratch=(), scalars=None, after=(), through=()
):
    operands, outs = list(operands), list(outs)
    in_specs = [whole(o.shape) for o in operands]
    out_specs = [whole(o.shape) for o in outs]
    if scalars is not None:
        operands = [scalars] + operands
        in_specs = [pl.BlockSpec(memory_space=pltpu.SMEM)] + in_specs
    count, results = len(operands), len(outs)
    extra = list(through) + list(after)

    def body(*refs):
        rest = refs[count + len(extra) :]
        kernel(*refs[:count], *rest[:results], *rest[results + len(through) :])

    return pl.pallas_call(
        body,
        name=name,
        grid=(1,),
        in_specs=in_specs + [pl.BlockSpec(memory_space=pl.ANY)] * len(extra),
        out_specs=out_specs + [pl.BlockSpec(memory_space=pl.ANY)] * len(through),
        out_shape=outs + [shape(o.shape, o.dtype) for o in through],
        input_output_aliases={count + i: results + i for i in range(len(through))},
        scratch_shapes=list(scratch),
        compiler_params=params,
        cost_estimate=brief,
    )(*operands, *extra)


def shape(dims, dtype):
    return jax.ShapeDtypeStruct(tuple(dims), dtype)


def fill_skew(line_ref, skew, heads):
    window = reach + tile
    row = lax.broadcasted_iota(jnp.int32, (tile, window), 0)
    column = lax.broadcasted_iota(jnp.int32, (tile, window), 1)
    usable = (column - row <= reach) & (column - row >= 1)
    for head in range(heads):
        line = jnp.broadcast_to(line_ref[head : head + 1, :], (tile, window))
        rolled = pltpu.roll(line, 0, 1, stride=1, stride_axis=0)
        skew[head * tile : (head + 1) * tile, :] = jnp.where(usable, rolled, excluded)


def fill_window(source_ref, padded):
    padded[:reach, :] = jnp.zeros((reach, padded.shape[1]), bf16)
    padded[reach:, :] = source_ref[...]


def spread_heads(values, heads, scale):
    span = values.shape[1]
    size = span // heads
    lane = lax.broadcasted_iota(jnp.int32, (tile, span), 1)
    wide = values.astype(f32) * scale
    parts = [
        jnp.where((lane >= head * size) & (lane < (head + 1) * size), wide, 0.0)
        for head in range(heads)
    ]
    return jnp.concatenate(parts, axis=0).astype(bf16)


def collect_heads(stacked, heads):
    span = stacked.shape[1]
    size = span // heads
    lane = lax.broadcasted_iota(jnp.int32, (tile, span), 1)
    total = stacked[:tile, :]
    for head in range(1, heads):
        total = jnp.where(lane < head * size, total, stacked[head * tile : (head + 1) * tile, :])
    return total


def window_powers(q_all, keys, skew, seg_q_ref, seg_k_ref, start, heads):
    window = reach + tile
    seg_q = jnp.concatenate([seg_q_ref[pl.ds(start, tile), :]] * heads, axis=0)
    seg_k = seg_k_ref[:, pl.ds(start, window)]
    scores = dot(q_all, keys, 1, 1) + skew[...]
    scores = jnp.where(seg_q == seg_k, scores, excluded)
    powers = jnp.exp(scores - jnp.max(scores, axis=-1, keepdims=True))
    return powers, 1.0 / jnp.sum(powers, axis=-1, keepdims=True)


def attend_kernel(heads, place, q_ref, k_ref, v_ref, seg_q_ref, seg_k_ref, line_ref, *rest):
    *out_refs, mixed, k_pad, v_pad, skew = rest
    window = reach + tile
    scale = (q_ref.shape[1] // heads) ** (-0.5)
    fill_skew(line_ref, skew, heads)
    fill_window(k_ref, k_pad)
    fill_window(v_ref, v_pad)

    def step(index, carry):
        start = pl.multiple_of(index * tile, tile)
        q_all = spread_heads(q_ref[pl.ds(start, tile), :], heads, scale)
        powers, inverse = window_powers(
            q_all, k_pad[pl.ds(start, window), :], skew, seg_q_ref, seg_k_ref, start, heads
        )
        probs = (powers * inverse).astype(bf16)
        part = dot(probs, v_pad[pl.ds(start, window), :], 1, 0)
        mixed[pl.ds(start, tile), :] = collect_heads(part, heads).astype(bf16)
        return carry

    lax.fori_loop(0, q_ref.shape[0] // tile, step, 0)
    rows = out_refs[0].shape[0]
    for r, out_ref in enumerate(out_refs):
        out_ref[...] = mixed[pl.ds(pl.multiple_of((place[1] ^ r) * rows, rows), rows), :]


def attend(place, query, key_rows, value_rows, seg_q, seg_k, line, heads, members, after):
    seq_len, span = query.shape
    window = reach + tile

    def kernel(place_ref, *refs):
        attend_kernel(heads, place_ref, *refs)

    return call(
        kernel,
        "attend",
        [query, key_rows, value_rows, seg_q, seg_k, line],
        [shape((seq_len // members, span), bf16)] * members,
        scratch=[
            pltpu.VMEM((seq_len, span), bf16),
            pltpu.VMEM((seq_len + reach, span), bf16),
            pltpu.VMEM((seq_len + reach, span), bf16),
            pltpu.VMEM((heads * tile, window), f32),
        ],
        scalars=place,
        after=after,
    )


def attend_back_kernel(heads, members, place, *refs):
    q_ref, k_ref, v_ref, seg_q_ref, seg_k_ref, line_ref = refs[:6]
    g_refs = refs[6 : 6 + members]
    dq_ref, dk_ref, dv_ref, line_grad_ref = refs[6 + members : 10 + members]
    grad, k_pad, v_pad, skew, dk_sum, dv_sum, bias_sum = refs[10 + members :]
    window = reach + tile
    scale = (q_ref.shape[1] // heads) ** (-0.5)
    rows = g_refs[0].shape[0]
    fill_skew(line_ref, skew, heads)
    fill_window(k_ref, k_pad)
    fill_window(v_ref, v_pad)
    dk_sum[...] = jnp.zeros_like(dk_sum)
    dv_sum[...] = jnp.zeros_like(dv_sum)
    bias_sum[...] = jnp.zeros_like(bias_sum)
    for r, g_ref in enumerate(g_refs):
        grad[pl.ds(pl.multiple_of((place[1] ^ r) * rows, rows), rows), :] = g_ref[...]

    def step(index, carry):
        start = pl.multiple_of(index * tile, tile)
        keys = k_pad[pl.ds(start, window), :]
        values = v_pad[pl.ds(start, window), :]
        q_all = spread_heads(q_ref[pl.ds(start, tile), :], heads, scale)
        g_all = spread_heads(grad[pl.ds(start, tile), :], heads, 1.0)
        powers, inverse = window_powers(q_all, keys, skew, seg_q_ref, seg_k_ref, start, heads)
        probs = powers * inverse
        dot_grad = dot(g_all, values, 1, 1)
        inner = jnp.sum(probs * dot_grad, axis=-1, keepdims=True)
        score_grad = (probs * (dot_grad - inner)).astype(bf16)
        bias_sum[...] += score_grad.astype(f32)
        part = collect_heads(dot(score_grad, keys, 1, 0), heads) * scale
        dq_ref[pl.ds(start, tile), :] = part.astype(bf16)
        dk_sum[pl.ds(start, window), :] += dot(score_grad, q_all, 0, 0)
        dv_sum[pl.ds(start, window), :] += dot(probs.astype(bf16), g_all, 0, 0)
        return carry

    lax.fori_loop(0, q_ref.shape[0] // tile, step, 0)
    dk_ref[...] = dk_sum[reach:, :].astype(bf16)
    dv_ref[...] = dv_sum[reach:, :].astype(bf16)
    line_grad_ref[...] = jnp.zeros_like(line_grad_ref)
    row = lax.broadcasted_iota(jnp.int32, (tile, tile), 0)
    column = lax.broadcasted_iota(jnp.int32, (tile, tile), 1)
    mirror = (row + column == tile - 1).astype(f32)
    for head in range(heads):
        part = bias_sum[head * tile : (head + 1) * tile, :]
        turned = dot(mirror, part, 1, 0, highest)
        straight = pltpu.roll(turned, window - tile + 1, 1, stride=1, stride_axis=0)
        line_grad_ref[head : head + 1, :] = jnp.sum(straight, axis=0, keepdims=True)


def attend_back(place, query, key_rows, value_rows, seg_q, seg_k, line, grads, heads, after):
    seq_len, span = query.shape
    window = reach + tile

    def kernel(place_ref, *refs):
        attend_back_kernel(heads, len(grads), place_ref, *refs)

    return call(
        kernel,
        "attend_back",
        [query, key_rows, value_rows, seg_q, seg_k, line] + grads,
        [shape((seq_len, span), bf16)] * 3 + [shape((8, window), f32)],
        scratch=[
            pltpu.VMEM((seq_len, span), bf16),
            pltpu.VMEM((seq_len + reach, span), bf16),
            pltpu.VMEM((seq_len + reach, span), bf16),
            pltpu.VMEM((heads * tile, window), f32),
            pltpu.VMEM((seq_len + reach, span), f32),
            pltpu.VMEM((seq_len + reach, span), f32),
            pltpu.VMEM((heads * tile, window), f32),
        ],
        scalars=place,
        after=after,
    )


def pack_weights(w_query, w_key, w_value, w_output):
    part, span = w_query.shape

    def kernel(q_ref, k_ref, v_ref, o_ref, pack_ref):
        for at, ref in enumerate((q_ref, k_ref, v_ref)):
            pack_ref[:, at * span : (at + 1) * span] = ref[...]
        pack_ref[:, 3 * span :] = o_ref[...].astype(f32).T.astype(bf16)

    (pack,) = call(
        kernel, "pack_weights", [w_query, w_key, w_value, w_output], [shape((part, 4 * span), bf16)]
    )
    return pack


def pair_up(pack, far, after):
    part = pack.shape[0]

    def kernel(near_ref, far_ref, both_ref):
        both_ref[:part, :] = near_ref[...]
        both_ref[part:, :] = far_ref[...]

    (both,) = call(
        kernel, "pair_up", [pack, far], [shape((2 * part, pack.shape[1]), bf16)], after=after
    )
    return both


def project(place, token_blocks, pack_blocks, gain, span):
    rows, width = token_blocks[0].shape
    members = len(token_blocks)
    seq_len = rows * members
    parts = sum(len(held) for _, held in pack_blocks)
    part = width // parts

    def kernel(place_ref, gain_ref, *refs):
        token_refs = refs[:members]
        pack_refs = refs[members : members + len(pack_blocks)]
        (normed_ref, q_ref, k_ref, v_ref, wq_ref, wk_ref, wv_ref, wo_ref, pack) = refs[
            members + len(pack_blocks) :
        ]
        for (_, held), ref in zip(pack_blocks, pack_refs):
            for i, r in enumerate(held):
                at = pl.multiple_of((place_ref[0] ^ r) * part, part) if parts > 1 else 0
                pack[pl.ds(at, part), :] = ref[i * part : (i + 1) * part, :]
        for at, ref in enumerate((wq_ref, wk_ref, wv_ref)):
            ref[...] = pack[:, at * span : (at + 1) * span]
        wo_ref[...] = pack[:, 3 * span :].astype(f32).T.astype(bf16)
        for r, ref in enumerate(token_refs):
            normed, _ = normalize(ref[...].astype(f32), gain_ref[...])
            normed = normed.astype(bf16)
            at = pl.ds(pl.multiple_of((place_ref[1] ^ r) * rows, rows), rows)
            normed_ref[at, :] = normed
            q_ref[at, :] = dot(normed, wq_ref[...], 1, 0).astype(bf16)
            k_ref[at, :] = dot(normed, wk_ref[...], 1, 0).astype(bf16)
            v_ref[at, :] = dot(normed, wv_ref[...], 1, 0).astype(bf16)

    return call(
        kernel,
        "project",
        [gain] + list(token_blocks) + [array for array, _ in pack_blocks],
        [shape((seq_len, width), bf16)]
        + [shape((seq_len, span), bf16)] * 3
        + [shape((width, span), bf16)] * 3
        + [shape((span, width), bf16)],
        scratch=[pltpu.VMEM((width, width), bf16)],
        scalars=place,
    )


def hot(slots_ref, first, count):
    tokens = slots_ref.shape[1]
    slot = lax.broadcasted_iota(jnp.int32, (count, tokens), 0) + first
    taken = (slot == slots_ref[0:1, :]) | (slot == slots_ref[1:2, :])
    return jnp.where(taken, 1.0, 0.0).astype(bf16)


def to_slots(name, sets, blocks, size, after=(), through=()):
    width = sets[0][0].shape[1]

    def kernel(*refs):
        out_refs = refs[2 * len(sets) :]
        for at in range(len(sets)):
            rows_ref, slots_ref = refs[2 * at], refs[2 * at + 1]
            for b, out_ref in enumerate(out_refs):
                part = dot(hot(slots_ref, b * size, size), rows_ref[...], 1, 0)
                out_ref[at * size : (at + 1) * size, :] = part.astype(bf16)

    operands = [item for pair in sets for item in pair]
    return call(
        kernel,
        name,
        operands,
        [shape((size * len(sets), width), bf16)] * blocks,
        after=after,
        through=through,
    )


def from_slots(name, blocks, slots, size, dtypes, after=(), through=()):
    count, sets = len(blocks), len(slots)
    width = blocks[0].shape[1]
    rows = slots[0].shape[1]

    def kernel(*refs):
        block_refs, slot_refs, out_refs = refs[:count], refs[count : count + sets], refs[count + sets :]
        for at in range(sets):
            total = None
            for b, ref in enumerate(block_refs):
                held = ref[at * size : (at + 1) * size, :]
                part = dot(hot(slot_refs[at], b * size, size), held, 0, 0)
                total = part if total is None else total + part
            out_refs[at][...] = total.astype(out_refs[at].dtype)

    return call(
        kernel,
        name,
        list(blocks) + list(slots),
        [shape((rows, width), dtype) for dtype in dtypes],
        after=after,
        through=through,
    )


def router_softmax(values, w_router, experts):
    logits = dot(values, w_router, 1, 0)
    lane = lax.broadcasted_iota(jnp.int32, logits.shape, 1)
    logits = jnp.where(lane < experts, logits, excluded)
    powers = jnp.exp(logits - jnp.max(logits, axis=-1, keepdims=True))
    return powers / jnp.sum(powers, axis=-1, keepdims=True)


def middle(tokens, mixed, weight_o, gain, w_router, slots, experts, blocks, size, after):
    rows, width = tokens.shape
    members = len(mixed)

    def kernel(*refs):
        token_ref, gain_ref, router_ref, slots_ref = refs[:4]
        mixed_refs, weight_refs = refs[4 : 4 + members], refs[4 + members : 4 + 2 * members]
        hidden_ref, input_ref, probs_ref, *send_refs = refs[4 + 2 * members :]
        hidden = token_ref[...].astype(f32)
        for left, right in zip(mixed_refs, weight_refs):
            hidden = hidden + dot(left[...], right[...], 1, 0)
        hidden_ref[...] = hidden
        normed, _ = normalize(hidden, gain_ref[...])
        normed = normed.astype(bf16)
        input_ref[...] = normed
        for b, ref in enumerate(send_refs):
            ref[...] = dot(hot(slots_ref, b * size, size), normed, 1, 0).astype(bf16)
        probs_ref[...] = router_softmax(normed, router_ref[...], experts)

    return call(
        kernel,
        "middle",
        [tokens, gain, w_router, slots] + mixed + weight_o,
        [shape((rows, width), f32), shape((rows, width), bf16), shape((rows, 128), f32)]
        + [shape((size, width), bf16)] * blocks,
        after=after,
    )


def join_rows(refs):
    return jnp.concatenate([ref[...] for ref in refs], axis=0)


def experts_forward(place, w_in, w_out, w_router, x_blocks, experts, blocks):
    width, units = w_in.shape
    count, size = len(x_blocks), x_blocks[0].shape[0]
    total, piece = size * count, 768
    each, chunk = total // blocks, min(256, total)

    def kernel(me_ref, w_in_ref, w_out_ref, router_ref, *refs):
        x_refs, out_refs = refs[:count], refs[count : count + blocks]
        active_ref, slope_ref, x_all, result_ref, gates_ref, result_sum = refs[count + blocks :]

        @pl.when(pl.program_id(0) == 0)
        def _():
            x_all[...] = join_rows(x_refs)
            probs = router_softmax(x_all[...], router_ref[...], experts)
            lane = lax.broadcasted_iota(jnp.int32, probs.shape, 1)
            own = jnp.sum(jnp.where(lane == me_ref[0], probs, 0.0), axis=1, keepdims=True)
            gates_ref[...] = jnp.broadcast_to(own, gates_ref.shape)
            result_sum[...] = jnp.zeros_like(result_sum)

        for c in range(total // chunk):
            at = slice(c * chunk, (c + 1) * chunk)
            pre_act = dot(x_all[at, :], w_in_ref[...], 1, 0)
            below = 0.5 + 0.5 * lax.erf(pre_act * math.sqrt(0.5))
            bell = jnp.exp(-0.5 * pre_act * pre_act) * (1.0 / math.sqrt(2.0 * math.pi))
            active = (pre_act * below).astype(bf16)
            active_ref[at, :] = active
            slope_ref[at, :] = (below + pre_act * bell).astype(bf16)
            result_sum[at, :] += dot(active, w_out_ref[...], 1, 0)

        @pl.when(pl.program_id(0) == pl.num_programs(0) - 1)
        def _():
            result = result_sum[...].astype(bf16)
            result_ref[...] = result
            gated = (gates_ref[:, 0:1] * result.astype(f32)).astype(bf16)
            for b, ref in enumerate(out_refs):
                ref[...] = gated[b * each : (b + 1) * each, :]

    columns = pl.BlockSpec((total, piece), lambda i: (0, i))
    outs = [shape((each, width), bf16)] * blocks
    kept = [shape((total, width), bf16)] * 2 + [shape((total, 128), f32)]
    flat = pl.pallas_call(
        kernel,
        name="experts_forward",
        grid=(units // piece,),
        in_specs=[
            pl.BlockSpec(memory_space=pltpu.SMEM),
            pl.BlockSpec((width, piece), lambda i: (0, i)),
            pl.BlockSpec((piece, width), lambda i: (i, 0)),
            whole(w_router.shape),
        ]
        + [whole(o.shape) for o in x_blocks],
        out_specs=[whole(o.shape) for o in outs]
        + [columns] * 2
        + [whole(o.shape) for o in kept],
        out_shape=outs + [shape((total, units), bf16)] * 2 + kept,
        scratch_shapes=[pltpu.VMEM((total, width), f32)],
        compiler_params=params,
        cost_estimate=brief,
    )(place, w_in, w_out, w_router, *x_blocks)
    return (flat[:blocks], *flat[blocks:])


def experts_backward(place, w_in, w_out, slope, result, gates, g_blocks, count):
    width, units = w_in.shape
    total, piece = slope.shape[0], 768
    size, chunk = total // count, min(256, total)

    def kernel(me_ref, w_in_ref, w_out_ref, slope_ref, result_ref, gates_ref, *refs):
        g_refs, back_refs = refs[: len(g_blocks)], refs[len(g_blocks) : len(g_blocks) + count]
        pre_grad_ref, s_all, back_sum = refs[len(g_blocks) + count :]

        @pl.when(pl.program_id(0) == 0)
        def _():
            s_all[...] = (gates_ref[:, 0:1] * join_rows(g_refs).astype(f32)).astype(bf16)
            back_sum[...] = jnp.zeros_like(back_sum)

        for c in range(total // chunk):
            at = slice(c * chunk, (c + 1) * chunk)
            active_grad = dot(s_all[at, :], w_out_ref[...], 1, 1)
            pre_grad = (active_grad * slope_ref[at, :].astype(f32)).astype(bf16)
            pre_grad_ref[at, :] = pre_grad
            back_sum[at, :] += dot(pre_grad, w_in_ref[...], 1, 1)

        @pl.when(pl.program_id(0) == pl.num_programs(0) - 1)
        def _():
            products = join_rows(g_refs).astype(f32) * result_ref[...].astype(f32)
            gate_grad = jnp.sum(products, axis=1, keepdims=True)
            upper = gate_grad.astype(bf16).astype(f32)
            lane = lax.broadcasted_iota(jnp.int32, (total, 128), 1)
            columns = jnp.where(
                lane == me_ref[0],
                upper,
                jnp.where(lane == me_ref[0] + 64, gate_grad - upper, 0.0),
            ).astype(bf16)
            back = back_sum[...].astype(bf16)
            for b, ref in enumerate(back_refs):
                ref[:, :width] = back[b * size : (b + 1) * size, :]
                ref[:, width:] = columns[b * size : (b + 1) * size, :]

    by_units = pl.BlockSpec((total, piece), lambda i: (0, i))
    outs = [shape((size, width + 128), bf16)] * count
    flat = pl.pallas_call(
        kernel,
        name="experts_backward",
        grid=(units // piece,),
        in_specs=[
            pl.BlockSpec(memory_space=pltpu.SMEM),
            pl.BlockSpec((width, piece), lambda i: (0, i)),
            pl.BlockSpec((piece, width), lambda i: (i, 0)),
            by_units,
            whole(result.shape),
            whole(gates.shape),
        ]
        + [whole(o.shape) for o in g_blocks],
        out_specs=[whole(o.shape) for o in outs] + [by_units, whole((total, width))],
        out_shape=outs + [shape((total, units), bf16), shape((total, width), bf16)],
        scratch_shapes=[pltpu.VMEM((total, width), f32)],
        compiler_params=params,
        cost_estimate=brief,
    )(place, w_in, w_out, slope, result, gates, *g_blocks)
    return (flat[:count], *flat[count:])


def home(
    own_back,
    far_sum,
    slots,
    hidden,
    probs,
    cotangent,
    gain,
    w_router,
    ffn_input,
    weight_o,
    mixed,
    size,
    experts,
    after,
    through,
):
    rows, width = hidden.shape
    count, members = len(own_back), len(weight_o)
    span = weight_o[0].shape[0]
    far = [] if far_sum is None else [far_sum]

    def kernel(*refs):
        slots_ref, hidden_ref, probs_ref, cot_ref, gain_ref, router_ref, input_ref = refs[:7]
        refs = refs[7:]
        back_refs, refs = refs[:count], refs[count:]
        far_refs, refs = refs[: len(far)], refs[len(far) :]
        weight_refs, mixed_refs, refs = refs[:members], refs[members : 2 * members], refs[2 * members :]
        grad_refs = refs[:members]
        hidden_grad_ref, gain_grad_ref, router_grad_ref, near_ref, base_ref = refs[members:]
        total = None
        for b, ref in enumerate(back_refs):
            part = dot(hot(slots_ref, b * size, size), ref[...], 0, 0)
            total = part if total is None else total + part
        for ref in far_refs:
            total = total + ref[...].astype(f32)
        columns = total[:, width:]
        lane = lax.broadcasted_iota(jnp.int32, columns.shape, 1)
        prob_grad = jnp.where(lane < 64, columns + pltpu.roll(columns, 64, 1), 0.0)
        router_probs = probs_ref[...]
        logit_grad = router_probs * (
            prob_grad - jnp.sum(router_probs * prob_grad, axis=-1, keepdims=True)
        )
        router_grad_ref[...] = dot(logit_grad, input_ref[...].astype(f32), 0, 0, highest)[:experts, :]
        grad = total[:, :width] + dot(logit_grad, router_ref[...].astype(f32), 1, 1, highest)
        hidden_now = hidden_ref[...]
        inverse = lax.rsqrt(jnp.mean(hidden_now * hidden_now, axis=-1, keepdims=True) + eps)
        scaled = grad * gain_ref[...]
        gain_grad_ref[...] = jnp.sum(grad * hidden_now * inverse, axis=0, keepdims=True)
        inner = jnp.mean(scaled * hidden_now, axis=-1, keepdims=True)
        hidden_grad = (
            cot_ref[...].astype(f32)
            + inverse * scaled
            - hidden_now * inverse * inverse * inverse * inner
        )
        hidden_grad_ref[...] = hidden_grad
        attn_grad = hidden_grad.astype(bf16)
        for ref, weight in zip(grad_refs, weight_refs):
            ref[...] = dot(attn_grad, weight[...], 1, 1).astype(bf16)
        for r, (ref, first) in enumerate(
            ((base_ref, 0), (near_ref, 0), (base_ref, span), (near_ref, span))
        ):
            part = dot(attn_grad, mixed_refs[r][...], 0, 0)
            ref[:, first : first + span] = part.astype(ref.dtype)

    return call(
        kernel,
        "home",
        [slots, hidden, probs, cotangent, gain, w_router, ffn_input]
        + list(own_back)
        + far
        + weight_o
        + mixed,
        [shape((rows, span), bf16)] * members
        + [
            shape((rows, width), f32),
            shape((1, width), f32),
            shape((experts, width), f32),
            shape((width, 2 * span), bf16),
            shape((width, 2 * span), f32),
        ],
        after=after,
        through=through,
    )


def expert_weight_grads(name, place, fixed, cut, cut_left, members):
    total, width = fixed.shape
    piece = cut.shape[1] // members
    dims = (piece, width) if cut_left else (width, piece)

    def kernel(place_ref, fixed_ref, cut_ref, near_ref, base_ref):
        pair = (cut_ref, fixed_ref) if cut_left else (fixed_ref, cut_ref)
        part = dot(pair[0][...], pair[1][...], 0, 0)

        @pl.when(pl.program_id(0) < 2)
        def _():
            near_ref[...] = part.astype(bf16)

        @pl.when(pl.program_id(0) >= 2)
        def _():
            base_ref[...] = part

    def cut_map(i, place_ref):
        return (0, place_ref[1] ^ jnp.where(i < 2, 2 * i + 1, 2 * i - 4))

    return pl.pallas_call(
        kernel,
        name=name,
        grid_spec=pltpu.PrefetchScalarGridSpec(
            num_scalar_prefetch=1,
            grid=(4,),
            in_specs=[
                pl.BlockSpec((total, width), lambda i, p: (0, 0)),
                pl.BlockSpec((total, piece), cut_map),
            ],
            out_specs=[
                pl.BlockSpec(dims, lambda i, p: (jnp.minimum(i, 1), 0)),
                pl.BlockSpec(dims, lambda i, p: (jnp.maximum(i - 2, 0), 0)),
            ],
        ),
        out_shape=[shape((2 * dims[0], dims[1]), bf16), shape((2 * dims[0], dims[1]), f32)],
        compiler_params=params,
        cost_estimate=long,
    )(place, fixed, cut)


def input_grads(
    place,
    proj_grads,
    normed,
    weights,
    output_sum,
    gain,
    line_grad,
    bucket_hot,
    ffn_gain_grad,
    router_grad,
    members,
    owners,
    heads,
    after,
):
    seq_len, width = normed.shape
    span = weights[0].shape[1]
    rows = seq_len // members
    part = width // owners
    few = owners == 8
    experts = router_grad.shape[0]

    def kernel(place_ref, *refs):
        dq_ref, dk_ref, dv_ref, normed_ref, wq_ref, wk_ref, wv_ref, out_ref, gain_ref = refs[:9]
        line_ref, hot_ref, ffn_gain_ref, router_ref = refs[9:13]
        near_ref, base_ref, far_ref, small_ref, *weight_refs, sums = refs[13:]
        for at, ref in enumerate((dq_ref, dk_ref, dv_ref)):
            sums[:, at * span : (at + 1) * span] = dot(normed_ref[...], ref[...], 0, 0)
        sums[:, 3 * span :] = out_ref[...]
        if few:
            for r, ref in enumerate(weight_refs):
                for i, far in enumerate((0, 4)):
                    at = pl.multiple_of((place_ref[0] ^ r ^ far) * part, part)
                    ref[i * part : (i + 1) * part, :] = sums[pl.ds(at, part), :].astype(ref.dtype)
        else:
            weight_refs[0][...] = sums[...]
        gain_grad = jnp.zeros((1, width), f32)
        for r, (ref, first) in enumerate(
            ((base_ref, 0), (near_ref, 0), (far_ref, 0), (near_ref, rows))
        ):
            at = pl.ds(pl.multiple_of((place_ref[1] ^ r) * rows, rows), rows)
            grad = (
                dot(dq_ref[at, :], wq_ref[...], 1, 1)
                + dot(dk_ref[at, :], wk_ref[...], 1, 1)
                + dot(dv_ref[at, :], wv_ref[...], 1, 1)
            )
            gain_grad = gain_grad + jnp.sum(
                grad * normed_ref[at, :].astype(f32), axis=0, keepdims=True
            )
            ref[first : first + rows, :] = grad.astype(ref.dtype)
        small_ref[...] = jnp.zeros_like(small_ref)
        small_ref[0:1, :] = gain_grad / gain_ref[...]
        small_ref[1:2, :] = ffn_gain_ref[...]
        table = dot(line_ref[...], hot_ref[...], 1, 0, highest)
        for m in range(members):
            own = jnp.where(place_ref[1] == m, table[:heads, :], 0.0)
            small_ref[2 + m * heads : 2 + (m + 1) * heads, :128] = own
        small_ref[16:, :] = router_ref[...]

    if few:
        weight_outs = [shape((2 * part, 4 * span), f32)] + [shape((2 * part, 4 * span), bf16)] * 3
    else:
        weight_outs = [shape((width, 4 * span), f32)]
    return call(
        kernel,
        "input_grads",
        list(proj_grads)
        + [normed]
        + list(weights)
        + [output_sum, gain, line_grad, bucket_hot, ffn_gain_grad, router_grad],
        [
            shape((2 * rows, width), bf16),
            shape((rows, width), f32),
            shape((rows, width), f32),
            shape((16 + experts, width), f32),
        ]
        + weight_outs,
        scratch=[pltpu.VMEM((width, 4 * span), f32)],
        scalars=place,
        after=after,
    )


def fold_weights(base, arrived, after):
    part, width = base.shape[0] // 2, base.shape[1]

    def kernel(base_ref, *refs):
        own_ref, far_ref = refs[-2:]
        total = base_ref[...]
        for ref in refs[:-2]:
            total = total + ref[...].astype(f32)
        own_ref[...] = total[:part, :]
        far_ref[...] = total[part:, :].astype(bf16)

    return call(
        kernel,
        "fold_weights",
        [base] + arrived,
        [shape((part, width), f32), shape((part, width), bf16)],
        after=after,
    )


def split_weights(parts, span):
    part = parts[0].shape[0]

    def kernel(*refs):
        q_ref, k_ref, v_ref, o_ref = refs[-4:]
        total = refs[0][...]
        for ref in refs[1:-4]:
            total = total + ref[...].astype(f32)
        for at, ref in enumerate((q_ref, k_ref, v_ref)):
            ref[...] = total[:, at * span : (at + 1) * span]
        o_ref[...] = total[:, 3 * span :].T

    return call(
        kernel,
        "split_weights",
        parts,
        [shape((part, span), f32)] * 3 + [shape((span, part), f32)],
    )


def gather_mp(values):
    across = swap(values, "mp", 2)
    return [values, swap(values, "mp", 1), across, swap(across, "mp", 1)]


def scatter_near(near, base, axis):
    size = base.shape[axis] // 2
    near = swap(near, "mp", 1)
    own, far = [
        lax.slice_in_dim(base, i * size, (i + 1) * size, axis=axis)
        + lax.slice_in_dim(near, i * size, (i + 1) * size, axis=axis).astype(f32)
        for i in (0, 1)
    ]
    return own, far.astype(bf16)


def sum_all(values):
    for axis in ("mp", "dp"):
        step = 1
        while step < lax.axis_size(axis):
            values = values + swap(values, axis, step)
            step = 2 * step
    return values


def all_to_all_dp(values):
    return lax.all_to_all(values, "dp", split_axis=0, concat_axis=0, tiled=True)


def slots_of(routes, place, capacity, experts, limit):
    rows = routes.shape[0]
    expert_ids = jnp.arange(experts, dtype=jnp.int32)[None, :]
    hits = (routes[:, 0:1] == expert_ids) | (routes[:, 1:2] == expert_ids)
    earlier = jnp.arange(rows)[:, None] > jnp.arange(rows)[None, :]
    ranks = jnp.dot(earlier.astype(bf16), hits.astype(bf16), preferred_element_type=f32)
    lines = []
    for k in (0, 1):
        rank = jnp.sum(jnp.where(routes[:, k : k + 1] == expert_ids, ranks, 0.0), axis=1)
        block = routes[:, k] ^ place
        lines.append(jnp.where(block < limit, block * capacity + rank.astype(jnp.int32), -1))
    return jnp.pad(jnp.stack(lines), ((0, 6), (0, 0)), constant_values=-1)


def on_device(
    tokens,
    norm_gain,
    w_query,
    w_key,
    w_value,
    w_output,
    bias_table,
    ffn_gain,
    w_router,
    w_in,
    w_out,
    segments,
    buckets,
    routes,
    cotangent,
):
    rows, width = tokens.shape
    heads = bias_table.shape[1]
    seq_len = buckets.shape[0]
    experts = w_router.shape[1]
    owners, members = lax.axis_size("dp"), lax.axis_size("mp")
    me, member = lax.axis_index("dp"), lax.axis_index("mp")
    place = jnp.stack([me, member]).astype(jnp.int32)
    capacity = 4 * rows // experts
    span = w_query.shape[1]
    window = reach + tile
    few = owners == 8

    token_blocks = gather_mp(tokens)
    pack = pack_weights(w_query, w_key, w_value, w_output)
    if few:
        both = pair_up(pack, swap(pack, "dp", 4), token_blocks[1:3])
        pack_blocks = [(both, (0, 4))] + [(swap(both, "dp", r), (r, r ^ 4)) for r in (1, 2, 3)]
    else:
        pack_blocks = [(lax.all_gather(pack, "dp", axis=0, tiled=True), (0,))]
    gain_one, gain_two = norm_gain.reshape(1, width), ffn_gain.reshape(1, width)
    normed, query, key_rows, value_rows, weight_q, weight_k, weight_v, w_o = project(
        place, token_blocks, pack_blocks, gain_one, span
    )
    weight_o = gather_mp(w_o)

    if few:
        blocks, size = 4, capacity
        slots = [slots_of(routes, me, capacity, experts, 4)]
        slots.append(slots_of(swap(routes, "dp", 4), me, capacity, experts, 4))
    else:
        blocks, size = 1, experts * capacity
        slots = [slots_of(routes, 0, capacity, experts, experts)]

    if few:
        far_cotangent = swap(cotangent, "dp", 4)
        held = to_slots(
            "grads_to_slots",
            [(cotangent, slots[0]), (far_cotangent, slots[1])],
            blocks,
            size,
            [query],
        )
    else:
        held = to_slots("grads_to_slots", [(cotangent, slots[0])], blocks, size, [query])

    line_buckets = jnp.pad(jnp.flip(buckets[: reach + 1]), (0, window - reach - 1))
    bucket_hot = (
        line_buckets[:, None] == jnp.arange(128, dtype=jnp.int32)[None, :]
    ).astype(f32)
    buckets_all = bias_table.shape[0]
    table = jnp.pad(bias_table.T, ((0, 8 - heads), (0, 128 - buckets_all)))
    line = jnp.dot(table, bucket_hot.T, precision=highest)
    seg_q = segments.reshape(seq_len, 1)
    seg_k = jnp.pad(segments.reshape(1, seq_len), ((0, 0), (reach, 0)), constant_values=-1)
    mixed_out = attend(
        place, query, key_rows, value_rows, seg_q, seg_k, line, heads, members, held[:1]
    )
    mixed_in = [mixed_out[0]] + [swap(mixed_out[r], "mp", r) for r in range(1, members)]

    router_wide = jnp.pad(w_router, ((0, 0), (0, 128 - experts)))
    hidden, ffn_input, router_probs, *send = middle(
        tokens,
        mixed_in,
        weight_o,
        gain_two,
        router_wide,
        slots[0],
        experts,
        blocks,
        size,
        [],
    )
    if few:
        far_input = swap(ffn_input, "dp", 4)
        own = [send[0]] + [swap(send[r], "dp", r) for r in (1, 2, 3)]
        far = to_slots(
            "far_to_slots", [(far_input, slots[1])], blocks, size, through=held[1:]
        )
        g_blocks = [held[0]] + [swap(far[blocks + r - 1], "dp", r) for r in (1, 2, 3)]
        far = [far[0]] + [swap(far[r], "dp", r) for r in (1, 2, 3)]
        x_blocks = [item for pair in zip(own, far) for item in pair]
    else:
        x_blocks = [all_to_all_dp(send[0])]
        g_blocks = [all_to_all_dp(held[0])]

    result, active, slope, arrived, plain_result, slot_gates = experts_forward(
        place, w_in[0], w_out[0], router_wide, x_blocks, experts, blocks
    )
    back, pre_grad, slot_grad = experts_backward(
        place, w_in[0], w_out[0], slope, plain_result, slot_gates, g_blocks, len(x_blocks)
    )
    near_in, base_in = expert_weight_grads(
        "w_in_grads", place, arrived, pre_grad, False, members
    )
    near_out, base_out = expert_weight_grads(
        "w_out_grads", place, slot_grad, active, True, members
    )
    if few:
        result_in = [result[0]] + [swap(result[r], "dp", r) for r in (1, 2, 3)]
        own_result, far_result = from_slots(
            "result_from_slots", result_in, slots, size, [f32, bf16]
        )
        far_result = swap(far_result, "dp", 4)
        far_back = [back[1]] + [swap(back[2 * r + 1], "dp", r) for r in (1, 2, 3)]
        far_total, *own_back = from_slots(
            "back_from_slots",
            far_back,
            [slots[1]],
            size,
            [bf16],
            after=[own_result],
            through=list(back[2::2]) + [near_in],
        )
        near_in = own_back.pop()
        far_sum = swap(far_total, "dp", 4)
        own_back = [back[0]] + [swap(own_back[r - 1], "dp", r) for r in (1, 2, 3)]
    else:
        (own_result,) = from_slots(
            "result_from_slots", [all_to_all_dp(result[0])], slots, size, [f32]
        )
        own_back, far_sum = [all_to_all_dp(back[0])], None
    own_in, far_in = scatter_near(near_in, base_in, 0)

    *grad_out, hidden_grad, ffn_gain_grad, router_grad, near_o, base_o, near_out = home(
        own_back,
        far_sum,
        slots[0],
        hidden,
        router_probs,
        cotangent,
        gain_two,
        router_wide,
        ffn_input,
        weight_o,
        mixed_in,
        size,
        experts,
        [far_in],
        [near_out],
    )
    grad_in = [grad_out[0]] + [swap(grad_out[r], "mp", r) for r in range(1, members)]
    own_out, far_out = scatter_near(near_out, base_out, 0)
    own_o, far_o = scatter_near(near_o, base_o, 1)

    *proj_grads, line_grad = attend_back(
        place,
        query,
        key_rows,
        value_rows,
        seg_q,
        seg_k,
        line,
        grad_in,
        heads,
        [far_out],
    )
    output_sum = own_o + swap(far_o, "mp", 2).astype(f32)
    far_in = swap(far_in, "mp", 2)
    far_out = swap(far_out, "mp", 2)
    near, base, base_far, small, *weight_sums = input_grads(
        place,
        proj_grads,
        normed,
        (weight_q, weight_k, weight_v),
        output_sum,
        gain_one,
        line_grad,
        bucket_hot,
        ffn_gain_grad,
        router_grad,
        members,
        owners,
        heads,
        [far_in],
    )
    if few:
        arrived_sums = [swap(weight_sums[r], "dp", r) for r in (1, 2, 3)]
        own_sum, far_part = fold_weights(weight_sums[0], arrived_sums, [far_out])
        weight_grads = split_weights([own_sum, swap(far_part, "dp", 4)], span)
    else:
        joined_grad = lax.psum_scatter(weight_sums[0], "dp", scatter_dimension=0, tiled=True)
        weight_grads = split_weights([joined_grad], span)
    near = swap(near, "mp", 1)
    far_normed = swap((base_far + near[rows:].astype(f32)).astype(bf16), "mp", 2)
    normed_grad = base + near[:rows].astype(f32) + far_normed.astype(f32)
    resid = tokens.astype(f32)
    _, inverse_one = normalize(resid, norm_gain)
    scaled = normed_grad * norm_gain
    inner = jnp.mean(scaled * resid, axis=-1, keepdims=True)
    tokens_grad = (
        hidden_grad + inverse_one * scaled - resid * inverse_one * inverse_one * inverse_one * inner
    ).astype(bf16)

    block_out = hidden + own_result
    if few:
        block_out = block_out + far_result.astype(f32)
    block_out = block_out.astype(bf16)
    w_in_grad = own_in + far_in.astype(f32)
    w_out_grad = own_out + far_out.astype(f32)
    small = sum_all(small)
    return (
        block_out,
        tokens_grad,
        small[0],
        *weight_grads,
        small[2 : 2 + heads * members, :buckets_all].T,
        small[1],
        small[16:].T,
        w_in_grad[None],
        w_out_grad[None],
    )


def solution(mesh):
    return jax.shard_map(
        on_device,
        mesh=mesh,
        in_specs=(
            P(("dp", "mp"), None),
            P(),
            P("dp", "mp"),
            P("dp", "mp"),
            P("dp", "mp"),
            P("mp", "dp"),
            P(None, "mp"),
            P(),
            P(),
            P("dp", None, None),
            P("dp", None, None),
            P("dp", None),
            P(),
            P(("dp", "mp"), None),
            P(("dp", "mp"), None),
        ),
        out_specs=(
            P(("dp", "mp"), None),
            P(("dp", "mp"), None),
            P(),
            P("dp", "mp"),
            P("dp", "mp"),
            P("dp", "mp"),
            P("mp", "dp"),
            P(),
            P(),
            P(),
            P("dp", None, "mp"),
            P("dp", "mp", None),
        ),
        check_vma=False,
    )
```

```python
import functools
import math

import jax
import jax.numpy as jnp
from jax import lax
from jax.experimental import pallas as pl
from jax.experimental.pallas import tpu as pltpu
from jax.sharding import PartitionSpec as P

eps = 1e-06
highest = lax.Precision.HIGHEST
f32, bf16 = jnp.float32, jnp.bfloat16
excluded = -1e30
reach = 512
tile = 128


def limit(mebibytes):
    return pltpu.CompilerParams(vmem_limit_bytes=mebibytes * 1024 * 1024)


brief = pl.CostEstimate(flops=10**9, bytes_accessed=10**6, transcendentals=0)
long = pl.CostEstimate(flops=2 * 10**10, bytes_accessed=10**7, transcendentals=0)


def normalize(values, gain):
    inverse = lax.rsqrt(jnp.mean(values * values, axis=-1, keepdims=True) + eps)
    return (values * inverse * gain, inverse)


def dot(left, right, left_dim, right_dim, precision=None):
    return lax.dot_general(
        left,
        right,
        (((left_dim,), (right_dim,)), ((), ())),
        precision=precision,
        preferred_element_type=f32,
    )


def swap(values, axis, step):
    count = lax.axis_size(axis)
    return lax.ppermute(values, axis, [(i, i ^ step) for i in range(count)])


def whole(dims):
    return pl.BlockSpec(tuple(dims), lambda *_: (0,) * len(dims), pipeline_mode=pl.Buffered(1))


def call(
    kernel, name, operands, outs, scratch=(), scalars=None, after=(), through=(), room=64
):
    operands, outs = list(operands), list(outs)
    in_specs = [whole(o.shape) for o in operands]
    out_specs = [whole(o.shape) for o in outs]
    if scalars is not None:
        operands = [scalars] + operands
        in_specs = [pl.BlockSpec(memory_space=pltpu.SMEM)] + in_specs
    count, results = len(operands), len(outs)
    extra = list(through) + list(after)

    def body(*refs):
        rest = refs[count + len(extra) :]
        kernel(*refs[:count], *rest[:results], *rest[results + len(through) :])

    return pl.pallas_call(
        body,
        name=name,
        grid=(1,),
        in_specs=in_specs + [pl.BlockSpec(memory_space=pl.ANY)] * len(extra),
        out_specs=out_specs + [pl.BlockSpec(memory_space=pl.ANY)] * len(through),
        out_shape=outs + [shape(o.shape, o.dtype) for o in through],
        input_output_aliases={count + i: results + i for i in range(len(through))},
        scratch_shapes=list(scratch),
        compiler_params=limit(room),
        cost_estimate=brief,
    )(*operands, *extra)


def shape(dims, dtype):
    return jax.ShapeDtypeStruct(tuple(dims), dtype)


def fill_skew(line_ref, skew, heads):
    window = reach + tile
    row = lax.broadcasted_iota(jnp.int32, (tile, window), 0)
    column = lax.broadcasted_iota(jnp.int32, (tile, window), 1)
    usable = (column - row <= reach) & (column - row >= 1)
    for head in range(heads):
        line = jnp.broadcast_to(line_ref[head : head + 1, :], (tile, window))
        rolled = pltpu.roll(line, 0, 1, stride=1, stride_axis=0)
        skew[head * tile : (head + 1) * tile, :] = jnp.where(usable, rolled, excluded)


def fill_window(source_ref, padded):
    padded[:reach, :] = jnp.zeros((reach, padded.shape[1]), bf16)
    padded[reach:, :] = source_ref[...]


def spread_heads(values, heads, scale):
    span = values.shape[1]
    size = span // heads
    lane = lax.broadcasted_iota(jnp.int32, (tile, span), 1)
    wide = values.astype(f32) * scale
    parts = [
        jnp.where((lane >= head * size) & (lane < (head + 1) * size), wide, 0.0)
        for head in range(heads)
    ]
    return jnp.concatenate(parts, axis=0).astype(bf16)


def collect_heads(stacked, heads):
    span = stacked.shape[1]
    size = span // heads
    lane = lax.broadcasted_iota(jnp.int32, (tile, span), 1)
    total = stacked[:tile, :]
    for head in range(1, heads):
        total = jnp.where(lane < head * size, total, stacked[head * tile : (head + 1) * tile, :])
    return total


def window_powers(q_all, keys, skew, seg_q_ref, seg_k_ref, start, heads):
    window = reach + tile
    seg_q = jnp.concatenate([seg_q_ref[pl.ds(start, tile), :]] * heads, axis=0)
    seg_k = seg_k_ref[:, pl.ds(start, window)]
    scores = dot(q_all, keys, 1, 1) + skew[...]
    scores = jnp.where(seg_q == seg_k, scores, excluded)
    powers = jnp.exp(scores - jnp.max(scores, axis=-1, keepdims=True))
    return powers, 1.0 / jnp.sum(powers, axis=-1, keepdims=True)


def attend_kernel(heads, place, q_ref, k_ref, v_ref, seg_q_ref, seg_k_ref, line_ref, *rest):
    *out_refs, mixed, k_pad, v_pad, skew = rest
    window = reach + tile
    scale = (q_ref.shape[1] // heads) ** (-0.5)
    fill_skew(line_ref, skew, heads)
    fill_window(k_ref, k_pad)
    fill_window(v_ref, v_pad)

    def step(index, carry):
        start = pl.multiple_of(index * tile, tile)
        q_all = spread_heads(q_ref[pl.ds(start, tile), :], heads, scale)
        powers, inverse = window_powers(
            q_all, k_pad[pl.ds(start, window), :], skew, seg_q_ref, seg_k_ref, start, heads
        )
        probs = (powers * inverse).astype(bf16)
        part = dot(probs, v_pad[pl.ds(start, window), :], 1, 0)
        mixed[pl.ds(start, tile), :] = collect_heads(part, heads).astype(bf16)
        return carry

    lax.fori_loop(0, q_ref.shape[0] // tile, step, 0)
    rows = out_refs[0].shape[0]
    for r, out_ref in enumerate(out_refs):
        out_ref[...] = mixed[pl.ds(pl.multiple_of((place[1] ^ r) * rows, rows), rows), :]


def attend(place, query, key_rows, value_rows, seg_q, seg_k, line, heads, members, after):
    seq_len, span = query.shape
    window = reach + tile

    def kernel(place_ref, *refs):
        attend_kernel(heads, place_ref, *refs)

    return call(
        kernel,
        "attend",
        [query, key_rows, value_rows, seg_q, seg_k, line],
        [shape((seq_len // members, span), bf16)] * members,
        scratch=[
            pltpu.VMEM((seq_len, span), bf16),
            pltpu.VMEM((seq_len + reach, span), bf16),
            pltpu.VMEM((seq_len + reach, span), bf16),
            pltpu.VMEM((heads * tile, window), f32),
        ],
        scalars=place,
        after=after,
    )


def attend_back_kernel(heads, members, place, *refs):
    q_ref, k_ref, v_ref, seg_q_ref, seg_k_ref, line_ref = refs[:6]
    g_refs = refs[6 : 6 + members]
    dq_ref, dk_ref, dv_ref, line_grad_ref = refs[6 + members : 10 + members]
    grad, k_pad, v_pad, skew, dk_sum, dv_sum, bias_sum = refs[10 + members :]
    window = reach + tile
    scale = (q_ref.shape[1] // heads) ** (-0.5)
    rows = g_refs[0].shape[0]
    fill_skew(line_ref, skew, heads)
    fill_window(k_ref, k_pad)
    fill_window(v_ref, v_pad)
    dk_sum[...] = jnp.zeros_like(dk_sum)
    dv_sum[...] = jnp.zeros_like(dv_sum)
    bias_sum[...] = jnp.zeros_like(bias_sum)
    for r, g_ref in enumerate(g_refs):
        grad[pl.ds(pl.multiple_of((place[1] ^ r) * rows, rows), rows), :] = g_ref[...]

    def step(index, carry):
        start = pl.multiple_of(index * tile, tile)
        keys = k_pad[pl.ds(start, window), :]
        values = v_pad[pl.ds(start, window), :]
        q_all = spread_heads(q_ref[pl.ds(start, tile), :], heads, scale)
        g_all = spread_heads(grad[pl.ds(start, tile), :], heads, 1.0)
        powers, inverse = window_powers(q_all, keys, skew, seg_q_ref, seg_k_ref, start, heads)
        probs = powers * inverse
        dot_grad = dot(g_all, values, 1, 1)
        inner = jnp.sum(probs * dot_grad, axis=-1, keepdims=True)
        score_grad = (probs * (dot_grad - inner)).astype(bf16)
        bias_sum[...] += score_grad.astype(f32)
        part = collect_heads(dot(score_grad, keys, 1, 0), heads) * scale
        dq_ref[pl.ds(start, tile), :] = part.astype(bf16)
        dk_sum[pl.ds(start, window), :] += dot(score_grad, q_all, 0, 0)
        dv_sum[pl.ds(start, window), :] += dot(probs.astype(bf16), g_all, 0, 0)
        return carry

    lax.fori_loop(0, q_ref.shape[0] // tile, step, 0)
    dk_ref[...] = dk_sum[reach:, :].astype(bf16)
    dv_ref[...] = dv_sum[reach:, :].astype(bf16)
    line_grad_ref[...] = jnp.zeros_like(line_grad_ref)
    row = lax.broadcasted_iota(jnp.int32, (tile, tile), 0)
    column = lax.broadcasted_iota(jnp.int32, (tile, tile), 1)
    mirror = (row + column == tile - 1).astype(f32)
    for head in range(heads):
        part = bias_sum[head * tile : (head + 1) * tile, :]
        turned = dot(mirror, part, 1, 0, highest)
        straight = pltpu.roll(turned, window - tile + 1, 1, stride=1, stride_axis=0)
        line_grad_ref[head : head + 1, :] = jnp.sum(straight, axis=0, keepdims=True)


def attend_back(place, query, key_rows, value_rows, seg_q, seg_k, line, grads, heads, after):
    seq_len, span = query.shape
    window = reach + tile

    def kernel(place_ref, *refs):
        attend_back_kernel(heads, len(grads), place_ref, *refs)

    return call(
        kernel,
        "attend_back",
        [query, key_rows, value_rows, seg_q, seg_k, line] + grads,
        [shape((seq_len, span), bf16)] * 3 + [shape((8, window), f32)],
        scratch=[
            pltpu.VMEM((seq_len, span), bf16),
            pltpu.VMEM((seq_len + reach, span), bf16),
            pltpu.VMEM((seq_len + reach, span), bf16),
            pltpu.VMEM((heads * tile, window), f32),
            pltpu.VMEM((seq_len + reach, span), f32),
            pltpu.VMEM((seq_len + reach, span), f32),
            pltpu.VMEM((heads * tile, window), f32),
        ],
        scalars=place,
        after=after,
    )


def pack_weights(w_query, w_key, w_value, w_output):
    part, span = w_query.shape

    def kernel(q_ref, k_ref, v_ref, o_ref, pack_ref):
        for at, ref in enumerate((q_ref, k_ref, v_ref)):
            pack_ref[:, at * span : (at + 1) * span] = ref[...]
        pack_ref[:, 3 * span :] = o_ref[...].astype(f32).T.astype(bf16)

    (pack,) = call(
        kernel, "pack_weights", [w_query, w_key, w_value, w_output], [shape((part, 4 * span), bf16)]
    )
    return pack


def pair_up(pack, far, after):
    part = pack.shape[0]

    def kernel(near_ref, far_ref, both_ref):
        both_ref[:part, :] = near_ref[...]
        both_ref[part:, :] = far_ref[...]

    (both,) = call(
        kernel, "pair_up", [pack, far], [shape((2 * part, pack.shape[1]), bf16)], after=after
    )
    return both


def project(place, token_blocks, pack_blocks, gain, span):
    rows, width = token_blocks[0].shape
    members = len(token_blocks)
    seq_len = rows * members
    parts = sum(len(held) for _, held in pack_blocks)
    part = width // parts

    def kernel(place_ref, gain_ref, *refs):
        token_refs = refs[:members]
        pack_refs = refs[members : members + len(pack_blocks)]
        (normed_ref, q_ref, k_ref, v_ref, wq_ref, wk_ref, wv_ref, wo_ref, pack) = refs[
            members + len(pack_blocks) :
        ]
        for (_, held), ref in zip(pack_blocks, pack_refs):
            for i, r in enumerate(held):
                at = pl.multiple_of((place_ref[0] ^ r) * part, part) if parts > 1 else 0
                pack[pl.ds(at, part), :] = ref[i * part : (i + 1) * part, :]
        for at, ref in enumerate((wq_ref, wk_ref, wv_ref)):
            ref[...] = pack[:, at * span : (at + 1) * span]
        wo_ref[...] = pack[:, 3 * span :].astype(f32).T.astype(bf16)
        for r, ref in enumerate(token_refs):
            normed, _ = normalize(ref[...].astype(f32), gain_ref[...])
            normed = normed.astype(bf16)
            at = pl.ds(pl.multiple_of((place_ref[1] ^ r) * rows, rows), rows)
            normed_ref[at, :] = normed
            q_ref[at, :] = dot(normed, wq_ref[...], 1, 0).astype(bf16)
            k_ref[at, :] = dot(normed, wk_ref[...], 1, 0).astype(bf16)
            v_ref[at, :] = dot(normed, wv_ref[...], 1, 0).astype(bf16)

    return call(
        kernel,
        "project",
        [gain] + list(token_blocks) + [array for array, _ in pack_blocks],
        [shape((seq_len, width), bf16)]
        + [shape((seq_len, span), bf16)] * 3
        + [shape((width, span), bf16)] * 3
        + [shape((span, width), bf16)],
        scratch=[pltpu.VMEM((width, width), bf16)],
        scalars=place,
    )


def hot(slots_ref, first, count):
    tokens = slots_ref.shape[1]
    slot = lax.broadcasted_iota(jnp.int32, (count, tokens), 0) + first
    taken = (slot == slots_ref[0:1, :]) | (slot == slots_ref[1:2, :])
    return jnp.where(taken, 1.0, 0.0).astype(bf16)


def to_slots(name, sets, blocks, size, after=(), through=()):
    width = sets[0][0].shape[1]

    def kernel(*refs):
        out_refs = refs[2 * len(sets) :]
        for at in range(len(sets)):
            rows_ref, slots_ref = refs[2 * at], refs[2 * at + 1]
            for b, out_ref in enumerate(out_refs):
                part = dot(hot(slots_ref, b * size, size), rows_ref[...], 1, 0)
                out_ref[at * size : (at + 1) * size, :] = part.astype(bf16)

    operands = [item for pair in sets for item in pair]
    return call(
        kernel,
        name,
        operands,
        [shape((size * len(sets), width), bf16)] * blocks,
        after=after,
        through=through,
    )


def from_slots(name, blocks, slots, size, dtypes, after=(), through=()):
    count, sets = len(blocks), len(slots)
    width = blocks[0].shape[1]
    rows = slots[0].shape[1]

    def kernel(*refs):
        block_refs, slot_refs, out_refs = refs[:count], refs[count : count + sets], refs[count + sets :]
        for at in range(sets):
            total = None
            for b, ref in enumerate(block_refs):
                held = ref[at * size : (at + 1) * size, :]
                part = dot(hot(slot_refs[at], b * size, size), held, 0, 0)
                total = part if total is None else total + part
            out_refs[at][...] = total.astype(out_refs[at].dtype)

    return call(
        kernel,
        name,
        list(blocks) + list(slots),
        [shape((rows, width), dtype) for dtype in dtypes],
        after=after,
        through=through,
    )


def router_softmax(values, w_router, experts):
    logits = dot(values, w_router, 1, 0)
    lane = lax.broadcasted_iota(jnp.int32, logits.shape, 1)
    logits = jnp.where(lane < experts, logits, excluded)
    powers = jnp.exp(logits - jnp.max(logits, axis=-1, keepdims=True))
    return powers / jnp.sum(powers, axis=-1, keepdims=True)


def middle(tokens, mixed, weight_o, gain, w_router, slots, experts, blocks, size, after):
    rows, width = tokens.shape
    members = len(mixed)

    def kernel(*refs):
        token_ref, gain_ref, router_ref, slots_ref = refs[:4]
        mixed_refs, weight_refs = refs[4 : 4 + members], refs[4 + members : 4 + 2 * members]
        hidden_ref, input_ref, probs_ref, *send_refs = refs[4 + 2 * members :]
        hidden = token_ref[...].astype(f32)
        for left, right in zip(mixed_refs, weight_refs):
            hidden = hidden + dot(left[...], right[...], 1, 0)
        hidden_ref[...] = hidden
        normed, _ = normalize(hidden, gain_ref[...])
        normed = normed.astype(bf16)
        input_ref[...] = normed
        for b, ref in enumerate(send_refs):
            ref[...] = dot(hot(slots_ref, b * size, size), normed, 1, 0).astype(bf16)
        probs_ref[...] = router_softmax(normed, router_ref[...], experts)

    return call(
        kernel,
        "middle",
        [tokens, gain, w_router, slots] + mixed + weight_o,
        [shape((rows, width), f32), shape((rows, width), bf16), shape((rows, 128), f32)]
        + [shape((size, width), bf16)] * blocks,
        after=after,
    )


def join_rows(refs):
    return jnp.concatenate([ref[...] for ref in refs], axis=0)


def experts_forward(name, place, w_in, w_out, w_router, x_blocks, experts, before, cost):
    width, units = w_in.shape
    count, size = len(x_blocks), x_blocks[0].shape[0]
    total, piece = size * count, 768
    chunk = min(256, total)
    sets = 1 if before is None else 1 + len(before) // 2
    blocks = 0 if before is None else count
    before = [] if before is None else list(before)

    def kernel(me_ref, w_in_ref, w_out_ref, router_ref, *refs):
        x_refs, refs = refs[:count], refs[count:]
        before_refs, refs = refs[: len(before)], refs[len(before) :]
        out_refs = refs[:blocks]
        active_ref, slope_ref, x_all, result_ref, gates_ref, result_sum = refs[blocks:]

        @pl.when(pl.program_id(0) == 0)
        def _():
            x_all[...] = join_rows(x_refs)
            probs = router_softmax(x_all[...], router_ref[...], experts)
            lane = lax.broadcasted_iota(jnp.int32, probs.shape, 1)
            own = jnp.sum(jnp.where(lane == me_ref[0], probs, 0.0), axis=1, keepdims=True)
            gates_ref[...] = jnp.broadcast_to(own, gates_ref.shape)
            result_sum[...] = jnp.zeros_like(result_sum)

        for c in range(total // chunk):
            at = slice(c * chunk, (c + 1) * chunk)
            pre_act = dot(x_all[at, :], w_in_ref[...], 1, 0)
            below = 0.5 + 0.5 * lax.erf(pre_act * math.sqrt(0.5))
            bell = jnp.exp(-0.5 * pre_act * pre_act) * (1.0 / math.sqrt(2.0 * math.pi))
            active = (pre_act * below).astype(bf16)
            active_ref[at, :] = active
            slope_ref[at, :] = (below + pre_act * bell).astype(bf16)
            result_sum[at, :] += dot(active, w_out_ref[...], 1, 0)

        @pl.when(pl.program_id(0) == pl.num_programs(0) - 1)
        def _():
            result = result_sum[...].astype(bf16)
            result_ref[...] = result
            if blocks:
                held = [(before_refs[i], before_refs[i + 1]) for i in range(0, len(before), 2)]
                held.append((result_ref, gates_ref))
                for at, (rows_ref, gate_ref) in enumerate(held):
                    gated = (gate_ref[:, 0:1] * rows_ref[...].astype(f32)).astype(bf16)
                    for b, ref in enumerate(out_refs):
                        ref[at * size : (at + 1) * size, :] = gated[b * size : (b + 1) * size, :]

    columns = pl.BlockSpec((total, piece), lambda i: (0, i))
    outs = [shape((size * sets, width), bf16)] * blocks
    kept = [shape((total, width), bf16)] * 2 + [shape((total, 128), f32)]
    flat = pl.pallas_call(
        kernel,
        name=name,
        grid=(units // piece,),
        in_specs=[
            pl.BlockSpec(memory_space=pltpu.SMEM),
            pl.BlockSpec((width, piece), lambda i: (0, i)),
            pl.BlockSpec((piece, width), lambda i: (i, 0)),
            whole(w_router.shape),
        ]
        + [whole(o.shape) for o in x_blocks]
        + [whole(o.shape) for o in before],
        out_specs=[whole(o.shape) for o in outs]
        + [columns] * 2
        + [whole(o.shape) for o in kept],
        out_shape=outs + [shape((total, units), bf16)] * 2 + kept,
        scratch_shapes=[pltpu.VMEM((total, width), f32)],
        compiler_params=limit(64),
        cost_estimate=cost,
    )(place, w_in, w_out, w_router, *x_blocks, *before)
    return (list(flat[:blocks]), *flat[blocks:])


def experts_backward(name, place, w_in, w_out, sets, at_set, slot_grad, g_blocks, count, cost):
    width, units = w_in.shape
    slope, result, _ = sets[at_set]
    total, piece = slope.shape[0], 768
    size, chunk = total // count, min(256, total)
    number = len(sets)
    first = slot_grad is None
    given = [gates for _, _, gates in sets] if first else [slot_grad]
    made = number if first else 0

    def kernel(me_ref, w_in_ref, w_out_ref, slope_ref, result_ref, *refs):
        given_refs, refs = refs[: len(given)], refs[len(given) :]
        g_refs, refs = refs[: len(g_blocks)], refs[len(g_blocks) :]
        back_refs, refs = refs[:count], refs[count:]
        s_refs, pre_grad_ref, back_sum = refs[:made], refs[made], refs[made + 1]
        s_ref = s_refs[at_set] if first else given_refs[0]

        @pl.when(pl.program_id(0) == 0)
        def _():
            back_sum[...] = jnp.zeros_like(back_sum)
            if first:
                for at in range(number):
                    for b, ref in enumerate(g_refs):
                        rows = slice(b * size, (b + 1) * size)
                        grad = ref[at * size : (at + 1) * size, :].astype(f32)
                        s_refs[at][rows, :] = (given_refs[at][rows, 0:1] * grad).astype(bf16)

        for c in range(total // chunk):
            at = slice(c * chunk, (c + 1) * chunk)
            active_grad = dot(s_ref[at, :], w_out_ref[...], 1, 1)
            pre_grad = (active_grad * slope_ref[at, :].astype(f32)).astype(bf16)
            pre_grad_ref[at, :] = pre_grad
            back_sum[at, :] += dot(pre_grad, w_in_ref[...], 1, 1)

        @pl.when(pl.program_id(0) == pl.num_programs(0) - 1)
        def _():
            lane = lax.broadcasted_iota(jnp.int32, (size, 128), 1)
            for b, (ref, g_ref) in enumerate(zip(back_refs, g_refs)):
                rows = slice(b * size, (b + 1) * size)
                grad = g_ref[at_set * size : (at_set + 1) * size, :].astype(f32)
                gate_grad = jnp.sum(
                    grad * result_ref[rows, :].astype(f32), axis=1, keepdims=True
                )
                upper = gate_grad.astype(bf16).astype(f32)
                ref[:, :width] = back_sum[rows, :].astype(bf16)
                ref[:, width:] = jnp.where(
                    lane == me_ref[0],
                    upper,
                    jnp.where(lane == me_ref[0] + 64, gate_grad - upper, 0.0),
                ).astype(bf16)

    by_units = pl.BlockSpec((total, piece), lambda i: (0, i))
    outs = [shape((size, width + 128), bf16)] * count + [shape((total, width), bf16)] * made
    flat = pl.pallas_call(
        kernel,
        name=name,
        grid=(units // piece,),
        in_specs=[
            pl.BlockSpec(memory_space=pltpu.SMEM),
            pl.BlockSpec((width, piece), lambda i: (0, i)),
            pl.BlockSpec((piece, width), lambda i: (i, 0)),
            by_units,
            whole(result.shape),
        ]
        + [whole(o.shape) for o in given]
        + [whole(o.shape) for o in g_blocks],
        out_specs=[whole(o.shape) for o in outs] + [by_units],
        out_shape=outs + [shape((total, units), bf16)],
        scratch_shapes=[pltpu.VMEM((total, width), f32)],
        compiler_params=limit(64),
        cost_estimate=cost,
    )(place, w_in, w_out, slope, result, *given, *g_blocks)
    return list(flat[:count]), list(flat[count : count + made]), flat[-1]


def home(
    own_back,
    far_sum,
    slots,
    hidden,
    probs,
    cotangent,
    gain,
    w_router,
    ffn_input,
    weight_o,
    mixed,
    size,
    experts,
    after,
    through,
):
    rows, width = hidden.shape
    count, members = len(own_back), len(weight_o)
    span = weight_o[0].shape[0]
    far = [] if far_sum is None else [far_sum]

    def kernel(*refs):
        slots_ref, hidden_ref, probs_ref, cot_ref, gain_ref, router_ref, input_ref = refs[:7]
        refs = refs[7:]
        back_refs, refs = refs[:count], refs[count:]
        far_refs, refs = refs[: len(far)], refs[len(far) :]
        weight_refs, mixed_refs, refs = refs[:members], refs[members : 2 * members], refs[2 * members :]
        grad_refs = refs[:members]
        hidden_grad_ref, gain_grad_ref, router_grad_ref, near_ref, base_ref = refs[members:]
        total = None
        for b, ref in enumerate(back_refs):
            part = dot(hot(slots_ref, b * size, size), ref[...], 0, 0)
            total = part if total is None else total + part
        for ref in far_refs:
            total = total + ref[...].astype(f32)
        columns = total[:, width:]
        lane = lax.broadcasted_iota(jnp.int32, columns.shape, 1)
        prob_grad = jnp.where(lane < 64, columns + pltpu.roll(columns, 64, 1), 0.0)
        router_probs = probs_ref[...]
        logit_grad = router_probs * (
            prob_grad - jnp.sum(router_probs * prob_grad, axis=-1, keepdims=True)
        )
        router_grad_ref[...] = dot(logit_grad, input_ref[...].astype(f32), 0, 0, highest)[:experts, :]
        grad = total[:, :width] + dot(logit_grad, router_ref[...].astype(f32), 1, 1, highest)
        hidden_now = hidden_ref[...]
        inverse = lax.rsqrt(jnp.mean(hidden_now * hidden_now, axis=-1, keepdims=True) + eps)
        scaled = grad * gain_ref[...]
        gain_grad_ref[...] = jnp.sum(grad * hidden_now * inverse, axis=0, keepdims=True)
        inner = jnp.mean(scaled * hidden_now, axis=-1, keepdims=True)
        hidden_grad = (
            cot_ref[...].astype(f32)
            + inverse * scaled
            - hidden_now * inverse * inverse * inverse * inner
        )
        hidden_grad_ref[...] = hidden_grad
        attn_grad = hidden_grad.astype(bf16)
        for ref, weight in zip(grad_refs, weight_refs):
            ref[...] = dot(attn_grad, weight[...], 1, 1).astype(bf16)
        for r, (ref, first) in enumerate(
            ((base_ref, 0), (near_ref, 0), (base_ref, span), (near_ref, span))
        ):
            part = dot(attn_grad, mixed_refs[r][...], 0, 0)
            ref[:, first : first + span] = part.astype(ref.dtype)

    return call(
        kernel,
        "home",
        [slots, hidden, probs, cotangent, gain, w_router, ffn_input]
        + list(own_back)
        + far
        + weight_o
        + mixed,
        [shape((rows, span), bf16)] * members
        + [
            shape((rows, width), f32),
            shape((1, width), f32),
            shape((experts, width), f32),
            shape((width, 2 * span), bf16),
            shape((width, 2 * span), f32),
        ],
        after=after,
        through=through,
    )


def expert_weight_grads(place, rows_in, pre_grads, actives, slot_grads, members):
    sets = len(rows_in)
    total, width = rows_in[0].shape
    piece = pre_grads[0].shape[1] // members

    def kernel(place_ref, *refs):
        x_refs, p_refs, a_refs, s_refs = [refs[i * sets : (i + 1) * sets] for i in range(4)]
        near_ref, base_ref, out = refs[4 * sets :]
        step = pl.program_id(0)

        def total_of(lefts, rights):
            held = dot(lefts[0][...], rights[0][...], 0, 0)
            for left, right in zip(lefts[1:], rights[1:]):
                held = held + dot(left[...], right[...], 0, 0)
            return held

        @pl.when(step < 4)
        def _():
            out[...] = total_of(x_refs, p_refs)

        @pl.when(step >= 4)
        def _():
            out[...] = total_of(a_refs, s_refs)

        @pl.when(step % 4 < 2)
        def _():
            near_ref[...] = out[...].astype(bf16)

        @pl.when(step % 4 >= 2)
        def _():
            base_ref[...] = out[...]

    def partner(i):
        return jnp.where(i < 2, 2 * i + 1, 2 * i - 4)

    fixed = pl.BlockSpec((total, width), lambda i, p: (0, 0))
    pre_cut = pl.BlockSpec((total, piece), lambda i, p: (0, p[1] ^ partner(jnp.minimum(i, 3))))
    act_cut = pl.BlockSpec((total, piece), lambda i, p: (0, p[1] ^ partner(jnp.maximum(i - 4, 0))))
    return pl.pallas_call(
        kernel,
        name="expert_weight_grads",
        grid_spec=pltpu.PrefetchScalarGridSpec(
            num_scalar_prefetch=1,
            grid=(8,),
            in_specs=[fixed] * sets + [pre_cut] * sets + [act_cut] * sets + [fixed] * sets,
            out_specs=[
                pl.BlockSpec(
                    (piece, width), lambda i, p: (2 * (i // 4) + jnp.minimum(i % 4, 1), 0)
                ),
                pl.BlockSpec(
                    (piece, width), lambda i, p: (2 * (i // 4) + jnp.maximum(i % 4 - 2, 0), 0)
                ),
            ],
            scratch_shapes=[pltpu.VMEM((piece, width), f32)],
        ),
        out_shape=[shape((4 * piece, width), bf16), shape((4 * piece, width), f32)],
        compiler_params=limit(64),
        cost_estimate=long,
    )(place, *rows_in, *pre_grads, *actives, *slot_grads)


def far_sums(near, base, cut, after, through):
    size, width = base.shape[0] // 4, base.shape[1]
    count = len(through)

    def block(at):
        return pl.BlockSpec(
            (size, width), lambda *_: (2 * at + 1, 0), pipeline_mode=pl.Buffered(1)
        )

    def kernel(near_in, near_out, base_in, base_out, *refs):
        first_ref, rest_ref = refs[count + len(after) : count + len(after) + 2]
        held = (base_in[...] + near_in[...].astype(f32)).astype(bf16)
        first_ref[...] = held[:cut, :]
        rest_ref[: size - cut, :] = held[cut:, :]
        rest_ref[size - cut :, :] = (base_out[...] + near_out[...].astype(f32)).astype(bf16)

    anywhere = pl.BlockSpec(memory_space=pl.ANY)
    return pl.pallas_call(
        kernel,
        name="far_sums",
        grid=(1,),
        in_specs=[block(0), block(1), block(0), block(1)] + [anywhere] * (count + len(after)),
        out_specs=[whole((cut, width)), whole((2 * size - cut, width))] + [anywhere] * count,
        out_shape=[shape((cut, width), bf16), shape((2 * size - cut, width), bf16)]
        + [shape(o.shape, o.dtype) for o in through],
        input_output_aliases={4 + i: 2 + i for i in range(count)},
        compiler_params=limit(64),
        cost_estimate=brief,
    )(near, near, base, base, *through, *after)


def input_grads(
    place,
    proj_grads,
    normed,
    weights,
    output_sum,
    gain,
    line_grad,
    bucket_hot,
    ffn_gain_grad,
    router_grad,
    members,
    owners,
    heads,
    after,
):
    seq_len, width = normed.shape
    span = weights[0].shape[1]
    rows = seq_len // members
    part = width // owners
    few = owners == 8
    experts = router_grad.shape[0]

    def kernel(place_ref, *refs):
        dq_ref, dk_ref, dv_ref, normed_ref, wq_ref, wk_ref, wv_ref, out_ref, gain_ref = refs[:9]
        line_ref, hot_ref, ffn_gain_ref, router_ref = refs[9:13]
        near_ref, base_ref, far_ref, small_ref, *weight_refs, sums = refs[13:]
        for at, ref in enumerate((dq_ref, dk_ref, dv_ref)):
            sums[:, at * span : (at + 1) * span] = dot(normed_ref[...], ref[...], 0, 0)
        sums[:, 3 * span :] = out_ref[...]
        if few:
            for r, ref in enumerate(weight_refs):
                for i, far in enumerate((0, 4)):
                    at = pl.multiple_of((place_ref[0] ^ r ^ far) * part, part)
                    ref[i * part : (i + 1) * part, :] = sums[pl.ds(at, part), :].astype(ref.dtype)
        else:
            weight_refs[0][...] = sums[...]
        gain_grad = jnp.zeros((1, width), f32)
        for r, (ref, first) in enumerate(
            ((base_ref, 0), (near_ref, 0), (far_ref, 0), (near_ref, rows))
        ):
            at = pl.ds(pl.multiple_of((place_ref[1] ^ r) * rows, rows), rows)
            grad = (
                dot(dq_ref[at, :], wq_ref[...], 1, 1)
                + dot(dk_ref[at, :], wk_ref[...], 1, 1)
                + dot(dv_ref[at, :], wv_ref[...], 1, 1)
            )
            gain_grad = gain_grad + jnp.sum(
                grad * normed_ref[at, :].astype(f32), axis=0, keepdims=True
            )
            ref[first : first + rows, :] = grad.astype(ref.dtype)
        small_ref[...] = jnp.zeros_like(small_ref)
        small_ref[0:1, :] = gain_grad / gain_ref[...]
        small_ref[1:2, :] = ffn_gain_ref[...]
        table = dot(line_ref[...], hot_ref[...], 1, 0, highest)
        for m in range(members):
            own = jnp.where(place_ref[1] == m, table[:heads, :], 0.0)
            small_ref[2 + m * heads : 2 + (m + 1) * heads, :128] = own
        small_ref[16:, :] = router_ref[...]

    if few:
        weight_outs = [shape((2 * part, 4 * span), f32)] + [shape((2 * part, 4 * span), bf16)] * 3
    else:
        weight_outs = [shape((width, 4 * span), f32)]
    return call(
        kernel,
        "input_grads",
        list(proj_grads)
        + [normed]
        + list(weights)
        + [output_sum, gain, line_grad, bucket_hot, ffn_gain_grad, router_grad],
        [
            shape((2 * rows, width), bf16),
            shape((rows, width), f32),
            shape((rows, width), f32),
            shape((16 + experts, width), f32),
        ]
        + weight_outs,
        scratch=[pltpu.VMEM((width, 4 * span), f32)],
        scalars=place,
        after=after,
    )


def fold_weights(base, arrived, after, through):
    part, width = base.shape[0] // 2, base.shape[1]

    def kernel(base_ref, *refs):
        own_ref, far_ref = refs[-2:]
        total = base_ref[...]
        for ref in refs[:-2]:
            total = total + ref[...].astype(f32)
        own_ref[...] = total[:part, :]
        far_ref[...] = total[part:, :].astype(bf16)

    return call(
        kernel,
        "fold_weights",
        [base] + arrived,
        [shape((part, width), f32), shape((part, width), bf16)],
        after=after,
        through=through,
    )


def split_weights(parts, span):
    part = parts[0].shape[0]

    def kernel(*refs):
        q_ref, k_ref, v_ref, o_ref = refs[-4:]
        total = refs[0][...]
        for ref in refs[1:-4]:
            total = total + ref[...].astype(f32)
        for at, ref in enumerate((q_ref, k_ref, v_ref)):
            ref[...] = total[:, at * span : (at + 1) * span]
        o_ref[...] = total[:, 3 * span :].T

    return call(
        kernel,
        "split_weights",
        parts,
        [shape((part, span), f32)] * 3 + [shape((span, part), f32)],
    )


def gather_mp(values):
    across = swap(values, "mp", 2)
    return [values, swap(values, "mp", 1), across, swap(across, "mp", 1)]


def sum_over(values, axis):
    step = 1
    while step < lax.axis_size(axis):
        values = values + swap(values, axis, step)
        step = 2 * step
    return values


def all_to_all_dp(values):
    return lax.all_to_all(values, "dp", split_axis=0, concat_axis=0, tiled=True)


def slots_of(routes, place, capacity, experts, limit):
    rows = routes.shape[0]
    expert_ids = jnp.arange(experts, dtype=jnp.int32)[None, :]
    hits = (routes[:, 0:1] == expert_ids) | (routes[:, 1:2] == expert_ids)
    earlier = jnp.arange(rows)[:, None] > jnp.arange(rows)[None, :]
    ranks = jnp.dot(earlier.astype(bf16), hits.astype(bf16), preferred_element_type=f32)
    lines = []
    for k in (0, 1):
        rank = jnp.sum(jnp.where(routes[:, k : k + 1] == expert_ids, ranks, 0.0), axis=1)
        block = routes[:, k] ^ place
        lines.append(jnp.where(block < limit, block * capacity + rank.astype(jnp.int32), -1))
    return jnp.pad(jnp.stack(lines), ((0, 6), (0, 0)), constant_values=-1)


def on_device(
    tokens,
    norm_gain,
    w_query,
    w_key,
    w_value,
    w_output,
    bias_table,
    ffn_gain,
    w_router,
    w_in,
    w_out,
    segments,
    buckets,
    routes,
    cotangent,
):
    rows, width = tokens.shape
    heads = bias_table.shape[1]
    seq_len = buckets.shape[0]
    experts = w_router.shape[1]
    owners, members = lax.axis_size("dp"), lax.axis_size("mp")
    me, member = lax.axis_index("dp"), lax.axis_index("mp")
    place = jnp.stack([me, member]).astype(jnp.int32)
    capacity = 4 * rows // experts
    span = w_query.shape[1]
    window = reach + tile
    few = owners == 8

    token_blocks = gather_mp(tokens)
    pack = pack_weights(w_query, w_key, w_value, w_output)
    if few:
        both = pair_up(pack, swap(pack, "dp", 4), token_blocks[1:3])
        pack_blocks = [(both, (0, 4))] + [(swap(both, "dp", r), (r, r ^ 4)) for r in (1, 2, 3)]
    else:
        pack_blocks = [(lax.all_gather(pack, "dp", axis=0, tiled=True), (0,))]
    gain_one, gain_two = norm_gain.reshape(1, width), ffn_gain.reshape(1, width)
    normed, query, key_rows, value_rows, weight_q, weight_k, weight_v, w_o = project(
        place, token_blocks, pack_blocks, gain_one, span
    )

    if few:
        blocks, size = 4, capacity
        slots = [slots_of(routes, me, capacity, experts, 4)]
        slots.append(slots_of(swap(routes, "dp", 4), me, capacity, experts, 4))
    else:
        blocks, size = 1, experts * capacity
        slots = [slots_of(routes, 0, capacity, experts, experts)]

    if few:
        far_cotangent = swap(cotangent, "dp", 4)
        held = to_slots(
            "grads_to_slots",
            [(cotangent, slots[0]), (far_cotangent, slots[1])],
            blocks,
            size,
            [query],
        )
    else:
        held = to_slots("grads_to_slots", [(cotangent, slots[0])], blocks, size, [query])

    line_buckets = jnp.pad(jnp.flip(buckets[: reach + 1]), (0, window - reach - 1))
    bucket_hot = (
        line_buckets[:, None] == jnp.arange(128, dtype=jnp.int32)[None, :]
    ).astype(f32)
    buckets_all = bias_table.shape[0]
    table = jnp.pad(bias_table.T, ((0, 8 - heads), (0, 128 - buckets_all)))
    line = jnp.dot(table, bucket_hot.T, precision=highest)
    seg_q = segments.reshape(seq_len, 1)
    seg_k = jnp.pad(segments.reshape(1, seq_len), ((0, 0), (reach, 0)), constant_values=-1)
    mixed_out = attend(
        place, query, key_rows, value_rows, seg_q, seg_k, line, heads, members, held[:1]
    )
    weight_o = gather_mp(w_o)
    mixed_in = [mixed_out[0]] + [swap(mixed_out[r], "mp", r) for r in range(1, members)]

    router_wide = jnp.pad(w_router, ((0, 0), (0, 128 - experts)))
    hidden, ffn_input, router_probs, *send = middle(
        tokens,
        mixed_in,
        weight_o,
        gain_two,
        router_wide,
        slots[0],
        experts,
        blocks,
        size,
        [],
    )
    if few:
        far_input = swap(ffn_input, "dp", 4)
        own = [send[0]] + [swap(send[r], "dp", r) for r in (1, 2, 3)]
        far = to_slots(
            "far_to_slots", [(far_input, slots[1])], blocks, size, through=held[1:]
        )
        g_blocks = [held[0]] + [swap(far[blocks + r - 1], "dp", r) for r in (1, 2, 3)]
        far = [far[0]] + [swap(far[r], "dp", r) for r in (1, 2, 3)]
        x_sets = [own, far]
    else:
        x_sets = [[all_to_all_dp(send[0])]]
        g_blocks = [all_to_all_dp(held[0])]

    kept, before = [], []
    for at, x_blocks in enumerate(x_sets):
        last = at == len(x_sets) - 1
        result, *held = experts_forward(
            "experts_forward" + str(at),
            place,
            w_in[0],
            w_out[0],
            router_wide,
            x_blocks,
            experts,
            before if last else None,
            brief if last else long,
        )
        kept.append(held)
        before = before + held[3:]
    actives, slopes, arrived, plain, slot_gates = zip(*kept)
    sets = list(zip(slopes, plain, slot_gates))
    back, slot_grads, pre_grad = experts_backward(
        "experts_backward" + str(len(sets) - 1),
        place,
        w_in[0],
        w_out[0],
        sets,
        len(sets) - 1,
        None,
        g_blocks,
        blocks,
        brief,
    )
    pre_grads = [pre_grad]
    if few:
        own_back, _, pre_grad = experts_backward(
            "experts_backward0",
            place,
            w_in[0],
            w_out[0],
            sets,
            0,
            slot_grads[0],
            g_blocks,
            blocks,
            long,
        )
        pre_grads = [pre_grad] + pre_grads
        far_back = [back[0]] + [swap(back[r], "dp", r) for r in (1, 2, 3)]
        far_total, *passed = from_slots(
            "back_from_slots", far_back, [slots[1]], size, [bf16], through=own_back[1:]
        )
        far_sum = swap(far_total, "dp", 4)
        own_back = [own_back[0]] + [swap(passed[r - 1], "dp", r) for r in (1, 2, 3)]
    else:
        own_back, far_sum = [all_to_all_dp(back[0])], None
    near_w, base_w = expert_weight_grads(place, arrived, pre_grads, actives, slot_grads, members)

    homed = home(
        own_back,
        far_sum,
        slots[0],
        hidden,
        router_probs,
        cotangent,
        gain_two,
        router_wide,
        ffn_input,
        weight_o,
        mixed_in,
        size,
        experts,
        [],
        [near_w],
    )
    grad_out, homed = homed[:members], homed[members:]
    hidden_grad, ffn_gain_grad, router_grad, near_o, base_o, near_w = homed
    grad_in = [grad_out[0]] + [swap(grad_out[r], "mp", r) for r in range(1, members)]
    near_o = swap(near_o, "mp", 1)
    sum_o = base_o + near_o.astype(f32)
    output_sum = sum_o[:, :span] + swap(sum_o[:, span:].astype(bf16), "mp", 2).astype(f32)
    near_w = swap(near_w, "mp", 1)
    far_first, far_rest, *passed = far_sums(
        near_w, base_w, 2 * rows, grad_in[1:] + [output_sum], result[1:]
    )
    result = result[:1] + passed

    *proj_grads, line_grad = attend_back(
        place,
        query,
        key_rows,
        value_rows,
        seg_q,
        seg_k,
        line,
        grad_in,
        heads,
        [far_first],
    )
    far_first = swap(far_first, "mp", 2)
    far_rest = swap(far_rest, "mp", 2)
    if few:
        result_in = [result[0]] + [swap(result[r], "dp", r) for r in (1, 2, 3)]
    else:
        result_in = [all_to_all_dp(result[0])]
    near, base, base_far, small, *weight_sums = input_grads(
        place,
        proj_grads,
        normed,
        (weight_q, weight_k, weight_v),
        output_sum,
        gain_one,
        line_grad,
        bucket_hot,
        ffn_gain_grad,
        router_grad,
        members,
        owners,
        heads,
        [far_first] + result_in[1:],
    )
    if few:
        arrived_sums = [swap(weight_sums[r], "dp", r) for r in (1, 2, 3)]
        own_sum, far_part, small = fold_weights(
            weight_sums[0], arrived_sums, [], [small]
        )
        weight_grads = split_weights([own_sum, swap(far_part, "dp", 4)], span)
    else:
        joined_grad = lax.psum_scatter(weight_sums[0], "dp", scatter_dimension=0, tiled=True)
        weight_grads = split_weights([joined_grad], span)
    near = swap(near, "mp", 1)
    far_normed = swap((base_far + near[rows:].astype(f32)).astype(bf16), "mp", 2)
    normed_grad = base + near[:rows].astype(f32) + far_normed.astype(f32)
    resid = tokens.astype(f32)
    _, inverse_one = normalize(resid, norm_gain)
    scaled = normed_grad * norm_gain
    inner = jnp.mean(scaled * resid, axis=-1, keepdims=True)
    tokens_grad = (
        hidden_grad + inverse_one * scaled - resid * inverse_one * inverse_one * inverse_one * inner
    ).astype(bf16)

    if few:
        own_result, far_result = from_slots(
            "result_from_slots", result_in, slots, size, [f32, bf16], after=[own_sum]
        )
        block_out = hidden + own_result + swap(far_result, "dp", 4).astype(f32)
    else:
        (own_result,) = from_slots("result_from_slots", result_in, slots, size, [f32])
        block_out = hidden + own_result
    block_out = block_out.astype(bf16)
    piece = w_in.shape[2] // members
    own_w = base_w[:piece] + near_w[:piece].astype(f32)
    w_in_grad = own_w + jnp.concatenate(
        [far_first, far_rest[: piece - far_first.shape[0]]], axis=0
    ).astype(f32)
    own_w = base_w[2 * piece : 3 * piece] + near_w[2 * piece : 3 * piece].astype(f32)
    w_out_grad = own_w + far_rest[piece - far_first.shape[0] :].astype(f32)
    small = sum_over(sum_over(small, "mp"), "dp")
    return (
        block_out,
        tokens_grad,
        small[0],
        *weight_grads,
        small[2 : 2 + heads * members, :buckets_all].T,
        small[1],
        small[16:].T,
        w_in_grad[None],
        w_out_grad[None],
    )


def solution(mesh):
    return jax.shard_map(
        on_device,
        mesh=mesh,
        in_specs=(
            P(("dp", "mp"), None),
            P(),
            P("dp", "mp"),
            P("dp", "mp"),
            P("dp", "mp"),
            P("mp", "dp"),
            P(None, "mp"),
            P(),
            P(),
            P("dp", None, None),
            P("dp", None, None),
            P("dp", None),
            P(),
            P(("dp", "mp"), None),
            P(("dp", "mp"), None),
        ),
        out_specs=(
            P(("dp", "mp"), None),
            P(("dp", "mp"), None),
            P(),
            P("dp", "mp"),
            P("dp", "mp"),
            P("dp", "mp"),
            P("mp", "dp"),
            P(),
            P(),
            P(),
            P("dp", None, "mp"),
            P("dp", "mp", None),
        ),
        check_vma=False,
    )
```

```python
import functools
import math

import jax
import jax.numpy as jnp
from jax import lax
from jax.experimental import pallas as pl
from jax.experimental.pallas import tpu as pltpu
from jax.sharding import PartitionSpec as P

eps = 1e-06
highest = lax.Precision.HIGHEST
f32, bf16 = jnp.float32, jnp.bfloat16
excluded = -1e30
reach = 512
tile = 128


def limit(mebibytes):
    return pltpu.CompilerParams(vmem_limit_bytes=mebibytes * 1024 * 1024)


brief = pl.CostEstimate(flops=10**7, bytes_accessed=10**4, transcendentals=0)
long = pl.CostEstimate(flops=2 * 10**10, bytes_accessed=10**7, transcendentals=0)


def normalize(values, gain):
    inverse = lax.rsqrt(jnp.mean(values * values, axis=-1, keepdims=True) + eps)
    return (values * inverse * gain, inverse)


def dot(left, right, left_dim, right_dim, precision=None):
    return lax.dot_general(
        left,
        right,
        (((left_dim,), (right_dim,)), ((), ())),
        precision=precision,
        preferred_element_type=f32,
    )


def swap(values, axis, step):
    count = lax.axis_size(axis)
    return lax.ppermute(values, axis, [(i, i ^ step) for i in range(count)])


def whole(dims):
    return pl.BlockSpec(tuple(dims), lambda *_: (0,) * len(dims), pipeline_mode=pl.Buffered(1))


def call(
    kernel, name, operands, outs, scratch=(), scalars=None, after=(), through=(), cost=None
):
    operands, outs = list(operands), list(outs)
    in_specs = [whole(o.shape) for o in operands]
    out_specs = [whole(o.shape) for o in outs]
    if scalars is not None:
        operands = [scalars] + operands
        in_specs = [pl.BlockSpec(memory_space=pltpu.SMEM)] + in_specs
    count, results = len(operands), len(outs)
    extra = list(through) + list(after)

    def body(*refs):
        rest = refs[count + len(extra) :]
        kernel(*refs[:count], *rest[:results], *rest[results + len(through) :])

    return pl.pallas_call(
        body,
        name=name,
        grid=(1,),
        in_specs=in_specs + [pl.BlockSpec(memory_space=pl.ANY)] * len(extra),
        out_specs=out_specs + [pl.BlockSpec(memory_space=pl.ANY)] * len(through),
        out_shape=outs + [shape(o.shape, o.dtype) for o in through],
        input_output_aliases={count + i: results + i for i in range(len(through))},
        scratch_shapes=list(scratch),
        compiler_params=limit(64),
        cost_estimate=cost or brief,
    )(*operands, *extra)


def shape(dims, dtype):
    return jax.ShapeDtypeStruct(tuple(dims), dtype)


def fill_skew(line_ref, skew, heads):
    window = reach + tile
    row = lax.broadcasted_iota(jnp.int32, (tile, window), 0)
    column = lax.broadcasted_iota(jnp.int32, (tile, window), 1)
    usable = (column - row <= reach) & (column - row >= 1)
    for head in range(heads):
        line = jnp.broadcast_to(line_ref[head : head + 1, :], (tile, window))
        rolled = pltpu.roll(line, 0, 1, stride=1, stride_axis=0)
        skew[head * tile : (head + 1) * tile, :] = jnp.where(usable, rolled, excluded)


def fill_window(source_ref, padded):
    padded[:reach, :] = jnp.zeros((reach, padded.shape[1]), bf16)
    padded[reach:, :] = source_ref[...]


def spread_heads(values, heads, scale):
    span = values.shape[1]
    size = span // heads
    lane = lax.broadcasted_iota(jnp.int32, (tile, span), 1)
    wide = values.astype(f32) * scale
    parts = [
        jnp.where((lane >= head * size) & (lane < (head + 1) * size), wide, 0.0)
        for head in range(heads)
    ]
    return jnp.concatenate(parts, axis=0).astype(bf16)


def collect_heads(stacked, heads):
    span = stacked.shape[1]
    size = span // heads
    lane = lax.broadcasted_iota(jnp.int32, (tile, span), 1)
    total = stacked[:tile, :]
    for head in range(1, heads):
        total = jnp.where(lane < head * size, total, stacked[head * tile : (head + 1) * tile, :])
    return total


def window_powers(q_all, keys, skew, seg_q_ref, seg_k_ref, start, heads):
    window = reach + tile
    seg_q = jnp.concatenate([seg_q_ref[pl.ds(start, tile), :]] * heads, axis=0)
    seg_k = seg_k_ref[:, pl.ds(start, window)]
    scores = dot(q_all, keys, 1, 1) + skew[...]
    scores = jnp.where(seg_q == seg_k, scores, excluded)
    powers = jnp.exp(scores - jnp.max(scores, axis=-1, keepdims=True))
    return powers, 1.0 / jnp.sum(powers, axis=-1, keepdims=True)


def attend_kernel(heads, place, q_ref, k_ref, v_ref, seg_q_ref, seg_k_ref, line_ref, *rest):
    *out_refs, mixed, k_pad, v_pad, skew = rest
    window = reach + tile
    scale = (q_ref.shape[1] // heads) ** (-0.5)
    fill_skew(line_ref, skew, heads)
    fill_window(k_ref, k_pad)
    fill_window(v_ref, v_pad)

    def step(index, carry):
        start = pl.multiple_of(index * tile, tile)
        q_all = spread_heads(q_ref[pl.ds(start, tile), :], heads, scale)
        powers, inverse = window_powers(
            q_all, k_pad[pl.ds(start, window), :], skew, seg_q_ref, seg_k_ref, start, heads
        )
        probs = (powers * inverse).astype(bf16)
        part = dot(probs, v_pad[pl.ds(start, window), :], 1, 0)
        mixed[pl.ds(start, tile), :] = collect_heads(part, heads).astype(bf16)
        return carry

    lax.fori_loop(0, q_ref.shape[0] // tile, step, 0)
    rows = out_refs[0].shape[0]
    for r, out_ref in enumerate(out_refs):
        out_ref[...] = mixed[pl.ds(pl.multiple_of((place[1] ^ r) * rows, rows), rows), :]


def attend(place, query, key_rows, value_rows, seg_q, seg_k, line, heads, members, after):
    seq_len, span = query.shape
    window = reach + tile

    def kernel(place_ref, *refs):
        attend_kernel(heads, place_ref, *refs)

    return call(
        kernel,
        "attend",
        [query, key_rows, value_rows, seg_q, seg_k, line],
        [shape((seq_len // members, span), bf16)] * members,
        scratch=[
            pltpu.VMEM((seq_len, span), bf16),
            pltpu.VMEM((seq_len + reach, span), bf16),
            pltpu.VMEM((seq_len + reach, span), bf16),
            pltpu.VMEM((heads * tile, window), f32),
        ],
        scalars=place,
        after=after,
    )


def attend_back_kernel(heads, members, place, *refs):
    q_ref, k_ref, v_ref, seg_q_ref, seg_k_ref, line_ref = refs[:6]
    g_refs = refs[6 : 6 + members]
    dq_ref, dk_ref, dv_ref, line_grad_ref = refs[6 + members : 10 + members]
    grad, k_pad, v_pad, skew, dk_sum, dv_sum, bias_sum = refs[10 + members :]
    window = reach + tile
    scale = (q_ref.shape[1] // heads) ** (-0.5)
    rows = g_refs[0].shape[0]
    fill_skew(line_ref, skew, heads)
    fill_window(k_ref, k_pad)
    fill_window(v_ref, v_pad)
    dk_sum[...] = jnp.zeros_like(dk_sum)
    dv_sum[...] = jnp.zeros_like(dv_sum)
    bias_sum[...] = jnp.zeros_like(bias_sum)
    for r, g_ref in enumerate(g_refs):
        grad[pl.ds(pl.multiple_of((place[1] ^ r) * rows, rows), rows), :] = g_ref[...]

    def step(index, carry):
        start = pl.multiple_of(index * tile, tile)
        keys = k_pad[pl.ds(start, window), :]
        values = v_pad[pl.ds(start, window), :]
        q_all = spread_heads(q_ref[pl.ds(start, tile), :], heads, scale)
        g_all = spread_heads(grad[pl.ds(start, tile), :], heads, 1.0)
        powers, inverse = window_powers(q_all, keys, skew, seg_q_ref, seg_k_ref, start, heads)
        probs = powers * inverse
        dot_grad = dot(g_all, values, 1, 1)
        inner = jnp.sum(probs * dot_grad, axis=-1, keepdims=True)
        score_grad = (probs * (dot_grad - inner)).astype(bf16)
        bias_sum[...] += score_grad.astype(f32)
        part = collect_heads(dot(score_grad, keys, 1, 0), heads) * scale
        dq_ref[pl.ds(start, tile), :] = part.astype(bf16)
        dk_sum[pl.ds(start, window), :] += dot(score_grad, q_all, 0, 0)
        dv_sum[pl.ds(start, window), :] += dot(probs.astype(bf16), g_all, 0, 0)
        return carry

    lax.fori_loop(0, q_ref.shape[0] // tile, step, 0)
    dk_ref[...] = dk_sum[reach:, :].astype(bf16)
    dv_ref[...] = dv_sum[reach:, :].astype(bf16)
    line_grad_ref[...] = jnp.zeros_like(line_grad_ref)
    row = lax.broadcasted_iota(jnp.int32, (tile, tile), 0)
    column = lax.broadcasted_iota(jnp.int32, (tile, tile), 1)
    mirror = (row + column == tile - 1).astype(f32)
    for head in range(heads):
        part = bias_sum[head * tile : (head + 1) * tile, :]
        turned = dot(mirror, part, 1, 0, highest)
        straight = pltpu.roll(turned, window - tile + 1, 1, stride=1, stride_axis=0)
        line_grad_ref[head : head + 1, :] = jnp.sum(straight, axis=0, keepdims=True)


def attend_back(place, query, key_rows, value_rows, seg_q, seg_k, line, grads, heads, after):
    seq_len, span = query.shape
    window = reach + tile

    def kernel(place_ref, *refs):
        attend_back_kernel(heads, len(grads), place_ref, *refs)

    return call(
        kernel,
        "attend_back",
        [query, key_rows, value_rows, seg_q, seg_k, line] + grads,
        [shape((seq_len, span), bf16)] * 3 + [shape((8, window), f32)],
        scratch=[
            pltpu.VMEM((seq_len, span), bf16),
            pltpu.VMEM((seq_len + reach, span), bf16),
            pltpu.VMEM((seq_len + reach, span), bf16),
            pltpu.VMEM((heads * tile, window), f32),
            pltpu.VMEM((seq_len + reach, span), f32),
            pltpu.VMEM((seq_len + reach, span), f32),
            pltpu.VMEM((heads * tile, window), f32),
        ],
        scalars=place,
        after=after,
    )


def pack_weights(w_query, w_key, w_value, w_output):
    part, span = w_query.shape

    def kernel(q_ref, k_ref, v_ref, o_ref, pack_ref):
        for at, ref in enumerate((q_ref, k_ref, v_ref)):
            pack_ref[:, at * span : (at + 1) * span] = ref[...]
        pack_ref[:, 3 * span :] = o_ref[...].astype(f32).T.astype(bf16)

    (pack,) = call(
        kernel, "pack_weights", [w_query, w_key, w_value, w_output], [shape((part, 4 * span), bf16)]
    )
    return pack


def pair_up(pack, far, after):
    part = pack.shape[0]

    def kernel(near_ref, far_ref, both_ref):
        both_ref[:part, :] = near_ref[...]
        both_ref[part:, :] = far_ref[...]

    (both,) = call(
        kernel, "pair_up", [pack, far], [shape((2 * part, pack.shape[1]), bf16)], after=after
    )
    return both


def project(place, token_blocks, pack_blocks, gain, cotangent, span):
    rows, width = token_blocks[0].shape
    members = len(token_blocks)
    seq_len = rows * members
    parts = sum(len(held) for _, held in pack_blocks)
    part = width // parts

    def kernel(place_ref, gain_ref, *refs):
        token_refs = refs[:members]
        pack_refs = refs[members : members + len(pack_blocks)]
        (normed_ref, q_ref, k_ref, v_ref, wq_ref, wk_ref, wv_ref, wo_ref, pack) = refs[
            members + len(pack_blocks) :
        ]
        for (_, held), ref in zip(pack_blocks, pack_refs):
            for i, r in enumerate(held):
                at = pl.multiple_of((place_ref[0] ^ r) * part, part) if parts > 1 else 0
                pack[pl.ds(at, part), :] = ref[i * part : (i + 1) * part, :]
        for at, ref in enumerate((wq_ref, wk_ref, wv_ref)):
            ref[...] = pack[:, at * span : (at + 1) * span]
        wo_ref[...] = pack[:, 3 * span :].astype(f32).T.astype(bf16)
        for r, ref in enumerate(token_refs):
            normed, _ = normalize(ref[...].astype(f32), gain_ref[...])
            normed = normed.astype(bf16)
            at = pl.ds(pl.multiple_of((place_ref[1] ^ r) * rows, rows), rows)
            normed_ref[at, :] = normed
            q_ref[at, :] = dot(normed, wq_ref[...], 1, 0).astype(bf16)
            k_ref[at, :] = dot(normed, wk_ref[...], 1, 0).astype(bf16)
            v_ref[at, :] = dot(normed, wv_ref[...], 1, 0).astype(bf16)

    return call(
        kernel,
        "project",
        [gain] + list(token_blocks) + [array for array, _ in pack_blocks],
        [shape((seq_len, width), bf16)]
        + [shape((seq_len, span), bf16)] * 3
        + [shape((width, span), bf16)] * 3
        + [shape((span, width), bf16)],
        scratch=[pltpu.VMEM((width, width), bf16)],
        scalars=place,
        through=[cotangent],
    )


def hot(slots_ref, first, count):
    tokens = slots_ref.shape[1]
    slot = lax.broadcasted_iota(jnp.int32, (count, tokens), 0) + first
    taken = (slot == slots_ref[0:1, :]) | (slot == slots_ref[1:2, :])
    return jnp.where(taken, 1.0, 0.0).astype(bf16)


def to_slots(name, sets, blocks, size, through=(), cost=None):
    width = sets[0][0].shape[1]

    def kernel(*refs):
        out_refs = refs[2 * len(sets) :]
        for at in range(len(sets)):
            rows_ref, slots_ref = refs[2 * at], refs[2 * at + 1]
            for b, out_ref in enumerate(out_refs):
                part = dot(hot(slots_ref, b * size, size), rows_ref[...], 1, 0)
                out_ref[at * size : (at + 1) * size, :] = part.astype(bf16)

    operands = [item for pair in sets for item in pair]
    return call(
        kernel,
        name,
        operands,
        [shape((size * len(sets), width), bf16)] * blocks,
        through=through,
        cost=cost,
    )


def from_slots(name, blocks, slots, size, dtypes, after=(), through=()):
    count, sets = len(blocks), len(slots)
    width = blocks[0].shape[1]
    rows = slots[0].shape[1]

    def kernel(*refs):
        block_refs, slot_refs, out_refs = refs[:count], refs[count : count + sets], refs[count + sets :]
        for at in range(sets):
            total = None
            for b, ref in enumerate(block_refs):
                held = ref[at * size : (at + 1) * size, :]
                part = dot(hot(slot_refs[at], b * size, size), held, 0, 0)
                total = part if total is None else total + part
            out_refs[at][...] = total.astype(out_refs[at].dtype)

    return call(
        kernel,
        name,
        list(blocks) + list(slots),
        [shape((rows, width), dtype) for dtype in dtypes],
        after=after,
        through=through,
    )


def router_softmax(values, w_router, experts):
    logits = dot(values, w_router, 1, 0)
    lane = lax.broadcasted_iota(jnp.int32, logits.shape, 1)
    logits = jnp.where(lane < experts, logits, excluded)
    powers = jnp.exp(logits - jnp.max(logits, axis=-1, keepdims=True))
    return powers / jnp.sum(powers, axis=-1, keepdims=True)


def middle(tokens, mixed, weight_o, gain, w_router, slots, experts, blocks, size, after):
    rows, width = tokens.shape
    members = len(mixed)

    def kernel(*refs):
        token_ref, gain_ref, router_ref, slots_ref = refs[:4]
        mixed_refs, weight_refs = refs[4 : 4 + members], refs[4 + members : 4 + 2 * members]
        hidden_ref, input_ref, probs_ref, *send_refs = refs[4 + 2 * members :]
        hidden = token_ref[...].astype(f32)
        for left, right in zip(mixed_refs, weight_refs):
            hidden = hidden + dot(left[...], right[...], 1, 0)
        hidden_ref[...] = hidden
        normed, _ = normalize(hidden, gain_ref[...])
        normed = normed.astype(bf16)
        input_ref[...] = normed
        for b, ref in enumerate(send_refs):
            ref[...] = dot(hot(slots_ref, b * size, size), normed, 1, 0).astype(bf16)
        probs_ref[...] = router_softmax(normed, router_ref[...], experts)

    return call(
        kernel,
        "middle",
        [tokens, gain, w_router, slots] + mixed + weight_o,
        [shape((rows, width), f32), shape((rows, width), bf16), shape((rows, 128), f32)]
        + [shape((size, width), bf16)] * blocks,
        after=after,
    )


def join_rows(refs):
    return jnp.concatenate([ref[...] for ref in refs], axis=0)


def experts_forward(name, place, w_in, w_out, w_router, x_blocks, experts, before, cost):
    width, units = w_in.shape
    count, size = len(x_blocks), x_blocks[0].shape[0]
    total, piece, chunk = size * count, 768, 256
    sets = 1 if before is None else 1 + len(before) // 2
    blocks = 0 if before is None else count
    before = [] if before is None else list(before)

    def kernel(me_ref, w_in_ref, w_out_ref, router_ref, *refs):
        x_refs, refs = refs[:count], refs[count:]
        before_refs, refs = refs[: len(before)], refs[len(before) :]
        out_refs = refs[:blocks]
        active_ref, slope_ref, x_all, result_ref, gates_ref, result_sum = refs[blocks:]

        @pl.when(pl.program_id(0) == 0)
        def _():
            x_all[...] = join_rows(x_refs)
            probs = router_softmax(x_all[...], router_ref[...], experts)
            lane = lax.broadcasted_iota(jnp.int32, probs.shape, 1)
            own = jnp.sum(jnp.where(lane == me_ref[0], probs, 0.0), axis=1, keepdims=True)
            gates_ref[...] = jnp.broadcast_to(own, gates_ref.shape)
            result_sum[...] = jnp.zeros_like(result_sum)

        for c in range(piece // chunk):
            at = slice(c * chunk, (c + 1) * chunk)
            pre_act = dot(x_all[...], w_in_ref[:, at], 1, 0)
            below = 0.5 + 0.5 * lax.erf(pre_act * math.sqrt(0.5))
            bell = jnp.exp(-0.5 * pre_act * pre_act) * (1.0 / math.sqrt(2.0 * math.pi))
            active_ref[:, at] = (pre_act * below).astype(bf16)
            slope_ref[:, at] = (below + pre_act * bell).astype(bf16)
        result_sum[...] += dot(active_ref[...], w_out_ref[...], 1, 0)

        @pl.when(pl.program_id(0) == pl.num_programs(0) - 1)
        def _():
            result = result_sum[...].astype(bf16)
            result_ref[...] = result
            if blocks:
                held = [(before_refs[i], before_refs[i + 1]) for i in range(0, len(before), 2)]
                held.append((result_ref, gates_ref))
                for at, (rows_ref, gate_ref) in enumerate(held):
                    gated = (gate_ref[:, 0:1] * rows_ref[...].astype(f32)).astype(bf16)
                    for b, ref in enumerate(out_refs):
                        ref[at * size : (at + 1) * size, :] = gated[b * size : (b + 1) * size, :]

    columns = pl.BlockSpec((total, piece), lambda i: (0, i))
    outs = [shape((size * sets, width), bf16)] * blocks
    kept = [shape((total, width), bf16)] * 2 + [shape((total, 128), f32)]
    flat = pl.pallas_call(
        kernel,
        name=name,
        grid=(units // piece,),
        in_specs=[
            pl.BlockSpec(memory_space=pltpu.SMEM),
            pl.BlockSpec((width, piece), lambda i: (0, i)),
            pl.BlockSpec((piece, width), lambda i: (i, 0)),
            whole(w_router.shape),
        ]
        + [whole(o.shape) for o in x_blocks]
        + [whole(o.shape) for o in before],
        out_specs=[whole(o.shape) for o in outs]
        + [columns] * 2
        + [whole(o.shape) for o in kept],
        out_shape=outs + [shape((total, units), bf16)] * 2 + kept,
        scratch_shapes=[pltpu.VMEM((total, width), f32)],
        compiler_params=limit(64),
        cost_estimate=cost,
    )(place, w_in, w_out, w_router, *x_blocks, *before)
    return (list(flat[:blocks]), *flat[blocks:])


def experts_backward(name, place, w_in, w_out, sets, at_set, slot_grad, g_blocks, count, cost):
    width, units = w_in.shape
    slope, result, _ = sets[at_set]
    total, piece, chunk = slope.shape[0], 768, 256
    size = total // count
    number = len(sets)
    first = slot_grad is None
    given = [gates for _, _, gates in sets] if first else [slot_grad]
    made = number if first else 0

    def kernel(me_ref, w_in_ref, w_out_ref, slope_ref, result_ref, *refs):
        given_refs, refs = refs[: len(given)], refs[len(given) :]
        g_refs, refs = refs[: len(g_blocks)], refs[len(g_blocks) :]
        back_refs, refs = refs[:count], refs[count:]
        s_refs, pre_grad_ref, back_sum = refs[:made], refs[made], refs[made + 1]
        s_ref = s_refs[at_set] if first else given_refs[0]

        @pl.when(pl.program_id(0) == 0)
        def _():
            back_sum[...] = jnp.zeros_like(back_sum)
            if first:
                for at in range(number):
                    for b, ref in enumerate(g_refs):
                        rows = slice(b * size, (b + 1) * size)
                        grad = ref[at * size : (at + 1) * size, :].astype(f32)
                        s_refs[at][rows, :] = (given_refs[at][rows, 0:1] * grad).astype(bf16)

        for c in range(piece // chunk):
            at = slice(c * chunk, (c + 1) * chunk)
            active_grad = dot(s_ref[...], w_out_ref[at, :], 1, 1)
            pre_grad_ref[:, at] = (active_grad * slope_ref[:, at].astype(f32)).astype(bf16)
        back_sum[...] += dot(pre_grad_ref[...], w_in_ref[...], 1, 1)

        @pl.when(pl.program_id(0) == pl.num_programs(0) - 1)
        def _():
            lane = lax.broadcasted_iota(jnp.int32, (size, 128), 1)
            for b, (ref, g_ref) in enumerate(zip(back_refs, g_refs)):
                rows = slice(b * size, (b + 1) * size)
                grad = g_ref[at_set * size : (at_set + 1) * size, :].astype(f32)
                gate_grad = jnp.sum(
                    grad * result_ref[rows, :].astype(f32), axis=1, keepdims=True
                )
                upper = gate_grad.astype(bf16).astype(f32)
                ref[:, :width] = back_sum[rows, :].astype(bf16)
                ref[:, width:] = jnp.where(
                    lane == me_ref[0],
                    upper,
                    jnp.where(lane == me_ref[0] + 64, gate_grad - upper, 0.0),
                ).astype(bf16)

    by_units = pl.BlockSpec((total, piece), lambda i: (0, i))
    outs = [shape((size, width + 128), bf16)] * count + [shape((total, width), bf16)] * made
    flat = pl.pallas_call(
        kernel,
        name=name,
        grid=(units // piece,),
        in_specs=[
            pl.BlockSpec(memory_space=pltpu.SMEM),
            pl.BlockSpec((width, piece), lambda i: (0, i)),
            pl.BlockSpec((piece, width), lambda i: (i, 0)),
            by_units,
            whole(result.shape),
        ]
        + [whole(o.shape) for o in given]
        + [whole(o.shape) for o in g_blocks],
        out_specs=[whole(o.shape) for o in outs] + [by_units],
        out_shape=outs + [shape((total, units), bf16)],
        scratch_shapes=[pltpu.VMEM((total, width), f32)],
        compiler_params=limit(64),
        cost_estimate=cost,
    )(place, w_in, w_out, slope, result, *given, *g_blocks)
    return list(flat[:count]), list(flat[count : count + made]), flat[-1]


def home(
    own_back,
    far_sum,
    slots,
    hidden,
    probs,
    cotangent,
    gain,
    w_router,
    ffn_input,
    weight_o,
    mixed,
    size,
    experts,
    after,
    through,
):
    rows, width = hidden.shape
    count, members = len(own_back), len(weight_o)
    span = weight_o[0].shape[0]
    far = [] if far_sum is None else [far_sum]

    def kernel(*refs):
        slots_ref, hidden_ref, probs_ref, cot_ref, gain_ref, router_ref, input_ref = refs[:7]
        refs = refs[7:]
        back_refs, refs = refs[:count], refs[count:]
        far_refs, refs = refs[: len(far)], refs[len(far) :]
        weight_refs, mixed_refs, refs = refs[:members], refs[members : 2 * members], refs[2 * members :]
        grad_refs = refs[:members]
        hidden_grad_ref, gain_grad_ref, router_grad_ref, near_ref, base_ref = refs[members:]
        total = None
        for b, ref in enumerate(back_refs):
            part = dot(hot(slots_ref, b * size, size), ref[...], 0, 0)
            total = part if total is None else total + part
        for ref in far_refs:
            total = total + ref[...].astype(f32)
        columns = total[:, width:]
        lane = lax.broadcasted_iota(jnp.int32, columns.shape, 1)
        prob_grad = jnp.where(lane < 64, columns + pltpu.roll(columns, 64, 1), 0.0)
        router_probs = probs_ref[...]
        logit_grad = router_probs * (
            prob_grad - jnp.sum(router_probs * prob_grad, axis=-1, keepdims=True)
        )
        router_grad_ref[...] = dot(logit_grad, input_ref[...].astype(f32), 0, 0, highest)[:experts, :]
        grad = total[:, :width] + dot(logit_grad, router_ref[...].astype(f32), 1, 1, highest)
        hidden_now = hidden_ref[...]
        inverse = lax.rsqrt(jnp.mean(hidden_now * hidden_now, axis=-1, keepdims=True) + eps)
        scaled = grad * gain_ref[...]
        gain_grad_ref[...] = jnp.sum(grad * hidden_now * inverse, axis=0, keepdims=True)
        inner = jnp.mean(scaled * hidden_now, axis=-1, keepdims=True)
        hidden_grad = (
            cot_ref[...].astype(f32)
            + inverse * scaled
            - hidden_now * inverse * inverse * inverse * inner
        )
        hidden_grad_ref[...] = hidden_grad
        attn_grad = hidden_grad.astype(bf16)
        for ref, weight in zip(grad_refs, weight_refs):
            ref[...] = dot(attn_grad, weight[...], 1, 1).astype(bf16)
        for r, (ref, first) in enumerate(
            ((base_ref, 0), (near_ref, 0), (base_ref, span), (near_ref, span))
        ):
            part = dot(mixed_refs[r][...], attn_grad, 0, 0)
            ref[first : first + span, :] = part.astype(ref.dtype)

    return call(
        kernel,
        "home",
        [slots, hidden, probs, cotangent, gain, w_router, ffn_input]
        + list(own_back)
        + far
        + weight_o
        + mixed,
        [shape((rows, span), bf16)] * members
        + [
            shape((rows, width), f32),
            shape((1, width), f32),
            shape((experts, width), f32),
            shape((2 * span, width), bf16),
            shape((2 * span, width), f32),
        ],
        after=after,
        through=through,
    )


def expert_weight_grads(place, rows_in, pre_grads, actives, slot_grads, members):
    sets = len(rows_in)
    total, width = rows_in[0].shape
    piece = pre_grads[0].shape[1] // members

    def kernel(place_ref, *refs):
        x_refs, p_refs, a_refs, s_refs = [refs[i * sets : (i + 1) * sets] for i in range(4)]
        near_ref, base_ref, out = refs[4 * sets :]
        step = pl.program_id(0)

        def total_of(lefts, rights):
            held = dot(lefts[0][...], rights[0][...], 0, 0)
            for left, right in zip(lefts[1:], rights[1:]):
                held = held + dot(left[...], right[...], 0, 0)
            return held

        @pl.when(step < 4)
        def _():
            out[...] = total_of(x_refs, p_refs)

        @pl.when(step >= 4)
        def _():
            out[...] = total_of(a_refs, s_refs)

        @pl.when(step % 4 < 2)
        def _():
            near_ref[...] = out[...].astype(bf16)

        @pl.when(step % 4 >= 2)
        def _():
            base_ref[...] = out[...]

    def partner(i):
        return jnp.where(i < 2, 2 * i + 1, 2 * i - 4)

    fixed = pl.BlockSpec((total, width), lambda i, p: (0, 0))
    pre_cut = pl.BlockSpec((total, piece), lambda i, p: (0, p[1] ^ partner(jnp.minimum(i, 3))))
    act_cut = pl.BlockSpec((total, piece), lambda i, p: (0, p[1] ^ partner(jnp.maximum(i - 4, 0))))
    return pl.pallas_call(
        kernel,
        name="expert_weight_grads",
        grid_spec=pltpu.PrefetchScalarGridSpec(
            num_scalar_prefetch=1,
            grid=(8,),
            in_specs=[fixed] * sets + [pre_cut] * sets + [act_cut] * sets + [fixed] * sets,
            out_specs=[
                pl.BlockSpec(
                    (piece, width), lambda i, p: (2 * (i // 4) + jnp.minimum(i % 4, 1), 0)
                ),
                pl.BlockSpec(
                    (piece, width), lambda i, p: (2 * (i // 4) + jnp.maximum(i % 4 - 2, 0), 0)
                ),
            ],
            scratch_shapes=[pltpu.VMEM((piece, width), f32)],
        ),
        out_shape=[shape((4 * piece, width), bf16), shape((4 * piece, width), f32)],
        compiler_params=limit(64),
        cost_estimate=long,
    )(place, *rows_in, *pre_grads, *actives, *slot_grads)


def far_sums(near, base, near_o, base_o, cuts, after):
    size, width = base.shape[0] // 4, base.shape[1]
    span = near_o.shape[0] // 2

    def block(rows, at):
        return pl.BlockSpec((rows, width), lambda *_: (at, 0), pipeline_mode=pl.Buffered(1))

    def kernel(near_in, near_out, base_in, base_out, near_o_ref, base_o_ref, *refs):
        out_refs = refs[len(after) :]
        out_refs[0][:span, :] = (base_o_ref[...] + near_o_ref[...].astype(f32)).astype(bf16)
        starts = [0] + cuts
        for i, ref in enumerate(out_refs):
            low, high = starts[i], starts[i + 1]
            at = span if i == 0 else 0
            for near_ref, base_ref, shift in ((near_in, base_in, 0), (near_out, base_out, size)):
                first, last = max(low, shift), min(high, shift + size)
                if first < last:
                    rows = slice(first - shift, last - shift)
                    held = base_ref[rows, :] + near_ref[rows, :].astype(f32)
                    ref[at + first - low : at + last - low, :] = held.astype(bf16)

    rows = [high - low for low, high in zip([0] + cuts, cuts)]
    rows[0] = rows[0] + span
    return pl.pallas_call(
        kernel,
        name="far_sums",
        grid=(1,),
        in_specs=[block(size, 1), block(size, 3), block(size, 1), block(size, 3)]
        + [block(span, 1), block(span, 1)]
        + [pl.BlockSpec(memory_space=pl.ANY)] * len(after),
        out_specs=[whole((count, width)) for count in rows],
        out_shape=[shape((count, width), bf16) for count in rows],
        compiler_params=limit(64),
        cost_estimate=brief,
    )(near, near, base, base, near_o, base_o, *after)


def input_grads(
    place,
    proj_grads,
    normed,
    weights,
    output_sum,
    gain,
    line_grad,
    bucket_hot,
    ffn_gain_grad,
    router_grad,
    members,
    owners,
    heads,
    after,
):
    seq_len, width = normed.shape
    span = weights[0].shape[1]
    rows = seq_len // members
    part = width // owners
    few = owners == 8
    experts = router_grad.shape[0]

    def kernel(place_ref, *refs):
        dq_ref, dk_ref, dv_ref, normed_ref, wq_ref, wk_ref, wv_ref, out_ref, gain_ref = refs[:9]
        line_ref, hot_ref, ffn_gain_ref, router_ref = refs[9:13]
        near_ref, base_ref, far_ref, small_ref, *weight_refs, sums = refs[13:]
        for at, ref in enumerate((dq_ref, dk_ref, dv_ref)):
            sums[:, at * span : (at + 1) * span] = dot(normed_ref[...], ref[...], 0, 0)
        sums[:, 3 * span :] = out_ref[...].T
        if few:
            for r, ref in enumerate(weight_refs):
                for i, far in enumerate((0, 4)):
                    at = pl.multiple_of((place_ref[0] ^ r ^ far) * part, part)
                    ref[i * part : (i + 1) * part, :] = sums[pl.ds(at, part), :].astype(ref.dtype)
        else:
            weight_refs[0][...] = sums[...]
        gain_grad = jnp.zeros((1, width), f32)
        for r, (ref, first) in enumerate(
            ((base_ref, 0), (near_ref, 0), (far_ref, 0), (near_ref, rows))
        ):
            at = pl.ds(pl.multiple_of((place_ref[1] ^ r) * rows, rows), rows)
            grad = (
                dot(dq_ref[at, :], wq_ref[...], 1, 1)
                + dot(dk_ref[at, :], wk_ref[...], 1, 1)
                + dot(dv_ref[at, :], wv_ref[...], 1, 1)
            )
            gain_grad = gain_grad + jnp.sum(
                grad * normed_ref[at, :].astype(f32), axis=0, keepdims=True
            )
            ref[first : first + rows, :] = grad.astype(ref.dtype)
        small_ref[...] = jnp.zeros_like(small_ref)
        small_ref[0:1, :] = gain_grad / gain_ref[...]
        small_ref[1:2, :] = ffn_gain_ref[...]
        table = dot(line_ref[...], hot_ref[...], 1, 0, highest)
        for m in range(members):
            own = jnp.where(place_ref[1] == m, table[:heads, :], 0.0)
            small_ref[2 + m * heads : 2 + (m + 1) * heads, :128] = own
        small_ref[16:, :] = router_ref[...]

    if few:
        weight_outs = [shape((2 * part, 4 * span), f32)] + [shape((2 * part, 4 * span), bf16)] * 3
    else:
        weight_outs = [shape((width, 4 * span), f32)]
    return call(
        kernel,
        "input_grads",
        list(proj_grads)
        + [normed]
        + list(weights)
        + [output_sum, gain, line_grad, bucket_hot, ffn_gain_grad, router_grad],
        [
            shape((2 * rows, width), bf16),
            shape((rows, width), f32),
            shape((rows, width), f32),
            shape((16 + experts, width), f32),
        ]
        + weight_outs,
        scratch=[pltpu.VMEM((width, 4 * span), f32)],
        scalars=place,
        after=after,
    )


def fold_weights(base, arrived, after, through):
    part, width = base.shape[0] // 2, base.shape[1]

    def kernel(base_ref, *refs):
        own_ref, far_ref = refs[-2:]
        total = base_ref[...]
        for ref in refs[:-2]:
            total = total + ref[...].astype(f32)
        own_ref[...] = total[:part, :]
        far_ref[...] = total[part:, :].astype(bf16)

    return call(
        kernel,
        "fold_weights",
        [base] + arrived,
        [shape((part, width), f32), shape((part, width), bf16)],
        after=after,
        through=through,
    )


def split_weights(parts, span):
    part = parts[0].shape[0]

    def kernel(*refs):
        q_ref, k_ref, v_ref, o_ref = refs[-4:]
        total = refs[0][...]
        for ref in refs[1:-4]:
            total = total + ref[...].astype(f32)
        for at, ref in enumerate((q_ref, k_ref, v_ref)):
            ref[...] = total[:, at * span : (at + 1) * span]
        o_ref[...] = total[:, 3 * span :].T

    return call(
        kernel,
        "split_weights",
        parts,
        [shape((part, span), f32)] * 3 + [shape((span, part), f32)],
    )


def gather_mp(values):
    across = swap(values, "mp", 2)
    return [values, swap(values, "mp", 1), across, swap(across, "mp", 1)]


def sum_over(values, axis):
    step = 1
    while step < lax.axis_size(axis):
        values = values + swap(values, axis, step)
        step = 2 * step
    return values


def all_to_all_dp(values):
    return lax.all_to_all(values, "dp", split_axis=0, concat_axis=0, tiled=True)


def slots_of(routes, place, capacity, experts, limit):
    rows = routes.shape[0]
    expert_ids = jnp.arange(experts, dtype=jnp.int32)[None, :]
    hits = (routes[:, 0:1] == expert_ids) | (routes[:, 1:2] == expert_ids)
    earlier = jnp.arange(rows)[:, None] > jnp.arange(rows)[None, :]
    ranks = jnp.dot(earlier.astype(bf16), hits.astype(bf16), preferred_element_type=f32)
    lines = []
    for k in (0, 1):
        rank = jnp.sum(jnp.where(routes[:, k : k + 1] == expert_ids, ranks, 0.0), axis=1)
        block = routes[:, k] ^ place
        lines.append(jnp.where(block < limit, block * capacity + rank.astype(jnp.int32), -1))
    return jnp.pad(jnp.stack(lines), ((0, 6), (0, 0)), constant_values=-1)


def on_device(
    tokens,
    norm_gain,
    w_query,
    w_key,
    w_value,
    w_output,
    bias_table,
    ffn_gain,
    w_router,
    w_in,
    w_out,
    segments,
    buckets,
    routes,
    cotangent,
):
    rows, width = tokens.shape
    heads = bias_table.shape[1]
    seq_len = buckets.shape[0]
    experts = w_router.shape[1]
    owners, members = lax.axis_size("dp"), lax.axis_size("mp")
    me, member = lax.axis_index("dp"), lax.axis_index("mp")
    place = jnp.stack([me, member]).astype(jnp.int32)
    capacity = 4 * rows // experts
    span = w_query.shape[1]
    window = reach + tile
    few = owners == 8

    token_blocks = gather_mp(tokens)
    pack = pack_weights(w_query, w_key, w_value, w_output)
    if few:
        both = pair_up(pack, swap(pack, "dp", 4), token_blocks[1:3])
        pack_blocks = [(both, (0, 4))] + [(swap(both, "dp", r), (r, r ^ 4)) for r in (1, 2, 3)]
    else:
        pack_blocks = [(lax.all_gather(pack, "dp", axis=0, tiled=True), (0,))]
    gain_one, gain_two = norm_gain.reshape(1, width), ffn_gain.reshape(1, width)
    normed, query, key_rows, value_rows, weight_q, weight_k, weight_v, w_o, late_cotangent = (
        project(place, token_blocks, pack_blocks, gain_one, cotangent, span)
    )

    if few:
        blocks, size = 4, capacity
        slots = [slots_of(routes, me, capacity, experts, 4)]
        slots.append(slots_of(swap(routes, "dp", 4), me, capacity, experts, 4))
    else:
        blocks, size = 1, experts * capacity
        slots = [slots_of(routes, 0, capacity, experts, experts)]

    if few:
        far_cotangent = swap(late_cotangent, "dp", 4)
        held = to_slots(
            "grads_to_slots",
            [(cotangent, slots[0]), (far_cotangent, slots[1])],
            blocks,
            size,
            cost=long,
        )
    else:
        held = to_slots("grads_to_slots", [(cotangent, slots[0])], blocks, size)

    line_buckets = jnp.pad(jnp.flip(buckets[: reach + 1]), (0, window - reach - 1))
    bucket_hot = (
        line_buckets[:, None] == jnp.arange(128, dtype=jnp.int32)[None, :]
    ).astype(f32)
    buckets_all = bias_table.shape[0]
    table = jnp.pad(bias_table.T, ((0, 8 - heads), (0, 128 - buckets_all)))
    line = jnp.dot(table, bucket_hot.T, precision=highest)
    seg_q = segments.reshape(seq_len, 1)
    seg_k = jnp.pad(segments.reshape(1, seq_len), ((0, 0), (reach, 0)), constant_values=-1)
    mixed_out = attend(
        place, query, key_rows, value_rows, seg_q, seg_k, line, heads, members, []
    )
    weight_o = gather_mp(w_o)
    mixed_in = [mixed_out[0]] + [swap(mixed_out[r], "mp", r) for r in range(1, members)]

    router_wide = jnp.pad(w_router, ((0, 0), (0, 128 - experts)))
    hidden, ffn_input, router_probs, *send = middle(
        tokens,
        mixed_in,
        weight_o,
        gain_two,
        router_wide,
        slots[0],
        experts,
        blocks,
        size,
        [far_cotangent] if few else [],
    )
    if few:
        far_input = swap(ffn_input, "dp", 4)
        own = [send[0]] + [swap(send[r], "dp", r) for r in (1, 2, 3)]
        far = to_slots(
            "far_to_slots", [(far_input, slots[1])], blocks, size, through=held[1:]
        )
        g_blocks = [held[0]] + [swap(far[blocks + r - 1], "dp", r) for r in (1, 2, 3)]
        far = [far[0]] + [swap(far[r], "dp", r) for r in (1, 2, 3)]
        x_sets = [own, far]
    else:
        x_sets = [[all_to_all_dp(send[0])]]
        g_blocks = [all_to_all_dp(held[0])]

    kept, before = [], []
    for at, x_blocks in enumerate(x_sets):
        last = at == len(x_sets) - 1
        result, *held = experts_forward(
            "experts_forward" + str(at),
            place,
            w_in[0],
            w_out[0],
            router_wide,
            x_blocks,
            experts,
            before if last else None,
            brief if last else long,
        )
        kept.append(held)
        before = before + held[3:]
    actives, slopes, arrived, plain, slot_gates = zip(*kept)
    sets = list(zip(slopes, plain, slot_gates))
    back, slot_grads, pre_grad = experts_backward(
        "experts_backward" + str(len(sets) - 1),
        place,
        w_in[0],
        w_out[0],
        sets,
        len(sets) - 1,
        None,
        g_blocks,
        blocks,
        brief,
    )
    pre_grads = [pre_grad]
    if few:
        own_back, _, pre_grad = experts_backward(
            "experts_backward0",
            place,
            w_in[0],
            w_out[0],
            sets,
            0,
            slot_grads[0],
            g_blocks,
            blocks,
            long,
        )
        pre_grads = [pre_grad] + pre_grads
        far_back = [back[0]] + [swap(back[r], "dp", r) for r in (1, 2, 3)]
        result_in = [result[0]] + [swap(result[r], "dp", r) for r in (1, 2, 3)]
        far_total, *passed = from_slots(
            "back_from_slots",
            far_back,
            [slots[1]],
            size,
            [bf16],
            after=result_in[1:],
            through=own_back[1:],
        )
        far_sum = swap(far_total, "dp", 4)
        own_back = [own_back[0]] + [swap(passed[r - 1], "dp", r) for r in (1, 2, 3)]
    else:
        own_back, far_sum = [all_to_all_dp(back[0])], None
        result_in = [all_to_all_dp(result[0])]
    near_w, base_w = expert_weight_grads(place, arrived, pre_grads, actives, slot_grads, members)

    homed = home(
        own_back,
        far_sum,
        slots[0],
        hidden,
        router_probs,
        cotangent,
        gain_two,
        router_wide,
        ffn_input,
        weight_o,
        mixed_in,
        size,
        experts,
        [],
        [near_w],
    )
    grad_out, homed = homed[:members], homed[members:]
    hidden_grad, ffn_gain_grad, router_grad, near_o, base_o, near_w = homed
    grad_in = [grad_out[0]] + [swap(grad_out[r], "mp", r) for r in range(1, members)]
    near_o, near_w = swap(near_o, "mp", 1), swap(near_w, "mp", 1)
    piece = w_in.shape[2] // members
    far_first, far_next, far_last = far_sums(
        near_w, base_w, near_o, base_o, [rows, piece, 2 * piece], grad_in[2:]
    )

    *proj_grads, line_grad = attend_back(
        place,
        query,
        key_rows,
        value_rows,
        seg_q,
        seg_k,
        line,
        grad_in,
        heads,
        [far_first],
    )
    far_first = swap(far_first, "mp", 2)
    far_next = swap(far_next, "mp", 2)
    far_last = swap(far_last, "mp", 2)
    output_sum = base_o[:span] + near_o[:span].astype(f32) + far_first[:span].astype(f32)
    near, base, base_far, small, *weight_sums = input_grads(
        place,
        proj_grads,
        normed,
        (weight_q, weight_k, weight_v),
        output_sum,
        gain_one,
        line_grad,
        bucket_hot,
        ffn_gain_grad,
        router_grad,
        members,
        owners,
        heads,
        [],
    )
    if few:
        arrived_sums = [swap(weight_sums[r], "dp", r) for r in (1, 2, 3)]
        own_sum, far_part, small = fold_weights(
            weight_sums[0], arrived_sums, [far_next], [small]
        )
        weight_grads = split_weights([own_sum, swap(far_part, "dp", 4)], span)
    else:
        joined_grad = lax.psum_scatter(weight_sums[0], "dp", scatter_dimension=0, tiled=True)
        weight_grads = split_weights([joined_grad], span)
    near = swap(near, "mp", 1)
    far_normed = swap((base_far + near[rows:].astype(f32)).astype(bf16), "mp", 2)
    normed_grad = base + near[:rows].astype(f32) + far_normed.astype(f32)
    resid = tokens.astype(f32)
    _, inverse_one = normalize(resid, norm_gain)
    scaled = normed_grad * norm_gain
    inner = jnp.mean(scaled * resid, axis=-1, keepdims=True)
    tokens_grad = (
        hidden_grad + inverse_one * scaled - resid * inverse_one * inverse_one * inverse_one * inner
    ).astype(bf16)

    if few:
        own_result, far_result = from_slots(
            "result_from_slots", result_in, slots, size, [f32, bf16], after=[base]
        )
        block_out = hidden + own_result + swap(far_result, "dp", 4).astype(f32)
    else:
        (own_result,) = from_slots("result_from_slots", result_in, slots, size, [f32])
        block_out = hidden + own_result
    block_out = block_out.astype(bf16)
    far_in = jnp.concatenate([far_first[span:], far_next], axis=0).astype(f32)
    w_in_grad = base_w[:piece] + near_w[:piece].astype(f32) + far_in
    own_out = base_w[2 * piece : 3 * piece] + near_w[2 * piece : 3 * piece].astype(f32)
    w_out_grad = own_out + far_last.astype(f32)
    small = sum_over(sum_over(small, "dp"), "mp")
    return (
        block_out,
        tokens_grad,
        small[0],
        *weight_grads,
        small[2 : 2 + heads * members, :buckets_all].T,
        small[1],
        small[16:].T,
        w_in_grad[None],
        w_out_grad[None],
    )


def solution(mesh):
    return jax.shard_map(
        on_device,
        mesh=mesh,
        in_specs=(
            P(("dp", "mp"), None),
            P(),
            P("dp", "mp"),
            P("dp", "mp"),
            P("dp", "mp"),
            P("mp", "dp"),
            P(None, "mp"),
            P(),
            P(),
            P("dp", None, None),
            P("dp", None, None),
            P("dp", None),
            P(),
            P(("dp", "mp"), None),
            P(("dp", "mp"), None),
        ),
        out_specs=(
            P(("dp", "mp"), None),
            P(("dp", "mp"), None),
            P(),
            P("dp", "mp"),
            P("dp", "mp"),
            P("dp", "mp"),
            P("mp", "dp"),
            P(),
            P(),
            P(),
            P("dp", None, "mp"),
            P("dp", "mp", None),
        ),
        check_vma=False,
    )
```

```python
import functools
import math

import jax
import jax.numpy as jnp
from jax import lax
from jax.experimental import pallas as pl
from jax.experimental.pallas import tpu as pltpu
from jax.sharding import PartitionSpec as P

eps = 1e-06
highest = lax.Precision.HIGHEST
f32, bf16 = jnp.float32, jnp.bfloat16
excluded = -1e30
reach = 512
tile = 128


def limit(mebibytes):
    return pltpu.CompilerParams(vmem_limit_bytes=mebibytes * 1024 * 1024)


brief = pl.CostEstimate(flops=10**7, bytes_accessed=10**4, transcendentals=0)
long = pl.CostEstimate(flops=2 * 10**10, bytes_accessed=10**7, transcendentals=0)


def normalize(values, gain):
    inverse = lax.rsqrt(jnp.mean(values * values, axis=-1, keepdims=True) + eps)
    return (values * inverse * gain, inverse)


def dot(left, right, left_dim, right_dim, precision=None):
    return lax.dot_general(
        left,
        right,
        (((left_dim,), (right_dim,)), ((), ())),
        precision=precision,
        preferred_element_type=f32,
    )


def swap(values, axis, step):
    count = lax.axis_size(axis)
    return lax.ppermute(values, axis, [(i, i ^ step) for i in range(count)])


def whole(dims):
    return pl.BlockSpec(tuple(dims), lambda *_: (0,) * len(dims), pipeline_mode=pl.Buffered(1))


def call(
    kernel, name, operands, outs, scratch=(), scalars=None, after=(), through=(), cost=None
):
    outs = list(outs)
    pairs = [o if isinstance(o, tuple) else (o, o.shape[0]) for o in operands]
    operands = [array for array, _ in pairs]
    in_specs = [whole((rows,) + array.shape[1:]) for array, rows in pairs]
    out_specs = [whole(o.shape) for o in outs]
    if scalars is not None:
        operands = [scalars] + operands
        in_specs = [pl.BlockSpec(memory_space=pltpu.SMEM)] + in_specs
    count, results = len(operands), len(outs)
    extra = list(through) + list(after)

    def body(*refs):
        rest = refs[count + len(extra) :]
        kernel(*refs[:count], *rest[:results], *rest[results + len(through) :])

    return pl.pallas_call(
        body,
        name=name,
        grid=(1,),
        in_specs=in_specs + [pl.BlockSpec(memory_space=pl.ANY)] * len(extra),
        out_specs=out_specs + [pl.BlockSpec(memory_space=pl.ANY)] * len(through),
        out_shape=outs + [shape(o.shape, o.dtype) for o in through],
        input_output_aliases={count + i: results + i for i in range(len(through))},
        scratch_shapes=list(scratch),
        compiler_params=limit(64),
        cost_estimate=cost or brief,
    )(*operands, *extra)


def shape(dims, dtype):
    return jax.ShapeDtypeStruct(tuple(dims), dtype)


def fill_skew(line_ref, skew, heads):
    window = reach + tile
    row = lax.broadcasted_iota(jnp.int32, (tile, window), 0)
    column = lax.broadcasted_iota(jnp.int32, (tile, window), 1)
    usable = (column - row <= reach) & (column - row >= 1)
    for head in range(heads):
        line = jnp.broadcast_to(line_ref[head : head + 1, :], (tile, window))
        rolled = pltpu.roll(line, 0, 1, stride=1, stride_axis=0)
        skew[head * tile : (head + 1) * tile, :] = jnp.where(usable, rolled, excluded)


def fill_window(source_ref, padded):
    padded[:reach, :] = jnp.zeros((reach, padded.shape[1]), bf16)
    padded[reach:, :] = source_ref[...]


def spread_heads(values, heads, scale):
    span = values.shape[1]
    size = span // heads
    lane = lax.broadcasted_iota(jnp.int32, (tile, span), 1)
    wide = values.astype(f32) * scale
    parts = [
        jnp.where((lane >= head * size) & (lane < (head + 1) * size), wide, 0.0)
        for head in range(heads)
    ]
    return jnp.concatenate(parts, axis=0).astype(bf16)


def collect_heads(stacked, heads):
    span = stacked.shape[1]
    size = span // heads
    lane = lax.broadcasted_iota(jnp.int32, (tile, span), 1)
    total = stacked[:tile, :]
    for head in range(1, heads):
        total = jnp.where(lane < head * size, total, stacked[head * tile : (head + 1) * tile, :])
    return total


def window_powers(q_all, keys, skew, seg_q_ref, seg_k_ref, start, heads):
    window = reach + tile
    seg_q = jnp.concatenate([seg_q_ref[pl.ds(start, tile), :]] * heads, axis=0)
    seg_k = seg_k_ref[:, pl.ds(start, window)]
    scores = dot(q_all, keys, 1, 1) + skew[...]
    scores = jnp.where(seg_q == seg_k, scores, excluded)
    powers = jnp.exp(scores - jnp.max(scores, axis=-1, keepdims=True))
    return powers, 1.0 / jnp.sum(powers, axis=-1, keepdims=True)


def attend_kernel(heads, place, q_ref, k_ref, v_ref, seg_q_ref, seg_k_ref, line_ref, *rest):
    *out_refs, mixed, k_pad, v_pad, skew = rest
    window = reach + tile
    scale = (q_ref.shape[1] // heads) ** (-0.5)
    fill_skew(line_ref, skew, heads)
    fill_window(k_ref, k_pad)
    fill_window(v_ref, v_pad)

    def step(index, carry):
        start = pl.multiple_of(index * tile, tile)
        q_all = spread_heads(q_ref[pl.ds(start, tile), :], heads, scale)
        powers, inverse = window_powers(
            q_all, k_pad[pl.ds(start, window), :], skew, seg_q_ref, seg_k_ref, start, heads
        )
        probs = (powers * inverse).astype(bf16)
        part = dot(probs, v_pad[pl.ds(start, window), :], 1, 0)
        mixed[pl.ds(start, tile), :] = collect_heads(part, heads).astype(bf16)
        return carry

    lax.fori_loop(0, q_ref.shape[0] // tile, step, 0)
    rows = out_refs[0].shape[0]
    for r, out_ref in enumerate(out_refs):
        out_ref[...] = mixed[pl.ds(pl.multiple_of((place[1] ^ r) * rows, rows), rows), :]


def attend(place, query, key_rows, value_rows, seg_q, seg_k, line, heads, members, after):
    seq_len, span = query.shape
    window = reach + tile

    def kernel(place_ref, *refs):
        attend_kernel(heads, place_ref, *refs)

    return call(
        kernel,
        "attend",
        [query, key_rows, value_rows, seg_q, seg_k, line],
        [shape((seq_len // members, span), bf16)] * members,
        scratch=[
            pltpu.VMEM((seq_len, span), bf16),
            pltpu.VMEM((seq_len + reach, span), bf16),
            pltpu.VMEM((seq_len + reach, span), bf16),
            pltpu.VMEM((heads * tile, window), f32),
        ],
        scalars=place,
        after=after,
    )


def attend_back_kernel(heads, members, place, *refs):
    q_ref, k_ref, v_ref, seg_q_ref, seg_k_ref, line_ref = refs[:6]
    g_refs = refs[6 : 6 + members]
    dq_ref, dk_ref, dv_ref, line_grad_ref = refs[6 + members : 10 + members]
    grad, k_pad, v_pad, skew, dk_sum, dv_sum, bias_sum = refs[10 + members :]
    window = reach + tile
    scale = (q_ref.shape[1] // heads) ** (-0.5)
    rows = g_refs[0].shape[0]
    fill_skew(line_ref, skew, heads)
    fill_window(k_ref, k_pad)
    fill_window(v_ref, v_pad)
    dk_sum[...] = jnp.zeros_like(dk_sum)
    dv_sum[...] = jnp.zeros_like(dv_sum)
    bias_sum[...] = jnp.zeros_like(bias_sum)
    for r, g_ref in enumerate(g_refs):
        grad[pl.ds(pl.multiple_of((place[1] ^ r) * rows, rows), rows), :] = g_ref[...]

    def step(index, carry):
        start = pl.multiple_of(index * tile, tile)
        keys = k_pad[pl.ds(start, window), :]
        values = v_pad[pl.ds(start, window), :]
        q_all = spread_heads(q_ref[pl.ds(start, tile), :], heads, scale)
        g_all = spread_heads(grad[pl.ds(start, tile), :], heads, 1.0)
        powers, inverse = window_powers(q_all, keys, skew, seg_q_ref, seg_k_ref, start, heads)
        probs = powers * inverse
        dot_grad = dot(g_all, values, 1, 1)
        inner = jnp.sum(probs * dot_grad, axis=-1, keepdims=True)
        score_grad = (probs * (dot_grad - inner)).astype(bf16)
        bias_sum[...] += score_grad.astype(f32)
        part = collect_heads(dot(score_grad, keys, 1, 0), heads) * scale
        dq_ref[pl.ds(start, tile), :] = part.astype(bf16)
        dk_sum[pl.ds(start, window), :] += dot(score_grad, q_all, 0, 0)
        dv_sum[pl.ds(start, window), :] += dot(probs.astype(bf16), g_all, 0, 0)
        return carry

    lax.fori_loop(0, q_ref.shape[0] // tile, step, 0)
    dk_ref[...] = dk_sum[reach:, :].astype(bf16)
    dv_ref[...] = dv_sum[reach:, :].astype(bf16)
    line_grad_ref[...] = jnp.zeros_like(line_grad_ref)
    row = lax.broadcasted_iota(jnp.int32, (tile, tile), 0)
    column = lax.broadcasted_iota(jnp.int32, (tile, tile), 1)
    mirror = (row + column == tile - 1).astype(f32)
    for head in range(heads):
        part = bias_sum[head * tile : (head + 1) * tile, :]
        turned = dot(mirror, part, 1, 0, highest)
        straight = pltpu.roll(turned, window - tile + 1, 1, stride=1, stride_axis=0)
        line_grad_ref[head : head + 1, :] = jnp.sum(straight, axis=0, keepdims=True)


def attend_back(place, query, key_rows, value_rows, seg_q, seg_k, line, grads, heads, after):
    seq_len, span = query.shape
    window = reach + tile

    def kernel(place_ref, *refs):
        attend_back_kernel(heads, len(grads), place_ref, *refs)

    return call(
        kernel,
        "attend_back",
        [query, key_rows, value_rows, seg_q, seg_k, line] + grads,
        [shape((seq_len, span), bf16)] * 3 + [shape((8, window), f32)],
        scratch=[
            pltpu.VMEM((seq_len, span), bf16),
            pltpu.VMEM((seq_len + reach, span), bf16),
            pltpu.VMEM((seq_len + reach, span), bf16),
            pltpu.VMEM((heads * tile, window), f32),
            pltpu.VMEM((seq_len + reach, span), f32),
            pltpu.VMEM((seq_len + reach, span), f32),
            pltpu.VMEM((heads * tile, window), f32),
        ],
        scalars=place,
        after=after,
    )


def pack_weights(w_query, w_key, w_value, w_output):
    part, span = w_query.shape

    def kernel(q_ref, k_ref, v_ref, o_ref, pack_ref):
        for at, ref in enumerate((q_ref, k_ref, v_ref)):
            pack_ref[:, at * span : (at + 1) * span] = ref[...]
        pack_ref[:, 3 * span :] = o_ref[...].astype(f32).T.astype(bf16)

    (pack,) = call(
        kernel, "pack_weights", [w_query, w_key, w_value, w_output], [shape((part, 4 * span), bf16)]
    )
    return pack


def pair_up(pack, far, after):
    part = pack.shape[0]

    def kernel(near_ref, far_ref, both_ref):
        both_ref[:part, :] = near_ref[...]
        both_ref[part:, :] = far_ref[...]

    (both,) = call(
        kernel, "pair_up", [pack, far], [shape((2 * part, pack.shape[1]), bf16)], after=after
    )
    return both


def project(place, token_blocks, pack_blocks, gain, cotangent, span):
    rows, width = token_blocks[0].shape
    members = len(token_blocks)
    seq_len = rows * members
    parts = sum(len(held) for _, held in pack_blocks)
    part = width // parts

    def kernel(place_ref, gain_ref, *refs):
        token_refs = refs[:members]
        pack_refs = refs[members : members + len(pack_blocks)]
        (normed_ref, q_ref, k_ref, v_ref, wq_ref, wk_ref, wv_ref, wo_ref, pack) = refs[
            members + len(pack_blocks) :
        ]
        for (_, held), ref in zip(pack_blocks, pack_refs):
            for i, r in enumerate(held):
                at = pl.multiple_of((place_ref[0] ^ r) * part, part) if parts > 1 else 0
                pack[pl.ds(at, part), :] = ref[i * part : (i + 1) * part, :]
        for at, ref in enumerate((wq_ref, wk_ref, wv_ref)):
            ref[...] = pack[:, at * span : (at + 1) * span]
        wo_ref[...] = pack[:, 3 * span :].astype(f32).T.astype(bf16)
        for r, ref in enumerate(token_refs):
            normed, _ = normalize(ref[...].astype(f32), gain_ref[...])
            normed = normed.astype(bf16)
            at = pl.ds(pl.multiple_of((place_ref[1] ^ r) * rows, rows), rows)
            normed_ref[at, :] = normed
            q_ref[at, :] = dot(normed, wq_ref[...], 1, 0).astype(bf16)
            k_ref[at, :] = dot(normed, wk_ref[...], 1, 0).astype(bf16)
            v_ref[at, :] = dot(normed, wv_ref[...], 1, 0).astype(bf16)

    return call(
        kernel,
        "project",
        [gain] + list(token_blocks) + [array for array, _ in pack_blocks],
        [shape((seq_len, width), bf16)]
        + [shape((seq_len, span), bf16)] * 3
        + [shape((width, span), bf16)] * 3
        + [shape((span, width), bf16)],
        scratch=[pltpu.VMEM((width, width), bf16)],
        scalars=place,
        through=[cotangent],
    )


def hot(slots_ref, first, count):
    tokens = slots_ref.shape[1]
    slot = lax.broadcasted_iota(jnp.int32, (count, tokens), 0) + first
    taken = (slot == slots_ref[0:1, :]) | (slot == slots_ref[1:2, :])
    return jnp.where(taken, 1.0, 0.0).astype(bf16)


def to_slots(name, sets, blocks, size, through=(), cost=None):
    width = sets[0][0].shape[1]

    def kernel(*refs):
        out_refs = refs[2 * len(sets) :]
        for at in range(len(sets)):
            rows_ref, slots_ref = refs[2 * at], refs[2 * at + 1]
            for b, out_ref in enumerate(out_refs):
                part = dot(hot(slots_ref, b * size, size), rows_ref[...], 1, 0)
                out_ref[at * size : (at + 1) * size, :] = part.astype(bf16)

    operands = [item for pair in sets for item in pair]
    return call(
        kernel,
        name,
        operands,
        [shape((size * len(sets), width), bf16)] * blocks,
        through=through,
        cost=cost,
    )


def from_slots(name, blocks, slots, size, dtypes, after=(), through=(), cost=None):
    count, sets = len(blocks), len(slots)
    width = blocks[0].shape[1]
    rows = slots[0].shape[1]

    def kernel(*refs):
        block_refs, slot_refs, out_refs = refs[:count], refs[count : count + sets], refs[count + sets :]
        for at in range(sets):
            total = None
            for b, ref in enumerate(block_refs):
                held = ref[at * size : (at + 1) * size, :]
                part = dot(hot(slot_refs[at], b * size, size), held, 0, 0)
                total = part if total is None else total + part
            out_refs[at][...] = total.astype(out_refs[at].dtype)

    return call(
        kernel,
        name,
        list(blocks) + list(slots),
        [shape((rows, width), dtype) for dtype in dtypes],
        after=after,
        through=through,
        cost=cost,
    )


def router_softmax(values, w_router, experts):
    logits = dot(values, w_router, 1, 0)
    lane = lax.broadcasted_iota(jnp.int32, logits.shape, 1)
    logits = jnp.where(lane < experts, logits, excluded)
    powers = jnp.exp(logits - jnp.max(logits, axis=-1, keepdims=True))
    return powers / jnp.sum(powers, axis=-1, keepdims=True)


def middle(tokens, mixed, weight_o, gain, w_router, slots, experts, blocks, size, after):
    rows, width = tokens.shape
    members = len(mixed)

    def kernel(*refs):
        token_ref, gain_ref, router_ref, slots_ref = refs[:4]
        mixed_refs, weight_refs = refs[4 : 4 + members], refs[4 + members : 4 + 2 * members]
        hidden_ref, input_ref, probs_ref, *send_refs = refs[4 + 2 * members :]
        hidden = token_ref[...].astype(f32)
        for left, right in zip(mixed_refs, weight_refs):
            hidden = hidden + dot(left[...], right[...], 1, 0)
        hidden_ref[...] = hidden
        normed, _ = normalize(hidden, gain_ref[...])
        normed = normed.astype(bf16)
        input_ref[...] = normed
        for b, ref in enumerate(send_refs):
            ref[...] = dot(hot(slots_ref, b * size, size), normed, 1, 0).astype(bf16)
        probs_ref[...] = router_softmax(normed, router_ref[...], experts)

    return call(
        kernel,
        "middle",
        [tokens, gain, w_router, slots] + mixed + weight_o,
        [shape((rows, width), f32), shape((rows, width), bf16), shape((rows, 128), f32)]
        + [shape((size, width), bf16)] * blocks,
        after=after,
    )


def join_rows(refs):
    return jnp.concatenate([ref[...] for ref in refs], axis=0)


def experts_forward(
    name, place, w_in, w_out, w_router, x_blocks, experts, before, cost, through=()
):
    width, units = w_in.shape
    count, size = len(x_blocks), x_blocks[0].shape[0]
    total, piece, chunk = size * count, 768, 256
    sets = 1 if before is None else 1 + len(before) // 2
    blocks = 0 if before is None else count
    before, through = [] if before is None else list(before), list(through)

    def kernel(me_ref, w_in_ref, w_out_ref, router_ref, *refs):
        x_refs, refs = refs[:count], refs[count:]
        before_refs, refs = refs[: len(before)], refs[len(before) + len(through) :]
        out_refs, refs = refs[:blocks], refs[blocks:]
        active_ref, slope_ref, x_all, result_ref, gates_ref = refs[:5]
        result_sum = refs[-1]

        @pl.when(pl.program_id(0) == 0)
        def _():
            x_all[...] = join_rows(x_refs)
            probs = router_softmax(x_all[...], router_ref[...], experts)
            lane = lax.broadcasted_iota(jnp.int32, probs.shape, 1)
            own = jnp.sum(jnp.where(lane == me_ref[0], probs, 0.0), axis=1, keepdims=True)
            gates_ref[...] = jnp.broadcast_to(own, gates_ref.shape)
            result_sum[...] = jnp.zeros_like(result_sum)

        for c in range(piece // chunk):
            at = slice(c * chunk, (c + 1) * chunk)
            pre_act = dot(x_all[...], w_in_ref[:, at], 1, 0)
            below = 0.5 + 0.5 * lax.erf(pre_act * math.sqrt(0.5))
            bell = jnp.exp(-0.5 * pre_act * pre_act) * (1.0 / math.sqrt(2.0 * math.pi))
            active_ref[:, at] = (pre_act * below).astype(bf16)
            slope_ref[:, at] = (below + pre_act * bell).astype(bf16)
        result_sum[...] += dot(active_ref[...], w_out_ref[...], 1, 0)

        @pl.when(pl.program_id(0) == pl.num_programs(0) - 1)
        def _():
            result = result_sum[...].astype(bf16)
            result_ref[...] = result
            if blocks:
                held = [(before_refs[i], before_refs[i + 1]) for i in range(0, len(before), 2)]
                held.append((result_ref, gates_ref))
                for at, (rows_ref, gate_ref) in enumerate(held):
                    gated = (gate_ref[:, 0:1] * rows_ref[...].astype(f32)).astype(bf16)
                    for b, ref in enumerate(out_refs):
                        ref[at * size : (at + 1) * size, :] = gated[b * size : (b + 1) * size, :]

    columns = pl.BlockSpec((total, piece), lambda i: (0, i))
    outs = [shape((size * sets, width), bf16)] * blocks
    kept = [shape((total, width), bf16)] * 2 + [shape((total, 128), f32)]
    flat = pl.pallas_call(
        kernel,
        name=name,
        grid=(units // piece,),
        in_specs=[
            pl.BlockSpec(memory_space=pltpu.SMEM),
            pl.BlockSpec((width, piece), lambda i: (0, i)),
            pl.BlockSpec((piece, width), lambda i: (i, 0)),
            whole(w_router.shape),
        ]
        + [whole(o.shape) for o in x_blocks]
        + [whole(o.shape) for o in before]
        + [pl.BlockSpec(memory_space=pl.ANY)] * len(through),
        out_specs=[whole(o.shape) for o in outs]
        + [columns] * 2
        + [whole(o.shape) for o in kept]
        + [pl.BlockSpec(memory_space=pl.ANY)] * len(through),
        out_shape=outs
        + [shape((total, units), bf16)] * 2
        + kept
        + [shape(o.shape, o.dtype) for o in through],
        input_output_aliases={
            4 + count + len(before) + i: blocks + 5 + i for i in range(len(through))
        },
        scratch_shapes=[pltpu.VMEM((total, width), f32)],
        compiler_params=limit(64),
        cost_estimate=cost,
    )(place, w_in, w_out, w_router, *x_blocks, *before, *through)
    return (list(flat[:blocks]), *flat[blocks:])


def experts_backward(name, place, w_in, w_out, sets, at_set, slot_grad, g_blocks, count, cost):
    width, units = w_in.shape
    slope, result, _ = sets[at_set]
    total, piece, chunk = slope.shape[0], 768, 256
    size = total // count
    number = len(sets)
    first = slot_grad is None
    given = [gates for _, _, gates in sets] if first else [slot_grad]
    made = number if first else 0

    def kernel(me_ref, w_in_ref, w_out_ref, slope_ref, result_ref, *refs):
        given_refs, refs = refs[: len(given)], refs[len(given) :]
        g_refs, refs = refs[: len(g_blocks)], refs[len(g_blocks) :]
        back_refs, refs = refs[:count], refs[count:]
        s_refs, pre_grad_ref, back_sum = refs[:made], refs[made], refs[made + 1]
        s_ref = s_refs[at_set] if first else given_refs[0]

        @pl.when(pl.program_id(0) == 0)
        def _():
            back_sum[...] = jnp.zeros_like(back_sum)
            if first:
                for at in range(number):
                    for b, ref in enumerate(g_refs):
                        rows = slice(b * size, (b + 1) * size)
                        grad = ref[at * size : (at + 1) * size, :].astype(f32)
                        s_refs[at][rows, :] = (given_refs[at][rows, 0:1] * grad).astype(bf16)

        for c in range(piece // chunk):
            at = slice(c * chunk, (c + 1) * chunk)
            active_grad = dot(s_ref[...], w_out_ref[at, :], 1, 1)
            pre_grad_ref[:, at] = (active_grad * slope_ref[:, at].astype(f32)).astype(bf16)
        back_sum[...] += dot(pre_grad_ref[...], w_in_ref[...], 1, 1)

        @pl.when(pl.program_id(0) == pl.num_programs(0) - 1)
        def _():
            lane = lax.broadcasted_iota(jnp.int32, (size, 128), 1)
            for b, (ref, g_ref) in enumerate(zip(back_refs, g_refs)):
                rows = slice(b * size, (b + 1) * size)
                grad = g_ref[at_set * size : (at_set + 1) * size, :].astype(f32)
                gate_grad = jnp.sum(
                    grad * result_ref[rows, :].astype(f32), axis=1, keepdims=True
                )
                upper = gate_grad.astype(bf16).astype(f32)
                ref[:, :width] = back_sum[rows, :].astype(bf16)
                ref[:, width:] = jnp.where(
                    lane == me_ref[0],
                    upper,
                    jnp.where(lane == me_ref[0] + 64, gate_grad - upper, 0.0),
                ).astype(bf16)

    by_units = pl.BlockSpec((total, piece), lambda i: (0, i))
    outs = [shape((size, width + 128), bf16)] * count + [shape((total, width), bf16)] * made
    flat = pl.pallas_call(
        kernel,
        name=name,
        grid=(units // piece,),
        in_specs=[
            pl.BlockSpec(memory_space=pltpu.SMEM),
            pl.BlockSpec((width, piece), lambda i: (0, i)),
            pl.BlockSpec((piece, width), lambda i: (i, 0)),
            by_units,
            whole(result.shape),
        ]
        + [whole(o.shape) for o in given]
        + [whole(o.shape) for o in g_blocks],
        out_specs=[whole(o.shape) for o in outs] + [by_units],
        out_shape=outs + [shape((total, units), bf16)],
        scratch_shapes=[pltpu.VMEM((total, width), f32)],
        compiler_params=limit(64),
        cost_estimate=cost,
    )(place, w_in, w_out, slope, result, *given, *g_blocks)
    return list(flat[:count]), list(flat[count : count + made]), flat[-1]


def home(
    own_back,
    far_sum,
    slots,
    hidden,
    probs,
    cotangent,
    gain,
    w_router,
    ffn_input,
    weight_o,
    mixed,
    size,
    experts,
    after,
    through,
):
    rows, width = hidden.shape
    count, members = len(own_back), len(weight_o)
    span = weight_o[0].shape[0]
    far = [] if far_sum is None else [far_sum]

    def kernel(*refs):
        slots_ref, hidden_ref, probs_ref, cot_ref, gain_ref, router_ref, input_ref = refs[:7]
        refs = refs[7:]
        back_refs, refs = refs[:count], refs[count:]
        far_refs, refs = refs[: len(far)], refs[len(far) :]
        weight_refs, mixed_refs, refs = refs[:members], refs[members : 2 * members], refs[2 * members :]
        grad_refs = refs[:members]
        hidden_grad_ref, gain_grad_ref, router_grad_ref, near_ref, base_ref = refs[members:]
        total = None
        for b, ref in enumerate(back_refs):
            part = dot(hot(slots_ref, b * size, size), ref[...], 0, 0)
            total = part if total is None else total + part
        for ref in far_refs:
            total = total + ref[...].astype(f32)
        columns = total[:, width:]
        lane = lax.broadcasted_iota(jnp.int32, columns.shape, 1)
        prob_grad = jnp.where(lane < 64, columns + pltpu.roll(columns, 64, 1), 0.0)
        router_probs = probs_ref[...]
        logit_grad = router_probs * (
            prob_grad - jnp.sum(router_probs * prob_grad, axis=-1, keepdims=True)
        )
        router_grad_ref[...] = dot(logit_grad, input_ref[...].astype(f32), 0, 0, highest)[:experts, :]
        grad = total[:, :width] + dot(logit_grad, router_ref[...].astype(f32), 1, 1, highest)
        hidden_now = hidden_ref[...]
        inverse = lax.rsqrt(jnp.mean(hidden_now * hidden_now, axis=-1, keepdims=True) + eps)
        scaled = grad * gain_ref[...]
        gain_grad_ref[...] = jnp.sum(grad * hidden_now * inverse, axis=0, keepdims=True)
        inner = jnp.mean(scaled * hidden_now, axis=-1, keepdims=True)
        hidden_grad = (
            cot_ref[...].astype(f32)
            + inverse * scaled
            - hidden_now * inverse * inverse * inverse * inner
        )
        hidden_grad_ref[...] = hidden_grad
        attn_grad = hidden_grad.astype(bf16)
        for ref, weight in zip(grad_refs, weight_refs):
            ref[...] = dot(attn_grad, weight[...], 1, 1).astype(bf16)
        for r, (ref, first) in enumerate(
            ((base_ref, 0), (near_ref, 0), (base_ref, span), (near_ref, span))
        ):
            part = dot(mixed_refs[r][...], attn_grad, 0, 0)
            ref[first : first + span, :] = part.astype(ref.dtype)

    return call(
        kernel,
        "home",
        [slots, hidden, probs, cotangent, gain, w_router, ffn_input]
        + list(own_back)
        + far
        + weight_o
        + mixed,
        [shape((rows, span), bf16)] * members
        + [
            shape((rows, width), f32),
            shape((1, width), f32),
            shape((experts, width), f32),
            shape((2 * span, width), bf16),
            shape((2 * span, width), f32),
        ],
        after=after,
        through=through,
    )


def expert_weight_grads(place, rows_in, pre_grads, actives, slot_grads, members):
    sets = len(rows_in)
    total, width = rows_in[0].shape
    piece = pre_grads[0].shape[1] // members

    def kernel(place_ref, *refs):
        x_refs, p_refs, a_refs, s_refs = [refs[i * sets : (i + 1) * sets] for i in range(4)]
        near_ref, base_ref, out = refs[4 * sets :]
        step = pl.program_id(0)

        def total_of(lefts, rights):
            held = dot(lefts[0][...], rights[0][...], 0, 0)
            for left, right in zip(lefts[1:], rights[1:]):
                held = held + dot(left[...], right[...], 0, 0)
            return held

        @pl.when(step < 4)
        def _():
            out[...] = total_of(x_refs, p_refs)

        @pl.when(step >= 4)
        def _():
            out[...] = total_of(a_refs, s_refs)

        @pl.when(step % 4 < 2)
        def _():
            near_ref[...] = out[...].astype(bf16)

        @pl.when(step % 4 >= 2)
        def _():
            base_ref[...] = out[...]

    def partner(i):
        return jnp.where(i < 2, 2 * i + 1, 2 * i - 4)

    fixed = pl.BlockSpec((total, width), lambda i, p: (0, 0))
    pre_cut = pl.BlockSpec((total, piece), lambda i, p: (0, p[1] ^ partner(jnp.minimum(i, 3))))
    act_cut = pl.BlockSpec((total, piece), lambda i, p: (0, p[1] ^ partner(jnp.maximum(i - 4, 0))))
    return pl.pallas_call(
        kernel,
        name="expert_weight_grads",
        grid_spec=pltpu.PrefetchScalarGridSpec(
            num_scalar_prefetch=1,
            grid=(8,),
            in_specs=[fixed] * sets + [pre_cut] * sets + [act_cut] * sets + [fixed] * sets,
            out_specs=[
                pl.BlockSpec(
                    (piece, width), lambda i, p: (2 * (i // 4) + jnp.minimum(i % 4, 1), 0)
                ),
                pl.BlockSpec(
                    (piece, width), lambda i, p: (2 * (i // 4) + jnp.maximum(i % 4 - 2, 0), 0)
                ),
            ],
            scratch_shapes=[pltpu.VMEM((piece, width), f32)],
        ),
        out_shape=[shape((4 * piece, width), bf16), shape((4 * piece, width), f32)],
        compiler_params=limit(64),
        cost_estimate=long,
    )(place, *rows_in, *pre_grads, *actives, *slot_grads)


def far_sums(near, base, near_o, base_o, cuts, after):
    size, width = base.shape[0] // 4, base.shape[1]
    span = near_o.shape[0] // 2

    def block(rows, at):
        return pl.BlockSpec((rows, width), lambda *_: (at, 0), pipeline_mode=pl.Buffered(1))

    def kernel(near_in, near_out, base_in, base_out, near_o_ref, base_o_ref, *refs):
        out_refs = refs[len(after) :]
        out_refs[0][:span, :] = (base_o_ref[...] + near_o_ref[...].astype(f32)).astype(bf16)
        starts = [0] + cuts
        for i, ref in enumerate(out_refs):
            low, high = starts[i], starts[i + 1]
            at = span if i == 0 else 0
            for near_ref, base_ref, shift in ((near_in, base_in, 0), (near_out, base_out, size)):
                first, last = max(low, shift), min(high, shift + size)
                if first < last:
                    rows = slice(first - shift, last - shift)
                    held = base_ref[rows, :] + near_ref[rows, :].astype(f32)
                    ref[at + first - low : at + last - low, :] = held.astype(bf16)

    rows = [high - low for low, high in zip([0] + cuts, cuts)]
    rows[0] = rows[0] + span
    return pl.pallas_call(
        kernel,
        name="far_sums",
        grid=(1,),
        in_specs=[block(size, 1), block(size, 3), block(size, 1), block(size, 3)]
        + [block(span, 1), block(span, 1)]
        + [pl.BlockSpec(memory_space=pl.ANY)] * len(after),
        out_specs=[whole((count, width)) for count in rows],
        out_shape=[shape((count, width), bf16) for count in rows],
        compiler_params=limit(64),
        cost_estimate=brief,
    )(near, near, base, base, near_o, base_o, *after)


def input_grads(
    place,
    proj_grads,
    normed,
    weights,
    output_parts,
    gain,
    line_grad,
    bucket_hot,
    ffn_gain_grad,
    router_grad,
    members,
    owners,
    heads,
    after,
):
    seq_len, width = normed.shape
    span = weights[0].shape[1]
    rows = seq_len // members
    part = width // owners
    few = owners == 8
    experts = router_grad.shape[0]

    def kernel(place_ref, *refs):
        dq_ref, dk_ref, dv_ref, normed_ref, wq_ref, wk_ref, wv_ref, gain_ref = refs[:8]
        line_ref, hot_ref, ffn_gain_ref, router_ref = refs[8:12]
        base_o_ref, near_o_ref, far_o_ref = refs[12:15]
        near_ref, base_ref, far_ref, small_ref, *weight_refs, sums = refs[15:]
        for at, ref in enumerate((dq_ref, dk_ref, dv_ref)):
            sums[:, at * span : (at + 1) * span] = dot(normed_ref[...], ref[...], 0, 0)
        output_sum = base_o_ref[...] + near_o_ref[...].astype(f32) + far_o_ref[...].astype(f32)
        sums[:, 3 * span :] = output_sum.T
        if few:
            for r, ref in enumerate(weight_refs):
                for i, far in enumerate((0, 4)):
                    at = pl.multiple_of((place_ref[0] ^ r ^ far) * part, part)
                    ref[i * part : (i + 1) * part, :] = sums[pl.ds(at, part), :].astype(ref.dtype)
        else:
            weight_refs[0][...] = sums[...]
        gain_grad = jnp.zeros((1, width), f32)
        for r, (ref, first) in enumerate(
            ((base_ref, 0), (near_ref, 0), (far_ref, 0), (near_ref, rows))
        ):
            at = pl.ds(pl.multiple_of((place_ref[1] ^ r) * rows, rows), rows)
            grad = (
                dot(dq_ref[at, :], wq_ref[...], 1, 1)
                + dot(dk_ref[at, :], wk_ref[...], 1, 1)
                + dot(dv_ref[at, :], wv_ref[...], 1, 1)
            )
            gain_grad = gain_grad + jnp.sum(
                grad * normed_ref[at, :].astype(f32), axis=0, keepdims=True
            )
            ref[first : first + rows, :] = grad.astype(ref.dtype)
        small_ref[...] = jnp.zeros_like(small_ref)
        small_ref[0:1, :] = gain_grad / gain_ref[...]
        small_ref[1:2, :] = ffn_gain_ref[...]
        table = dot(line_ref[...], hot_ref[...], 1, 0, highest)
        for m in range(members):
            own = jnp.where(place_ref[1] == m, table[:heads, :], 0.0)
            small_ref[2 + m * heads : 2 + (m + 1) * heads, :128] = own
        small_ref[16:, :] = router_ref[...]

    if few:
        weight_outs = [shape((2 * part, 4 * span), f32)] + [shape((2 * part, 4 * span), bf16)] * 3
    else:
        weight_outs = [shape((width, 4 * span), f32)]
    return call(
        kernel,
        "input_grads",
        list(proj_grads)
        + [normed]
        + list(weights)
        + [gain, line_grad, bucket_hot, ffn_gain_grad, router_grad]
        + [(part, span) for part in output_parts],
        [
            shape((2 * rows, width), bf16),
            shape((rows, width), f32),
            shape((rows, width), f32),
            shape((16 + experts, width), f32),
        ]
        + weight_outs,
        scratch=[pltpu.VMEM((width, 4 * span), f32)],
        scalars=place,
        after=after,
    )


def fold_weights(base, arrived, after, through):
    part, width = base.shape[0] // 2, base.shape[1]

    def kernel(base_ref, *refs):
        own_ref, far_ref = refs[-2:]
        total = base_ref[...]
        for ref in refs[:-2]:
            total = total + ref[...].astype(f32)
        own_ref[...] = total[:part, :]
        far_ref[...] = total[part:, :].astype(bf16)

    return call(
        kernel,
        "fold_weights",
        [base] + arrived,
        [shape((part, width), f32), shape((part, width), bf16)],
        after=after,
        through=through,
    )


def split_weights(parts, span, after):
    part = parts[0].shape[0]

    def kernel(*refs):
        q_ref, k_ref, v_ref, o_ref = refs[-4:]
        total = refs[0][...]
        for ref in refs[1:-4]:
            total = total + ref[...].astype(f32)
        for at, ref in enumerate((q_ref, k_ref, v_ref)):
            ref[...] = total[:, at * span : (at + 1) * span]
        o_ref[...] = total[:, 3 * span :].T

    return call(
        kernel,
        "split_weights",
        parts,
        [shape((part, span), f32)] * 3 + [shape((span, part), f32)],
        after=after,
    )


def gather_mp(values):
    across = swap(values, "mp", 2)
    return [values, swap(values, "mp", 1), across, swap(across, "mp", 1)]


def sum_over(values, axis):
    step = 1
    while step < lax.axis_size(axis):
        values = values + swap(values, axis, step)
        step = 2 * step
    return values


def all_to_all_dp(values):
    return lax.all_to_all(values, "dp", split_axis=0, concat_axis=0, tiled=True)


def slots_of(routes, place, capacity, experts, limit):
    rows = routes.shape[0]
    expert_ids = jnp.arange(experts, dtype=jnp.int32)[None, :]
    hits = (routes[:, 0:1] == expert_ids) | (routes[:, 1:2] == expert_ids)
    earlier = jnp.arange(rows)[:, None] > jnp.arange(rows)[None, :]
    ranks = jnp.dot(earlier.astype(bf16), hits.astype(bf16), preferred_element_type=f32)
    lines = []
    for k in (0, 1):
        rank = jnp.sum(jnp.where(routes[:, k : k + 1] == expert_ids, ranks, 0.0), axis=1)
        block = routes[:, k] ^ place
        lines.append(jnp.where(block < limit, block * capacity + rank.astype(jnp.int32), -1))
    return jnp.pad(jnp.stack(lines), ((0, 6), (0, 0)), constant_values=-1)


def on_device(
    tokens,
    norm_gain,
    w_query,
    w_key,
    w_value,
    w_output,
    bias_table,
    ffn_gain,
    w_router,
    w_in,
    w_out,
    segments,
    buckets,
    routes,
    cotangent,
):
    rows, width = tokens.shape
    heads = bias_table.shape[1]
    seq_len = buckets.shape[0]
    experts = w_router.shape[1]
    owners, members = lax.axis_size("dp"), lax.axis_size("mp")
    me, member = lax.axis_index("dp"), lax.axis_index("mp")
    place = jnp.stack([me, member]).astype(jnp.int32)
    capacity = 4 * rows // experts
    span = w_query.shape[1]
    window = reach + tile
    few = owners == 8

    token_blocks = gather_mp(tokens)
    pack = pack_weights(w_query, w_key, w_value, w_output)
    if few:
        both = pair_up(pack, swap(pack, "dp", 4), token_blocks[1:3])
        pack_blocks = [(both, (0, 4))] + [(swap(both, "dp", r), (r, r ^ 4)) for r in (1, 2, 3)]
    else:
        pack_blocks = [(lax.all_gather(pack, "dp", axis=0, tiled=True), (0,))]
    gain_one, gain_two = norm_gain.reshape(1, width), ffn_gain.reshape(1, width)
    normed, query, key_rows, value_rows, weight_q, weight_k, weight_v, w_o, late_cotangent = (
        project(place, token_blocks, pack_blocks, gain_one, cotangent, span)
    )

    if few:
        blocks, size = 4, capacity
        slots = [slots_of(routes, me, capacity, experts, 4)]
        slots.append(slots_of(swap(routes, "dp", 4), me, capacity, experts, 4))
    else:
        blocks, size = 1, experts * capacity
        slots = [slots_of(routes, 0, capacity, experts, experts)]

    if few:
        far_cotangent = swap(late_cotangent, "dp", 4)
        held = to_slots(
            "grads_to_slots",
            [(cotangent, slots[0]), (far_cotangent, slots[1])],
            blocks,
            size,
            cost=long,
        )
    else:
        held = to_slots("grads_to_slots", [(cotangent, slots[0])], blocks, size)

    line_buckets = jnp.pad(jnp.flip(buckets[: reach + 1]), (0, window - reach - 1))
    bucket_hot = (
        line_buckets[:, None] == jnp.arange(128, dtype=jnp.int32)[None, :]
    ).astype(f32)
    buckets_all = bias_table.shape[0]
    table = jnp.pad(bias_table.T, ((0, 8 - heads), (0, 128 - buckets_all)))
    line = jnp.dot(table, bucket_hot.T, precision=highest)
    seg_q = segments.reshape(seq_len, 1)
    seg_k = jnp.pad(segments.reshape(1, seq_len), ((0, 0), (reach, 0)), constant_values=-1)
    mixed_out = attend(
        place, query, key_rows, value_rows, seg_q, seg_k, line, heads, members, []
    )
    weight_o = gather_mp(w_o)
    mixed_in = [mixed_out[0]] + [swap(mixed_out[r], "mp", r) for r in range(1, members)]

    router_wide = jnp.pad(w_router, ((0, 0), (0, 128 - experts)))
    hidden, ffn_input, router_probs, *send = middle(
        tokens,
        mixed_in,
        weight_o,
        gain_two,
        router_wide,
        slots[0],
        experts,
        blocks,
        size,
        [far_cotangent] if few else [],
    )
    if few:
        far_input = swap(ffn_input, "dp", 4)
        own = [send[0]] + [swap(send[r], "dp", r) for r in (1, 2, 3)]
        far = to_slots(
            "far_to_slots", [(far_input, slots[1])], blocks, size, through=held[1:]
        )
        held = [held[0]] + list(far[blocks:])
        far = [far[0]] + [swap(far[r], "dp", r) for r in (1, 2, 3)]
        x_sets = [own, far]
    else:
        x_sets = [[all_to_all_dp(send[0])]]
        g_blocks = [all_to_all_dp(held[0])]

    kept, before, passed = [], [], list(held[1:])
    for at, x_blocks in enumerate(x_sets):
        last = at == len(x_sets) - 1
        result, *state = experts_forward(
            "experts_forward" + str(at),
            place,
            w_in[0],
            w_out[0],
            router_wide,
            x_blocks,
            experts,
            before if last else None,
            brief if last else long,
            [] if last else passed,
        )
        passed = passed if last else state[5:]
        kept.append(state[:5])
        before = before + list(state[3:5])
    if few:
        g_blocks = [held[0]] + [swap(passed[r - 1], "dp", r) for r in (1, 2, 3)]
    actives, slopes, arrived, plain, slot_gates = zip(*kept)
    sets = list(zip(slopes, plain, slot_gates))
    back, slot_grads, pre_grad = experts_backward(
        "experts_backward" + str(len(sets) - 1),
        place,
        w_in[0],
        w_out[0],
        sets,
        len(sets) - 1,
        None,
        g_blocks,
        blocks,
        brief,
    )
    pre_grads = [pre_grad]
    if few:
        own_back, _, pre_grad = experts_backward(
            "experts_backward0",
            place,
            w_in[0],
            w_out[0],
            sets,
            0,
            slot_grads[0],
            g_blocks,
            blocks,
            long,
        )
        pre_grads = [pre_grad] + pre_grads
        far_back = [back[0]] + [swap(back[r], "dp", r) for r in (1, 2, 3)]
        result_in = [result[0]] + [swap(result[r], "dp", r) for r in (1, 2, 3)]
        far_total, *passed = from_slots(
            "back_from_slots",
            far_back,
            [slots[1]],
            size,
            [bf16],
            after=result_in[1:],
            through=own_back[1:],
        )
        far_sum = swap(far_total, "dp", 4)
        own_back = [own_back[0]] + [swap(passed[r - 1], "dp", r) for r in (1, 2, 3)]
    else:
        own_back, far_sum = [all_to_all_dp(back[0])], None
        result_in = [all_to_all_dp(result[0])]
    near_w, base_w = expert_weight_grads(place, arrived, pre_grads, actives, slot_grads, members)

    homed = home(
        own_back,
        far_sum,
        slots[0],
        hidden,
        router_probs,
        cotangent,
        gain_two,
        router_wide,
        ffn_input,
        weight_o,
        mixed_in,
        size,
        experts,
        [],
        [near_w],
    )
    grad_out, homed = homed[:members], homed[members:]
    hidden_grad, ffn_gain_grad, router_grad, near_o, base_o, near_w = homed
    grad_in = [grad_out[0]] + [swap(grad_out[r], "mp", r) for r in range(1, members)]
    if few:
        own_result, far_result = from_slots(
            "result_from_slots",
            result_in,
            slots,
            size,
            [f32, bf16],
            after=[hidden_grad],
            cost=long,
        )
        far_result = swap(far_result, "dp", 4)
    else:
        (own_result,) = from_slots("result_from_slots", result_in, slots, size, [f32])
        far_result = own_result
    near_o, near_w = swap(near_o, "mp", 1), swap(near_w, "mp", 1)
    piece = w_in.shape[2] // members
    far_first, far_next, far_last = far_sums(
        near_w, base_w, near_o, base_o, [rows, piece, 2 * piece], grad_in[2:] + [own_result]
    )

    *proj_grads, line_grad = attend_back(
        place,
        query,
        key_rows,
        value_rows,
        seg_q,
        seg_k,
        line,
        grad_in,
        heads,
        [far_first],
    )
    far_first = swap(far_first, "mp", 2)
    far_next = swap(far_next, "mp", 2)
    far_last = swap(far_last, "mp", 2)
    near, base, base_far, small, *weight_sums = input_grads(
        place,
        proj_grads,
        normed,
        (weight_q, weight_k, weight_v),
        (base_o, near_o, far_first),
        gain_one,
        line_grad,
        bucket_hot,
        ffn_gain_grad,
        router_grad,
        members,
        owners,
        heads,
        [far_result],
    )
    near = swap(near, "mp", 1)
    far_normed = swap((base_far + near[rows:].astype(f32)).astype(bf16), "mp", 2)
    if few:
        arrived_sums = [swap(weight_sums[r], "dp", r) for r in (1, 2, 3)]
        own_sum, far_part, small = fold_weights(
            weight_sums[0], arrived_sums, [far_next, near], [small]
        )
        weight_grads = split_weights([own_sum, swap(far_part, "dp", 4)], span, [far_normed])
    else:
        joined_grad = lax.psum_scatter(weight_sums[0], "dp", scatter_dimension=0, tiled=True)
        weight_grads = split_weights([joined_grad], span, [far_normed])
    normed_grad = base + near[:rows].astype(f32) + far_normed.astype(f32)
    resid = tokens.astype(f32)
    _, inverse_one = normalize(resid, norm_gain)
    scaled = normed_grad * norm_gain
    inner = jnp.mean(scaled * resid, axis=-1, keepdims=True)
    tokens_grad = (
        hidden_grad + inverse_one * scaled - resid * inverse_one * inverse_one * inverse_one * inner
    ).astype(bf16)

    block_out = hidden + own_result
    if few:
        block_out = block_out + far_result.astype(f32)
    block_out = block_out.astype(bf16)
    far_in = jnp.concatenate([far_first[span:], far_next], axis=0).astype(f32)
    w_in_grad = base_w[:piece] + near_w[:piece].astype(f32) + far_in
    own_out = base_w[2 * piece : 3 * piece] + near_w[2 * piece : 3 * piece].astype(f32)
    w_out_grad = own_out + far_last.astype(f32)
    small = sum_over(sum_over(small, "dp"), "mp")
    return (
        block_out,
        tokens_grad,
        small[0],
        *weight_grads,
        small[2 : 2 + heads * members, :buckets_all].T,
        small[1],
        small[16:].T,
        w_in_grad[None],
        w_out_grad[None],
    )


def solution(mesh):
    return jax.shard_map(
        on_device,
        mesh=mesh,
        in_specs=(
            P(("dp", "mp"), None),
            P(),
            P("dp", "mp"),
            P("dp", "mp"),
            P("dp", "mp"),
            P("mp", "dp"),
            P(None, "mp"),
            P(),
            P(),
            P("dp", None, None),
            P("dp", None, None),
            P("dp", None),
            P(),
            P(("dp", "mp"), None),
            P(("dp", "mp"), None),
        ),
        out_specs=(
            P(("dp", "mp"), None),
            P(("dp", "mp"), None),
            P(),
            P("dp", "mp"),
            P("dp", "mp"),
            P("dp", "mp"),
            P("mp", "dp"),
            P(),
            P(),
            P(),
            P("dp", None, "mp"),
            P("dp", "mp", None),
        ),
        check_vma=False,
    )
```

```python
import functools
import math

import jax
import jax.numpy as jnp
from jax import lax
from jax.experimental import pallas as pl
from jax.experimental.pallas import tpu as pltpu
from jax.sharding import PartitionSpec as P

eps = 1e-06
highest = lax.Precision.HIGHEST
f32, bf16 = jnp.float32, jnp.bfloat16
excluded = -1e30
reach = 512
tile = 128


def limit(mebibytes):
    return pltpu.CompilerParams(vmem_limit_bytes=mebibytes * 1024 * 1024)


brief = pl.CostEstimate(flops=10**7, bytes_accessed=10**4, transcendentals=0)
long = pl.CostEstimate(flops=2 * 10**10, bytes_accessed=10**7, transcendentals=0)


def normalize(values, gain):
    inverse = lax.rsqrt(jnp.mean(values * values, axis=-1, keepdims=True) + eps)
    return (values * inverse * gain, inverse)


def dot(left, right, left_dim, right_dim, precision=None):
    return lax.dot_general(
        left,
        right,
        (((left_dim,), (right_dim,)), ((), ())),
        precision=precision,
        preferred_element_type=f32,
    )


def swap(values, axis, step):
    count = lax.axis_size(axis)
    return lax.ppermute(values, axis, [(i, i ^ step) for i in range(count)])


def whole(dims):
    return pl.BlockSpec(tuple(dims), lambda *_: (0,) * len(dims), pipeline_mode=pl.Buffered(1))


def call(
    kernel, name, operands, outs, scratch=(), scalars=None, after=(), through=(), cost=None
):
    outs = list(outs)
    pairs = [o if isinstance(o, tuple) else (o, o.shape[0]) for o in operands]
    operands = [array for array, _ in pairs]
    in_specs = [whole((rows,) + array.shape[1:]) for array, rows in pairs]
    out_specs = [whole(o.shape) for o in outs]
    if scalars is not None:
        operands = [scalars] + operands
        in_specs = [pl.BlockSpec(memory_space=pltpu.SMEM)] + in_specs
    count, results = len(operands), len(outs)
    extra = list(through) + list(after)

    def body(*refs):
        rest = refs[count + len(extra) :]
        kernel(*refs[:count], *rest[:results], *rest[results + len(through) :])

    return pl.pallas_call(
        body,
        name=name,
        grid=(1,),
        in_specs=in_specs + [pl.BlockSpec(memory_space=pl.ANY)] * len(extra),
        out_specs=out_specs + [pl.BlockSpec(memory_space=pl.ANY)] * len(through),
        out_shape=outs + [shape(o.shape, o.dtype) for o in through],
        input_output_aliases={count + i: results + i for i in range(len(through))},
        scratch_shapes=list(scratch),
        compiler_params=limit(64),
        cost_estimate=cost or brief,
    )(*operands, *extra)


def shape(dims, dtype):
    return jax.ShapeDtypeStruct(tuple(dims), dtype)


def fill_skew(line_ref, skew, heads):
    window = reach + tile
    row = lax.broadcasted_iota(jnp.int32, (tile, window), 0)
    column = lax.broadcasted_iota(jnp.int32, (tile, window), 1)
    usable = (column - row <= reach) & (column - row >= 1)
    for head in range(heads):
        line = jnp.broadcast_to(line_ref[head : head + 1, :], (tile, window))
        rolled = pltpu.roll(line, 0, 1, stride=1, stride_axis=0)
        skew[head * tile : (head + 1) * tile, :] = jnp.where(usable, rolled, excluded)


def fill_window(source_ref, padded):
    padded[:reach, :] = jnp.zeros((reach, padded.shape[1]), bf16)
    padded[reach:, :] = source_ref[...]


def spread_heads(values, heads, scale):
    span = values.shape[1]
    size = span // heads
    lane = lax.broadcasted_iota(jnp.int32, (tile, span), 1)
    wide = values.astype(f32) * scale
    parts = [
        jnp.where((lane >= head * size) & (lane < (head + 1) * size), wide, 0.0)
        for head in range(heads)
    ]
    return jnp.concatenate(parts, axis=0).astype(bf16)


def collect_heads(stacked, heads):
    span = stacked.shape[1]
    size = span // heads
    lane = lax.broadcasted_iota(jnp.int32, (tile, span), 1)
    total = stacked[:tile, :]
    for head in range(1, heads):
        total = jnp.where(lane < head * size, total, stacked[head * tile : (head + 1) * tile, :])
    return total


def window_powers(q_all, keys, skew, seg_q_ref, seg_k_ref, start, heads):
    window = reach + tile
    seg_q = jnp.concatenate([seg_q_ref[pl.ds(start, tile), :]] * heads, axis=0)
    seg_k = seg_k_ref[:, pl.ds(start, window)]
    scores = dot(q_all, keys, 1, 1) + skew[...]
    scores = jnp.where(seg_q == seg_k, scores, excluded)
    powers = jnp.exp(scores - jnp.max(scores, axis=-1, keepdims=True))
    return powers, 1.0 / jnp.sum(powers, axis=-1, keepdims=True)


def attend_kernel(heads, place, q_ref, k_ref, v_ref, seg_q_ref, seg_k_ref, line_ref, *rest):
    *out_refs, mixed, k_pad, v_pad, skew = rest
    window = reach + tile
    scale = (q_ref.shape[1] // heads) ** (-0.5)
    fill_skew(line_ref, skew, heads)
    fill_window(k_ref, k_pad)
    fill_window(v_ref, v_pad)

    def step(index, carry):
        start = pl.multiple_of(index * tile, tile)
        q_all = spread_heads(q_ref[pl.ds(start, tile), :], heads, scale)
        powers, inverse = window_powers(
            q_all, k_pad[pl.ds(start, window), :], skew, seg_q_ref, seg_k_ref, start, heads
        )
        probs = (powers * inverse).astype(bf16)
        part = dot(probs, v_pad[pl.ds(start, window), :], 1, 0)
        mixed[pl.ds(start, tile), :] = collect_heads(part, heads).astype(bf16)
        return carry

    lax.fori_loop(0, q_ref.shape[0] // tile, step, 0)
    rows = out_refs[0].shape[0]
    for r, out_ref in enumerate(out_refs):
        out_ref[...] = mixed[pl.ds(pl.multiple_of((place[1] ^ r) * rows, rows), rows), :]


def attend(place, query, key_rows, value_rows, seg_q, seg_k, line, heads, members, after):
    seq_len, span = query.shape
    window = reach + tile

    def kernel(place_ref, *refs):
        attend_kernel(heads, place_ref, *refs)

    return call(
        kernel,
        "attend",
        [query, key_rows, value_rows, seg_q, seg_k, line],
        [shape((seq_len // members, span), bf16)] * members,
        scratch=[
            pltpu.VMEM((seq_len, span), bf16),
            pltpu.VMEM((seq_len + reach, span), bf16),
            pltpu.VMEM((seq_len + reach, span), bf16),
            pltpu.VMEM((heads * tile, window), f32),
        ],
        scalars=place,
        after=after,
    )


def attend_back_kernel(heads, members, place, *refs):
    q_ref, k_ref, v_ref, seg_q_ref, seg_k_ref, line_ref = refs[:6]
    g_refs = refs[6 : 6 + members]
    dq_ref, dk_ref, dv_ref, line_grad_ref = refs[6 + members : 10 + members]
    grad, k_pad, v_pad, skew, dk_sum, dv_sum, bias_sum = refs[10 + members :]
    window = reach + tile
    scale = (q_ref.shape[1] // heads) ** (-0.5)
    rows = g_refs[0].shape[0]
    fill_skew(line_ref, skew, heads)
    fill_window(k_ref, k_pad)
    fill_window(v_ref, v_pad)
    dk_sum[...] = jnp.zeros_like(dk_sum)
    dv_sum[...] = jnp.zeros_like(dv_sum)
    bias_sum[...] = jnp.zeros_like(bias_sum)
    for r, g_ref in enumerate(g_refs):
        grad[pl.ds(pl.multiple_of((place[1] ^ r) * rows, rows), rows), :] = g_ref[...]

    def step(index, carry):
        start = pl.multiple_of(index * tile, tile)
        keys = k_pad[pl.ds(start, window), :]
        values = v_pad[pl.ds(start, window), :]
        q_all = spread_heads(q_ref[pl.ds(start, tile), :], heads, scale)
        g_all = spread_heads(grad[pl.ds(start, tile), :], heads, 1.0)
        powers, inverse = window_powers(q_all, keys, skew, seg_q_ref, seg_k_ref, start, heads)
        probs = powers * inverse
        dot_grad = dot(g_all, values, 1, 1)
        inner = jnp.sum(probs * dot_grad, axis=-1, keepdims=True)
        score_grad = (probs * (dot_grad - inner)).astype(bf16)
        bias_sum[...] += score_grad.astype(f32)
        part = collect_heads(dot(score_grad, keys, 1, 0), heads) * scale
        dq_ref[pl.ds(start, tile), :] = part.astype(bf16)
        dk_sum[pl.ds(start, window), :] += dot(score_grad, q_all, 0, 0)
        dv_sum[pl.ds(start, window), :] += dot(probs.astype(bf16), g_all, 0, 0)
        return carry

    lax.fori_loop(0, q_ref.shape[0] // tile, step, 0)
    dk_ref[...] = dk_sum[reach:, :].astype(bf16)
    dv_ref[...] = dv_sum[reach:, :].astype(bf16)
    line_grad_ref[...] = jnp.zeros_like(line_grad_ref)
    row = lax.broadcasted_iota(jnp.int32, (tile, tile), 0)
    column = lax.broadcasted_iota(jnp.int32, (tile, tile), 1)
    mirror = (row + column == tile - 1).astype(f32)
    for head in range(heads):
        part = bias_sum[head * tile : (head + 1) * tile, :]
        turned = dot(mirror, part, 1, 0, highest)
        straight = pltpu.roll(turned, window - tile + 1, 1, stride=1, stride_axis=0)
        line_grad_ref[head : head + 1, :] = jnp.sum(straight, axis=0, keepdims=True)


def attend_back(place, query, key_rows, value_rows, seg_q, seg_k, line, grads, heads, after):
    seq_len, span = query.shape
    window = reach + tile

    def kernel(place_ref, *refs):
        attend_back_kernel(heads, len(grads), place_ref, *refs)

    return call(
        kernel,
        "attend_back",
        [query, key_rows, value_rows, seg_q, seg_k, line] + grads,
        [shape((seq_len, span), bf16)] * 3 + [shape((8, window), f32)],
        scratch=[
            pltpu.VMEM((seq_len, span), bf16),
            pltpu.VMEM((seq_len + reach, span), bf16),
            pltpu.VMEM((seq_len + reach, span), bf16),
            pltpu.VMEM((heads * tile, window), f32),
            pltpu.VMEM((seq_len + reach, span), f32),
            pltpu.VMEM((seq_len + reach, span), f32),
            pltpu.VMEM((heads * tile, window), f32),
        ],
        scalars=place,
        after=after,
    )


def pack_weights(w_query, w_key, w_value, w_output):
    part, span = w_query.shape

    def kernel(q_ref, k_ref, v_ref, o_ref, pack_ref):
        for at, ref in enumerate((q_ref, k_ref, v_ref)):
            pack_ref[:, at * span : (at + 1) * span] = ref[...]
        pack_ref[:, 3 * span :] = o_ref[...].astype(f32).T.astype(bf16)

    (pack,) = call(
        kernel, "pack_weights", [w_query, w_key, w_value, w_output], [shape((part, 4 * span), bf16)]
    )
    return pack


def pair_up(pack, far, after):
    part = pack.shape[0]

    def kernel(near_ref, far_ref, both_ref):
        both_ref[:part, :] = near_ref[...]
        both_ref[part:, :] = far_ref[...]

    (both,) = call(
        kernel, "pair_up", [pack, far], [shape((2 * part, pack.shape[1]), bf16)], after=after
    )
    return both


def project(place, token_blocks, pack_blocks, gain, cotangent, span):
    rows, width = token_blocks[0].shape
    members = len(token_blocks)
    seq_len = rows * members
    parts = sum(len(held) for _, held in pack_blocks)
    part = width // parts

    def kernel(place_ref, gain_ref, *refs):
        token_refs = refs[:members]
        pack_refs = refs[members : members + len(pack_blocks)]
        (normed_ref, q_ref, k_ref, v_ref, wq_ref, wk_ref, wv_ref, wo_ref, pack) = refs[
            members + len(pack_blocks) :
        ]
        for (_, held), ref in zip(pack_blocks, pack_refs):
            for i, r in enumerate(held):
                at = pl.multiple_of((place_ref[0] ^ r) * part, part) if parts > 1 else 0
                pack[pl.ds(at, part), :] = ref[i * part : (i + 1) * part, :]
        for at, ref in enumerate((wq_ref, wk_ref, wv_ref)):
            ref[...] = pack[:, at * span : (at + 1) * span]
        wo_ref[...] = pack[:, 3 * span :].astype(f32).T.astype(bf16)
        for r, ref in enumerate(token_refs):
            normed, _ = normalize(ref[...].astype(f32), gain_ref[...])
            normed = normed.astype(bf16)
            at = pl.ds(pl.multiple_of((place_ref[1] ^ r) * rows, rows), rows)
            normed_ref[at, :] = normed
            q_ref[at, :] = dot(normed, wq_ref[...], 1, 0).astype(bf16)
            k_ref[at, :] = dot(normed, wk_ref[...], 1, 0).astype(bf16)
            v_ref[at, :] = dot(normed, wv_ref[...], 1, 0).astype(bf16)

    return call(
        kernel,
        "project",
        [gain] + list(token_blocks) + [array for array, _ in pack_blocks],
        [shape((seq_len, width), bf16)]
        + [shape((seq_len, span), bf16)] * 3
        + [shape((width, span), bf16)] * 3
        + [shape((span, width), bf16)],
        scratch=[pltpu.VMEM((width, width), bf16)],
        scalars=place,
        through=[cotangent],
    )


def hot(slots_ref, first, count):
    tokens = slots_ref.shape[1]
    slot = lax.broadcasted_iota(jnp.int32, (count, tokens), 0) + first
    taken = (slot == slots_ref[0:1, :]) | (slot == slots_ref[1:2, :])
    return jnp.where(taken, 1.0, 0.0).astype(bf16)


def to_slots(name, sets, blocks, size, after=()):
    width = sets[0][0].shape[1]

    def kernel(*refs):
        out_refs = refs[2 * len(sets) :]
        for at in range(len(sets)):
            rows_ref, slots_ref = refs[2 * at], refs[2 * at + 1]
            for b, out_ref in enumerate(out_refs):
                part = dot(hot(slots_ref, b * size, size), rows_ref[...], 1, 0)
                out_ref[at * size : (at + 1) * size, :] = part.astype(bf16)

    operands = [item for pair in sets for item in pair]
    return call(
        kernel,
        name,
        operands,
        [shape((size * len(sets), width), bf16)] * blocks,
        after=after,
    )


def from_slots(name, blocks, slots, size, dtypes, after=(), through=(), cost=None):
    count, sets = len(blocks), len(slots)
    width = blocks[0].shape[1]
    rows = slots[0].shape[1]

    def kernel(*refs):
        block_refs, slot_refs, out_refs = refs[:count], refs[count : count + sets], refs[count + sets :]
        for at in range(sets):
            total = None
            for b, ref in enumerate(block_refs):
                held = ref[at * size : (at + 1) * size, :]
                part = dot(hot(slot_refs[at], b * size, size), held, 0, 0)
                total = part if total is None else total + part
            out_refs[at][...] = total.astype(out_refs[at].dtype)

    return call(
        kernel,
        name,
        list(blocks) + list(slots),
        [shape((rows, width), dtype) for dtype in dtypes],
        after=after,
        through=through,
        cost=cost,
    )


def router_softmax(values, w_router, experts):
    logits = dot(values, w_router, 1, 0)
    lane = lax.broadcasted_iota(jnp.int32, logits.shape, 1)
    logits = jnp.where(lane < experts, logits, excluded)
    powers = jnp.exp(logits - jnp.max(logits, axis=-1, keepdims=True))
    return powers / jnp.sum(powers, axis=-1, keepdims=True)


def middle(tokens, mixed, weight_o, gain, w_router, slots, experts, blocks, size, after):
    rows, width = tokens.shape
    members = len(mixed)

    def kernel(*refs):
        token_ref, gain_ref, router_ref, slots_ref = refs[:4]
        mixed_refs, weight_refs = refs[4 : 4 + members], refs[4 + members : 4 + 2 * members]
        hidden_ref, input_ref, probs_ref, *send_refs = refs[4 + 2 * members :]
        hidden = token_ref[...].astype(f32)
        for left, right in zip(mixed_refs, weight_refs):
            hidden = hidden + dot(left[...], right[...], 1, 0)
        hidden_ref[...] = hidden
        normed, _ = normalize(hidden, gain_ref[...])
        normed = normed.astype(bf16)
        input_ref[...] = normed
        for b, ref in enumerate(send_refs):
            ref[...] = dot(hot(slots_ref, b * size, size), normed, 1, 0).astype(bf16)
        probs_ref[...] = router_softmax(normed, router_ref[...], experts)

    return call(
        kernel,
        "middle",
        [tokens, gain, w_router, slots] + mixed + weight_o,
        [shape((rows, width), f32), shape((rows, width), bf16), shape((rows, 128), f32)]
        + [shape((size, width), bf16)] * blocks,
        after=after,
    )


def join_rows(refs):
    return jnp.concatenate([ref[...] for ref in refs], axis=0)


def run_experts(
    name, place, w_in, w_out, w_router, x_blocks, g_blocks, at_set, before, cost, after
):
    width, units = w_in.shape
    count, size = len(x_blocks), x_blocks[0].shape[0]
    total, piece, chunk = size * count, 512, 256
    experts = before[0]
    held = list(before[1:])
    sets = g_blocks[0].shape[0] // size
    last = at_set == sets - 1

    def kernel(me_ref, w_in_ref, w_out_ref, router_ref, *refs):
        x_refs, refs = refs[:count], refs[count:]
        g_refs, refs = refs[:count], refs[count:]
        held_refs, refs = refs[: len(held)], refs[len(held) + len(after) :]
        back_refs, refs = refs[:count], refs[count:]
        result_refs, refs = refs[:count] if last else refs[:1], refs[count if last else 1 :]
        active_ref, pre_grad_ref, x_all, s_all, gates, result_sum, back_sum = refs

        @pl.when(pl.program_id(0) == 0)
        def _():
            for b in range(count):
                rows = slice(b * size, (b + 1) * size)
                x_all[rows, :] = x_refs[b][...]
            probs = router_softmax(x_all[...], router_ref[...], experts)
            lane = lax.broadcasted_iota(jnp.int32, probs.shape, 1)
            own = jnp.sum(jnp.where(lane == me_ref[0], probs, 0.0), axis=1, keepdims=True)
            gates[...] = jnp.broadcast_to(own, gates.shape)
            for b in range(count):
                rows = slice(b * size, (b + 1) * size)
                grad = g_refs[b][at_set * size : (at_set + 1) * size, :].astype(f32)
                s_all[rows, :] = (gates[rows, 0:1] * grad).astype(bf16)
            result_sum[...] = jnp.zeros_like(result_sum)
            back_sum[...] = jnp.zeros_like(back_sum)

        for c in range(piece // chunk):
            at = slice(c * chunk, (c + 1) * chunk)
            pre_act = dot(x_all[...], w_in_ref[:, at], 1, 0)
            active_grad = dot(s_all[...], w_out_ref[at, :], 1, 1)
            below = 0.5 + 0.5 * lax.erf(pre_act * math.sqrt(0.5))
            bell = jnp.exp(-0.5 * pre_act * pre_act) * (1.0 / math.sqrt(2.0 * math.pi))
            active_ref[:, at] = (pre_act * below).astype(bf16)
            pre_grad_ref[:, at] = (active_grad * (below + pre_act * bell)).astype(bf16)
        result_sum[...] += dot(active_ref[...], w_out_ref[...], 1, 0)
        back_sum[...] += dot(pre_grad_ref[...], w_in_ref[...], 1, 1)

        @pl.when(pl.program_id(0) == pl.num_programs(0) - 1)
        def _():
            lane = lax.broadcasted_iota(jnp.int32, (size, 128), 1)
            for b, (ref, g_ref) in enumerate(zip(back_refs, g_refs)):
                rows = slice(b * size, (b + 1) * size)
                result = result_sum[rows, :].astype(bf16).astype(f32)
                grad = g_ref[at_set * size : (at_set + 1) * size, :].astype(f32)
                gate_grad = jnp.sum(grad * result, axis=1, keepdims=True)
                upper = gate_grad.astype(bf16).astype(f32)
                ref[:, :width] = back_sum[rows, :].astype(bf16)
                ref[:, width:] = jnp.where(
                    lane == me_ref[0],
                    upper,
                    jnp.where(lane == me_ref[0] + 64, gate_grad - upper, 0.0),
                ).astype(bf16)
                gated = (gates[rows, 0:1] * result).astype(bf16)
                if last:
                    for at, other in enumerate(held_refs):
                        result_refs[b][at * size : (at + 1) * size, :] = other[rows, :]
                    result_refs[b][at_set * size : (at_set + 1) * size, :] = gated
                else:
                    result_refs[0][rows, :] = gated

    columns = pl.BlockSpec((total, piece), lambda i: (0, i))
    outs = [shape((size, width + 128), bf16)] * count
    results = [shape((size * sets, width), bf16)] * count if last else [shape((total, width), bf16)]
    rows_out = [shape((total, width), bf16)] * 2
    flat = pl.pallas_call(
        kernel,
        name=name,
        grid=(units // piece,),
        in_specs=[
            pl.BlockSpec(memory_space=pltpu.SMEM),
            pl.BlockSpec((width, piece), lambda i: (0, i)),
            pl.BlockSpec((piece, width), lambda i: (i, 0)),
            whole(w_router.shape),
        ]
        + [whole(o.shape) for o in list(x_blocks) + list(g_blocks) + held]
        + [pl.BlockSpec(memory_space=pl.ANY)] * len(after),
        out_specs=[whole(o.shape) for o in outs + results]
        + [columns] * 2
        + [whole(o.shape) for o in rows_out],
        out_shape=outs + results + [shape((total, units), bf16)] * 2 + rows_out,
        scratch_shapes=[
            pltpu.VMEM((total, 128), f32),
            pltpu.VMEM((total, width), f32),
            pltpu.VMEM((total, width), f32),
        ],
        compiler_params=limit(64),
        cost_estimate=cost,
    )(place, w_in, w_out, w_router, *x_blocks, *g_blocks, *held, *after)
    return list(flat[:count]), list(flat[count:-4]), flat[-4:]


def home(
    own_back,
    far_sum,
    slots,
    hidden,
    probs,
    cotangent,
    gain,
    w_router,
    ffn_input,
    weight_o,
    mixed,
    size,
    experts,
    after,
    through,
):
    rows, width = hidden.shape
    count, members = len(own_back), len(weight_o)
    span = weight_o[0].shape[0]
    far = [] if far_sum is None else [far_sum]

    def kernel(*refs):
        slots_ref, hidden_ref, probs_ref, cot_ref, gain_ref, router_ref, input_ref = refs[:7]
        refs = refs[7:]
        back_refs, refs = refs[:count], refs[count:]
        far_refs, refs = refs[: len(far)], refs[len(far) :]
        weight_refs, mixed_refs, refs = refs[:members], refs[members : 2 * members], refs[2 * members :]
        grad_refs = refs[:members]
        hidden_grad_ref, gain_grad_ref, router_grad_ref, near_ref, base_ref = refs[members:]
        total = None
        for b, ref in enumerate(back_refs):
            part = dot(hot(slots_ref, b * size, size), ref[...], 0, 0)
            total = part if total is None else total + part
        for ref in far_refs:
            total = total + ref[...].astype(f32)
        columns = total[:, width:]
        lane = lax.broadcasted_iota(jnp.int32, columns.shape, 1)
        prob_grad = jnp.where(lane < 64, columns + pltpu.roll(columns, 64, 1), 0.0)
        router_probs = probs_ref[...]
        logit_grad = router_probs * (
            prob_grad - jnp.sum(router_probs * prob_grad, axis=-1, keepdims=True)
        )
        router_grad_ref[...] = dot(logit_grad, input_ref[...].astype(f32), 0, 0, highest)[:experts, :]
        grad = total[:, :width] + dot(logit_grad, router_ref[...].astype(f32), 1, 1, highest)
        hidden_now = hidden_ref[...]
        inverse = lax.rsqrt(jnp.mean(hidden_now * hidden_now, axis=-1, keepdims=True) + eps)
        scaled = grad * gain_ref[...]
        gain_grad_ref[...] = jnp.sum(grad * hidden_now * inverse, axis=0, keepdims=True)
        inner = jnp.mean(scaled * hidden_now, axis=-1, keepdims=True)
        hidden_grad = (
            cot_ref[...].astype(f32)
            + inverse * scaled
            - hidden_now * inverse * inverse * inverse * inner
        )
        hidden_grad_ref[...] = hidden_grad
        attn_grad = hidden_grad.astype(bf16)
        for ref, weight in zip(grad_refs, weight_refs):
            ref[...] = dot(attn_grad, weight[...], 1, 1).astype(bf16)
        for r, (ref, first) in enumerate(
            ((base_ref, 0), (near_ref, 0), (base_ref, span), (near_ref, span))
        ):
            part = dot(mixed_refs[r][...], attn_grad, 0, 0)
            ref[first : first + span, :] = part.astype(ref.dtype)

    return call(
        kernel,
        "home",
        [slots, hidden, probs, cotangent, gain, w_router, ffn_input]
        + list(own_back)
        + far
        + weight_o
        + mixed,
        [shape((rows, span), bf16)] * members
        + [
            shape((rows, width), f32),
            shape((1, width), f32),
            shape((experts, width), f32),
            shape((2 * span, width), bf16),
            shape((2 * span, width), f32),
        ],
        after=after,
        through=through,
    )


def expert_weight_grads(place, rows_in, pre_grads, actives, slot_grads, members):
    sets = len(rows_in)
    total, width = rows_in[0].shape
    piece = pre_grads[0].shape[1] // members

    def kernel(place_ref, *refs):
        x_refs, p_refs, a_refs, s_refs = [refs[i * sets : (i + 1) * sets] for i in range(4)]
        near_ref, base_ref, out = refs[4 * sets :]
        step = pl.program_id(0)

        def total_of(lefts, rights):
            held = dot(lefts[0][...], rights[0][...], 0, 0)
            for left, right in zip(lefts[1:], rights[1:]):
                held = held + dot(left[...], right[...], 0, 0)
            return held

        @pl.when(step < 4)
        def _():
            out[...] = total_of(x_refs, p_refs)

        @pl.when(step >= 4)
        def _():
            out[...] = total_of(a_refs, s_refs)

        @pl.when(step % 4 < 2)
        def _():
            near_ref[...] = out[...].astype(bf16)

        @pl.when(step % 4 >= 2)
        def _():
            base_ref[...] = out[...]

    def partner(i):
        return jnp.where(i < 2, 2 * i + 1, 2 * i - 4)

    fixed = pl.BlockSpec((total, width), lambda i, p: (0, 0))
    pre_cut = pl.BlockSpec((total, piece), lambda i, p: (0, p[1] ^ partner(jnp.minimum(i, 3))))
    act_cut = pl.BlockSpec((total, piece), lambda i, p: (0, p[1] ^ partner(jnp.maximum(i - 4, 0))))
    return pl.pallas_call(
        kernel,
        name="expert_weight_grads",
        grid_spec=pltpu.PrefetchScalarGridSpec(
            num_scalar_prefetch=1,
            grid=(8,),
            in_specs=[fixed] * sets + [pre_cut] * sets + [act_cut] * sets + [fixed] * sets,
            out_specs=[
                pl.BlockSpec(
                    (piece, width), lambda i, p: (2 * (i // 4) + jnp.minimum(i % 4, 1), 0)
                ),
                pl.BlockSpec(
                    (piece, width), lambda i, p: (2 * (i // 4) + jnp.maximum(i % 4 - 2, 0), 0)
                ),
            ],
            scratch_shapes=[pltpu.VMEM((piece, width), f32)],
        ),
        out_shape=[shape((4 * piece, width), bf16), shape((4 * piece, width), f32)],
        compiler_params=limit(64),
        cost_estimate=long,
    )(place, *rows_in, *pre_grads, *actives, *slot_grads)


def far_sums(near, base, near_o, base_o, cuts, after):
    size, width = base.shape[0] // 4, base.shape[1]
    span = near_o.shape[0] // 2

    def block(rows, at):
        return pl.BlockSpec((rows, width), lambda *_: (at, 0), pipeline_mode=pl.Buffered(1))

    def kernel(near_in, near_out, base_in, base_out, near_o_ref, base_o_ref, *refs):
        out_refs = refs[len(after) :]
        out_refs[0][:span, :] = (base_o_ref[...] + near_o_ref[...].astype(f32)).astype(bf16)
        starts = [0] + cuts
        for i, ref in enumerate(out_refs):
            low, high = starts[i], starts[i + 1]
            at = span if i == 0 else 0
            for near_ref, base_ref, shift in ((near_in, base_in, 0), (near_out, base_out, size)):
                first, last = max(low, shift), min(high, shift + size)
                if first < last:
                    rows = slice(first - shift, last - shift)
                    held = base_ref[rows, :] + near_ref[rows, :].astype(f32)
                    ref[at + first - low : at + last - low, :] = held.astype(bf16)

    rows = [high - low for low, high in zip([0] + cuts, cuts)]
    rows[0] = rows[0] + span
    return pl.pallas_call(
        kernel,
        name="far_sums",
        grid=(1,),
        in_specs=[block(size, 1), block(size, 3), block(size, 1), block(size, 3)]
        + [block(span, 1), block(span, 1)]
        + [pl.BlockSpec(memory_space=pl.ANY)] * len(after),
        out_specs=[whole((count, width)) for count in rows],
        out_shape=[shape((count, width), bf16) for count in rows],
        compiler_params=limit(64),
        cost_estimate=brief,
    )(near, near, base, base, near_o, base_o, *after)


def input_grads(
    place,
    proj_grads,
    normed,
    weights,
    output_parts,
    gain,
    line_grad,
    bucket_hot,
    ffn_gain_grad,
    router_grad,
    members,
    owners,
    heads,
    after,
):
    seq_len, width = normed.shape
    span = weights[0].shape[1]
    rows = seq_len // members
    part = width // owners
    few = owners == 8
    experts = router_grad.shape[0]

    def kernel(place_ref, *refs):
        dq_ref, dk_ref, dv_ref, normed_ref, wq_ref, wk_ref, wv_ref, gain_ref = refs[:8]
        line_ref, hot_ref, ffn_gain_ref, router_ref = refs[8:12]
        base_o_ref, near_o_ref, far_o_ref = refs[12:15]
        near_ref, base_ref, far_ref, small_ref, *weight_refs, sums = refs[15:]
        for at, ref in enumerate((dq_ref, dk_ref, dv_ref)):
            sums[:, at * span : (at + 1) * span] = dot(normed_ref[...], ref[...], 0, 0)
        output_sum = base_o_ref[...] + near_o_ref[...].astype(f32) + far_o_ref[...].astype(f32)
        sums[:, 3 * span :] = output_sum.T
        if few:
            for r, ref in enumerate(weight_refs):
                for i, far in enumerate((0, 4)):
                    at = pl.multiple_of((place_ref[0] ^ r ^ far) * part, part)
                    ref[i * part : (i + 1) * part, :] = sums[pl.ds(at, part), :].astype(ref.dtype)
        else:
            weight_refs[0][...] = sums[...]
        gain_grad = jnp.zeros((1, width), f32)
        for r, (ref, first) in enumerate(
            ((base_ref, 0), (near_ref, 0), (far_ref, 0), (near_ref, rows))
        ):
            at = pl.ds(pl.multiple_of((place_ref[1] ^ r) * rows, rows), rows)
            grad = (
                dot(dq_ref[at, :], wq_ref[...], 1, 1)
                + dot(dk_ref[at, :], wk_ref[...], 1, 1)
                + dot(dv_ref[at, :], wv_ref[...], 1, 1)
            )
            gain_grad = gain_grad + jnp.sum(
                grad * normed_ref[at, :].astype(f32), axis=0, keepdims=True
            )
            ref[first : first + rows, :] = grad.astype(ref.dtype)
        small_ref[...] = jnp.zeros_like(small_ref)
        small_ref[0:1, :] = gain_grad / gain_ref[...]
        small_ref[1:2, :] = ffn_gain_ref[...]
        table = dot(line_ref[...], hot_ref[...], 1, 0, highest)
        for m in range(members):
            own = jnp.where(place_ref[1] == m, table[:heads, :], 0.0)
            small_ref[2 + m * heads : 2 + (m + 1) * heads, :128] = own
        small_ref[16:, :] = router_ref[...]

    if few:
        weight_outs = [shape((2 * part, 4 * span), f32)] + [shape((2 * part, 4 * span), bf16)] * 3
    else:
        weight_outs = [shape((width, 4 * span), f32)]
    return call(
        kernel,
        "input_grads",
        list(proj_grads)
        + [normed]
        + list(weights)
        + [gain, line_grad, bucket_hot, ffn_gain_grad, router_grad]
        + [(part, span) for part in output_parts],
        [
            shape((2 * rows, width), bf16),
            shape((rows, width), f32),
            shape((rows, width), f32),
            shape((16 + experts, width), f32),
        ]
        + weight_outs,
        scratch=[pltpu.VMEM((width, 4 * span), f32)],
        scalars=place,
        after=after,
    )


def add_up(base, near, parts, after):
    size, width = base.shape[0] // 4, base.shape[1]

    def kernel(in_base, in_near, out_base, out_near, *refs):
        part_refs, (in_ref, out_ref) = refs[: len(parts)], refs[-2:]
        first = 0
        for (array, at), ref in zip(parts[:-1], part_refs[:-1]):
            rows = slice(first, first + array.shape[0] - at)
            total = in_base[rows, :] + in_near[rows, :].astype(f32)
            in_ref[rows, :] = total + ref[at:, :].astype(f32)
            first = first + array.shape[0] - at
        total = out_base[...] + out_near[...].astype(f32)
        out_ref[...] = total + part_refs[-1][...].astype(f32)

    def block(at):
        return pl.BlockSpec((size, width), lambda *_: (at, 0), pipeline_mode=pl.Buffered(1))

    specs = [block(0), block(0), block(2), block(2)] + [whole(o.shape) for o, _ in parts]
    return pl.pallas_call(
        kernel,
        name="add_up",
        grid=(1,),
        in_specs=specs + [pl.BlockSpec(memory_space=pl.ANY)] * len(after),
        out_specs=[whole((size, width))] * 2,
        out_shape=[shape((size, width), f32)] * 2,
        compiler_params=limit(64),
        cost_estimate=brief,
    )(base, near, base, near, *[array for array, _ in parts], *after)


def fold_weights(base, arrived, after, through):
    part, width = base.shape[0] // 2, base.shape[1]

    def kernel(base_ref, *refs):
        own_ref, far_ref = refs[-2:]
        total = base_ref[...]
        for ref in refs[:-2]:
            total = total + ref[...].astype(f32)
        own_ref[...] = total[:part, :]
        far_ref[...] = total[part:, :].astype(bf16)

    return call(
        kernel,
        "fold_weights",
        [base] + arrived,
        [shape((part, width), f32), shape((part, width), bf16)],
        after=after,
        through=through,
    )


def split_weights(parts, span, after):
    part = parts[0].shape[0]

    def kernel(*refs):
        q_ref, k_ref, v_ref, o_ref = refs[-4:]
        total = refs[0][...]
        for ref in refs[1:-4]:
            total = total + ref[...].astype(f32)
        for at, ref in enumerate((q_ref, k_ref, v_ref)):
            ref[...] = total[:, at * span : (at + 1) * span]
        o_ref[...] = total[:, 3 * span :].T

    return call(
        kernel,
        "split_weights",
        parts,
        [shape((part, span), f32)] * 3 + [shape((span, part), f32)],
        after=after,
    )


def gather_mp(values):
    across = swap(values, "mp", 2)
    return [values, swap(values, "mp", 1), across, swap(across, "mp", 1)]


def sum_over(values, axis):
    step = 1
    while step < lax.axis_size(axis):
        values = values + swap(values, axis, step)
        step = 2 * step
    return values


def all_to_all_dp(values):
    return lax.all_to_all(values, "dp", split_axis=0, concat_axis=0, tiled=True)


def slots_of(routes, place, capacity, experts, limit):
    rows = routes.shape[0]
    expert_ids = jnp.arange(experts, dtype=jnp.int32)[None, :]
    hits = (routes[:, 0:1] == expert_ids) | (routes[:, 1:2] == expert_ids)
    earlier = jnp.arange(rows)[:, None] > jnp.arange(rows)[None, :]
    ranks = jnp.dot(earlier.astype(bf16), hits.astype(bf16), preferred_element_type=f32)
    lines = []
    for k in (0, 1):
        rank = jnp.sum(jnp.where(routes[:, k : k + 1] == expert_ids, ranks, 0.0), axis=1)
        block = routes[:, k] ^ place
        lines.append(jnp.where(block < limit, block * capacity + rank.astype(jnp.int32), -1))
    return jnp.pad(jnp.stack(lines), ((0, 6), (0, 0)), constant_values=-1)


def on_device(
    tokens,
    norm_gain,
    w_query,
    w_key,
    w_value,
    w_output,
    bias_table,
    ffn_gain,
    w_router,
    w_in,
    w_out,
    segments,
    buckets,
    routes,
    cotangent,
):
    rows, width = tokens.shape
    heads = bias_table.shape[1]
    seq_len = buckets.shape[0]
    experts = w_router.shape[1]
    owners, members = lax.axis_size("dp"), lax.axis_size("mp")
    me, member = lax.axis_index("dp"), lax.axis_index("mp")
    place = jnp.stack([me, member]).astype(jnp.int32)
    capacity = 4 * rows // experts
    span = w_query.shape[1]
    window = reach + tile
    few = owners == 8

    token_blocks = gather_mp(tokens)
    pack = pack_weights(w_query, w_key, w_value, w_output)
    if few:
        both = pair_up(pack, swap(pack, "dp", 4), token_blocks[1:3])
        pack_blocks = [(both, (0, 4))] + [(swap(both, "dp", r), (r, r ^ 4)) for r in (1, 2, 3)]
    else:
        pack_blocks = [(lax.all_gather(pack, "dp", axis=0, tiled=True), (0,))]
    gain_one, gain_two = norm_gain.reshape(1, width), ffn_gain.reshape(1, width)
    normed, query, key_rows, value_rows, weight_q, weight_k, weight_v, w_o, late_cotangent = (
        project(place, token_blocks, pack_blocks, gain_one, cotangent, span)
    )

    if few:
        blocks, size = 4, capacity
        slots = [slots_of(routes, me, capacity, experts, 4)]
        slots.append(slots_of(swap(routes, "dp", 4), me, capacity, experts, 4))
    else:
        blocks, size = 1, experts * capacity
        slots = [slots_of(routes, 0, capacity, experts, experts)]

    if few:
        far_cotangent = swap(late_cotangent, "dp", 4)

    line_buckets = jnp.pad(jnp.flip(buckets[: reach + 1]), (0, window - reach - 1))
    bucket_hot = (
        line_buckets[:, None] == jnp.arange(128, dtype=jnp.int32)[None, :]
    ).astype(f32)
    buckets_all = bias_table.shape[0]
    table = jnp.pad(bias_table.T, ((0, 8 - heads), (0, 128 - buckets_all)))
    line = jnp.dot(table, bucket_hot.T, precision=highest)
    seg_q = segments.reshape(seq_len, 1)
    seg_k = jnp.pad(segments.reshape(1, seq_len), ((0, 0), (reach, 0)), constant_values=-1)
    mixed_out = attend(
        place, query, key_rows, value_rows, seg_q, seg_k, line, heads, members, [bucket_hot]
    )
    weight_o = gather_mp(w_o)
    mixed_in = [mixed_out[0]] + [swap(mixed_out[r], "mp", r) for r in range(1, members)]

    router_wide = jnp.pad(w_router, ((0, 0), (0, 128 - experts)))
    hidden, ffn_input, router_probs, *send = middle(
        tokens,
        mixed_in,
        weight_o,
        gain_two,
        router_wide,
        slots[0],
        experts,
        blocks,
        size,
        [far_cotangent] if few else [],
    )
    if few:
        held = to_slots(
            "grads_to_slots",
            [(cotangent, slots[0]), (far_cotangent, slots[1])],
            blocks,
            size,
            after=[ffn_input],
        )
        g_blocks = [held[0]] + [swap(held[r], "dp", r) for r in (1, 2, 3)]
        far_input = swap(ffn_input, "dp", 4)
        own = [send[0]] + [swap(send[r], "dp", r) for r in (1, 2, 3)]
        far = to_slots(
            "far_to_slots", [(far_input, slots[1])], blocks, size, after=g_blocks[1:]
        )
        far = [far[0]] + [swap(far[r], "dp", r) for r in (1, 2, 3)]
        x_sets = [own, far]
    else:
        held = to_slots("grads_to_slots", [(cotangent, slots[0])], blocks, size)
        g_blocks = [all_to_all_dp(held[0])]
        x_sets = [[all_to_all_dp(send[0])]]

    kept, before, backs = [], [experts], []
    for at, x_blocks in enumerate(x_sets):
        back, result, state = run_experts(
            "run_experts" + str(at),
            place,
            w_in[0],
            w_out[0],
            router_wide,
            x_blocks,
            g_blocks,
            at,
            before,
            brief if at == len(x_sets) - 1 else long,
            [] if at == len(x_sets) - 1 else [x_sets[-1][0]],
        )
        kept.append(state)
        backs.append(back)
        before = before + result
    actives, pre_grads, arrived, slot_grads = zip(*kept)
    if few:
        own_back, far_back = backs
        far_back = [far_back[0]] + [swap(far_back[r], "dp", r) for r in (1, 2, 3)]
        far_total, *passed = from_slots(
            "back_from_slots", far_back, [slots[1]], size, [bf16], through=own_back[1:]
        )
        far_sum = swap(far_total, "dp", 4)
        own_back = [own_back[0]] + [swap(passed[r - 1], "dp", r) for r in (1, 2, 3)]
        result_in = [result[0]] + [swap(result[r], "dp", r) for r in (1, 2, 3)]
    else:
        own_back, far_sum = [all_to_all_dp(backs[0][0])], None
        result_in = [all_to_all_dp(result[0])]
    near_w, base_w = expert_weight_grads(place, arrived, pre_grads, actives, slot_grads, members)

    homed = home(
        own_back,
        far_sum,
        slots[0],
        hidden,
        router_probs,
        cotangent,
        gain_two,
        router_wide,
        ffn_input,
        weight_o,
        mixed_in,
        size,
        experts,
        [],
        [near_w],
    )
    grad_out, homed = homed[:members], homed[members:]
    hidden_grad, ffn_gain_grad, router_grad, near_o, base_o, near_w = homed
    grad_in = [grad_out[0]] + [swap(grad_out[r], "mp", r) for r in range(1, members)]
    near_o, near_w = swap(near_o, "mp", 1), swap(near_w, "mp", 1)
    piece = w_in.shape[2] // members
    far_first, far_next, far_last = far_sums(
        near_w, base_w, near_o, base_o, [rows, piece, 2 * piece], grad_in[2:]
    )

    *proj_grads, line_grad = attend_back(
        place,
        query,
        key_rows,
        value_rows,
        seg_q,
        seg_k,
        line,
        grad_in,
        heads,
        [far_first],
    )
    far_first = swap(far_first, "mp", 2)
    far_next = swap(far_next, "mp", 2)
    far_last = swap(far_last, "mp", 2)
    near, base, base_far, small, *weight_sums = input_grads(
        place,
        proj_grads,
        normed,
        (weight_q, weight_k, weight_v),
        (base_o, near_o, far_first),
        gain_one,
        line_grad,
        bucket_hot,
        ffn_gain_grad,
        router_grad,
        members,
        owners,
        heads,
        result_in[1:],
    )
    near = swap(near, "mp", 1)
    far_normed = swap((base_far + near[rows:].astype(f32)).astype(bf16), "mp", 2)
    if few:
        arrived_sums = [swap(weight_sums[r], "dp", r) for r in (1, 2, 3)]
        own_sum, far_part, small = fold_weights(
            weight_sums[0], arrived_sums, [far_next, near], [small]
        )
        weight_grads = split_weights([own_sum, swap(far_part, "dp", 4)], span, [])
    else:
        joined_grad = lax.psum_scatter(weight_sums[0], "dp", scatter_dimension=0, tiled=True)
        weight_grads = split_weights([joined_grad], span, [])
    normed_grad = base + near[:rows].astype(f32) + far_normed.astype(f32)
    resid = tokens.astype(f32)
    _, inverse_one = normalize(resid, norm_gain)
    scaled = normed_grad * norm_gain
    inner = jnp.mean(scaled * resid, axis=-1, keepdims=True)
    tokens_grad = (
        hidden_grad + inverse_one * scaled - resid * inverse_one * inverse_one * inverse_one * inner
    ).astype(bf16)

    if few:
        own_result, far_result = from_slots(
            "result_from_slots", result_in, slots, size, [f32, bf16], after=[own_sum]
        )
        block_out = hidden + own_result + swap(far_result, "dp", 4).astype(f32)
    else:
        (own_result,) = from_slots("result_from_slots", result_in, slots, size, [f32])
        block_out = hidden + own_result
    block_out = block_out.astype(bf16)
    w_in_grad, w_out_grad = add_up(
        base_w, near_w, [(far_first, span), (far_next, 0), (far_last, 0)], [far_normed]
    )
    small = sum_over(sum_over(small, "dp"), "mp")
    return (
        block_out,
        tokens_grad,
        small[0],
        *weight_grads,
        small[2 : 2 + heads * members, :buckets_all].T,
        small[1],
        small[16:].T,
        w_in_grad[None],
        w_out_grad[None],
    )


def solution(mesh):
    return jax.shard_map(
        on_device,
        mesh=mesh,
        in_specs=(
            P(("dp", "mp"), None),
            P(),
            P("dp", "mp"),
            P("dp", "mp"),
            P("dp", "mp"),
            P("mp", "dp"),
            P(None, "mp"),
            P(),
            P(),
            P("dp", None, None),
            P("dp", None, None),
            P("dp", None),
            P(),
            P(("dp", "mp"), None),
            P(("dp", "mp"), None),
        ),
        out_specs=(
            P(("dp", "mp"), None),
            P(("dp", "mp"), None),
            P(),
            P("dp", "mp"),
            P("dp", "mp"),
            P("dp", "mp"),
            P("mp", "dp"),
            P(),
            P(),
            P(),
            P("dp", None, "mp"),
            P("dp", "mp", None),
        ),
        check_vma=False,
    )
```

```python
import functools
import math

import jax
import jax.numpy as jnp
from jax import lax
from jax.experimental import pallas as pl
from jax.experimental.pallas import tpu as pltpu
from jax.sharding import PartitionSpec as P

eps = 1e-06
highest = lax.Precision.HIGHEST
f32, bf16 = jnp.float32, jnp.bfloat16
excluded = -1e30
reach = 512
tile = 128


def limit(mebibytes):
    return pltpu.CompilerParams(vmem_limit_bytes=mebibytes * 1024 * 1024)


brief = pl.CostEstimate(flops=10**7, bytes_accessed=10**4, transcendentals=0)
long = pl.CostEstimate(flops=2 * 10**10, bytes_accessed=10**7, transcendentals=0)


def normalize(values, gain):
    inverse = lax.rsqrt(jnp.mean(values * values, axis=-1, keepdims=True) + eps)
    return (values * inverse * gain, inverse)


def dot(left, right, left_dim, right_dim, precision=None):
    return lax.dot_general(
        left,
        right,
        (((left_dim,), (right_dim,)), ((), ())),
        precision=precision,
        preferred_element_type=f32,
    )


def swap(values, axis, step):
    count = lax.axis_size(axis)
    return lax.ppermute(values, axis, [(i, i ^ step) for i in range(count)])


def whole(dims):
    return pl.BlockSpec(tuple(dims), lambda *_: (0,) * len(dims), pipeline_mode=pl.Buffered(1))


def call(
    kernel, name, operands, outs, scratch=(), scalars=None, after=(), through=(), cost=None
):
    outs = list(outs)
    pairs = [o if isinstance(o, tuple) else (o, o.shape[0]) for o in operands]
    operands = [array for array, _ in pairs]
    in_specs = [whole((rows,) + array.shape[1:]) for array, rows in pairs]
    out_specs = [whole(o.shape) for o in outs]
    if scalars is not None:
        operands = [scalars] + operands
        in_specs = [pl.BlockSpec(memory_space=pltpu.SMEM)] + in_specs
    count, results = len(operands), len(outs)
    extra = list(through) + list(after)

    def body(*refs):
        rest = refs[count + len(extra) :]
        kernel(*refs[:count], *rest[:results], *rest[results + len(through) :])

    return pl.pallas_call(
        body,
        name=name,
        grid=(1,),
        in_specs=in_specs + [pl.BlockSpec(memory_space=pl.ANY)] * len(extra),
        out_specs=out_specs + [pl.BlockSpec(memory_space=pl.ANY)] * len(through),
        out_shape=outs + [shape(o.shape, o.dtype) for o in through],
        input_output_aliases={count + i: results + i for i in range(len(through))},
        scratch_shapes=list(scratch),
        compiler_params=limit(64),
        cost_estimate=cost or brief,
    )(*operands, *extra)


def shape(dims, dtype):
    return jax.ShapeDtypeStruct(tuple(dims), dtype)


def fill_skew(line_ref, skew, heads):
    window = reach + tile
    row = lax.broadcasted_iota(jnp.int32, (tile, window), 0)
    column = lax.broadcasted_iota(jnp.int32, (tile, window), 1)
    usable = (column - row <= reach) & (column - row >= 1)
    for head in range(heads):
        line = jnp.broadcast_to(line_ref[head : head + 1, :], (tile, window))
        rolled = pltpu.roll(line, 0, 1, stride=1, stride_axis=0)
        skew[head * tile : (head + 1) * tile, :] = jnp.where(usable, rolled, excluded)


def fill_window(source_ref, padded):
    padded[:reach, :] = jnp.zeros((reach, padded.shape[1]), bf16)
    padded[reach:, :] = source_ref[...]


def spread_heads(values, heads, scale):
    span = values.shape[1]
    size = span // heads
    lane = lax.broadcasted_iota(jnp.int32, (tile, span), 1)
    wide = values.astype(f32) * scale
    parts = [
        jnp.where((lane >= head * size) & (lane < (head + 1) * size), wide, 0.0)
        for head in range(heads)
    ]
    return jnp.concatenate(parts, axis=0).astype(bf16)


def collect_heads(stacked, heads):
    span = stacked.shape[1]
    size = span // heads
    lane = lax.broadcasted_iota(jnp.int32, (tile, span), 1)
    total = stacked[:tile, :]
    for head in range(1, heads):
        total = jnp.where(lane < head * size, total, stacked[head * tile : (head + 1) * tile, :])
    return total


def window_powers(q_all, keys, skew, seg_q_ref, seg_k_ref, start, heads):
    window = reach + tile
    seg_q = jnp.concatenate([seg_q_ref[pl.ds(start, tile), :]] * heads, axis=0)
    seg_k = seg_k_ref[:, pl.ds(start, window)]
    scores = dot(q_all, keys, 1, 1) + skew[...]
    scores = jnp.where(seg_q == seg_k, scores, excluded)
    powers = jnp.exp(scores - jnp.max(scores, axis=-1, keepdims=True))
    return powers, 1.0 / jnp.sum(powers, axis=-1, keepdims=True)


def attend_kernel(heads, place, q_ref, k_ref, v_ref, seg_q_ref, seg_k_ref, line_ref, *rest):
    *out_refs, mixed, k_pad, v_pad, skew = rest
    window = reach + tile
    scale = (q_ref.shape[1] // heads) ** (-0.5)
    fill_skew(line_ref, skew, heads)
    fill_window(k_ref, k_pad)
    fill_window(v_ref, v_pad)

    def step(index, carry):
        start = pl.multiple_of(index * tile, tile)
        q_all = spread_heads(q_ref[pl.ds(start, tile), :], heads, scale)
        powers, inverse = window_powers(
            q_all, k_pad[pl.ds(start, window), :], skew, seg_q_ref, seg_k_ref, start, heads
        )
        probs = (powers * inverse).astype(bf16)
        part = dot(probs, v_pad[pl.ds(start, window), :], 1, 0)
        mixed[pl.ds(start, tile), :] = collect_heads(part, heads).astype(bf16)
        return carry

    lax.fori_loop(0, q_ref.shape[0] // tile, step, 0)
    rows = out_refs[0].shape[0]
    for r, out_ref in enumerate(out_refs):
        out_ref[...] = mixed[pl.ds(pl.multiple_of((place[1] ^ r) * rows, rows), rows), :]


def attend(place, query, key_rows, value_rows, seg_q, seg_k, line, heads, members, after):
    seq_len, span = query.shape
    window = reach + tile

    def kernel(place_ref, *refs):
        attend_kernel(heads, place_ref, *refs)

    return call(
        kernel,
        "attend",
        [query, key_rows, value_rows, seg_q, seg_k, line],
        [shape((seq_len // members, span), bf16)] * members,
        scratch=[
            pltpu.VMEM((seq_len, span), bf16),
            pltpu.VMEM((seq_len + reach, span), bf16),
            pltpu.VMEM((seq_len + reach, span), bf16),
            pltpu.VMEM((heads * tile, window), f32),
        ],
        scalars=place,
        after=after,
    )


def attend_back_kernel(heads, members, place, *refs):
    q_ref, k_ref, v_ref, seg_q_ref, seg_k_ref, line_ref = refs[:6]
    g_refs = refs[6 : 6 + members]
    dq_ref, dk_ref, dv_ref, line_grad_ref = refs[6 + members : 10 + members]
    grad, k_pad, v_pad, skew, dk_sum, dv_sum, bias_sum = refs[10 + members :]
    window = reach + tile
    scale = (q_ref.shape[1] // heads) ** (-0.5)
    rows = g_refs[0].shape[0]
    fill_skew(line_ref, skew, heads)
    fill_window(k_ref, k_pad)
    fill_window(v_ref, v_pad)
    dk_sum[...] = jnp.zeros_like(dk_sum)
    dv_sum[...] = jnp.zeros_like(dv_sum)
    bias_sum[...] = jnp.zeros_like(bias_sum)
    for r, g_ref in enumerate(g_refs):
        grad[pl.ds(pl.multiple_of((place[1] ^ r) * rows, rows), rows), :] = g_ref[...]

    def step(index, carry):
        start = pl.multiple_of(index * tile, tile)
        keys = k_pad[pl.ds(start, window), :]
        values = v_pad[pl.ds(start, window), :]
        q_all = spread_heads(q_ref[pl.ds(start, tile), :], heads, scale)
        g_all = spread_heads(grad[pl.ds(start, tile), :], heads, 1.0)
        powers, inverse = window_powers(q_all, keys, skew, seg_q_ref, seg_k_ref, start, heads)
        probs = powers * inverse
        dot_grad = dot(g_all, values, 1, 1)
        inner = jnp.sum(probs * dot_grad, axis=-1, keepdims=True)
        score_grad = (probs * (dot_grad - inner)).astype(bf16)
        bias_sum[...] += score_grad.astype(f32)
        part = collect_heads(dot(score_grad, keys, 1, 0), heads) * scale
        dq_ref[pl.ds(start, tile), :] = part.astype(bf16)
        dk_sum[pl.ds(start, window), :] += dot(score_grad, q_all, 0, 0)
        dv_sum[pl.ds(start, window), :] += dot(probs.astype(bf16), g_all, 0, 0)
        return carry

    lax.fori_loop(0, q_ref.shape[0] // tile, step, 0)
    dk_ref[...] = dk_sum[reach:, :].astype(bf16)
    dv_ref[...] = dv_sum[reach:, :].astype(bf16)
    line_grad_ref[...] = jnp.zeros_like(line_grad_ref)
    row = lax.broadcasted_iota(jnp.int32, (tile, tile), 0)
    column = lax.broadcasted_iota(jnp.int32, (tile, tile), 1)
    mirror = (row + column == tile - 1).astype(f32)
    for head in range(heads):
        part = bias_sum[head * tile : (head + 1) * tile, :]
        turned = dot(mirror, part, 1, 0, highest)
        straight = pltpu.roll(turned, window - tile + 1, 1, stride=1, stride_axis=0)
        line_grad_ref[head : head + 1, :] = jnp.sum(straight, axis=0, keepdims=True)


def attend_back(place, query, key_rows, value_rows, seg_q, seg_k, line, grads, heads, after):
    seq_len, span = query.shape
    window = reach + tile

    def kernel(place_ref, *refs):
        attend_back_kernel(heads, len(grads), place_ref, *refs)

    return call(
        kernel,
        "attend_back",
        [query, key_rows, value_rows, seg_q, seg_k, line] + grads,
        [shape((seq_len, span), bf16)] * 3 + [shape((8, window), f32)],
        scratch=[
            pltpu.VMEM((seq_len, span), bf16),
            pltpu.VMEM((seq_len + reach, span), bf16),
            pltpu.VMEM((seq_len + reach, span), bf16),
            pltpu.VMEM((heads * tile, window), f32),
            pltpu.VMEM((seq_len + reach, span), f32),
            pltpu.VMEM((seq_len + reach, span), f32),
            pltpu.VMEM((heads * tile, window), f32),
        ],
        scalars=place,
        after=after,
    )


def pack_weights(w_query, w_key, w_value, w_output):
    part, span = w_query.shape

    def kernel(q_ref, k_ref, v_ref, o_ref, pack_ref):
        for at, ref in enumerate((q_ref, k_ref, v_ref)):
            pack_ref[:, at * span : (at + 1) * span] = ref[...]
        pack_ref[:, 3 * span :] = o_ref[...].astype(f32).T.astype(bf16)

    (pack,) = call(
        kernel, "pack_weights", [w_query, w_key, w_value, w_output], [shape((part, 4 * span), bf16)]
    )
    return pack


def pair_up(pack, far, after):
    part = pack.shape[0]

    def kernel(near_ref, far_ref, both_ref):
        both_ref[:part, :] = near_ref[...]
        both_ref[part:, :] = far_ref[...]

    (both,) = call(
        kernel, "pair_up", [pack, far], [shape((2 * part, pack.shape[1]), bf16)], after=after
    )
    return both


def project(place, token_blocks, pack_blocks, gain, cotangent, span, after):
    rows, width = token_blocks[0].shape
    members = len(token_blocks)
    seq_len = rows * members
    parts = sum(len(held) for _, held in pack_blocks)
    part = width // parts

    def kernel(place_ref, gain_ref, *refs):
        token_refs = refs[:members]
        pack_refs = refs[members : members + len(pack_blocks)]
        (normed_ref, q_ref, k_ref, v_ref, wq_ref, wk_ref, wv_ref, wo_ref, pack) = refs[
            members + len(pack_blocks) :
        ]
        for (_, held), ref in zip(pack_blocks, pack_refs):
            for i, r in enumerate(held):
                at = pl.multiple_of((place_ref[0] ^ r) * part, part) if parts > 1 else 0
                pack[pl.ds(at, part), :] = ref[i * part : (i + 1) * part, :]
        for at, ref in enumerate((wq_ref, wk_ref, wv_ref)):
            ref[...] = pack[:, at * span : (at + 1) * span]
        wo_ref[...] = pack[:, 3 * span :].astype(f32).T.astype(bf16)
        for r, ref in enumerate(token_refs):
            normed, _ = normalize(ref[...].astype(f32), gain_ref[...])
            normed = normed.astype(bf16)
            at = pl.ds(pl.multiple_of((place_ref[1] ^ r) * rows, rows), rows)
            normed_ref[at, :] = normed
            q_ref[at, :] = dot(normed, wq_ref[...], 1, 0).astype(bf16)
            k_ref[at, :] = dot(normed, wk_ref[...], 1, 0).astype(bf16)
            v_ref[at, :] = dot(normed, wv_ref[...], 1, 0).astype(bf16)

    return call(
        kernel,
        "project",
        [gain] + list(token_blocks) + [array for array, _ in pack_blocks],
        [shape((seq_len, width), bf16)]
        + [shape((seq_len, span), bf16)] * 3
        + [shape((width, span), bf16)] * 3
        + [shape((span, width), bf16)],
        scratch=[pltpu.VMEM((width, width), bf16)],
        scalars=place,
        through=[cotangent],
        after=after,
    )


def hot(slots_ref, first, count):
    tokens = slots_ref.shape[1]
    slot = lax.broadcasted_iota(jnp.int32, (count, tokens), 0) + first
    taken = (slot == slots_ref[0:1, :]) | (slot == slots_ref[1:2, :])
    return jnp.where(taken, 1.0, 0.0).astype(bf16)


def to_slots(name, sets, blocks, size, after=()):
    width = sets[0][0].shape[1]

    def kernel(*refs):
        out_refs = refs[2 * len(sets) :]
        for at in range(len(sets)):
            rows_ref, slots_ref = refs[2 * at], refs[2 * at + 1]
            for b, out_ref in enumerate(out_refs):
                part = dot(hot(slots_ref, b * size, size), rows_ref[...], 1, 0)
                out_ref[at * size : (at + 1) * size, :] = part.astype(bf16)

    operands = [item for pair in sets for item in pair]
    return call(
        kernel,
        name,
        operands,
        [shape((size * len(sets), width), bf16)] * blocks,
        after=after,
    )


def from_slots(name, blocks, slots, size, dtypes, after=(), through=(), cost=None):
    count, sets = len(blocks), len(slots)
    width = blocks[0].shape[1]
    rows = slots[0].shape[1]

    def kernel(*refs):
        block_refs, slot_refs, out_refs = refs[:count], refs[count : count + sets], refs[count + sets :]
        for at in range(sets):
            total = None
            for b, ref in enumerate(block_refs):
                held = ref[at * size : (at + 1) * size, :]
                part = dot(hot(slot_refs[at], b * size, size), held, 0, 0)
                total = part if total is None else total + part
            out_refs[at][...] = total.astype(out_refs[at].dtype)

    return call(
        kernel,
        name,
        list(blocks) + list(slots),
        [shape((rows, width), dtype) for dtype in dtypes],
        after=after,
        through=through,
        cost=cost,
    )


def router_softmax(values, w_router, experts):
    logits = dot(values, w_router, 1, 0)
    lane = lax.broadcasted_iota(jnp.int32, logits.shape, 1)
    logits = jnp.where(lane < experts, logits, excluded)
    powers = jnp.exp(logits - jnp.max(logits, axis=-1, keepdims=True))
    return powers / jnp.sum(powers, axis=-1, keepdims=True)


def middle(tokens, mixed, weight_o, gain, w_router, slots, experts, blocks, size, after):
    rows, width = tokens.shape
    members = len(mixed)

    def kernel(*refs):
        token_ref, gain_ref, router_ref, slots_ref = refs[:4]
        mixed_refs, weight_refs = refs[4 : 4 + members], refs[4 + members : 4 + 2 * members]
        hidden_ref, input_ref, probs_ref, *send_refs = refs[4 + 2 * members :]
        hidden = token_ref[...].astype(f32)
        for left, right in zip(mixed_refs, weight_refs):
            hidden = hidden + dot(left[...], right[...], 1, 0)
        hidden_ref[...] = hidden
        normed, _ = normalize(hidden, gain_ref[...])
        normed = normed.astype(bf16)
        input_ref[...] = normed
        for b, ref in enumerate(send_refs):
            ref[...] = dot(hot(slots_ref, b * size, size), normed, 1, 0).astype(bf16)
        probs_ref[...] = router_softmax(normed, router_ref[...], experts)

    return call(
        kernel,
        "middle",
        [tokens, gain, w_router, slots] + mixed + weight_o,
        [shape((rows, width), f32), shape((rows, width), bf16), shape((rows, 128), f32)]
        + [shape((size, width), bf16)] * blocks,
        after=after,
    )


def join_rows(refs):
    return jnp.concatenate([ref[...] for ref in refs], axis=0)


def experts_forward(place, w_in, w_out, w_router, x_blocks, experts, after):
    width, units = w_in.shape
    count, size = len(x_blocks), x_blocks[0].shape[0]
    total, piece, chunk = size * count, 768, 256

    def kernel(me_ref, w_in_ref, w_out_ref, router_ref, *refs):
        x_refs, refs = refs[:count], refs[count + len(after) :]
        active_ref, slope_ref, x_all, result_ref, gates_ref, gated_ref, result_sum = refs

        @pl.when(pl.program_id(0) == 0)
        def _():
            x_all[...] = jnp.concatenate([ref[...] for ref in x_refs], axis=0)
            probs = router_softmax(x_all[...], router_ref[...], experts)
            lane = lax.broadcasted_iota(jnp.int32, probs.shape, 1)
            own = jnp.sum(jnp.where(lane == me_ref[0], probs, 0.0), axis=1, keepdims=True)
            gates_ref[...] = jnp.broadcast_to(own, gates_ref.shape)
            result_sum[...] = jnp.zeros_like(result_sum)

        for c in range(piece // chunk):
            at = slice(c * chunk, (c + 1) * chunk)
            pre_act = dot(x_all[...], w_in_ref[:, at], 1, 0)
            below = 0.5 + 0.5 * lax.erf(pre_act * math.sqrt(0.5))
            bell = jnp.exp(-0.5 * pre_act * pre_act) * (1.0 / math.sqrt(2.0 * math.pi))
            active_ref[:, at] = (pre_act * below).astype(bf16)
            slope_ref[:, at] = (below + pre_act * bell).astype(bf16)
        result_sum[...] += dot(active_ref[...], w_out_ref[...], 1, 0)

        @pl.when(pl.program_id(0) == pl.num_programs(0) - 1)
        def _():
            result = result_sum[...].astype(bf16)
            result_ref[...] = result
            gated_ref[...] = (gates_ref[:, 0:1] * result.astype(f32)).astype(bf16)

    columns = pl.BlockSpec((total, piece), lambda i: (0, i))
    rows = shape((total, width), bf16)
    kept = [rows, rows, shape((total, 128), f32), rows]
    return pl.pallas_call(
        kernel,
        name="experts_forward",
        grid=(units // piece,),
        in_specs=[
            pl.BlockSpec(memory_space=pltpu.SMEM),
            pl.BlockSpec((width, piece), lambda i: (0, i)),
            pl.BlockSpec((piece, width), lambda i: (i, 0)),
            whole(w_router.shape),
        ]
        + [whole(o.shape) for o in x_blocks]
        + [pl.BlockSpec(memory_space=pl.ANY)] * len(after),
        out_specs=[columns] * 2 + [whole(o.shape) for o in kept],
        out_shape=[shape((total, units), bf16)] * 2 + kept,
        scratch_shapes=[pltpu.VMEM((total, width), f32)],
        compiler_params=limit(64),
        cost_estimate=long,
    )(place, w_in, w_out, w_router, *x_blocks, *after)


def experts_backward(place, w_in, w_out, slope, result, gates, g_blocks, size):
    width, units = w_in.shape
    total, piece, chunk = slope.shape[0], 768, 256
    count = len(g_blocks)

    def kernel(me_ref, w_in_ref, w_out_ref, slope_ref, result_ref, gates_ref, *refs):
        g_refs, back_refs = refs[:count], refs[count : 2 * count]
        pre_grad_ref, s_all, back_sum = refs[2 * count :]

        @pl.when(pl.program_id(0) == 0)
        def _():
            back_sum[...] = jnp.zeros_like(back_sum)
            for b, ref in enumerate(g_refs):
                rows = slice(b * size, (b + 1) * size)
                s_all[rows, :] = (gates_ref[rows, 0:1] * ref[...].astype(f32)).astype(bf16)

        for c in range(piece // chunk):
            at = slice(c * chunk, (c + 1) * chunk)
            active_grad = dot(s_all[...], w_out_ref[at, :], 1, 1)
            pre_grad_ref[:, at] = (active_grad * slope_ref[:, at].astype(f32)).astype(bf16)
        back_sum[...] += dot(pre_grad_ref[...], w_in_ref[...], 1, 1)

        @pl.when(pl.program_id(0) == pl.num_programs(0) - 1)
        def _():
            lane = lax.broadcasted_iota(jnp.int32, (size, 128), 1)
            for b, (ref, g_ref) in enumerate(zip(back_refs, g_refs)):
                rows = slice(b * size, (b + 1) * size)
                products = g_ref[...].astype(f32) * result_ref[rows, :].astype(f32)
                gate_grad = jnp.sum(products, axis=1, keepdims=True)
                upper = gate_grad.astype(bf16).astype(f32)
                ref[:, :width] = back_sum[rows, :].astype(bf16)
                ref[:, width:] = jnp.where(
                    lane == me_ref[0],
                    upper,
                    jnp.where(lane == me_ref[0] + 64, gate_grad - upper, 0.0),
                ).astype(bf16)

    by_units = pl.BlockSpec((total, piece), lambda i: (0, i))
    outs = [shape((size, width + 128), bf16)] * count
    flat = pl.pallas_call(
        kernel,
        name="experts_backward",
        grid=(units // piece,),
        in_specs=[
            pl.BlockSpec(memory_space=pltpu.SMEM),
            pl.BlockSpec((width, piece), lambda i: (0, i)),
            pl.BlockSpec((piece, width), lambda i: (i, 0)),
            by_units,
            whole(result.shape),
            whole(gates.shape),
        ]
        + [whole((size, width))] * count,
        out_specs=[whole(o.shape) for o in outs] + [by_units, whole((total, width))],
        out_shape=outs + [shape((total, units), bf16), shape((total, width), bf16)],
        scratch_shapes=[pltpu.VMEM((total, width), f32)],
        compiler_params=limit(64),
        cost_estimate=long,
    )(place, w_in, w_out, slope, result, gates, *g_blocks)
    return list(flat[:count]), flat[count], flat[count + 1]


def run_experts(
    name, place, w_in, w_out, w_router, x_blocks, g_blocks, at_set, before, cost, after
):
    width, units = w_in.shape
    count, size = len(x_blocks), x_blocks[0].shape[0]
    total, piece, chunk = size * count, 512, 256
    experts = before[0]
    held = list(before[1:])
    sets = g_blocks[0].shape[0] // size
    last = at_set == sets - 1

    def kernel(me_ref, w_in_ref, w_out_ref, router_ref, *refs):
        x_refs, refs = refs[:count], refs[count:]
        g_refs, refs = refs[:count], refs[count:]
        held_refs, refs = refs[: len(held)], refs[len(held) + len(after) :]
        back_refs, refs = refs[:count], refs[count:]
        result_refs, refs = refs[:count] if last else refs[:1], refs[count if last else 1 :]
        active_ref, pre_grad_ref, x_all, s_all, gates, result_sum, back_sum = refs

        @pl.when(pl.program_id(0) == 0)
        def _():
            for b in range(count):
                rows = slice(b * size, (b + 1) * size)
                x_all[rows, :] = x_refs[b][...]
            probs = router_softmax(x_all[...], router_ref[...], experts)
            lane = lax.broadcasted_iota(jnp.int32, probs.shape, 1)
            own = jnp.sum(jnp.where(lane == me_ref[0], probs, 0.0), axis=1, keepdims=True)
            gates[...] = jnp.broadcast_to(own, gates.shape)
            for b in range(count):
                rows = slice(b * size, (b + 1) * size)
                grad = g_refs[b][at_set * size : (at_set + 1) * size, :].astype(f32)
                s_all[rows, :] = (gates[rows, 0:1] * grad).astype(bf16)
            result_sum[...] = jnp.zeros_like(result_sum)
            back_sum[...] = jnp.zeros_like(back_sum)

        for c in range(piece // chunk):
            at = slice(c * chunk, (c + 1) * chunk)
            pre_act = dot(x_all[...], w_in_ref[:, at], 1, 0)
            active_grad = dot(s_all[...], w_out_ref[at, :], 1, 1)
            below = 0.5 + 0.5 * lax.erf(pre_act * math.sqrt(0.5))
            bell = jnp.exp(-0.5 * pre_act * pre_act) * (1.0 / math.sqrt(2.0 * math.pi))
            active_ref[:, at] = (pre_act * below).astype(bf16)
            pre_grad_ref[:, at] = (active_grad * (below + pre_act * bell)).astype(bf16)
        result_sum[...] += dot(active_ref[...], w_out_ref[...], 1, 0)
        back_sum[...] += dot(pre_grad_ref[...], w_in_ref[...], 1, 1)

        @pl.when(pl.program_id(0) == pl.num_programs(0) - 1)
        def _():
            lane = lax.broadcasted_iota(jnp.int32, (size, 128), 1)
            for b, (ref, g_ref) in enumerate(zip(back_refs, g_refs)):
                rows = slice(b * size, (b + 1) * size)
                result = result_sum[rows, :].astype(bf16).astype(f32)
                grad = g_ref[at_set * size : (at_set + 1) * size, :].astype(f32)
                gate_grad = jnp.sum(grad * result, axis=1, keepdims=True)
                upper = gate_grad.astype(bf16).astype(f32)
                ref[:, :width] = back_sum[rows, :].astype(bf16)
                ref[:, width:] = jnp.where(
                    lane == me_ref[0],
                    upper,
                    jnp.where(lane == me_ref[0] + 64, gate_grad - upper, 0.0),
                ).astype(bf16)
                gated = (gates[rows, 0:1] * result).astype(bf16)
                if last:
                    for at, other in enumerate(held_refs):
                        result_refs[b][at * size : (at + 1) * size, :] = other[rows, :]
                    result_refs[b][at_set * size : (at_set + 1) * size, :] = gated
                else:
                    result_refs[0][rows, :] = gated

    columns = pl.BlockSpec((total, piece), lambda i: (0, i))
    outs = [shape((size, width + 128), bf16)] * count
    results = [shape((size * sets, width), bf16)] * count if last else [shape((total, width), bf16)]
    rows_out = [shape((total, width), bf16)] * 2
    flat = pl.pallas_call(
        kernel,
        name=name,
        grid=(units // piece,),
        in_specs=[
            pl.BlockSpec(memory_space=pltpu.SMEM),
            pl.BlockSpec((width, piece), lambda i: (0, i)),
            pl.BlockSpec((piece, width), lambda i: (i, 0)),
            whole(w_router.shape),
        ]
        + [whole(o.shape) for o in list(x_blocks) + list(g_blocks) + held]
        + [pl.BlockSpec(memory_space=pl.ANY)] * len(after),
        out_specs=[whole(o.shape) for o in outs + results]
        + [columns] * 2
        + [whole(o.shape) for o in rows_out],
        out_shape=outs + results + [shape((total, units), bf16)] * 2 + rows_out,
        scratch_shapes=[
            pltpu.VMEM((total, 128), f32),
            pltpu.VMEM((total, width), f32),
            pltpu.VMEM((total, width), f32),
        ],
        compiler_params=limit(64),
        cost_estimate=cost,
    )(place, w_in, w_out, w_router, *x_blocks, *g_blocks, *held, *after)
    return list(flat[:count]), list(flat[count:-4]), flat[-4:]


def home(
    own_back,
    far_sum,
    slots,
    hidden,
    probs,
    cotangent,
    gain,
    w_router,
    ffn_input,
    weight_o,
    mixed,
    size,
    experts,
    after,
    through,
):
    rows, width = hidden.shape
    count, members = len(own_back), len(weight_o)
    span = weight_o[0].shape[0]
    far = [] if far_sum is None else [far_sum]

    def kernel(*refs):
        slots_ref, hidden_ref, probs_ref, cot_ref, gain_ref, router_ref, input_ref = refs[:7]
        refs = refs[7:]
        back_refs, refs = refs[:count], refs[count:]
        far_refs, refs = refs[: len(far)], refs[len(far) :]
        weight_refs, mixed_refs, refs = refs[:members], refs[members : 2 * members], refs[2 * members :]
        grad_refs = refs[:members]
        hidden_grad_ref, gain_grad_ref, router_grad_ref, near_ref, base_ref = refs[members:]
        total = None
        for b, ref in enumerate(back_refs):
            part = dot(hot(slots_ref, b * size, size), ref[...], 0, 0)
            total = part if total is None else total + part
        for ref in far_refs:
            total = total + ref[...].astype(f32)
        columns = total[:, width:]
        lane = lax.broadcasted_iota(jnp.int32, columns.shape, 1)
        prob_grad = jnp.where(lane < 64, columns + pltpu.roll(columns, 64, 1), 0.0)
        router_probs = probs_ref[...]
        logit_grad = router_probs * (
            prob_grad - jnp.sum(router_probs * prob_grad, axis=-1, keepdims=True)
        )
        router_grad_ref[...] = dot(logit_grad, input_ref[...].astype(f32), 0, 0, highest)[:experts, :]
        grad = total[:, :width] + dot(logit_grad, router_ref[...].astype(f32), 1, 1, highest)
        hidden_now = hidden_ref[...]
        inverse = lax.rsqrt(jnp.mean(hidden_now * hidden_now, axis=-1, keepdims=True) + eps)
        scaled = grad * gain_ref[...]
        gain_grad_ref[...] = jnp.sum(grad * hidden_now * inverse, axis=0, keepdims=True)
        inner = jnp.mean(scaled * hidden_now, axis=-1, keepdims=True)
        hidden_grad = (
            cot_ref[...].astype(f32)
            + inverse * scaled
            - hidden_now * inverse * inverse * inverse * inner
        )
        hidden_grad_ref[...] = hidden_grad
        attn_grad = hidden_grad.astype(bf16)
        for ref, weight in zip(grad_refs, weight_refs):
            ref[...] = dot(attn_grad, weight[...], 1, 1).astype(bf16)
        for r, (ref, first) in enumerate(
            ((base_ref, 0), (near_ref, 0), (base_ref, span), (near_ref, span))
        ):
            part = dot(mixed_refs[r][...], attn_grad, 0, 0)
            ref[first : first + span, :] = part.astype(ref.dtype)

    return call(
        kernel,
        "home",
        [slots, hidden, probs, cotangent, gain, w_router, ffn_input]
        + list(own_back)
        + far
        + weight_o
        + mixed,
        [shape((rows, span), bf16)] * members
        + [
            shape((rows, width), f32),
            shape((1, width), f32),
            shape((experts, width), f32),
            shape((2 * span, width), bf16),
            shape((2 * span, width), f32),
        ],
        after=after,
        through=through,
    )


def expert_weight_grads(place, rows_in, pre_grads, actives, slot_grads, members):
    sets = len(rows_in)
    total, width = rows_in[0].shape
    piece = pre_grads[0].shape[1] // members

    def kernel(place_ref, *refs):
        x_refs, p_refs, a_refs, s_refs = [refs[i * sets : (i + 1) * sets] for i in range(4)]
        near_ref, base_ref, out = refs[4 * sets :]
        step = pl.program_id(0)

        def total_of(lefts, rights):
            held = dot(lefts[0][...], rights[0][...], 0, 0)
            for left, right in zip(lefts[1:], rights[1:]):
                held = held + dot(left[...], right[...], 0, 0)
            return held

        @pl.when(step < 4)
        def _():
            out[...] = total_of(x_refs, p_refs)

        @pl.when(step >= 4)
        def _():
            out[...] = total_of(a_refs, s_refs)

        @pl.when(step % 4 < 2)
        def _():
            near_ref[...] = out[...].astype(bf16)

        @pl.when(step % 4 >= 2)
        def _():
            base_ref[...] = out[...]

    def partner(i):
        return jnp.where(i < 2, 2 * i + 1, 2 * i - 4)

    fixed = pl.BlockSpec((total, width), lambda i, p: (0, 0))
    pre_cut = pl.BlockSpec((total, piece), lambda i, p: (0, p[1] ^ partner(jnp.minimum(i, 3))))
    act_cut = pl.BlockSpec((total, piece), lambda i, p: (0, p[1] ^ partner(jnp.maximum(i - 4, 0))))
    return pl.pallas_call(
        kernel,
        name="expert_weight_grads",
        grid_spec=pltpu.PrefetchScalarGridSpec(
            num_scalar_prefetch=1,
            grid=(8,),
            in_specs=[fixed] * sets + [pre_cut] * sets + [act_cut] * sets + [fixed] * sets,
            out_specs=[
                pl.BlockSpec(
                    (piece, width), lambda i, p: (2 * (i // 4) + jnp.minimum(i % 4, 1), 0)
                ),
                pl.BlockSpec(
                    (piece, width), lambda i, p: (2 * (i // 4) + jnp.maximum(i % 4 - 2, 0), 0)
                ),
            ],
            scratch_shapes=[pltpu.VMEM((piece, width), f32)],
        ),
        out_shape=[shape((4 * piece, width), bf16), shape((4 * piece, width), f32)],
        compiler_params=limit(64),
        cost_estimate=long,
    )(place, *rows_in, *pre_grads, *actives, *slot_grads)


def far_sums(near, base, near_o, base_o, cuts, after):
    size, width = base.shape[0] // 4, base.shape[1]
    span = near_o.shape[0] // 2

    def block(rows, at):
        return pl.BlockSpec((rows, width), lambda *_: (at, 0), pipeline_mode=pl.Buffered(1))

    def kernel(near_in, near_out, base_in, base_out, near_o_ref, base_o_ref, *refs):
        out_refs = refs[len(after) :]
        out_refs[0][:span, :] = (base_o_ref[...] + near_o_ref[...].astype(f32)).astype(bf16)
        starts = [0] + cuts
        for i, ref in enumerate(out_refs):
            low, high = starts[i], starts[i + 1]
            at = span if i == 0 else 0
            for near_ref, base_ref, shift in ((near_in, base_in, 0), (near_out, base_out, size)):
                first, last = max(low, shift), min(high, shift + size)
                if first < last:
                    rows = slice(first - shift, last - shift)
                    held = base_ref[rows, :] + near_ref[rows, :].astype(f32)
                    ref[at + first - low : at + last - low, :] = held.astype(bf16)

    rows = [high - low for low, high in zip([0] + cuts, cuts)]
    rows[0] = rows[0] + span
    return pl.pallas_call(
        kernel,
        name="far_sums",
        grid=(1,),
        in_specs=[block(size, 1), block(size, 3), block(size, 1), block(size, 3)]
        + [block(span, 1), block(span, 1)]
        + [pl.BlockSpec(memory_space=pl.ANY)] * len(after),
        out_specs=[whole((count, width)) for count in rows],
        out_shape=[shape((count, width), bf16) for count in rows],
        compiler_params=limit(64),
        cost_estimate=brief,
    )(near, near, base, base, near_o, base_o, *after)


def input_grads(
    place,
    proj_grads,
    normed,
    weights,
    output_parts,
    gain,
    line_grad,
    bucket_hot,
    ffn_gain_grad,
    router_grad,
    members,
    owners,
    heads,
    buckets_all,
    after,
):
    seq_len, width = normed.shape
    span = weights[0].shape[1]
    rows = seq_len // members
    part = width // owners
    few = owners == 8
    experts = router_grad.shape[0]
    extra = -(-(3 + experts) // 16) * 16

    def kernel(place_ref, *refs):
        dq_ref, dk_ref, dv_ref, normed_ref, wq_ref, wk_ref, wv_ref, gain_ref = refs[:8]
        line_ref, hot_ref, ffn_gain_ref, router_ref = refs[8:12]
        base_o_ref, near_o_ref, far_o_ref = refs[12:15]
        near_ref, base_ref, far_ref, small_ref, *weight_refs, sums = refs[15:]
        for at, ref in enumerate((dq_ref, dk_ref, dv_ref)):
            sums[:, at * span : (at + 1) * span] = dot(normed_ref[...], ref[...], 0, 0)
        output_sum = base_o_ref[...] + near_o_ref[...].astype(f32) + far_o_ref[...].astype(f32)
        sums[:, 3 * span :] = output_sum.T
        if few:
            for r, ref in enumerate(weight_refs):
                for i, far in enumerate((0, 4)):
                    at = pl.multiple_of((place_ref[0] ^ r ^ far) * part, part)
                    ref[i * part : (i + 1) * part, :] = sums[pl.ds(at, part), :].astype(ref.dtype)
        else:
            weight_refs[0][...] = sums[...]
        gain_grad = jnp.zeros((1, width), f32)
        for r, (ref, first) in enumerate(
            ((base_ref, 0), (near_ref, 0), (far_ref, 0), (near_ref, rows))
        ):
            at = pl.ds(pl.multiple_of((place_ref[1] ^ r) * rows, rows), rows)
            grad = (
                dot(dq_ref[at, :], wq_ref[...], 1, 1)
                + dot(dk_ref[at, :], wk_ref[...], 1, 1)
                + dot(dv_ref[at, :], wv_ref[...], 1, 1)
            )
            gain_grad = gain_grad + jnp.sum(
                grad * normed_ref[at, :].astype(f32), axis=0, keepdims=True
            )
            ref[first : first + rows, :] = grad.astype(ref.dtype)
        table = dot(line_ref[...], hot_ref[...], 1, 0, highest)
        bucket = lax.broadcasted_iota(jnp.int32, (128, width), 0)
        lane = lax.broadcasted_iota(jnp.int32, (128, width), 1)
        flat = jnp.zeros((1, width), f32)
        for head in range(heads):
            first = (place_ref[1] * heads + head) * buckets_all
            spread = jnp.where((bucket < buckets_all) & (lane == bucket + first), 1.0, 0.0)
            flat = flat + dot(table[head : head + 1, :], spread, 1, 0, highest)
        small_ref[...] = jnp.zeros_like(small_ref)
        small_ref[0:1, :] = gain_grad / gain_ref[...]
        small_ref[1:2, :] = ffn_gain_ref[...]
        small_ref[2:3, :] = flat
        small_ref[3 : 3 + experts, :] = router_ref[...]
        if few:
            upper, lower = two_halves(small_ref[...])
            small_ref[...] = upper.astype(f32) + lower.astype(f32)
            for ref in weight_refs[1:]:
                ref[2 * part : 2 * part + extra, :] = upper
                ref[2 * part + extra :, :] = lower

    if few:
        weight_outs = [shape((2 * part, 4 * span), f32)]
        weight_outs += [shape((2 * part + 2 * extra, 4 * span), bf16)] * 3
    else:
        weight_outs = [shape((width, 4 * span), f32)]
    return call(
        kernel,
        "input_grads",
        list(proj_grads)
        + [normed]
        + list(weights)
        + [gain, line_grad, bucket_hot, ffn_gain_grad, router_grad]
        + [(part, span) for part in output_parts],
        [
            shape((2 * rows, width), bf16),
            shape((rows, width), f32),
            shape((rows, width), f32),
            shape((extra, width), f32),
        ]
        + weight_outs,
        scratch=[pltpu.VMEM((width, 4 * span), f32)],
        scalars=place,
        after=after,
    )


def add_up(base, near, parts):
    size, width = base.shape[0] // 4, base.shape[1]

    def kernel(in_base, in_near, out_base, out_near, *refs):
        part_refs, (in_ref, out_ref) = refs[: len(parts)], refs[-2:]
        first = 0
        for (array, at), ref in zip(parts[:-1], part_refs[:-1]):
            rows = slice(first, first + array.shape[0] - at)
            total = in_base[rows, :] + in_near[rows, :].astype(f32)
            in_ref[rows, :] = total + ref[at:, :].astype(f32)
            first = first + array.shape[0] - at
        total = out_base[...] + out_near[...].astype(f32)
        out_ref[...] = total + part_refs[-1][...].astype(f32)

    def block(at):
        return pl.BlockSpec((size, width), lambda *_: (at, 0), pipeline_mode=pl.Buffered(1))

    specs = [block(0), block(0), block(2), block(2)] + [whole(o.shape) for o, _ in parts]
    return pl.pallas_call(
        kernel,
        name="add_up",
        grid=(1,),
        in_specs=specs,
        out_specs=[whole((size, width))] * 2,
        out_shape=[shape((size, width), f32)] * 2,
        compiler_params=limit(64),
        cost_estimate=long,
    )(base, near, base, near, *[array for array, _ in parts])


def two_halves(values):
    upper = values.astype(bf16)
    return upper, (values - upper.astype(f32)).astype(bf16)


def fold_weights(base, arrived, small, after):
    part, width, extra = base.shape[0] // 2, base.shape[1], small.shape[0]

    def kernel(base_ref, one_ref, two_ref, three_ref, small_ref, own_ref, far_ref, half_ref):
        refs = (one_ref, two_ref, three_ref)
        total = base_ref[...]
        for ref in refs:
            total = total + ref[: 2 * part, :].astype(f32)
        own_ref[...] = total[:part, :]
        far_ref[:part, :] = total[part:, :].astype(bf16)
        one, two, three = [
            ref[2 * part : 2 * part + extra, :].astype(f32)
            + ref[2 * part + extra :, :].astype(f32)
            for ref in refs
        ]
        upper, lower = two_halves((small_ref[...] + one) + (two + three))
        far_ref[part : part + extra, :] = upper
        far_ref[part + extra :, :] = lower
        half_ref[...] = upper.astype(f32) + lower.astype(f32)

    return call(
        kernel,
        "fold_weights",
        [base] + arrived + [small],
        [
            shape((part, width), f32),
            shape((part + 2 * extra, width), bf16),
            shape((extra, width), f32),
        ],
        after=after,
    )


def split_weights(own, far, small, span, after):
    part, extra = own.shape[0], small.shape[0]

    def kernel(*refs):
        own_ref, small_ref, *far_refs = refs[:-5]
        q_ref, k_ref, v_ref, o_ref, sum_ref = refs[-5:]
        total, sums = own_ref[...], small_ref[...]
        for ref in far_refs:
            total = total + ref[:part, :].astype(f32)
            sums = sums + (
                ref[part : part + extra, :].astype(f32) + ref[part + extra :, :].astype(f32)
            )
        for at, ref in enumerate((q_ref, k_ref, v_ref)):
            ref[...] = total[:, at * span : (at + 1) * span]
        o_ref[...] = total[:, 3 * span :].T
        sum_ref[...] = sums

    return call(
        kernel,
        "split_weights",
        [own, small] + ([] if far is None else [far]),
        [shape((part, span), f32)] * 3
        + [shape((span, part), f32), shape((extra, own.shape[1]), f32)],
        after=after,
    )


def gather_mp(values):
    across = swap(values, "mp", 2)
    return [values, swap(values, "mp", 1), across, swap(across, "mp", 1)]


def sum_over(values, axis):
    step = 1
    while step < lax.axis_size(axis):
        values = values + swap(values, axis, step)
        step = 2 * step
    return values


def all_to_all_dp(values):
    return lax.all_to_all(values, "dp", split_axis=0, concat_axis=0, tiled=True)


def slots_of(routes, place, capacity, experts, limit):
    rows = routes.shape[0]
    expert_ids = jnp.arange(experts, dtype=jnp.int32)[None, :]
    hits = (routes[:, 0:1] == expert_ids) | (routes[:, 1:2] == expert_ids)
    earlier = jnp.arange(rows)[:, None] > jnp.arange(rows)[None, :]
    ranks = jnp.dot(earlier.astype(bf16), hits.astype(bf16), preferred_element_type=f32)
    lines = []
    for k in (0, 1):
        rank = jnp.sum(jnp.where(routes[:, k : k + 1] == expert_ids, ranks, 0.0), axis=1)
        block = routes[:, k] ^ place
        lines.append(jnp.where(block < limit, block * capacity + rank.astype(jnp.int32), -1))
    return jnp.pad(jnp.stack(lines), ((0, 6), (0, 0)), constant_values=-1)


def on_device(
    tokens,
    norm_gain,
    w_query,
    w_key,
    w_value,
    w_output,
    bias_table,
    ffn_gain,
    w_router,
    w_in,
    w_out,
    segments,
    buckets,
    routes,
    cotangent,
):
    rows, width = tokens.shape
    heads = bias_table.shape[1]
    seq_len = buckets.shape[0]
    experts = w_router.shape[1]
    owners, members = lax.axis_size("dp"), lax.axis_size("mp")
    me, member = lax.axis_index("dp"), lax.axis_index("mp")
    place = jnp.stack([me, member]).astype(jnp.int32)
    capacity = 4 * rows // experts
    span = w_query.shape[1]
    window = reach + tile
    few = owners == 8

    token_blocks = gather_mp(tokens)
    pack = pack_weights(w_query, w_key, w_value, w_output)
    if few:
        both = pair_up(pack, swap(pack, "dp", 4), token_blocks[1:3])
        pack_blocks = [(both, (0, 4))] + [(swap(both, "dp", r), (r, r ^ 4)) for r in (1, 2, 3)]
    else:
        pack_blocks = [(lax.all_gather(pack, "dp", axis=0, tiled=True), (0,))]
    gain_one, gain_two = norm_gain.reshape(1, width), ffn_gain.reshape(1, width)
    if few:
        blocks, size = 4, capacity
        slots = [slots_of(routes, me, capacity, experts, 4)]
        slots.append(slots_of(swap(routes, "dp", 4), me, capacity, experts, 4))
    else:
        blocks, size = 1, experts * capacity
        slots = [slots_of(routes, 0, capacity, experts, experts)]

    line_buckets = jnp.pad(jnp.flip(buckets[: reach + 1]), (0, window - reach - 1))
    bucket_hot = (
        line_buckets[:, None] == jnp.arange(128, dtype=jnp.int32)[None, :]
    ).astype(f32)
    buckets_all = bias_table.shape[0]
    table = jnp.pad(bias_table.T, ((0, 8 - heads), (0, 128 - buckets_all)))
    line = jnp.dot(table, bucket_hot.T, precision=highest)
    seg_q = segments.reshape(seq_len, 1)
    seg_k = jnp.pad(segments.reshape(1, seq_len), ((0, 0), (reach, 0)), constant_values=-1)
    router_wide = jnp.pad(w_router, ((0, 0), (0, 128 - experts)))
    ready = [line, bucket_hot, seg_q, seg_k, router_wide, gain_two] + slots
    normed, query, key_rows, value_rows, weight_q, weight_k, weight_v, w_o, late_cotangent = (
        project(place, token_blocks, pack_blocks, gain_one, cotangent, span, ready)
    )


    if few:
        far_cotangent = swap(late_cotangent, "dp", 4)

    mixed_out = attend(
        place, query, key_rows, value_rows, seg_q, seg_k, line, heads, members, [bucket_hot]
    )
    weight_o = gather_mp(w_o)
    mixed_in = [mixed_out[0]] + [swap(mixed_out[r], "mp", r) for r in range(1, members)]

    hidden, ffn_input, router_probs, *send = middle(
        tokens,
        mixed_in,
        weight_o,
        gain_two,
        router_wide,
        slots[0],
        experts,
        blocks,
        size,
        [far_cotangent] if few else [],
    )
    if few:
        held = to_slots(
            "grads_to_slots",
            [(cotangent, slots[0]), (far_cotangent, slots[1])],
            blocks,
            size,
            after=[ffn_input],
        )
        g_blocks = [held[0]] + [swap(held[r], "dp", r) for r in (1, 2, 3)]
        far_input = swap(ffn_input, "dp", 4)
        own = [send[0]] + [swap(send[r], "dp", r) for r in (1, 2, 3)]
        far = to_slots(
            "far_to_slots", [(far_input, slots[1])], blocks, size, after=g_blocks[1:3]
        )
        far = [far[0]] + [swap(far[r], "dp", r) for r in (1, 2, 3)]
        x_sets = [own, far]
    else:
        held = to_slots("grads_to_slots", [(cotangent, slots[0])], blocks, size)
        g_blocks = [all_to_all_dp(held[0])]
        x_sets = [[all_to_all_dp(send[0])]]

    before = [experts]
    if few:
        active, slope, rows_in, plain, slot_gates, gated = experts_forward(
            place, w_in[0], w_out[0], router_wide, x_sets[0], experts, far[:1]
        )
        before = before + [gated]
    back, result, state = run_experts(
        "run_experts",
        place,
        w_in[0],
        w_out[0],
        router_wide,
        x_sets[-1],
        g_blocks,
        len(x_sets) - 1,
        before,
        brief,
        [],
    )
    kept, backs = [state], [back]
    if few:
        back, pre_grad, slot_grad = experts_backward(
            place, w_in[0], w_out[0], slope, plain, slot_gates, g_blocks, size
        )
        kept = [(active, pre_grad, rows_in, slot_grad)] + kept
        backs = [back] + backs
    actives, pre_grads, arrived, slot_grads = zip(*kept)
    if few:
        own_back, far_back = backs
        far_back = [far_back[0]] + [swap(far_back[r], "dp", r) for r in (1, 2, 3)]
        far_total, *passed = from_slots(
            "back_from_slots", far_back, [slots[1]], size, [bf16], through=own_back[1:]
        )
        far_sum = swap(far_total, "dp", 4)
        own_back = [own_back[0]] + [swap(passed[r - 1], "dp", r) for r in (1, 2, 3)]
        result_in = [result[0]] + [swap(result[r], "dp", r) for r in (1, 2, 3)]
    else:
        own_back, far_sum = [all_to_all_dp(backs[0][0])], None
        result_in = [all_to_all_dp(result[0])]
    near_w, base_w = expert_weight_grads(place, arrived, pre_grads, actives, slot_grads, members)

    homed = home(
        own_back,
        far_sum,
        slots[0],
        hidden,
        router_probs,
        cotangent,
        gain_two,
        router_wide,
        ffn_input,
        weight_o,
        mixed_in,
        size,
        experts,
        [],
        [near_w],
    )
    grad_out, homed = homed[:members], homed[members:]
    hidden_grad, ffn_gain_grad, router_grad, near_o, base_o, near_w = homed
    grad_in = [grad_out[0]] + [swap(grad_out[r], "mp", r) for r in range(1, members)]
    near_o, near_w = swap(near_o, "mp", 1), swap(near_w, "mp", 1)
    piece = w_in.shape[2] // members
    far_first, far_next, far_last = far_sums(
        near_w, base_w, near_o, base_o, [rows, piece, 2 * piece], grad_in[2:]
    )

    *proj_grads, line_grad = attend_back(
        place,
        query,
        key_rows,
        value_rows,
        seg_q,
        seg_k,
        line,
        grad_in,
        heads,
        [far_first],
    )
    far_first = swap(far_first, "mp", 2)
    far_next = swap(far_next, "mp", 2)
    far_last = swap(far_last, "mp", 2)
    near, base, base_far, small, *weight_sums = input_grads(
        place,
        proj_grads,
        normed,
        (weight_q, weight_k, weight_v),
        (base_o, near_o, far_first),
        gain_one,
        line_grad,
        bucket_hot,
        ffn_gain_grad,
        router_grad,
        members,
        owners,
        heads,
        buckets_all,
        result_in[1:],
    )
    w_in_grad, w_out_grad = add_up(
        base_w, near_w, [(far_first, span), (far_next, 0), (far_last, 0)]
    )
    near = swap(near, "mp", 1)
    far_normed = swap((base_far + near[rows:].astype(f32)).astype(bf16), "mp", 2)
    if few:
        arrived_sums = [swap(weight_sums[r], "dp", r) for r in (1, 2, 3)]
        own_sum, far_part, small = fold_weights(
            weight_sums[0], arrived_sums, small, [far_next, near]
        )
        own_result, far_result = from_slots(
            "result_from_slots", result_in, slots, size, [f32, bf16], after=[own_sum]
        )
        far_result = swap(far_result, "dp", 4)
        *weight_grads, small = split_weights(
            own_sum, swap(far_part, "dp", 4), small, span, [w_in_grad, far_normed]
        )
    else:
        joined_grad = lax.psum_scatter(weight_sums[0], "dp", scatter_dimension=0, tiled=True)
        *weight_grads, small = split_weights(
            joined_grad, None, sum_over(small, "dp"), span, []
        )
        (own_result,) = from_slots("result_from_slots", result_in, slots, size, [f32])
    small = sum_over(small, "mp")
    normed_grad = base + near[:rows].astype(f32) + far_normed.astype(f32)
    resid = tokens.astype(f32)
    _, inverse_one = normalize(resid, norm_gain)
    scaled = normed_grad * norm_gain
    inner = jnp.mean(scaled * resid, axis=-1, keepdims=True)
    tokens_grad = (
        hidden_grad + inverse_one * scaled - resid * inverse_one * inverse_one * inverse_one * inner
    ).astype(bf16)

    block_out = hidden + own_result
    if few:
        block_out = block_out + far_result.astype(f32)
    block_out = block_out.astype(bf16)
    return (
        block_out,
        tokens_grad,
        small[0],
        *weight_grads,
        small[2, : heads * members * buckets_all].reshape(heads * members, buckets_all).T,
        small[1],
        small[3 : 3 + experts].T,
        w_in_grad[None],
        w_out_grad[None],
    )


def solution(mesh):
    return jax.shard_map(
        on_device,
        mesh=mesh,
        in_specs=(
            P(("dp", "mp"), None),
            P(),
            P("dp", "mp"),
            P("dp", "mp"),
            P("dp", "mp"),
            P("mp", "dp"),
            P(None, "mp"),
            P(),
            P(),
            P("dp", None, None),
            P("dp", None, None),
            P("dp", None),
            P(),
            P(("dp", "mp"), None),
            P(("dp", "mp"), None),
        ),
        out_specs=(
            P(("dp", "mp"), None),
            P(("dp", "mp"), None),
            P(),
            P("dp", "mp"),
            P("dp", "mp"),
            P("dp", "mp"),
            P("mp", "dp"),
            P(),
            P(),
            P(),
            P("dp", None, "mp"),
            P("dp", "mp", None),
        ),
        check_vma=False,
    )
```

```python
import functools
import math

import jax
import jax.numpy as jnp
from jax import lax
from jax.experimental import pallas as pl
from jax.experimental.pallas import tpu as pltpu
from jax.sharding import PartitionSpec as P

eps = 1e-06
highest = lax.Precision.HIGHEST
f32, bf16 = jnp.float32, jnp.bfloat16
excluded = -1e30
reach = 512
tile = 128


def limit(mebibytes):
    return pltpu.CompilerParams(vmem_limit_bytes=mebibytes * 1024 * 1024)


brief = pl.CostEstimate(flops=10**7, bytes_accessed=10**4, transcendentals=0)
long = pl.CostEstimate(flops=2 * 10**10, bytes_accessed=10**7, transcendentals=0)


def normalize(values, gain):
    inverse = lax.rsqrt(jnp.mean(values * values, axis=-1, keepdims=True) + eps)
    return (values * inverse * gain, inverse)


def dot(left, right, left_dim, right_dim, precision=None):
    return lax.dot_general(
        left,
        right,
        (((left_dim,), (right_dim,)), ((), ())),
        precision=precision,
        preferred_element_type=f32,
    )


def swap(values, axis, step):
    count = lax.axis_size(axis)
    return lax.ppermute(values, axis, [(i, i ^ step) for i in range(count)])


def whole(dims):
    return pl.BlockSpec(tuple(dims), lambda *_: (0,) * len(dims), pipeline_mode=pl.Buffered(1))


def call(
    kernel, name, operands, outs, scratch=(), scalars=None, after=(), through=(), cost=None
):
    outs = list(outs)
    pairs = [o if isinstance(o, tuple) else (o, o.shape[0]) for o in operands]
    operands = [array for array, _ in pairs]
    in_specs = [whole((rows,) + array.shape[1:]) for array, rows in pairs]
    out_specs = [whole(o.shape) for o in outs]
    if scalars is not None:
        operands = [scalars] + operands
        in_specs = [pl.BlockSpec(memory_space=pltpu.SMEM)] + in_specs
    count, results = len(operands), len(outs)
    extra = list(through) + list(after)

    def body(*refs):
        rest = refs[count + len(extra) :]
        kernel(*refs[:count], *rest[:results], *rest[results + len(through) :])

    return pl.pallas_call(
        body,
        name=name,
        grid=(1,),
        in_specs=in_specs + [pl.BlockSpec(memory_space=pl.ANY)] * len(extra),
        out_specs=out_specs + [pl.BlockSpec(memory_space=pl.ANY)] * len(through),
        out_shape=outs + [shape(o.shape, o.dtype) for o in through],
        input_output_aliases={count + i: results + i for i in range(len(through))},
        scratch_shapes=list(scratch),
        compiler_params=limit(64),
        cost_estimate=cost or brief,
    )(*operands, *extra)


def shape(dims, dtype):
    return jax.ShapeDtypeStruct(tuple(dims), dtype)


def fill_skew(line_ref, skew, heads):
    window = reach + tile
    row = lax.broadcasted_iota(jnp.int32, (tile, window), 0)
    column = lax.broadcasted_iota(jnp.int32, (tile, window), 1)
    usable = (column - row <= reach) & (column - row >= 1)
    for head in range(heads):
        line = jnp.broadcast_to(line_ref[head : head + 1, :], (tile, window))
        rolled = pltpu.roll(line, 0, 1, stride=1, stride_axis=0)
        skew[head * tile : (head + 1) * tile, :] = jnp.where(usable, rolled, excluded)


def fill_window(source_ref, padded):
    padded[:reach, :] = jnp.zeros((reach, padded.shape[1]), bf16)
    padded[reach:, :] = source_ref[...]


def spread_heads(values, heads, scale):
    span = values.shape[1]
    size = span // heads
    lane = lax.broadcasted_iota(jnp.int32, (tile, span), 1)
    wide = values.astype(f32) * scale
    parts = [
        jnp.where((lane >= head * size) & (lane < (head + 1) * size), wide, 0.0)
        for head in range(heads)
    ]
    return jnp.concatenate(parts, axis=0).astype(bf16)


def collect_heads(stacked, heads):
    span = stacked.shape[1]
    size = span // heads
    lane = lax.broadcasted_iota(jnp.int32, (tile, span), 1)
    total = stacked[:tile, :]
    for head in range(1, heads):
        total = jnp.where(lane < head * size, total, stacked[head * tile : (head + 1) * tile, :])
    return total


def window_powers(q_all, keys, skew, seg_q_ref, seg_k_ref, start, heads):
    window = reach + tile
    seg_q = jnp.concatenate([seg_q_ref[pl.ds(start, tile), :]] * heads, axis=0)
    seg_k = seg_k_ref[:, pl.ds(start, window)]
    scores = dot(q_all, keys, 1, 1) + skew[...]
    scores = jnp.where(seg_q == seg_k, scores, excluded)
    powers = jnp.exp(scores - jnp.max(scores, axis=-1, keepdims=True))
    return powers, 1.0 / jnp.sum(powers, axis=-1, keepdims=True)


def attend_kernel(heads, place, q_ref, k_ref, v_ref, seg_q_ref, seg_k_ref, line_ref, *rest):
    *out_refs, mixed, k_pad, v_pad, skew = rest
    window = reach + tile
    scale = (q_ref.shape[1] // heads) ** (-0.5)
    fill_skew(line_ref, skew, heads)
    fill_window(k_ref, k_pad)
    fill_window(v_ref, v_pad)

    def step(index, carry):
        start = pl.multiple_of(index * tile, tile)
        q_all = spread_heads(q_ref[pl.ds(start, tile), :], heads, scale)
        powers, inverse = window_powers(
            q_all, k_pad[pl.ds(start, window), :], skew, seg_q_ref, seg_k_ref, start, heads
        )
        probs = (powers * inverse).astype(bf16)
        part = dot(probs, v_pad[pl.ds(start, window), :], 1, 0)
        mixed[pl.ds(start, tile), :] = collect_heads(part, heads).astype(bf16)
        return carry

    lax.fori_loop(0, q_ref.shape[0] // tile, step, 0)
    rows = out_refs[0].shape[0]
    for r, out_ref in enumerate(out_refs):
        out_ref[...] = mixed[pl.ds(pl.multiple_of((place[1] ^ r) * rows, rows), rows), :]


def attend(place, query, key_rows, value_rows, seg_q, seg_k, line, heads, members, after):
    seq_len, span = query.shape
    window = reach + tile

    def kernel(place_ref, *refs):
        attend_kernel(heads, place_ref, *refs)

    return call(
        kernel,
        "attend",
        [query, key_rows, value_rows, seg_q, seg_k, line],
        [shape((seq_len // members, span), bf16)] * members,
        scratch=[
            pltpu.VMEM((seq_len, span), bf16),
            pltpu.VMEM((seq_len + reach, span), bf16),
            pltpu.VMEM((seq_len + reach, span), bf16),
            pltpu.VMEM((heads * tile, window), f32),
        ],
        scalars=place,
        after=after,
    )


def attend_back_kernel(heads, members, place, *refs):
    q_ref, k_ref, v_ref, seg_q_ref, seg_k_ref, line_ref = refs[:6]
    g_refs = refs[6 : 6 + members]
    dq_ref, dk_ref, dv_ref, line_grad_ref = refs[6 + members : 10 + members]
    grad, k_pad, v_pad, skew, dk_sum, dv_sum, bias_sum = refs[10 + members :]
    window = reach + tile
    scale = (q_ref.shape[1] // heads) ** (-0.5)
    rows = g_refs[0].shape[0]
    fill_skew(line_ref, skew, heads)
    fill_window(k_ref, k_pad)
    fill_window(v_ref, v_pad)
    dk_sum[...] = jnp.zeros_like(dk_sum)
    dv_sum[...] = jnp.zeros_like(dv_sum)
    bias_sum[...] = jnp.zeros_like(bias_sum)
    for r, g_ref in enumerate(g_refs):
        grad[pl.ds(pl.multiple_of((place[1] ^ r) * rows, rows), rows), :] = g_ref[...]

    def step(index, carry):
        start = pl.multiple_of(index * tile, tile)
        keys = k_pad[pl.ds(start, window), :]
        values = v_pad[pl.ds(start, window), :]
        q_all = spread_heads(q_ref[pl.ds(start, tile), :], heads, scale)
        g_all = spread_heads(grad[pl.ds(start, tile), :], heads, 1.0)
        powers, inverse = window_powers(q_all, keys, skew, seg_q_ref, seg_k_ref, start, heads)
        probs = powers * inverse
        dot_grad = dot(g_all, values, 1, 1)
        inner = jnp.sum(probs * dot_grad, axis=-1, keepdims=True)
        score_grad = (probs * (dot_grad - inner)).astype(bf16)
        bias_sum[...] += score_grad.astype(f32)
        part = collect_heads(dot(score_grad, keys, 1, 0), heads) * scale
        dq_ref[pl.ds(start, tile), :] = part.astype(bf16)
        dk_sum[pl.ds(start, window), :] += dot(score_grad, q_all, 0, 0)
        dv_sum[pl.ds(start, window), :] += dot(probs.astype(bf16), g_all, 0, 0)
        return carry

    lax.fori_loop(0, q_ref.shape[0] // tile, step, 0)
    dk_ref[...] = dk_sum[reach:, :].astype(bf16)
    dv_ref[...] = dv_sum[reach:, :].astype(bf16)
    line_grad_ref[...] = jnp.zeros_like(line_grad_ref)
    row = lax.broadcasted_iota(jnp.int32, (tile, tile), 0)
    column = lax.broadcasted_iota(jnp.int32, (tile, tile), 1)
    mirror = (row + column == tile - 1).astype(f32)
    for head in range(heads):
        part = bias_sum[head * tile : (head + 1) * tile, :]
        turned = dot(mirror, part, 1, 0, highest)
        straight = pltpu.roll(turned, window - tile + 1, 1, stride=1, stride_axis=0)
        line_grad_ref[head : head + 1, :] = jnp.sum(straight, axis=0, keepdims=True)


def attend_back(place, query, key_rows, value_rows, seg_q, seg_k, line, grads, heads, after):
    seq_len, span = query.shape
    window = reach + tile

    def kernel(place_ref, *refs):
        attend_back_kernel(heads, len(grads), place_ref, *refs)

    return call(
        kernel,
        "attend_back",
        [query, key_rows, value_rows, seg_q, seg_k, line] + grads,
        [shape((seq_len, span), bf16)] * 3 + [shape((8, window), f32)],
        scratch=[
            pltpu.VMEM((seq_len, span), bf16),
            pltpu.VMEM((seq_len + reach, span), bf16),
            pltpu.VMEM((seq_len + reach, span), bf16),
            pltpu.VMEM((heads * tile, window), f32),
            pltpu.VMEM((seq_len + reach, span), f32),
            pltpu.VMEM((seq_len + reach, span), f32),
            pltpu.VMEM((heads * tile, window), f32),
        ],
        scalars=place,
        after=after,
    )


def pack_weights(w_query, w_key, w_value, w_output):
    part, span = w_query.shape

    def kernel(q_ref, k_ref, v_ref, o_ref, pack_ref):
        for at, ref in enumerate((q_ref, k_ref, v_ref)):
            pack_ref[:, at * span : (at + 1) * span] = ref[...]
        pack_ref[:, 3 * span :] = o_ref[...].astype(f32).T.astype(bf16)

    (pack,) = call(
        kernel, "pack_weights", [w_query, w_key, w_value, w_output], [shape((part, 4 * span), bf16)]
    )
    return pack


def pair_up(pack, far, after):
    part = pack.shape[0]

    def kernel(near_ref, far_ref, both_ref):
        both_ref[:part, :] = near_ref[...]
        both_ref[part:, :] = far_ref[...]

    (both,) = call(
        kernel, "pair_up", [pack, far], [shape((2 * part, pack.shape[1]), bf16)], after=after
    )
    return both


def project(place, token_blocks, pack_blocks, gain, cotangent, span, after):
    rows, width = token_blocks[0].shape
    members = len(token_blocks)
    seq_len = rows * members
    parts = sum(len(held) for _, held in pack_blocks)
    part = width // parts

    def kernel(place_ref, gain_ref, *refs):
        token_refs = refs[:members]
        pack_refs = refs[members : members + len(pack_blocks)]
        (normed_ref, q_ref, k_ref, v_ref, wq_ref, wk_ref, wv_ref, wo_ref, pack) = refs[
            members + len(pack_blocks) :
        ]
        for (_, held), ref in zip(pack_blocks, pack_refs):
            for i, r in enumerate(held):
                at = pl.multiple_of((place_ref[0] ^ r) * part, part) if parts > 1 else 0
                pack[pl.ds(at, part), :] = ref[i * part : (i + 1) * part, :]
        for at, ref in enumerate((wq_ref, wk_ref, wv_ref)):
            ref[...] = pack[:, at * span : (at + 1) * span]
        wo_ref[...] = pack[:, 3 * span :].astype(f32).T.astype(bf16)
        for r, ref in enumerate(token_refs):
            normed, _ = normalize(ref[...].astype(f32), gain_ref[...])
            normed = normed.astype(bf16)
            at = pl.ds(pl.multiple_of((place_ref[1] ^ r) * rows, rows), rows)
            normed_ref[at, :] = normed
            q_ref[at, :] = dot(normed, wq_ref[...], 1, 0).astype(bf16)
            k_ref[at, :] = dot(normed, wk_ref[...], 1, 0).astype(bf16)
            v_ref[at, :] = dot(normed, wv_ref[...], 1, 0).astype(bf16)

    return call(
        kernel,
        "project",
        [gain] + list(token_blocks) + [array for array, _ in pack_blocks],
        [shape((seq_len, width), bf16)]
        + [shape((seq_len, span), bf16)] * 3
        + [shape((width, span), bf16)] * 3
        + [shape((span, width), bf16)],
        scratch=[pltpu.VMEM((width, width), bf16)],
        scalars=place,
        through=[cotangent],
        after=after,
    )


def hot(slots_ref, first, count):
    tokens = slots_ref.shape[1]
    slot = lax.broadcasted_iota(jnp.int32, (count, tokens), 0) + first
    taken = (slot == slots_ref[0:1, :]) | (slot == slots_ref[1:2, :])
    return jnp.where(taken, 1.0, 0.0).astype(bf16)


def to_slots(name, sets, blocks, size, after=()):
    width = sets[0][0].shape[1]

    def kernel(*refs):
        out_refs = refs[2 * len(sets) :]
        for at in range(len(sets)):
            rows_ref, slots_ref = refs[2 * at], refs[2 * at + 1]
            for b, out_ref in enumerate(out_refs):
                part = dot(hot(slots_ref, b * size, size), rows_ref[...], 1, 0)
                out_ref[at * size : (at + 1) * size, :] = part.astype(bf16)

    operands = [item for pair in sets for item in pair]
    return call(
        kernel,
        name,
        operands,
        [shape((size * len(sets), width), bf16)] * blocks,
        after=after,
    )


def from_slots(name, blocks, slots, size, dtypes, after=(), through=(), cost=None):
    count, sets = len(blocks), len(slots)
    width = blocks[0].shape[1]
    rows = slots[0].shape[1]

    def kernel(*refs):
        block_refs, slot_refs, out_refs = refs[:count], refs[count : count + sets], refs[count + sets :]
        for at in range(sets):
            total = None
            for b, ref in enumerate(block_refs):
                held = ref[at * size : (at + 1) * size, :]
                part = dot(hot(slot_refs[at], b * size, size), held, 0, 0)
                total = part if total is None else total + part
            out_refs[at][...] = total.astype(out_refs[at].dtype)

    return call(
        kernel,
        name,
        list(blocks) + list(slots),
        [shape((rows, width), dtype) for dtype in dtypes],
        after=after,
        through=through,
        cost=cost,
    )


def router_softmax(values, w_router, experts):
    logits = dot(values, w_router, 1, 0)
    lane = lax.broadcasted_iota(jnp.int32, logits.shape, 1)
    logits = jnp.where(lane < experts, logits, excluded)
    powers = jnp.exp(logits - jnp.max(logits, axis=-1, keepdims=True))
    return powers / jnp.sum(powers, axis=-1, keepdims=True)


def middle(tokens, mixed, weight_o, gain, w_router, slots, experts, blocks, size, after):
    rows, width = tokens.shape
    members = len(mixed)

    def kernel(*refs):
        token_ref, gain_ref, router_ref, slots_ref = refs[:4]
        mixed_refs, weight_refs = refs[4 : 4 + members], refs[4 + members : 4 + 2 * members]
        hidden_ref, input_ref, probs_ref, *send_refs = refs[4 + 2 * members :]
        hidden = token_ref[...].astype(f32)
        for left, right in zip(mixed_refs, weight_refs):
            hidden = hidden + dot(left[...], right[...], 1, 0)
        hidden_ref[...] = hidden
        normed, _ = normalize(hidden, gain_ref[...])
        normed = normed.astype(bf16)
        input_ref[...] = normed
        for b, ref in enumerate(send_refs):
            ref[...] = dot(hot(slots_ref, b * size, size), normed, 1, 0).astype(bf16)
        probs_ref[...] = router_softmax(normed, router_ref[...], experts)

    return call(
        kernel,
        "middle",
        [tokens, gain, w_router, slots] + mixed + weight_o,
        [shape((rows, width), f32), shape((rows, width), bf16), shape((rows, 128), f32)]
        + [shape((size, width), bf16)] * blocks,
        after=after,
    )


def join_rows(refs):
    return jnp.concatenate([ref[...] for ref in refs], axis=0)


def experts_forward(place, w_in, w_out, w_router, x_blocks, experts, after):
    width, units = w_in.shape
    count, size = len(x_blocks), x_blocks[0].shape[0]
    total, piece, chunk = size * count, 768, 256

    def kernel(me_ref, w_in_ref, w_out_ref, router_ref, *refs):
        x_refs, refs = refs[:count], refs[count + len(after) :]
        active_ref, slope_ref, x_all, result_ref, gates_ref, gated_ref, result_sum = refs

        @pl.when(pl.program_id(0) == 0)
        def _():
            x_all[...] = jnp.concatenate([ref[...] for ref in x_refs], axis=0)
            probs = router_softmax(x_all[...], router_ref[...], experts)
            lane = lax.broadcasted_iota(jnp.int32, probs.shape, 1)
            own = jnp.sum(jnp.where(lane == me_ref[0], probs, 0.0), axis=1, keepdims=True)
            gates_ref[...] = jnp.broadcast_to(own, gates_ref.shape)
            result_sum[...] = jnp.zeros_like(result_sum)

        for c in range(piece // chunk):
            at = slice(c * chunk, (c + 1) * chunk)
            pre_act = dot(x_all[...], w_in_ref[:, at], 1, 0)
            below = 0.5 + 0.5 * lax.erf(pre_act * math.sqrt(0.5))
            bell = jnp.exp(-0.5 * pre_act * pre_act) * (1.0 / math.sqrt(2.0 * math.pi))
            active_ref[:, at] = (pre_act * below).astype(bf16)
            slope_ref[:, at] = (below + pre_act * bell).astype(bf16)
        result_sum[...] += dot(active_ref[...], w_out_ref[...], 1, 0)

        @pl.when(pl.program_id(0) == pl.num_programs(0) - 1)
        def _():
            result = result_sum[...].astype(bf16)
            result_ref[...] = result
            gated_ref[...] = (gates_ref[:, 0:1] * result.astype(f32)).astype(bf16)

    columns = pl.BlockSpec((total, piece), lambda i: (0, i))
    rows = shape((total, width), bf16)
    kept = [rows, rows, shape((total, 128), f32), rows]
    return pl.pallas_call(
        kernel,
        name="experts_forward",
        grid=(units // piece,),
        in_specs=[
            pl.BlockSpec(memory_space=pltpu.SMEM),
            pl.BlockSpec((width, piece), lambda i: (0, i)),
            pl.BlockSpec((piece, width), lambda i: (i, 0)),
            whole(w_router.shape),
        ]
        + [whole(o.shape) for o in x_blocks]
        + [pl.BlockSpec(memory_space=pl.ANY)] * len(after),
        out_specs=[columns] * 2 + [whole(o.shape) for o in kept],
        out_shape=[shape((total, units), bf16)] * 2 + kept,
        scratch_shapes=[pltpu.VMEM((total, width), f32)],
        compiler_params=limit(64),
        cost_estimate=long,
    )(place, w_in, w_out, w_router, *x_blocks, *after)


def experts_backward(place, w_in, w_out, slope, result, gates, g_blocks, size):
    width, units = w_in.shape
    total, piece, chunk = slope.shape[0], 768, 256
    count = len(g_blocks)

    def kernel(me_ref, w_in_ref, w_out_ref, slope_ref, result_ref, gates_ref, *refs):
        g_refs, back_refs = refs[:count], refs[count : 2 * count]
        pre_grad_ref, s_all, back_sum = refs[2 * count :]

        @pl.when(pl.program_id(0) == 0)
        def _():
            back_sum[...] = jnp.zeros_like(back_sum)
            for b, ref in enumerate(g_refs):
                rows = slice(b * size, (b + 1) * size)
                s_all[rows, :] = (gates_ref[rows, 0:1] * ref[...].astype(f32)).astype(bf16)

        for c in range(piece // chunk):
            at = slice(c * chunk, (c + 1) * chunk)
            active_grad = dot(s_all[...], w_out_ref[at, :], 1, 1)
            pre_grad_ref[:, at] = (active_grad * slope_ref[:, at].astype(f32)).astype(bf16)
        back_sum[...] += dot(pre_grad_ref[...], w_in_ref[...], 1, 1)

        @pl.when(pl.program_id(0) == pl.num_programs(0) - 1)
        def _():
            lane = lax.broadcasted_iota(jnp.int32, (size, 128), 1)
            for b, (ref, g_ref) in enumerate(zip(back_refs, g_refs)):
                rows = slice(b * size, (b + 1) * size)
                products = g_ref[...].astype(f32) * result_ref[rows, :].astype(f32)
                gate_grad = jnp.sum(products, axis=1, keepdims=True)
                upper = gate_grad.astype(bf16).astype(f32)
                ref[:, :width] = back_sum[rows, :].astype(bf16)
                ref[:, width:] = jnp.where(
                    lane == me_ref[0],
                    upper,
                    jnp.where(lane == me_ref[0] + 64, gate_grad - upper, 0.0),
                ).astype(bf16)

    by_units = pl.BlockSpec((total, piece), lambda i: (0, i))
    outs = [shape((size, width + 128), bf16)] * count
    flat = pl.pallas_call(
        kernel,
        name="experts_backward",
        grid=(units // piece,),
        in_specs=[
            pl.BlockSpec(memory_space=pltpu.SMEM),
            pl.BlockSpec((width, piece), lambda i: (0, i)),
            pl.BlockSpec((piece, width), lambda i: (i, 0)),
            by_units,
            whole(result.shape),
            whole(gates.shape),
        ]
        + [whole((size, width))] * count,
        out_specs=[whole(o.shape) for o in outs] + [by_units, whole((total, width))],
        out_shape=outs + [shape((total, units), bf16), shape((total, width), bf16)],
        scratch_shapes=[pltpu.VMEM((total, width), f32)],
        compiler_params=limit(64),
        cost_estimate=long,
    )(place, w_in, w_out, slope, result, gates, *g_blocks)
    return list(flat[:count]), flat[count], flat[count + 1]


def run_experts(
    name, place, w_in, w_out, w_router, x_blocks, g_blocks, at_set, before, cost, after
):
    width, units = w_in.shape
    count, size = len(x_blocks), x_blocks[0].shape[0]
    total, piece, chunk = size * count, 512, 256
    experts = before[0]
    held = list(before[1:])
    sets = g_blocks[0].shape[0] // size
    last = at_set == sets - 1

    def kernel(me_ref, w_in_ref, w_out_ref, router_ref, *refs):
        x_refs, refs = refs[:count], refs[count:]
        g_refs, refs = refs[:count], refs[count:]
        held_refs, refs = refs[: len(held)], refs[len(held) + len(after) :]
        back_refs, refs = refs[:count], refs[count:]
        result_refs, refs = refs[:count] if last else refs[:1], refs[count if last else 1 :]
        active_ref, pre_grad_ref, x_all, s_all, gates, result_sum, back_sum = refs

        @pl.when(pl.program_id(0) == 0)
        def _():
            for b in range(count):
                rows = slice(b * size, (b + 1) * size)
                x_all[rows, :] = x_refs[b][...]
            probs = router_softmax(x_all[...], router_ref[...], experts)
            lane = lax.broadcasted_iota(jnp.int32, probs.shape, 1)
            own = jnp.sum(jnp.where(lane == me_ref[0], probs, 0.0), axis=1, keepdims=True)
            gates[...] = jnp.broadcast_to(own, gates.shape)
            for b in range(count):
                rows = slice(b * size, (b + 1) * size)
                grad = g_refs[b][at_set * size : (at_set + 1) * size, :].astype(f32)
                s_all[rows, :] = (gates[rows, 0:1] * grad).astype(bf16)
            result_sum[...] = jnp.zeros_like(result_sum)
            back_sum[...] = jnp.zeros_like(back_sum)

        for c in range(piece // chunk):
            at = slice(c * chunk, (c + 1) * chunk)
            pre_act = dot(x_all[...], w_in_ref[:, at], 1, 0)
            active_grad = dot(s_all[...], w_out_ref[at, :], 1, 1)
            below = 0.5 + 0.5 * lax.erf(pre_act * math.sqrt(0.5))
            bell = jnp.exp(-0.5 * pre_act * pre_act) * (1.0 / math.sqrt(2.0 * math.pi))
            active_ref[:, at] = (pre_act * below).astype(bf16)
            pre_grad_ref[:, at] = (active_grad * (below + pre_act * bell)).astype(bf16)
        result_sum[...] += dot(active_ref[...], w_out_ref[...], 1, 0)
        back_sum[...] += dot(pre_grad_ref[...], w_in_ref[...], 1, 1)

        @pl.when(pl.program_id(0) == pl.num_programs(0) - 1)
        def _():
            lane = lax.broadcasted_iota(jnp.int32, (size, 128), 1)
            for b, (ref, g_ref) in enumerate(zip(back_refs, g_refs)):
                rows = slice(b * size, (b + 1) * size)
                result = result_sum[rows, :].astype(bf16).astype(f32)
                grad = g_ref[at_set * size : (at_set + 1) * size, :].astype(f32)
                gate_grad = jnp.sum(grad * result, axis=1, keepdims=True)
                upper = gate_grad.astype(bf16).astype(f32)
                ref[:, :width] = back_sum[rows, :].astype(bf16)
                ref[:, width:] = jnp.where(
                    lane == me_ref[0],
                    upper,
                    jnp.where(lane == me_ref[0] + 64, gate_grad - upper, 0.0),
                ).astype(bf16)
                gated = (gates[rows, 0:1] * result).astype(bf16)
                if last:
                    for at, other in enumerate(held_refs):
                        result_refs[b][at * size : (at + 1) * size, :] = other[rows, :]
                    result_refs[b][at_set * size : (at_set + 1) * size, :] = gated
                else:
                    result_refs[0][rows, :] = gated

    columns = pl.BlockSpec((total, piece), lambda i: (0, i))
    outs = [shape((size, width + 128), bf16)] * count
    results = [shape((size * sets, width), bf16)] * count if last else [shape((total, width), bf16)]
    rows_out = [shape((total, width), bf16)] * 2
    flat = pl.pallas_call(
        kernel,
        name=name,
        grid=(units // piece,),
        in_specs=[
            pl.BlockSpec(memory_space=pltpu.SMEM),
            pl.BlockSpec((width, piece), lambda i: (0, i)),
            pl.BlockSpec((piece, width), lambda i: (i, 0)),
            whole(w_router.shape),
        ]
        + [whole(o.shape) for o in list(x_blocks) + list(g_blocks) + held]
        + [pl.BlockSpec(memory_space=pl.ANY)] * len(after),
        out_specs=[whole(o.shape) for o in outs + results]
        + [columns] * 2
        + [whole(o.shape) for o in rows_out],
        out_shape=outs + results + [shape((total, units), bf16)] * 2 + rows_out,
        scratch_shapes=[
            pltpu.VMEM((total, 128), f32),
            pltpu.VMEM((total, width), f32),
            pltpu.VMEM((total, width), f32),
        ],
        compiler_params=limit(64),
        cost_estimate=cost,
    )(place, w_in, w_out, w_router, *x_blocks, *g_blocks, *held, *after)
    return list(flat[:count]), list(flat[count:-4]), flat[-4:]


def home(
    own_back,
    far_sum,
    slots,
    hidden,
    probs,
    cotangent,
    gain,
    w_router,
    ffn_input,
    weight_o,
    mixed,
    size,
    experts,
    after,
    through,
):
    rows, width = hidden.shape
    count, members = len(own_back), len(weight_o)
    span = weight_o[0].shape[0]
    far = [] if far_sum is None else [far_sum]

    def kernel(*refs):
        slots_ref, hidden_ref, probs_ref, cot_ref, gain_ref, router_ref, input_ref = refs[:7]
        refs = refs[7:]
        back_refs, refs = refs[:count], refs[count:]
        far_refs, refs = refs[: len(far)], refs[len(far) :]
        weight_refs, mixed_refs, refs = refs[:members], refs[members : 2 * members], refs[2 * members :]
        grad_refs = refs[:members]
        hidden_grad_ref, gain_grad_ref, router_grad_ref, near_ref, base_ref = refs[members:]
        total = None
        for b, ref in enumerate(back_refs):
            part = dot(hot(slots_ref, b * size, size), ref[...], 0, 0)
            total = part if total is None else total + part
        for ref in far_refs:
            total = total + ref[...].astype(f32)
        columns = total[:, width:]
        lane = lax.broadcasted_iota(jnp.int32, columns.shape, 1)
        prob_grad = jnp.where(lane < 64, columns + pltpu.roll(columns, 64, 1), 0.0)
        router_probs = probs_ref[...]
        logit_grad = router_probs * (
            prob_grad - jnp.sum(router_probs * prob_grad, axis=-1, keepdims=True)
        )
        router_grad_ref[...] = dot(logit_grad, input_ref[...].astype(f32), 0, 0, highest)[:experts, :]
        grad = total[:, :width] + dot(logit_grad, router_ref[...].astype(f32), 1, 1, highest)
        hidden_now = hidden_ref[...]
        inverse = lax.rsqrt(jnp.mean(hidden_now * hidden_now, axis=-1, keepdims=True) + eps)
        scaled = grad * gain_ref[...]
        gain_grad_ref[...] = jnp.sum(grad * hidden_now * inverse, axis=0, keepdims=True)
        inner = jnp.mean(scaled * hidden_now, axis=-1, keepdims=True)
        hidden_grad = (
            cot_ref[...].astype(f32)
            + inverse * scaled
            - hidden_now * inverse * inverse * inverse * inner
        )
        hidden_grad_ref[...] = hidden_grad
        attn_grad = hidden_grad.astype(bf16)
        for ref, weight in zip(grad_refs, weight_refs):
            ref[...] = dot(attn_grad, weight[...], 1, 1).astype(bf16)
        for r, (ref, first) in enumerate(
            ((base_ref, 0), (near_ref, 0), (base_ref, span), (near_ref, span))
        ):
            part = dot(mixed_refs[r][...], attn_grad, 0, 0)
            ref[first : first + span, :] = part.astype(ref.dtype)

    return call(
        kernel,
        "home",
        [slots, hidden, probs, cotangent, gain, w_router, ffn_input]
        + list(own_back)
        + far
        + weight_o
        + mixed,
        [shape((rows, span), bf16)] * members
        + [
            shape((rows, width), f32),
            shape((1, width), f32),
            shape((experts, width), f32),
            shape((2 * span, width), bf16),
            shape((2 * span, width), f32),
        ],
        after=after,
        through=through,
    )


def expert_weight_grads(place, rows_in, pre_grads, actives, slot_grads, members):
    sets = len(rows_in)
    total, width = rows_in[0].shape
    piece = pre_grads[0].shape[1] // members

    def kernel(place_ref, *refs):
        x_refs, p_refs, a_refs, s_refs = [refs[i * sets : (i + 1) * sets] for i in range(4)]
        near_ref, base_ref, out = refs[4 * sets :]
        step = pl.program_id(0)

        def total_of(lefts, rights):
            held = dot(lefts[0][...], rights[0][...], 0, 0)
            for left, right in zip(lefts[1:], rights[1:]):
                held = held + dot(left[...], right[...], 0, 0)
            return held

        @pl.when(step < 4)
        def _():
            out[...] = total_of(x_refs, p_refs)

        @pl.when(step >= 4)
        def _():
            out[...] = total_of(a_refs, s_refs)

        @pl.when(step % 4 < 2)
        def _():
            near_ref[...] = out[...].astype(bf16)

        @pl.when(step % 4 >= 2)
        def _():
            base_ref[...] = out[...]

    def partner(i):
        return jnp.where(i < 2, 2 * i + 1, 2 * i - 4)

    fixed = pl.BlockSpec((total, width), lambda i, p: (0, 0))
    pre_cut = pl.BlockSpec((total, piece), lambda i, p: (0, p[1] ^ partner(jnp.minimum(i, 3))))
    act_cut = pl.BlockSpec((total, piece), lambda i, p: (0, p[1] ^ partner(jnp.maximum(i - 4, 0))))
    return pl.pallas_call(
        kernel,
        name="expert_weight_grads",
        grid_spec=pltpu.PrefetchScalarGridSpec(
            num_scalar_prefetch=1,
            grid=(8,),
            in_specs=[fixed] * sets + [pre_cut] * sets + [act_cut] * sets + [fixed] * sets,
            out_specs=[
                pl.BlockSpec(
                    (piece, width), lambda i, p: (2 * (i // 4) + jnp.minimum(i % 4, 1), 0)
                ),
                pl.BlockSpec(
                    (piece, width), lambda i, p: (2 * (i // 4) + jnp.maximum(i % 4 - 2, 0), 0)
                ),
            ],
            scratch_shapes=[pltpu.VMEM((piece, width), f32)],
        ),
        out_shape=[shape((4 * piece, width), bf16), shape((4 * piece, width), f32)],
        compiler_params=limit(64),
        cost_estimate=long,
    )(place, *rows_in, *pre_grads, *actives, *slot_grads)


def far_sums(near, base, near_o, base_o, cuts, after):
    size, width = base.shape[0] // 4, base.shape[1]
    span = near_o.shape[0] // 2

    def block(rows, at):
        return pl.BlockSpec((rows, width), lambda *_: (at, 0), pipeline_mode=pl.Buffered(1))

    def kernel(near_in, near_out, base_in, base_out, near_o_ref, base_o_ref, *refs):
        out_refs = refs[len(after) :]
        out_refs[0][:span, :] = (base_o_ref[...] + near_o_ref[...].astype(f32)).astype(bf16)
        starts = [0] + cuts
        for i, ref in enumerate(out_refs):
            low, high = starts[i], starts[i + 1]
            at = span if i == 0 else 0
            for near_ref, base_ref, shift in ((near_in, base_in, 0), (near_out, base_out, size)):
                first, last = max(low, shift), min(high, shift + size)
                if first < last:
                    rows = slice(first - shift, last - shift)
                    held = base_ref[rows, :] + near_ref[rows, :].astype(f32)
                    ref[at + first - low : at + last - low, :] = held.astype(bf16)

    rows = [high - low for low, high in zip([0] + cuts, cuts)]
    rows[0] = rows[0] + span
    return pl.pallas_call(
        kernel,
        name="far_sums",
        grid=(1,),
        in_specs=[block(size, 1), block(size, 3), block(size, 1), block(size, 3)]
        + [block(span, 1), block(span, 1)]
        + [pl.BlockSpec(memory_space=pl.ANY)] * len(after),
        out_specs=[whole((count, width)) for count in rows],
        out_shape=[shape((count, width), bf16) for count in rows],
        compiler_params=limit(64),
        cost_estimate=brief,
    )(near, near, base, base, near_o, base_o, *after)


def input_grads(
    place,
    proj_grads,
    normed,
    weights,
    output_parts,
    gain,
    line_grad,
    bucket_hot,
    ffn_gain_grad,
    router_grad,
    members,
    owners,
    heads,
    buckets_all,
    after,
):
    seq_len, width = normed.shape
    span = weights[0].shape[1]
    rows = seq_len // members
    part = width // owners
    few = owners == 8
    experts = router_grad.shape[0]
    extra = -(-(3 + experts) // 16) * 16

    def kernel(place_ref, *refs):
        dq_ref, dk_ref, dv_ref, normed_ref, wq_ref, wk_ref, wv_ref, gain_ref = refs[:8]
        line_ref, hot_ref, ffn_gain_ref, router_ref = refs[8:12]
        base_o_ref, near_o_ref, far_o_ref = refs[12:15]
        near_ref, base_ref, far_ref, small_ref, *weight_refs, sums = refs[15:]
        for at, ref in enumerate((dq_ref, dk_ref, dv_ref)):
            sums[:, at * span : (at + 1) * span] = dot(normed_ref[...], ref[...], 0, 0)
        output_sum = base_o_ref[...] + near_o_ref[...].astype(f32) + far_o_ref[...].astype(f32)
        sums[:, 3 * span :] = output_sum.T
        if few:
            for r, ref in enumerate(weight_refs):
                for i, far in enumerate((0, 4)):
                    at = pl.multiple_of((place_ref[0] ^ r ^ far) * part, part)
                    ref[i * part : (i + 1) * part, :] = sums[pl.ds(at, part), :].astype(ref.dtype)
        else:
            weight_refs[0][...] = sums[...]
        gain_grad = jnp.zeros((1, width), f32)
        for r, (ref, first) in enumerate(
            ((base_ref, 0), (near_ref, 0), (far_ref, 0), (near_ref, rows))
        ):
            at = pl.ds(pl.multiple_of((place_ref[1] ^ r) * rows, rows), rows)
            grad = (
                dot(dq_ref[at, :], wq_ref[...], 1, 1)
                + dot(dk_ref[at, :], wk_ref[...], 1, 1)
                + dot(dv_ref[at, :], wv_ref[...], 1, 1)
            )
            gain_grad = gain_grad + jnp.sum(
                grad * normed_ref[at, :].astype(f32), axis=0, keepdims=True
            )
            ref[first : first + rows, :] = grad.astype(ref.dtype)
        table = dot(line_ref[...], hot_ref[...], 1, 0, highest)
        bucket = lax.broadcasted_iota(jnp.int32, (128, width), 0)
        lane = lax.broadcasted_iota(jnp.int32, (128, width), 1)
        flat = jnp.zeros((1, width), f32)
        for head in range(heads):
            first = (place_ref[1] * heads + head) * buckets_all
            spread = jnp.where((bucket < buckets_all) & (lane == bucket + first), 1.0, 0.0)
            flat = flat + dot(table[head : head + 1, :], spread, 1, 0, highest)
        small_ref[...] = jnp.zeros_like(small_ref)
        small_ref[0:1, :] = gain_grad / gain_ref[...]
        small_ref[1:2, :] = ffn_gain_ref[...]
        small_ref[2:3, :] = flat
        small_ref[3 : 3 + experts, :] = router_ref[...]
        if few:
            upper, lower = two_halves(small_ref[...])
            small_ref[...] = upper.astype(f32) + lower.astype(f32)
            for ref in weight_refs[1:]:
                ref[2 * part : 2 * part + extra, :] = upper
                ref[2 * part + extra :, :] = lower

    if few:
        weight_outs = [shape((2 * part, 4 * span), f32)]
        weight_outs += [shape((2 * part + 2 * extra, 4 * span), bf16)] * 3
    else:
        weight_outs = [shape((width, 4 * span), f32)]
    return call(
        kernel,
        "input_grads",
        list(proj_grads)
        + [normed]
        + list(weights)
        + [gain, line_grad, bucket_hot, ffn_gain_grad, router_grad]
        + [(part, span) for part in output_parts],
        [
            shape((2 * rows, width), bf16),
            shape((rows, width), f32),
            shape((rows, width), f32),
            shape((extra, width), f32),
        ]
        + weight_outs,
        scratch=[pltpu.VMEM((width, 4 * span), f32)],
        scalars=place,
        after=after,
    )


def add_up(base, near, parts, after):
    size, width = base.shape[0] // 4, base.shape[1]

    def kernel(in_base, in_near, out_base, out_near, *refs):
        part_refs, (in_ref, out_ref) = refs[: len(parts)], refs[-2:]
        first = 0
        for (array, at), ref in zip(parts[:-1], part_refs[:-1]):
            rows = slice(first, first + array.shape[0] - at)
            total = in_base[rows, :] + in_near[rows, :].astype(f32)
            in_ref[rows, :] = total + ref[at:, :].astype(f32)
            first = first + array.shape[0] - at
        total = out_base[...] + out_near[...].astype(f32)
        out_ref[...] = total + part_refs[-1][...].astype(f32)

    def block(at):
        return pl.BlockSpec((size, width), lambda *_: (at, 0), pipeline_mode=pl.Buffered(1))

    specs = [block(0), block(0), block(2), block(2)] + [whole(o.shape) for o, _ in parts]
    return pl.pallas_call(
        kernel,
        name="add_up",
        grid=(1,),
        in_specs=specs + [pl.BlockSpec(memory_space=pl.ANY)] * len(after),
        out_specs=[whole((size, width))] * 2,
        out_shape=[shape((size, width), f32)] * 2,
        compiler_params=limit(64),
        cost_estimate=long,
    )(base, near, base, near, *[array for array, _ in parts], *after)


def two_halves(values):
    upper = values.astype(bf16)
    return upper, (values - upper.astype(f32)).astype(bf16)


def fold_weights(base, arrived, small, after):
    part, width, extra = base.shape[0] // 2, base.shape[1], small.shape[0]

    def kernel(base_ref, one_ref, two_ref, three_ref, small_ref, own_ref, far_ref, half_ref):
        refs = (one_ref, two_ref, three_ref)
        total = base_ref[...]
        for ref in refs:
            total = total + ref[: 2 * part, :].astype(f32)
        own_ref[...] = total[:part, :]
        far_ref[:part, :] = total[part:, :].astype(bf16)
        one, two, three = [
            ref[2 * part : 2 * part + extra, :].astype(f32)
            + ref[2 * part + extra :, :].astype(f32)
            for ref in refs
        ]
        upper, lower = two_halves((small_ref[...] + one) + (two + three))
        far_ref[part : part + extra, :] = upper
        far_ref[part + extra :, :] = lower
        half_ref[...] = upper.astype(f32) + lower.astype(f32)

    return call(
        kernel,
        "fold_weights",
        [base] + arrived + [small],
        [
            shape((part, width), f32),
            shape((part + 2 * extra, width), bf16),
            shape((extra, width), f32),
        ],
        after=after,
    )


def split_weights(own, far, small, span, after):
    part, extra = own.shape[0], small.shape[0]

    def kernel(*refs):
        own_ref, small_ref, *far_refs = refs[:-5]
        q_ref, k_ref, v_ref, o_ref, sum_ref = refs[-5:]
        total, sums = own_ref[...], small_ref[...]
        for ref in far_refs:
            total = total + ref[:part, :].astype(f32)
            sums = sums + (
                ref[part : part + extra, :].astype(f32) + ref[part + extra :, :].astype(f32)
            )
        for at, ref in enumerate((q_ref, k_ref, v_ref)):
            ref[...] = total[:, at * span : (at + 1) * span]
        o_ref[...] = total[:, 3 * span :].T
        sum_ref[...] = sums

    return call(
        kernel,
        "split_weights",
        [own, small] + ([] if far is None else [far]),
        [shape((part, span), f32)] * 3
        + [shape((span, part), f32), shape((extra, own.shape[1]), f32)],
        after=after,
    )


def gather_mp(values):
    across = swap(values, "mp", 2)
    return [values, swap(values, "mp", 1), across, swap(across, "mp", 1)]


def sum_over(values, axis):
    step = 1
    while step < lax.axis_size(axis):
        values = values + swap(values, axis, step)
        step = 2 * step
    return values


def all_to_all_dp(values):
    return lax.all_to_all(values, "dp", split_axis=0, concat_axis=0, tiled=True)


def slots_of(routes, place, capacity, experts, limit):
    rows = routes.shape[0]
    expert_ids = jnp.arange(experts, dtype=jnp.int32)[None, :]
    hits = (routes[:, 0:1] == expert_ids) | (routes[:, 1:2] == expert_ids)
    earlier = jnp.arange(rows)[:, None] > jnp.arange(rows)[None, :]
    ranks = jnp.dot(earlier.astype(bf16), hits.astype(bf16), preferred_element_type=f32)
    lines = []
    for k in (0, 1):
        rank = jnp.sum(jnp.where(routes[:, k : k + 1] == expert_ids, ranks, 0.0), axis=1)
        block = routes[:, k] ^ place
        lines.append(jnp.where(block < limit, block * capacity + rank.astype(jnp.int32), -1))
    return jnp.pad(jnp.stack(lines), ((0, 6), (0, 0)), constant_values=-1)


def on_device(
    tokens,
    norm_gain,
    w_query,
    w_key,
    w_value,
    w_output,
    bias_table,
    ffn_gain,
    w_router,
    w_in,
    w_out,
    segments,
    buckets,
    routes,
    cotangent,
):
    rows, width = tokens.shape
    heads = bias_table.shape[1]
    seq_len = buckets.shape[0]
    experts = w_router.shape[1]
    owners, members = lax.axis_size("dp"), lax.axis_size("mp")
    me, member = lax.axis_index("dp"), lax.axis_index("mp")
    place = jnp.stack([me, member]).astype(jnp.int32)
    capacity = 4 * rows // experts
    span = w_query.shape[1]
    window = reach + tile
    few = owners == 8

    token_blocks = gather_mp(tokens)
    pack = pack_weights(w_query, w_key, w_value, w_output)
    if few:
        both = pair_up(pack, swap(pack, "dp", 4), token_blocks[1:3])
        pack_blocks = [(both, (0, 4))] + [(swap(both, "dp", r), (r, r ^ 4)) for r in (1, 2, 3)]
    else:
        pack_blocks = [(lax.all_gather(pack, "dp", axis=0, tiled=True), (0,))]
    gain_one, gain_two = norm_gain.reshape(1, width), ffn_gain.reshape(1, width)
    if few:
        blocks, size = 4, capacity
        slots = [slots_of(routes, me, capacity, experts, 4)]
        slots.append(slots_of(swap(routes, "dp", 4), me, capacity, experts, 4))
    else:
        blocks, size = 1, experts * capacity
        slots = [slots_of(routes, 0, capacity, experts, experts)]

    line_buckets = jnp.pad(jnp.flip(buckets[: reach + 1]), (0, window - reach - 1))
    bucket_hot = (
        line_buckets[:, None] == jnp.arange(128, dtype=jnp.int32)[None, :]
    ).astype(f32)
    buckets_all = bias_table.shape[0]
    table = jnp.pad(bias_table.T, ((0, 8 - heads), (0, 128 - buckets_all)))
    line = jnp.dot(table, bucket_hot.T, precision=highest)
    seg_q = segments.reshape(seq_len, 1)
    seg_k = jnp.pad(segments.reshape(1, seq_len), ((0, 0), (reach, 0)), constant_values=-1)
    router_wide = jnp.pad(w_router, ((0, 0), (0, 128 - experts)))
    ready = slots[:1] + [seg_q, seg_k, router_wide, gain_two]
    normed, query, key_rows, value_rows, weight_q, weight_k, weight_v, w_o, late_cotangent = (
        project(place, token_blocks, pack_blocks, gain_one, cotangent, span, ready)
    )


    if few:
        far_cotangent = swap(late_cotangent, "dp", 4)

    mixed_out = attend(
        place, query, key_rows, value_rows, seg_q, seg_k, line, heads, members, [bucket_hot]
    )
    weight_o = gather_mp(w_o)
    mixed_in = [mixed_out[0]] + [swap(mixed_out[r], "mp", r) for r in range(1, members)]

    hidden, ffn_input, router_probs, *send = middle(
        tokens,
        mixed_in,
        weight_o,
        gain_two,
        router_wide,
        slots[0],
        experts,
        blocks,
        size,
        [far_cotangent] if few else [],
    )
    if few:
        held = to_slots(
            "grads_to_slots",
            [(cotangent, slots[0]), (far_cotangent, slots[1])],
            blocks,
            size,
            after=[ffn_input],
        )
        g_blocks = [held[0]] + [swap(held[r], "dp", r) for r in (1, 2, 3)]
        far_input = swap(ffn_input, "dp", 4)
        own = [send[0]] + [swap(send[r], "dp", r) for r in (1, 2, 3)]
        far = to_slots(
            "far_to_slots", [(far_input, slots[1])], blocks, size, after=g_blocks[1:3]
        )
        far = [far[0]] + [swap(far[r], "dp", r) for r in (1, 2, 3)]
        x_sets = [own, far]
    else:
        held = to_slots("grads_to_slots", [(cotangent, slots[0])], blocks, size)
        g_blocks = [all_to_all_dp(held[0])]
        x_sets = [[all_to_all_dp(send[0])]]

    before = [experts]
    if few:
        active, slope, rows_in, plain, slot_gates, gated = experts_forward(
            place, w_in[0], w_out[0], router_wide, x_sets[0], experts, far[:1]
        )
        before = before + [gated]
    back, result, state = run_experts(
        "run_experts",
        place,
        w_in[0],
        w_out[0],
        router_wide,
        x_sets[-1],
        g_blocks,
        len(x_sets) - 1,
        before,
        brief,
        [],
    )
    kept, backs = [state], [back]
    if few:
        back, pre_grad, slot_grad = experts_backward(
            place, w_in[0], w_out[0], slope, plain, slot_gates, g_blocks, size
        )
        kept = [(active, pre_grad, rows_in, slot_grad)] + kept
        backs = [back] + backs
    actives, pre_grads, arrived, slot_grads = zip(*kept)
    if few:
        own_back, far_back = backs
        far_back = [far_back[0]] + [swap(far_back[r], "dp", r) for r in (1, 2, 3)]
        far_total, *passed = from_slots(
            "back_from_slots", far_back, [slots[1]], size, [bf16], through=own_back[1:]
        )
        far_sum = swap(far_total, "dp", 4)
        own_back = [own_back[0]] + [swap(passed[r - 1], "dp", r) for r in (1, 2, 3)]
        result_in = [result[0]] + [swap(result[r], "dp", r) for r in (1, 2, 3)]
    else:
        own_back, far_sum = [all_to_all_dp(backs[0][0])], None
        result_in = [all_to_all_dp(result[0])]
    near_w, base_w = expert_weight_grads(place, arrived, pre_grads, actives, slot_grads, members)

    homed = home(
        own_back,
        far_sum,
        slots[0],
        hidden,
        router_probs,
        cotangent,
        gain_two,
        router_wide,
        ffn_input,
        weight_o,
        mixed_in,
        size,
        experts,
        [],
        [near_w],
    )
    grad_out, homed = homed[:members], homed[members:]
    hidden_grad, ffn_gain_grad, router_grad, near_o, base_o, near_w = homed
    grad_in = [grad_out[0]] + [swap(grad_out[r], "mp", r) for r in range(1, members)]
    near_o, near_w = swap(near_o, "mp", 1), swap(near_w, "mp", 1)
    piece = w_in.shape[2] // members
    far_first, far_next, far_last = far_sums(
        near_w, base_w, near_o, base_o, [rows, piece, 2 * piece], grad_in[2:]
    )

    *proj_grads, line_grad = attend_back(
        place,
        query,
        key_rows,
        value_rows,
        seg_q,
        seg_k,
        line,
        grad_in,
        heads,
        [far_first],
    )
    far_first = swap(far_first, "mp", 2)
    far_next = swap(far_next, "mp", 2)
    far_last = swap(far_last, "mp", 2)
    near, base, base_far, small, *weight_sums = input_grads(
        place,
        proj_grads,
        normed,
        (weight_q, weight_k, weight_v),
        (base_o, near_o, far_first),
        gain_one,
        line_grad,
        bucket_hot,
        ffn_gain_grad,
        router_grad,
        members,
        owners,
        heads,
        buckets_all,
        result_in[1:],
    )
    far_parts = [(far_first, span), (far_next, 0), (far_last, 0)]
    near = swap(near, "mp", 1)
    far_normed = swap((base_far + near[rows:].astype(f32)).astype(bf16), "mp", 2)
    if few:
        arrived_sums = [swap(weight_sums[r], "dp", r) for r in (1, 2, 3)]
        own_sum, far_part, small = fold_weights(
            weight_sums[0], arrived_sums, small, [near]
        )
        own_result, far_result = from_slots(
            "result_from_slots", result_in, slots, size, [f32, bf16], after=[own_sum]
        )
        far_result = swap(far_result, "dp", 4)
        w_in_grad, w_out_grad = add_up(base_w, near_w, far_parts, [own_result])
        *weight_grads, small = split_weights(
            own_sum, swap(far_part, "dp", 4), small, span, [w_in_grad, far_normed]
        )
    else:
        joined_grad = lax.psum_scatter(weight_sums[0], "dp", scatter_dimension=0, tiled=True)
        *weight_grads, small = split_weights(
            joined_grad, None, sum_over(small, "dp"), span, []
        )
        (own_result,) = from_slots("result_from_slots", result_in, slots, size, [f32])
        w_in_grad, w_out_grad = add_up(base_w, near_w, far_parts, [])
    small = sum_over(small, "mp")
    normed_grad = base + near[:rows].astype(f32) + far_normed.astype(f32)
    resid = tokens.astype(f32)
    _, inverse_one = normalize(resid, norm_gain)
    scaled = normed_grad * norm_gain
    inner = jnp.mean(scaled * resid, axis=-1, keepdims=True)
    tokens_grad = (
        hidden_grad + inverse_one * scaled - resid * inverse_one * inverse_one * inverse_one * inner
    ).astype(bf16)

    block_out = hidden + own_result
    if few:
        block_out = block_out + far_result.astype(f32)
    block_out = block_out.astype(bf16)
    return (
        block_out,
        tokens_grad,
        small[0],
        *weight_grads,
        small[2, : heads * members * buckets_all].reshape(heads * members, buckets_all).T,
        small[1],
        small[3 : 3 + experts].T,
        w_in_grad[None],
        w_out_grad[None],
    )


def solution(mesh):
    return jax.shard_map(
        on_device,
        mesh=mesh,
        in_specs=(
            P(("dp", "mp"), None),
            P(),
            P("dp", "mp"),
            P("dp", "mp"),
            P("dp", "mp"),
            P("mp", "dp"),
            P(None, "mp"),
            P(),
            P(),
            P("dp", None, None),
            P("dp", None, None),
            P("dp", None),
            P(),
            P(("dp", "mp"), None),
            P(("dp", "mp"), None),
        ),
        out_specs=(
            P(("dp", "mp"), None),
            P(("dp", "mp"), None),
            P(),
            P("dp", "mp"),
            P("dp", "mp"),
            P("dp", "mp"),
            P("mp", "dp"),
            P(),
            P(),
            P(),
            P("dp", None, "mp"),
            P("dp", "mp", None),
        ),
        check_vma=False,
    )
```

```python
import functools
import math

import jax
import jax.numpy as jnp
from jax import lax
from jax.experimental import pallas as pl
from jax.experimental.pallas import tpu as pltpu
from jax.sharding import PartitionSpec as P

eps = 1e-06
highest = lax.Precision.HIGHEST
f32, bf16 = jnp.float32, jnp.bfloat16
excluded = -1e30
reach = 512
tile = 128


def limit(mebibytes):
    return pltpu.CompilerParams(vmem_limit_bytes=mebibytes * 1024 * 1024)


brief = pl.CostEstimate(flops=10**7, bytes_accessed=10**4, transcendentals=0)
long = pl.CostEstimate(flops=2 * 10**10, bytes_accessed=10**7, transcendentals=0)


def normalize(values, gain):
    inverse = lax.rsqrt(jnp.mean(values * values, axis=-1, keepdims=True) + eps)
    return (values * inverse * gain, inverse)


def dot(left, right, left_dim, right_dim, precision=None):
    return lax.dot_general(
        left,
        right,
        (((left_dim,), (right_dim,)), ((), ())),
        precision=precision,
        preferred_element_type=f32,
    )


def swap(values, axis, step):
    count = lax.axis_size(axis)
    return lax.ppermute(values, axis, [(i, i ^ step) for i in range(count)])


def whole(dims):
    return pl.BlockSpec(tuple(dims), lambda *_: (0,) * len(dims), pipeline_mode=pl.Buffered(1))


def call(
    kernel, name, operands, outs, scratch=(), scalars=None, after=(), through=(), cost=None
):
    outs = list(outs)
    pairs = [o if isinstance(o, tuple) else (o, o.shape[0]) for o in operands]
    operands = [array for array, _ in pairs]
    in_specs = [whole((rows,) + array.shape[1:]) for array, rows in pairs]
    out_specs = [whole(o.shape) for o in outs]
    if scalars is not None:
        operands = [scalars] + operands
        in_specs = [pl.BlockSpec(memory_space=pltpu.SMEM)] + in_specs
    count, results = len(operands), len(outs)
    extra = list(through) + list(after)

    def body(*refs):
        rest = refs[count + len(extra) :]
        kernel(*refs[:count], *rest[:results], *rest[results + len(through) :])

    return pl.pallas_call(
        body,
        name=name,
        grid=(1,),
        in_specs=in_specs + [pl.BlockSpec(memory_space=pl.ANY)] * len(extra),
        out_specs=out_specs + [pl.BlockSpec(memory_space=pl.ANY)] * len(through),
        out_shape=outs + [shape(o.shape, o.dtype) for o in through],
        input_output_aliases={count + i: results + i for i in range(len(through))},
        scratch_shapes=list(scratch),
        compiler_params=limit(64),
        cost_estimate=cost or brief,
    )(*operands, *extra)


def shape(dims, dtype):
    return jax.ShapeDtypeStruct(tuple(dims), dtype)


def fill_skew(line_ref, skew, heads):
    window = reach + tile
    row = lax.broadcasted_iota(jnp.int32, (tile, window), 0)
    column = lax.broadcasted_iota(jnp.int32, (tile, window), 1)
    usable = (column - row <= reach) & (column - row >= 1)
    for head in range(heads):
        line = jnp.broadcast_to(line_ref[head : head + 1, :], (tile, window))
        rolled = pltpu.roll(line, 0, 1, stride=1, stride_axis=0)
        skew[head * tile : (head + 1) * tile, :] = jnp.where(usable, rolled, excluded)


def fill_window(source_ref, padded):
    padded[:reach, :] = jnp.zeros((reach, padded.shape[1]), bf16)
    padded[reach:, :] = source_ref[...]


def spread_heads(values, heads, scale):
    span = values.shape[1]
    size = span // heads
    lane = lax.broadcasted_iota(jnp.int32, (tile, span), 1)
    wide = values.astype(f32) * scale
    parts = [
        jnp.where((lane >= head * size) & (lane < (head + 1) * size), wide, 0.0)
        for head in range(heads)
    ]
    return jnp.concatenate(parts, axis=0).astype(bf16)


def collect_heads(stacked, heads):
    span = stacked.shape[1]
    size = span // heads
    lane = lax.broadcasted_iota(jnp.int32, (tile, span), 1)
    total = stacked[:tile, :]
    for head in range(1, heads):
        total = jnp.where(lane < head * size, total, stacked[head * tile : (head + 1) * tile, :])
    return total


def window_powers(q_all, keys, skew, seg_q_ref, seg_k_ref, start, heads):
    window = reach + tile
    seg_q = jnp.concatenate([seg_q_ref[pl.ds(start, tile), :]] * heads, axis=0)
    seg_k = seg_k_ref[:, pl.ds(start, window)]
    scores = dot(q_all, keys, 1, 1) + skew[...]
    scores = jnp.where(seg_q == seg_k, scores, excluded)
    powers = jnp.exp(scores - jnp.max(scores, axis=-1, keepdims=True))
    return powers, 1.0 / jnp.sum(powers, axis=-1, keepdims=True)


def attend_kernel(heads, place, q_ref, k_ref, v_ref, seg_q_ref, seg_k_ref, line_ref, *rest):
    *out_refs, mixed, k_pad, v_pad, skew = rest
    window = reach + tile
    scale = (q_ref.shape[1] // heads) ** (-0.5)
    fill_skew(line_ref, skew, heads)
    fill_window(k_ref, k_pad)
    fill_window(v_ref, v_pad)

    def step(index, carry):
        start = pl.multiple_of(index * tile, tile)
        q_all = spread_heads(q_ref[pl.ds(start, tile), :], heads, scale)
        powers, inverse = window_powers(
            q_all, k_pad[pl.ds(start, window), :], skew, seg_q_ref, seg_k_ref, start, heads
        )
        probs = (powers * inverse).astype(bf16)
        part = dot(probs, v_pad[pl.ds(start, window), :], 1, 0)
        mixed[pl.ds(start, tile), :] = collect_heads(part, heads).astype(bf16)
        return carry

    lax.fori_loop(0, q_ref.shape[0] // tile, step, 0)
    rows = out_refs[0].shape[0]
    for r, out_ref in enumerate(out_refs):
        out_ref[...] = mixed[pl.ds(pl.multiple_of((place[1] ^ r) * rows, rows), rows), :]


def attend(place, query, key_rows, value_rows, seg_q, seg_k, line, heads, members, after):
    seq_len, span = query.shape
    window = reach + tile

    def kernel(place_ref, *refs):
        attend_kernel(heads, place_ref, *refs)

    return call(
        kernel,
        "attend",
        [query, key_rows, value_rows, seg_q, seg_k, line],
        [shape((seq_len // members, span), bf16)] * members,
        scratch=[
            pltpu.VMEM((seq_len, span), bf16),
            pltpu.VMEM((seq_len + reach, span), bf16),
            pltpu.VMEM((seq_len + reach, span), bf16),
            pltpu.VMEM((heads * tile, window), f32),
        ],
        scalars=place,
        after=after,
    )


def attend_back_kernel(heads, members, place, *refs):
    q_ref, k_ref, v_ref, seg_q_ref, seg_k_ref, line_ref = refs[:6]
    g_refs = refs[6 : 6 + members]
    dq_ref, dk_ref, dv_ref, line_grad_ref = refs[6 + members : 10 + members]
    grad, k_pad, v_pad, skew, dk_sum, dv_sum, bias_sum = refs[10 + members :]
    window = reach + tile
    scale = (q_ref.shape[1] // heads) ** (-0.5)
    rows = g_refs[0].shape[0]
    fill_skew(line_ref, skew, heads)
    fill_window(k_ref, k_pad)
    fill_window(v_ref, v_pad)
    dk_sum[...] = jnp.zeros_like(dk_sum)
    dv_sum[...] = jnp.zeros_like(dv_sum)
    bias_sum[...] = jnp.zeros_like(bias_sum)
    for r, g_ref in enumerate(g_refs):
        grad[pl.ds(pl.multiple_of((place[1] ^ r) * rows, rows), rows), :] = g_ref[...]

    def step(index, carry):
        start = pl.multiple_of(index * tile, tile)
        keys = k_pad[pl.ds(start, window), :]
        values = v_pad[pl.ds(start, window), :]
        q_all = spread_heads(q_ref[pl.ds(start, tile), :], heads, scale)
        g_all = spread_heads(grad[pl.ds(start, tile), :], heads, 1.0)
        powers, inverse = window_powers(q_all, keys, skew, seg_q_ref, seg_k_ref, start, heads)
        probs = powers * inverse
        dot_grad = dot(g_all, values, 1, 1)
        inner = jnp.sum(probs * dot_grad, axis=-1, keepdims=True)
        score_grad = (probs * (dot_grad - inner)).astype(bf16)
        bias_sum[...] += score_grad.astype(f32)
        part = collect_heads(dot(score_grad, keys, 1, 0), heads) * scale
        dq_ref[pl.ds(start, tile), :] = part.astype(bf16)
        dk_sum[pl.ds(start, window), :] += dot(score_grad, q_all, 0, 0)
        dv_sum[pl.ds(start, window), :] += dot(probs.astype(bf16), g_all, 0, 0)
        return carry

    lax.fori_loop(0, q_ref.shape[0] // tile, step, 0)
    dk_ref[...] = dk_sum[reach:, :].astype(bf16)
    dv_ref[...] = dv_sum[reach:, :].astype(bf16)
    line_grad_ref[...] = jnp.zeros_like(line_grad_ref)
    row = lax.broadcasted_iota(jnp.int32, (tile, tile), 0)
    column = lax.broadcasted_iota(jnp.int32, (tile, tile), 1)
    mirror = (row + column == tile - 1).astype(f32)
    for head in range(heads):
        part = bias_sum[head * tile : (head + 1) * tile, :]
        turned = dot(mirror, part, 1, 0, highest)
        straight = pltpu.roll(turned, window - tile + 1, 1, stride=1, stride_axis=0)
        line_grad_ref[head : head + 1, :] = jnp.sum(straight, axis=0, keepdims=True)


def attend_back(place, query, key_rows, value_rows, seg_q, seg_k, line, grads, heads, after):
    seq_len, span = query.shape
    window = reach + tile

    def kernel(place_ref, *refs):
        attend_back_kernel(heads, len(grads), place_ref, *refs)

    return call(
        kernel,
        "attend_back",
        [query, key_rows, value_rows, seg_q, seg_k, line] + grads,
        [shape((seq_len, span), bf16)] * 3 + [shape((8, window), f32)],
        scratch=[
            pltpu.VMEM((seq_len, span), bf16),
            pltpu.VMEM((seq_len + reach, span), bf16),
            pltpu.VMEM((seq_len + reach, span), bf16),
            pltpu.VMEM((heads * tile, window), f32),
            pltpu.VMEM((seq_len + reach, span), f32),
            pltpu.VMEM((seq_len + reach, span), f32),
            pltpu.VMEM((heads * tile, window), f32),
        ],
        scalars=place,
        after=after,
    )


def pack_weights(w_query, w_key, w_value, w_output):
    part, span = w_query.shape

    def kernel(q_ref, k_ref, v_ref, o_ref, pack_ref):
        for at, ref in enumerate((q_ref, k_ref, v_ref)):
            pack_ref[:, at * span : (at + 1) * span] = ref[...]
        pack_ref[:, 3 * span :] = o_ref[...].astype(f32).T.astype(bf16)

    (pack,) = call(
        kernel, "pack_weights", [w_query, w_key, w_value, w_output], [shape((part, 4 * span), bf16)]
    )
    return pack


def pair_up(pack, far, after):
    part = pack.shape[0]

    def kernel(near_ref, far_ref, both_ref):
        both_ref[:part, :] = near_ref[...]
        both_ref[part:, :] = far_ref[...]

    (both,) = call(
        kernel, "pair_up", [pack, far], [shape((2 * part, pack.shape[1]), bf16)], after=after
    )
    return both


def project(place, token_blocks, pack_blocks, gain, cotangent, span, after):
    rows, width = token_blocks[0].shape
    members = len(token_blocks)
    seq_len = rows * members
    parts = sum(len(held) for _, held in pack_blocks)
    part = width // parts

    def kernel(place_ref, gain_ref, *refs):
        token_refs = refs[:members]
        pack_refs = refs[members : members + len(pack_blocks)]
        (normed_ref, q_ref, k_ref, v_ref, wq_ref, wk_ref, wv_ref, wo_ref, pack) = refs[
            members + len(pack_blocks) :
        ]
        for (_, held), ref in zip(pack_blocks, pack_refs):
            for i, r in enumerate(held):
                at = pl.multiple_of((place_ref[0] ^ r) * part, part) if parts > 1 else 0
                pack[pl.ds(at, part), :] = ref[i * part : (i + 1) * part, :]
        for at, ref in enumerate((wq_ref, wk_ref, wv_ref)):
            ref[...] = pack[:, at * span : (at + 1) * span]
        wo_ref[...] = pack[:, 3 * span :].astype(f32).T.astype(bf16)
        for r, ref in enumerate(token_refs):
            normed, _ = normalize(ref[...].astype(f32), gain_ref[...])
            normed = normed.astype(bf16)
            at = pl.ds(pl.multiple_of((place_ref[1] ^ r) * rows, rows), rows)
            normed_ref[at, :] = normed
            q_ref[at, :] = dot(normed, wq_ref[...], 1, 0).astype(bf16)
            k_ref[at, :] = dot(normed, wk_ref[...], 1, 0).astype(bf16)
            v_ref[at, :] = dot(normed, wv_ref[...], 1, 0).astype(bf16)

    return call(
        kernel,
        "project",
        [gain] + list(token_blocks) + [array for array, _ in pack_blocks],
        [shape((seq_len, width), bf16)]
        + [shape((seq_len, span), bf16)] * 3
        + [shape((width, span), bf16)] * 3
        + [shape((span, width), bf16)],
        scratch=[pltpu.VMEM((width, width), bf16)],
        scalars=place,
        through=[cotangent],
        after=after,
    )


def hot(slots_ref, first, count):
    tokens = slots_ref.shape[1]
    slot = lax.broadcasted_iota(jnp.int32, (count, tokens), 0) + first
    taken = (slot == slots_ref[0:1, :]) | (slot == slots_ref[1:2, :])
    return jnp.where(taken, 1.0, 0.0).astype(bf16)


def to_slots(name, sets, blocks, size, after=()):
    width = sets[0][0].shape[1]

    def kernel(*refs):
        out_refs = refs[2 * len(sets) :]
        for at in range(len(sets)):
            rows_ref, slots_ref = refs[2 * at], refs[2 * at + 1]
            for b, out_ref in enumerate(out_refs):
                part = dot(hot(slots_ref, b * size, size), rows_ref[...], 1, 0)
                out_ref[at * size : (at + 1) * size, :] = part.astype(bf16)

    operands = [item for pair in sets for item in pair]
    return call(
        kernel,
        name,
        operands,
        [shape((size * len(sets), width), bf16)] * blocks,
        after=after,
    )


def from_slots(name, blocks, slots, size, dtypes, after=(), through=(), cost=None):
    count, sets = len(blocks), len(slots)
    width = blocks[0].shape[1]
    rows = slots[0].shape[1]

    def kernel(*refs):
        block_refs, slot_refs, out_refs = refs[:count], refs[count : count + sets], refs[count + sets :]
        for at in range(sets):
            total = None
            for b, ref in enumerate(block_refs):
                held = ref[at * size : (at + 1) * size, :]
                part = dot(hot(slot_refs[at], b * size, size), held, 0, 0)
                total = part if total is None else total + part
            out_refs[at][...] = total.astype(out_refs[at].dtype)

    return call(
        kernel,
        name,
        list(blocks) + list(slots),
        [shape((rows, width), dtype) for dtype in dtypes],
        after=after,
        through=through,
        cost=cost,
    )


def router_softmax(values, w_router, experts):
    logits = dot(values, w_router, 1, 0)
    lane = lax.broadcasted_iota(jnp.int32, logits.shape, 1)
    logits = jnp.where(lane < experts, logits, excluded)
    powers = jnp.exp(logits - jnp.max(logits, axis=-1, keepdims=True))
    return powers / jnp.sum(powers, axis=-1, keepdims=True)


def middle(tokens, mixed, weight_o, gain, w_router, slots, experts, blocks, size, after):
    rows, width = tokens.shape
    members = len(mixed)

    def kernel(*refs):
        token_ref, gain_ref, router_ref, slots_ref = refs[:4]
        mixed_refs, weight_refs = refs[4 : 4 + members], refs[4 + members : 4 + 2 * members]
        hidden_ref, input_ref, probs_ref, *send_refs = refs[4 + 2 * members :]
        hidden = token_ref[...].astype(f32)
        for left, right in zip(mixed_refs, weight_refs):
            hidden = hidden + dot(left[...], right[...], 1, 0)
        hidden_ref[...] = hidden
        normed, _ = normalize(hidden, gain_ref[...])
        normed = normed.astype(bf16)
        input_ref[...] = normed
        for b, ref in enumerate(send_refs):
            ref[...] = dot(hot(slots_ref, b * size, size), normed, 1, 0).astype(bf16)
        probs_ref[...] = router_softmax(normed, router_ref[...], experts)

    return call(
        kernel,
        "middle",
        [tokens, gain, w_router, slots] + mixed + weight_o,
        [shape((rows, width), f32), shape((rows, width), bf16), shape((rows, 128), f32)]
        + [shape((size, width), bf16)] * blocks,
        after=after,
    )


def join_rows(refs):
    return jnp.concatenate([ref[...] for ref in refs], axis=0)


def experts_forward(place, w_in, w_out, w_router, x_blocks, experts, after):
    width, units = w_in.shape
    count, size = len(x_blocks), x_blocks[0].shape[0]
    total, piece, chunk = size * count, 768, 256

    def kernel(me_ref, w_in_ref, w_out_ref, router_ref, *refs):
        x_refs, refs = refs[:count], refs[count + len(after) :]
        active_ref, slope_ref, x_all, result_ref, gates_ref, gated_ref, result_sum = refs

        @pl.when(pl.program_id(0) == 0)
        def _():
            x_all[...] = jnp.concatenate([ref[...] for ref in x_refs], axis=0)
            probs = router_softmax(x_all[...], router_ref[...], experts)
            lane = lax.broadcasted_iota(jnp.int32, probs.shape, 1)
            own = jnp.sum(jnp.where(lane == me_ref[0], probs, 0.0), axis=1, keepdims=True)
            gates_ref[...] = jnp.broadcast_to(own, gates_ref.shape)
            result_sum[...] = jnp.zeros_like(result_sum)

        for c in range(piece // chunk):
            at = slice(c * chunk, (c + 1) * chunk)
            pre_act = dot(x_all[...], w_in_ref[:, at], 1, 0)
            below = 0.5 + 0.5 * lax.erf(pre_act * math.sqrt(0.5))
            bell = jnp.exp(-0.5 * pre_act * pre_act) * (1.0 / math.sqrt(2.0 * math.pi))
            active_ref[:, at] = (pre_act * below).astype(bf16)
            slope_ref[:, at] = (below + pre_act * bell).astype(bf16)
        result_sum[...] += dot(active_ref[...], w_out_ref[...], 1, 0)

        @pl.when(pl.program_id(0) == pl.num_programs(0) - 1)
        def _():
            result = result_sum[...].astype(bf16)
            result_ref[...] = result
            gated_ref[...] = (gates_ref[:, 0:1] * result.astype(f32)).astype(bf16)

    columns = pl.BlockSpec((total, piece), lambda i: (0, i))
    rows = shape((total, width), bf16)
    kept = [rows, rows, shape((total, 128), f32), rows]
    return pl.pallas_call(
        kernel,
        name="experts_forward",
        grid=(units // piece,),
        in_specs=[
            pl.BlockSpec(memory_space=pltpu.SMEM),
            pl.BlockSpec((width, piece), lambda i: (0, i)),
            pl.BlockSpec((piece, width), lambda i: (i, 0)),
            whole(w_router.shape),
        ]
        + [whole(o.shape) for o in x_blocks]
        + [pl.BlockSpec(memory_space=pl.ANY)] * len(after),
        out_specs=[columns] * 2 + [whole(o.shape) for o in kept],
        out_shape=[shape((total, units), bf16)] * 2 + kept,
        scratch_shapes=[pltpu.VMEM((total, width), f32)],
        compiler_params=limit(64),
        cost_estimate=long,
    )(place, w_in, w_out, w_router, *x_blocks, *after)


def experts_backward(place, w_in, w_out, slope, result, gates, g_blocks, size):
    width, units = w_in.shape
    total, piece, chunk = slope.shape[0], 768, 256
    count = len(g_blocks)

    def kernel(me_ref, w_in_ref, w_out_ref, slope_ref, result_ref, gates_ref, *refs):
        g_refs, back_refs = refs[:count], refs[count : 2 * count]
        pre_grad_ref, s_all, back_sum = refs[2 * count :]

        @pl.when(pl.program_id(0) == 0)
        def _():
            back_sum[...] = jnp.zeros_like(back_sum)
            for b, ref in enumerate(g_refs):
                rows = slice(b * size, (b + 1) * size)
                s_all[rows, :] = (gates_ref[rows, 0:1] * ref[...].astype(f32)).astype(bf16)

        for c in range(piece // chunk):
            at = slice(c * chunk, (c + 1) * chunk)
            active_grad = dot(s_all[...], w_out_ref[at, :], 1, 1)
            pre_grad_ref[:, at] = (active_grad * slope_ref[:, at].astype(f32)).astype(bf16)
        back_sum[...] += dot(pre_grad_ref[...], w_in_ref[...], 1, 1)

        @pl.when(pl.program_id(0) == pl.num_programs(0) - 1)
        def _():
            lane = lax.broadcasted_iota(jnp.int32, (size, 128), 1)
            for b, (ref, g_ref) in enumerate(zip(back_refs, g_refs)):
                rows = slice(b * size, (b + 1) * size)
                products = g_ref[...].astype(f32) * result_ref[rows, :].astype(f32)
                gate_grad = jnp.sum(products, axis=1, keepdims=True)
                upper = gate_grad.astype(bf16).astype(f32)
                ref[:, :width] = back_sum[rows, :].astype(bf16)
                ref[:, width:] = jnp.where(
                    lane == me_ref[0],
                    upper,
                    jnp.where(lane == me_ref[0] + 64, gate_grad - upper, 0.0),
                ).astype(bf16)

    by_units = pl.BlockSpec((total, piece), lambda i: (0, i))
    outs = [shape((size, width + 128), bf16)] * count
    flat = pl.pallas_call(
        kernel,
        name="experts_backward",
        grid=(units // piece,),
        in_specs=[
            pl.BlockSpec(memory_space=pltpu.SMEM),
            pl.BlockSpec((width, piece), lambda i: (0, i)),
            pl.BlockSpec((piece, width), lambda i: (i, 0)),
            by_units,
            whole(result.shape),
            whole(gates.shape),
        ]
        + [whole((size, width))] * count,
        out_specs=[whole(o.shape) for o in outs] + [by_units, whole((total, width))],
        out_shape=outs + [shape((total, units), bf16), shape((total, width), bf16)],
        scratch_shapes=[pltpu.VMEM((total, width), f32)],
        compiler_params=limit(64),
        cost_estimate=long,
    )(place, w_in, w_out, slope, result, gates, *g_blocks)
    return list(flat[:count]), flat[count], flat[count + 1]


def run_experts(
    name, place, w_in, w_out, w_router, x_blocks, g_blocks, at_set, before, cost, after
):
    width, units = w_in.shape
    count, size = len(x_blocks), x_blocks[0].shape[0]
    total, piece, chunk = size * count, 512, 256
    experts = before[0]
    held = list(before[1:])
    sets = g_blocks[0].shape[0] // size
    last = at_set == sets - 1

    def kernel(me_ref, w_in_ref, w_out_ref, router_ref, *refs):
        x_refs, refs = refs[:count], refs[count:]
        g_refs, refs = refs[:count], refs[count:]
        held_refs, refs = refs[: len(held)], refs[len(held) + len(after) :]
        back_refs, refs = refs[:count], refs[count:]
        result_refs, refs = refs[:count] if last else refs[:1], refs[count if last else 1 :]
        active_ref, pre_grad_ref, x_all, s_all, gates, result_sum, back_sum = refs

        @pl.when(pl.program_id(0) == 0)
        def _():
            for b in range(count):
                rows = slice(b * size, (b + 1) * size)
                x_all[rows, :] = x_refs[b][...]
            probs = router_softmax(x_all[...], router_ref[...], experts)
            lane = lax.broadcasted_iota(jnp.int32, probs.shape, 1)
            own = jnp.sum(jnp.where(lane == me_ref[0], probs, 0.0), axis=1, keepdims=True)
            gates[...] = jnp.broadcast_to(own, gates.shape)
            for b in range(count):
                rows = slice(b * size, (b + 1) * size)
                grad = g_refs[b][at_set * size : (at_set + 1) * size, :].astype(f32)
                s_all[rows, :] = (gates[rows, 0:1] * grad).astype(bf16)
            result_sum[...] = jnp.zeros_like(result_sum)
            back_sum[...] = jnp.zeros_like(back_sum)

        for c in range(piece // chunk):
            at = slice(c * chunk, (c + 1) * chunk)
            pre_act = dot(x_all[...], w_in_ref[:, at], 1, 0)
            active_grad = dot(s_all[...], w_out_ref[at, :], 1, 1)
            below = 0.5 + 0.5 * lax.erf(pre_act * math.sqrt(0.5))
            bell = jnp.exp(-0.5 * pre_act * pre_act) * (1.0 / math.sqrt(2.0 * math.pi))
            active_ref[:, at] = (pre_act * below).astype(bf16)
            pre_grad_ref[:, at] = (active_grad * (below + pre_act * bell)).astype(bf16)
        result_sum[...] += dot(active_ref[...], w_out_ref[...], 1, 0)
        back_sum[...] += dot(pre_grad_ref[...], w_in_ref[...], 1, 1)

        @pl.when(pl.program_id(0) == pl.num_programs(0) - 1)
        def _():
            lane = lax.broadcasted_iota(jnp.int32, (size, 128), 1)
            for b, (ref, g_ref) in enumerate(zip(back_refs, g_refs)):
                rows = slice(b * size, (b + 1) * size)
                result = result_sum[rows, :].astype(bf16).astype(f32)
                grad = g_ref[at_set * size : (at_set + 1) * size, :].astype(f32)
                gate_grad = jnp.sum(grad * result, axis=1, keepdims=True)
                upper = gate_grad.astype(bf16).astype(f32)
                ref[:, :width] = back_sum[rows, :].astype(bf16)
                ref[:, width:] = jnp.where(
                    lane == me_ref[0],
                    upper,
                    jnp.where(lane == me_ref[0] + 64, gate_grad - upper, 0.0),
                ).astype(bf16)
                gated = (gates[rows, 0:1] * result).astype(bf16)
                if last:
                    for at, other in enumerate(held_refs):
                        result_refs[b][at * size : (at + 1) * size, :] = other[rows, :]
                    result_refs[b][at_set * size : (at_set + 1) * size, :] = gated
                else:
                    result_refs[0][rows, :] = gated

    columns = pl.BlockSpec((total, piece), lambda i: (0, i))
    outs = [shape((size, width + 128), bf16)] * count
    results = [shape((size * sets, width), bf16)] * count if last else [shape((total, width), bf16)]
    rows_out = [shape((total, width), bf16)] * 2
    flat = pl.pallas_call(
        kernel,
        name=name,
        grid=(units // piece,),
        in_specs=[
            pl.BlockSpec(memory_space=pltpu.SMEM),
            pl.BlockSpec((width, piece), lambda i: (0, i)),
            pl.BlockSpec((piece, width), lambda i: (i, 0)),
            whole(w_router.shape),
        ]
        + [whole(o.shape) for o in list(x_blocks) + list(g_blocks) + held]
        + [pl.BlockSpec(memory_space=pl.ANY)] * len(after),
        out_specs=[whole(o.shape) for o in outs + results]
        + [columns] * 2
        + [whole(o.shape) for o in rows_out],
        out_shape=outs + results + [shape((total, units), bf16)] * 2 + rows_out,
        scratch_shapes=[
            pltpu.VMEM((total, 128), f32),
            pltpu.VMEM((total, width), f32),
            pltpu.VMEM((total, width), f32),
        ],
        compiler_params=limit(64),
        cost_estimate=cost,
    )(place, w_in, w_out, w_router, *x_blocks, *g_blocks, *held, *after)
    return list(flat[:count]), list(flat[count:-4]), flat[-4:]


def home(
    own_back,
    far_sum,
    slots,
    hidden,
    probs,
    cotangent,
    gain,
    w_router,
    ffn_input,
    weight_o,
    mixed,
    size,
    experts,
    after,
    through,
):
    rows, width = hidden.shape
    count, members = len(own_back), len(weight_o)
    span = weight_o[0].shape[0]
    far = [] if far_sum is None else [far_sum]

    def kernel(*refs):
        slots_ref, hidden_ref, probs_ref, cot_ref, gain_ref, router_ref, input_ref = refs[:7]
        refs = refs[7:]
        back_refs, refs = refs[:count], refs[count:]
        far_refs, refs = refs[: len(far)], refs[len(far) :]
        weight_refs, mixed_refs, refs = refs[:members], refs[members : 2 * members], refs[2 * members :]
        grad_refs = refs[:members]
        hidden_grad_ref, gain_grad_ref, router_grad_ref, near_ref, base_ref = refs[members:]
        total = None
        for b, ref in enumerate(back_refs):
            part = dot(hot(slots_ref, b * size, size), ref[...], 0, 0)
            total = part if total is None else total + part
        for ref in far_refs:
            total = total + ref[...].astype(f32)
        columns = total[:, width:]
        lane = lax.broadcasted_iota(jnp.int32, columns.shape, 1)
        prob_grad = jnp.where(lane < 64, columns + pltpu.roll(columns, 64, 1), 0.0)
        router_probs = probs_ref[...]
        logit_grad = router_probs * (
            prob_grad - jnp.sum(router_probs * prob_grad, axis=-1, keepdims=True)
        )
        router_grad_ref[...] = dot(logit_grad, input_ref[...].astype(f32), 0, 0, highest)[:experts, :]
        grad = total[:, :width] + dot(logit_grad, router_ref[...].astype(f32), 1, 1, highest)
        hidden_now = hidden_ref[...]
        inverse = lax.rsqrt(jnp.mean(hidden_now * hidden_now, axis=-1, keepdims=True) + eps)
        scaled = grad * gain_ref[...]
        gain_grad_ref[...] = jnp.sum(grad * hidden_now * inverse, axis=0, keepdims=True)
        inner = jnp.mean(scaled * hidden_now, axis=-1, keepdims=True)
        hidden_grad = (
            cot_ref[...].astype(f32)
            + inverse * scaled
            - hidden_now * inverse * inverse * inverse * inner
        )
        hidden_grad_ref[...] = hidden_grad
        attn_grad = hidden_grad.astype(bf16)
        for ref, weight in zip(grad_refs, weight_refs):
            ref[...] = dot(attn_grad, weight[...], 1, 1).astype(bf16)
        for r, (ref, first) in enumerate(
            ((base_ref, 0), (near_ref, 0), (base_ref, span), (near_ref, span))
        ):
            part = dot(mixed_refs[r][...], attn_grad, 0, 0)
            ref[first : first + span, :] = part.astype(ref.dtype)

    return call(
        kernel,
        "home",
        [slots, hidden, probs, cotangent, gain, w_router, ffn_input]
        + list(own_back)
        + far
        + weight_o
        + mixed,
        [shape((rows, span), bf16)] * members
        + [
            shape((rows, width), f32),
            shape((1, width), f32),
            shape((experts, width), f32),
            shape((2 * span, width), bf16),
            shape((2 * span, width), f32),
        ],
        after=after,
        through=through,
    )


def expert_weight_grads(place, rows_in, pre_grads, actives, slot_grads, members):
    sets = len(rows_in)
    total, width = rows_in[0].shape
    piece = pre_grads[0].shape[1] // members

    def kernel(place_ref, *refs):
        x_refs, p_refs, a_refs, s_refs = [refs[i * sets : (i + 1) * sets] for i in range(4)]
        near_ref, base_ref = refs[4 * sets :]
        step = pl.program_id(0)

        def total_of(lefts, rights):
            held = dot(lefts[0][...], rights[0][...], 0, 0)
            for left, right in zip(lefts[1:], rights[1:]):
                held = held + dot(left[...], right[...], 0, 0)
            return held

        @pl.when(step < 2)
        def _():
            near_ref[...] = total_of(x_refs, p_refs).astype(bf16)

        @pl.when((step >= 2) & (step < 4))
        def _():
            base_ref[...] = total_of(x_refs, p_refs)

        @pl.when((step >= 4) & (step < 6))
        def _():
            near_ref[...] = total_of(a_refs, s_refs).astype(bf16)

        @pl.when(step >= 6)
        def _():
            base_ref[...] = total_of(a_refs, s_refs)

    def partner(i):
        return jnp.where(i < 2, 2 * i + 1, 2 * i - 4)

    fixed = pl.BlockSpec((total, width), lambda i, p: (0, 0))
    pre_cut = pl.BlockSpec((total, piece), lambda i, p: (0, p[1] ^ partner(jnp.minimum(i, 3))))
    act_cut = pl.BlockSpec((total, piece), lambda i, p: (0, p[1] ^ partner(jnp.maximum(i - 4, 0))))
    return pl.pallas_call(
        kernel,
        name="expert_weight_grads",
        grid_spec=pltpu.PrefetchScalarGridSpec(
            num_scalar_prefetch=1,
            grid=(8,),
            in_specs=[fixed] * sets + [pre_cut] * sets + [act_cut] * sets + [fixed] * sets,
            out_specs=[
                pl.BlockSpec(
                    (piece, width), lambda i, p: (2 * (i // 4) + jnp.minimum(i % 4, 1), 0)
                ),
                pl.BlockSpec(
                    (piece, width), lambda i, p: (2 * (i // 4) + jnp.maximum(i % 4 - 2, 0), 0)
                ),
            ],
        ),
        out_shape=[shape((4 * piece, width), bf16), shape((4 * piece, width), f32)],
        compiler_params=limit(64),
        cost_estimate=long,
    )(place, *rows_in, *pre_grads, *actives, *slot_grads)


def far_sums(near, base, near_o, base_o, cuts, after):
    size, width = base.shape[0] // 4, base.shape[1]
    span = near_o.shape[0] // 2

    def block(rows, at):
        return pl.BlockSpec((rows, width), lambda *_: (at, 0), pipeline_mode=pl.Buffered(1))

    def kernel(near_in, near_out, base_in, base_out, near_o_ref, base_o_ref, *refs):
        out_refs = refs[len(after) :]
        out_refs[0][:span, :] = (base_o_ref[...] + near_o_ref[...].astype(f32)).astype(bf16)
        starts = [0] + cuts
        for i, ref in enumerate(out_refs):
            low, high = starts[i], starts[i + 1]
            at = span if i == 0 else 0
            for near_ref, base_ref, shift in ((near_in, base_in, 0), (near_out, base_out, size)):
                first, last = max(low, shift), min(high, shift + size)
                if first < last:
                    rows = slice(first - shift, last - shift)
                    held = base_ref[rows, :] + near_ref[rows, :].astype(f32)
                    ref[at + first - low : at + last - low, :] = held.astype(bf16)

    rows = [high - low for low, high in zip([0] + cuts, cuts)]
    rows[0] = rows[0] + span
    return pl.pallas_call(
        kernel,
        name="far_sums",
        grid=(1,),
        in_specs=[block(size, 1), block(size, 3), block(size, 1), block(size, 3)]
        + [block(span, 1), block(span, 1)]
        + [pl.BlockSpec(memory_space=pl.ANY)] * len(after),
        out_specs=[whole((count, width)) for count in rows],
        out_shape=[shape((count, width), bf16) for count in rows],
        compiler_params=limit(64),
        cost_estimate=brief,
    )(near, near, base, base, near_o, base_o, *after)


def input_grads(
    place,
    proj_grads,
    normed,
    weights,
    output_parts,
    gain,
    line_grad,
    bucket_hot,
    ffn_gain_grad,
    router_grad,
    members,
    owners,
    heads,
    buckets_all,
    after,
):
    seq_len, width = normed.shape
    span = weights[0].shape[1]
    rows = seq_len // members
    part = width // owners
    few = owners == 8
    experts = router_grad.shape[0]
    extra = -(-(3 + experts) // 16) * 16

    def kernel(place_ref, *refs):
        dq_ref, dk_ref, dv_ref, normed_ref, wq_ref, wk_ref, wv_ref, gain_ref = refs[:8]
        line_ref, hot_ref, ffn_gain_ref, router_ref = refs[8:12]
        base_o_ref, near_o_ref, far_o_ref = refs[12:15]
        near_ref, base_ref, far_ref, small_ref, *weight_refs, sums = refs[15:]
        for at, ref in enumerate((dq_ref, dk_ref, dv_ref)):
            sums[:, at * span : (at + 1) * span] = dot(normed_ref[...], ref[...], 0, 0)
        output_sum = base_o_ref[...] + near_o_ref[...].astype(f32) + far_o_ref[...].astype(f32)
        sums[:, 3 * span :] = output_sum.T
        if few:
            for r, ref in enumerate(weight_refs):
                for i, far in enumerate((0, 4)):
                    at = pl.multiple_of((place_ref[0] ^ r ^ far) * part, part)
                    ref[i * part : (i + 1) * part, :] = sums[pl.ds(at, part), :].astype(ref.dtype)
        else:
            weight_refs[0][...] = sums[...]
        gain_grad = jnp.zeros((1, width), f32)
        for r, (ref, first) in enumerate(
            ((base_ref, 0), (near_ref, 0), (far_ref, 0), (near_ref, rows))
        ):
            at = pl.ds(pl.multiple_of((place_ref[1] ^ r) * rows, rows), rows)
            grad = (
                dot(dq_ref[at, :], wq_ref[...], 1, 1)
                + dot(dk_ref[at, :], wk_ref[...], 1, 1)
                + dot(dv_ref[at, :], wv_ref[...], 1, 1)
            )
            gain_grad = gain_grad + jnp.sum(
                grad * normed_ref[at, :].astype(f32), axis=0, keepdims=True
            )
            ref[first : first + rows, :] = grad.astype(ref.dtype)
        table = dot(line_ref[...], hot_ref[...], 1, 0, highest)
        bucket = lax.broadcasted_iota(jnp.int32, (128, width), 0)
        lane = lax.broadcasted_iota(jnp.int32, (128, width), 1)
        flat = jnp.zeros((1, width), f32)
        for head in range(heads):
            first = (place_ref[1] * heads + head) * buckets_all
            spread = jnp.where((bucket < buckets_all) & (lane == bucket + first), 1.0, 0.0)
            flat = flat + dot(table[head : head + 1, :], spread, 1, 0, highest)
        small_ref[...] = jnp.zeros_like(small_ref)
        small_ref[0:1, :] = gain_grad / gain_ref[...]
        small_ref[1:2, :] = ffn_gain_ref[...]
        small_ref[2:3, :] = flat
        small_ref[3 : 3 + experts, :] = router_ref[...]
        if few:
            upper, lower = two_halves(small_ref[...])
            small_ref[...] = upper.astype(f32) + lower.astype(f32)
            for ref in weight_refs[1:]:
                ref[2 * part : 2 * part + extra, :] = upper
                ref[2 * part + extra :, :] = lower

    if few:
        weight_outs = [shape((2 * part, 4 * span), f32)]
        weight_outs += [shape((2 * part + 2 * extra, 4 * span), bf16)] * 3
    else:
        weight_outs = [shape((width, 4 * span), f32)]
    return call(
        kernel,
        "input_grads",
        list(proj_grads)
        + [normed]
        + list(weights)
        + [gain, line_grad, bucket_hot, ffn_gain_grad, router_grad]
        + [(part, span) for part in output_parts],
        [
            shape((2 * rows, width), bf16),
            shape((rows, width), f32),
            shape((rows, width), f32),
            shape((extra, width), f32),
        ]
        + weight_outs,
        scratch=[pltpu.VMEM((width, 4 * span), f32)],
        scalars=place,
        after=after,
    )


def add_up(base, near, parts, after):
    size, width = base.shape[0] // 4, base.shape[1]

    def kernel(in_base, in_near, out_base, out_near, *refs):
        part_refs, (in_ref, out_ref) = refs[: len(parts)], refs[-2:]
        first = 0
        for (array, at), ref in zip(parts[:-1], part_refs[:-1]):
            rows = slice(first, first + array.shape[0] - at)
            total = in_base[rows, :] + in_near[rows, :].astype(f32)
            in_ref[rows, :] = total + ref[at:, :].astype(f32)
            first = first + array.shape[0] - at
        total = out_base[...] + out_near[...].astype(f32)
        out_ref[...] = total + part_refs[-1][...].astype(f32)

    def block(at):
        return pl.BlockSpec((size, width), lambda *_: (at, 0), pipeline_mode=pl.Buffered(1))

    specs = [block(0), block(0), block(2), block(2)] + [whole(o.shape) for o, _ in parts]
    return pl.pallas_call(
        kernel,
        name="add_up",
        grid=(1,),
        in_specs=specs + [pl.BlockSpec(memory_space=pl.ANY)] * len(after),
        out_specs=[whole((size, width))] * 2,
        out_shape=[shape((size, width), f32)] * 2,
        compiler_params=limit(64),
        cost_estimate=long,
    )(base, near, base, near, *[array for array, _ in parts], *after)


def two_halves(values):
    upper = values.astype(bf16)
    return upper, (values - upper.astype(f32)).astype(bf16)


def fold_weights(base, arrived, small, after):
    part, width, extra = base.shape[0] // 2, base.shape[1], small.shape[0]

    def kernel(base_ref, one_ref, two_ref, three_ref, small_ref, own_ref, far_ref, half_ref):
        refs = (one_ref, two_ref, three_ref)
        total = base_ref[...]
        for ref in refs:
            total = total + ref[: 2 * part, :].astype(f32)
        own_ref[...] = total[:part, :]
        far_ref[:part, :] = total[part:, :].astype(bf16)
        one, two, three = [
            ref[2 * part : 2 * part + extra, :].astype(f32)
            + ref[2 * part + extra :, :].astype(f32)
            for ref in refs
        ]
        upper, lower = two_halves((small_ref[...] + one) + (two + three))
        far_ref[part : part + extra, :] = upper
        far_ref[part + extra :, :] = lower
        half_ref[...] = upper.astype(f32) + lower.astype(f32)

    return call(
        kernel,
        "fold_weights",
        [base] + arrived + [small],
        [
            shape((part, width), f32),
            shape((part + 2 * extra, width), bf16),
            shape((extra, width), f32),
        ],
        after=after,
    )


def split_weights(own, far, small, span, after):
    part, extra = own.shape[0], small.shape[0]

    def kernel(*refs):
        own_ref, small_ref, *far_refs = refs[:-5]
        q_ref, k_ref, v_ref, o_ref, sum_ref = refs[-5:]
        total, sums = own_ref[...], small_ref[...]
        for ref in far_refs:
            total = total + ref[:part, :].astype(f32)
            sums = sums + (
                ref[part : part + extra, :].astype(f32) + ref[part + extra :, :].astype(f32)
            )
        for at, ref in enumerate((q_ref, k_ref, v_ref)):
            ref[...] = total[:, at * span : (at + 1) * span]
        o_ref[...] = total[:, 3 * span :].T
        sum_ref[...] = sums

    return call(
        kernel,
        "split_weights",
        [own, small] + ([] if far is None else [far]),
        [shape((part, span), f32)] * 3
        + [shape((span, part), f32), shape((extra, own.shape[1]), f32)],
        after=after,
    )


def gather_mp(values):
    across = swap(values, "mp", 2)
    return [values, swap(values, "mp", 1), across, swap(across, "mp", 1)]


def sum_over(values, axis):
    step = 1
    while step < lax.axis_size(axis):
        values = values + swap(values, axis, step)
        step = 2 * step
    return values


def all_to_all_dp(values):
    return lax.all_to_all(values, "dp", split_axis=0, concat_axis=0, tiled=True)


def slots_of(routes, place, capacity, experts, limit):
    rows = routes.shape[0]
    expert_ids = jnp.arange(experts, dtype=jnp.int32)[None, :]
    hits = (routes[:, 0:1] == expert_ids) | (routes[:, 1:2] == expert_ids)
    earlier = jnp.arange(rows)[:, None] > jnp.arange(rows)[None, :]
    ranks = jnp.dot(earlier.astype(bf16), hits.astype(bf16), preferred_element_type=f32)
    lines = []
    for k in (0, 1):
        rank = jnp.sum(jnp.where(routes[:, k : k + 1] == expert_ids, ranks, 0.0), axis=1)
        block = routes[:, k] ^ place
        lines.append(jnp.where(block < limit, block * capacity + rank.astype(jnp.int32), -1))
    return jnp.pad(jnp.stack(lines), ((0, 6), (0, 0)), constant_values=-1)


def on_device(
    tokens,
    norm_gain,
    w_query,
    w_key,
    w_value,
    w_output,
    bias_table,
    ffn_gain,
    w_router,
    w_in,
    w_out,
    segments,
    buckets,
    routes,
    cotangent,
):
    rows, width = tokens.shape
    heads = bias_table.shape[1]
    seq_len = buckets.shape[0]
    experts = w_router.shape[1]
    owners, members = lax.axis_size("dp"), lax.axis_size("mp")
    me, member = lax.axis_index("dp"), lax.axis_index("mp")
    place = jnp.stack([me, member]).astype(jnp.int32)
    capacity = 4 * rows // experts
    span = w_query.shape[1]
    window = reach + tile
    few = owners == 8

    token_blocks = gather_mp(tokens)
    pack = pack_weights(w_query, w_key, w_value, w_output)
    if few:
        both = pair_up(pack, swap(pack, "dp", 4), token_blocks[1:3])
        pack_blocks = [(both, (0, 4))] + [(swap(both, "dp", r), (r, r ^ 4)) for r in (1, 2, 3)]
    else:
        pack_blocks = [(lax.all_gather(pack, "dp", axis=0, tiled=True), (0,))]
    gain_one, gain_two = norm_gain.reshape(1, width), ffn_gain.reshape(1, width)
    if few:
        blocks, size = 4, capacity
        slots = [slots_of(routes, me, capacity, experts, 4)]
        slots.append(slots_of(swap(routes, "dp", 4), me, capacity, experts, 4))
    else:
        blocks, size = 1, experts * capacity
        slots = [slots_of(routes, 0, capacity, experts, experts)]

    line_buckets = jnp.pad(jnp.flip(buckets[: reach + 1]), (0, window - reach - 1))
    bucket_hot = (
        line_buckets[:, None] == jnp.arange(128, dtype=jnp.int32)[None, :]
    ).astype(f32)
    buckets_all = bias_table.shape[0]
    table = jnp.pad(bias_table.T, ((0, 8 - heads), (0, 128 - buckets_all)))
    line = jnp.dot(table, bucket_hot.T, precision=highest)
    seg_q = segments.reshape(seq_len, 1)
    seg_k = jnp.pad(segments.reshape(1, seq_len), ((0, 0), (reach, 0)), constant_values=-1)
    router_wide = jnp.pad(w_router, ((0, 0), (0, 128 - experts)))
    ready = slots[:1] + [seg_q, seg_k, router_wide, gain_two]
    normed, query, key_rows, value_rows, weight_q, weight_k, weight_v, w_o, late_cotangent = (
        project(place, token_blocks, pack_blocks, gain_one, cotangent, span, ready)
    )


    if few:
        far_cotangent = swap(late_cotangent, "dp", 4)

    mixed_out = attend(
        place, query, key_rows, value_rows, seg_q, seg_k, line, heads, members, [bucket_hot]
    )
    weight_o = gather_mp(w_o)
    mixed_in = [mixed_out[0]] + [swap(mixed_out[r], "mp", r) for r in range(1, members)]

    hidden, ffn_input, router_probs, *send = middle(
        tokens,
        mixed_in,
        weight_o,
        gain_two,
        router_wide,
        slots[0],
        experts,
        blocks,
        size,
        [far_cotangent] if few else [],
    )
    if few:
        held = to_slots(
            "grads_to_slots",
            [(cotangent, slots[0]), (far_cotangent, slots[1])],
            blocks,
            size,
            after=[ffn_input],
        )
        g_blocks = [held[0]] + [swap(held[r], "dp", r) for r in (1, 2, 3)]
        far_input = swap(ffn_input, "dp", 4)
        own = [send[0]] + [swap(send[r], "dp", r) for r in (1, 2, 3)]
        far = to_slots(
            "far_to_slots", [(far_input, slots[1])], blocks, size, after=g_blocks[1:3]
        )
        far = [far[0]] + [swap(far[r], "dp", r) for r in (1, 2, 3)]
        x_sets = [own, far]
    else:
        held = to_slots("grads_to_slots", [(cotangent, slots[0])], blocks, size)
        g_blocks = [all_to_all_dp(held[0])]
        x_sets = [[all_to_all_dp(send[0])]]

    before = [experts]
    if few:
        active, slope, rows_in, plain, slot_gates, gated = experts_forward(
            place, w_in[0], w_out[0], router_wide, x_sets[0], experts, far[:1]
        )
        before = before + [gated]
    back, result, state = run_experts(
        "run_experts",
        place,
        w_in[0],
        w_out[0],
        router_wide,
        x_sets[-1],
        g_blocks,
        len(x_sets) - 1,
        before,
        brief,
        [],
    )
    kept, backs = [state], [back]
    if few:
        back, pre_grad, slot_grad = experts_backward(
            place, w_in[0], w_out[0], slope, plain, slot_gates, g_blocks, size
        )
        kept = [(active, pre_grad, rows_in, slot_grad)] + kept
        backs = [back] + backs
    actives, pre_grads, arrived, slot_grads = zip(*kept)
    if few:
        own_back, far_back = backs
        far_back = [far_back[0]] + [swap(far_back[r], "dp", r) for r in (1, 2, 3)]
        far_total, *passed = from_slots(
            "back_from_slots", far_back, [slots[1]], size, [bf16], through=own_back[1:]
        )
        far_sum = swap(far_total, "dp", 4)
        own_back = [own_back[0]] + [swap(passed[r - 1], "dp", r) for r in (1, 2, 3)]
        result_in = [result[0]] + [swap(result[r], "dp", r) for r in (1, 2, 3)]
    else:
        own_back, far_sum = [all_to_all_dp(backs[0][0])], None
        result_in = [all_to_all_dp(result[0])]
    near_w, base_w = expert_weight_grads(place, arrived, pre_grads, actives, slot_grads, members)

    homed = home(
        own_back,
        far_sum,
        slots[0],
        hidden,
        router_probs,
        cotangent,
        gain_two,
        router_wide,
        ffn_input,
        weight_o,
        mixed_in,
        size,
        experts,
        [],
        [near_w],
    )
    grad_out, homed = homed[:members], homed[members:]
    hidden_grad, ffn_gain_grad, router_grad, near_o, base_o, near_w = homed
    grad_in = [grad_out[0]] + [swap(grad_out[r], "mp", r) for r in range(1, members)]
    near_o, near_w = swap(near_o, "mp", 1), swap(near_w, "mp", 1)
    piece = w_in.shape[2] // members
    far_first, far_next, far_last = far_sums(
        near_w, base_w, near_o, base_o, [rows, piece, 2 * piece], grad_in[2:]
    )

    *proj_grads, line_grad = attend_back(
        place,
        query,
        key_rows,
        value_rows,
        seg_q,
        seg_k,
        line,
        grad_in,
        heads,
        [far_first],
    )
    far_first = swap(far_first, "mp", 2)
    far_next = swap(far_next, "mp", 2)
    far_last = swap(far_last, "mp", 2)
    near, base, base_far, small, *weight_sums = input_grads(
        place,
        proj_grads,
        normed,
        (weight_q, weight_k, weight_v),
        (base_o, near_o, far_first),
        gain_one,
        line_grad,
        bucket_hot,
        ffn_gain_grad,
        router_grad,
        members,
        owners,
        heads,
        buckets_all,
        result_in[1:],
    )
    far_parts = [(far_first, span), (far_next, 0), (far_last, 0)]
    near = swap(near, "mp", 1)
    far_normed = swap((base_far + near[rows:].astype(f32)).astype(bf16), "mp", 2)
    if few:
        arrived_sums = [swap(weight_sums[r], "dp", r) for r in (1, 2, 3)]
        own_sum, far_part, small = fold_weights(
            weight_sums[0], arrived_sums, small, [near]
        )
        own_result, far_result = from_slots(
            "result_from_slots", result_in, slots, size, [f32, bf16], after=[own_sum]
        )
        far_result = swap(far_result, "dp", 4)
        w_in_grad, w_out_grad = add_up(base_w, near_w, far_parts, [own_result])
        *weight_grads, small = split_weights(
            own_sum, swap(far_part, "dp", 4), small, span, [w_in_grad, far_normed]
        )
    else:
        joined_grad = lax.psum_scatter(weight_sums[0], "dp", scatter_dimension=0, tiled=True)
        *weight_grads, small = split_weights(
            joined_grad, None, sum_over(small, "dp"), span, []
        )
        (own_result,) = from_slots("result_from_slots", result_in, slots, size, [f32])
        w_in_grad, w_out_grad = add_up(base_w, near_w, far_parts, [])
    small = sum_over(small, "mp")
    normed_grad = base + near[:rows].astype(f32) + far_normed.astype(f32)
    resid = tokens.astype(f32)
    _, inverse_one = normalize(resid, norm_gain)
    scaled = normed_grad * norm_gain
    inner = jnp.mean(scaled * resid, axis=-1, keepdims=True)
    tokens_grad = (
        hidden_grad + inverse_one * scaled - resid * inverse_one * inverse_one * inverse_one * inner
    ).astype(bf16)

    block_out = hidden + own_result
    if few:
        block_out = block_out + far_result.astype(f32)
    block_out = block_out.astype(bf16)
    return (
        block_out,
        tokens_grad,
        small[0],
        *weight_grads,
        small[2, : heads * members * buckets_all].reshape(heads * members, buckets_all).T,
        small[1],
        small[3 : 3 + experts].T,
        w_in_grad[None],
        w_out_grad[None],
    )


def solution(mesh):
    return jax.shard_map(
        on_device,
        mesh=mesh,
        in_specs=(
            P(("dp", "mp"), None),
            P(),
            P("dp", "mp"),
            P("dp", "mp"),
            P("dp", "mp"),
            P("mp", "dp"),
            P(None, "mp"),
            P(),
            P(),
            P("dp", None, None),
            P("dp", None, None),
            P("dp", None),
            P(),
            P(("dp", "mp"), None),
            P(("dp", "mp"), None),
        ),
        out_specs=(
            P(("dp", "mp"), None),
            P(("dp", "mp"), None),
            P(),
            P("dp", "mp"),
            P("dp", "mp"),
            P("dp", "mp"),
            P("mp", "dp"),
            P(),
            P(),
            P(),
            P("dp", None, "mp"),
            P("dp", "mp", None),
        ),
        check_vma=False,
    )
```

```python
import functools
import math

import jax
import jax.numpy as jnp
from jax import lax
from jax.experimental import pallas as pl
from jax.experimental.pallas import tpu as pltpu
from jax.sharding import PartitionSpec as P

eps = 1e-06
highest = lax.Precision.HIGHEST
f32, bf16 = jnp.float32, jnp.bfloat16
excluded = -1e30
reach = 512
tile = 128


def limit(mebibytes):
    return pltpu.CompilerParams(vmem_limit_bytes=mebibytes * 1024 * 1024)


brief = pl.CostEstimate(flops=10**7, bytes_accessed=10**4, transcendentals=0)
long = pl.CostEstimate(flops=2 * 10**10, bytes_accessed=10**7, transcendentals=0)


def normalize(values, gain):
    inverse = lax.rsqrt(jnp.mean(values * values, axis=-1, keepdims=True) + eps)
    return (values * inverse * gain, inverse)


def dot(left, right, left_dim, right_dim, precision=None):
    return lax.dot_general(
        left,
        right,
        (((left_dim,), (right_dim,)), ((), ())),
        precision=precision,
        preferred_element_type=f32,
    )


def swap(values, axis, step):
    count = lax.axis_size(axis)
    return lax.ppermute(values, axis, [(i, i ^ step) for i in range(count)])


def whole(dims):
    return pl.BlockSpec(tuple(dims), lambda *_: (0,) * len(dims), pipeline_mode=pl.Buffered(1))


def call(
    kernel, name, operands, outs, scratch=(), scalars=None, after=(), through=(), cost=None
):
    outs = list(outs)
    pairs = [o if isinstance(o, tuple) else (o, o.shape[0]) for o in operands]
    operands = [array for array, _ in pairs]
    in_specs = [whole((rows,) + array.shape[1:]) for array, rows in pairs]
    out_specs = [whole(o.shape) for o in outs]
    if scalars is not None:
        operands = [scalars] + operands
        in_specs = [pl.BlockSpec(memory_space=pltpu.SMEM)] + in_specs
    count, results = len(operands), len(outs)
    extra = list(through) + list(after)

    def body(*refs):
        rest = refs[count + len(extra) :]
        kernel(*refs[:count], *rest[:results], *rest[results + len(through) :])

    return pl.pallas_call(
        body,
        name=name,
        grid=(1,),
        in_specs=in_specs + [pl.BlockSpec(memory_space=pl.ANY)] * len(extra),
        out_specs=out_specs + [pl.BlockSpec(memory_space=pl.ANY)] * len(through),
        out_shape=outs + [shape(o.shape, o.dtype) for o in through],
        input_output_aliases={count + i: results + i for i in range(len(through))},
        scratch_shapes=list(scratch),
        compiler_params=limit(64),
        cost_estimate=cost or brief,
    )(*operands, *extra)


def shape(dims, dtype):
    return jax.ShapeDtypeStruct(tuple(dims), dtype)


def fill_skew(line_ref, skew, heads):
    window = reach + tile
    row = lax.broadcasted_iota(jnp.int32, (tile, window), 0)
    column = lax.broadcasted_iota(jnp.int32, (tile, window), 1)
    usable = (column - row <= reach) & (column - row >= 1)
    for head in range(heads):
        line = jnp.broadcast_to(line_ref[head : head + 1, :], (tile, window))
        rolled = pltpu.roll(line, 0, 1, stride=1, stride_axis=0)
        skew[head * tile : (head + 1) * tile, :] = jnp.where(usable, rolled, excluded)


def fill_window(source_ref, padded):
    padded[:reach, :] = jnp.zeros((reach, padded.shape[1]), bf16)
    padded[reach:, :] = source_ref[...]


def spread_heads(values, heads, scale):
    span = values.shape[1]
    size = span // heads
    lane = lax.broadcasted_iota(jnp.int32, (tile, span), 1)
    wide = values.astype(f32) * scale
    parts = [
        jnp.where((lane >= head * size) & (lane < (head + 1) * size), wide, 0.0)
        for head in range(heads)
    ]
    return jnp.concatenate(parts, axis=0).astype(bf16)


def collect_heads(stacked, heads):
    span = stacked.shape[1]
    size = span // heads
    lane = lax.broadcasted_iota(jnp.int32, (tile, span), 1)
    total = stacked[:tile, :]
    for head in range(1, heads):
        total = jnp.where(lane < head * size, total, stacked[head * tile : (head + 1) * tile, :])
    return total


def window_powers(q_all, keys, skew, seg_q_ref, seg_k_ref, start, heads):
    window = reach + tile
    seg_q = jnp.concatenate([seg_q_ref[pl.ds(start, tile), :]] * heads, axis=0)
    seg_k = seg_k_ref[:, pl.ds(start, window)]
    scores = dot(q_all, keys, 1, 1) + skew[...]
    scores = jnp.where(seg_q == seg_k, scores, excluded)
    powers = jnp.exp(scores - jnp.max(scores, axis=-1, keepdims=True))
    return powers, 1.0 / jnp.sum(powers, axis=-1, keepdims=True)


def attend_kernel(heads, place, q_ref, k_ref, v_ref, seg_q_ref, seg_k_ref, line_ref, *rest):
    *out_refs, mixed, k_pad, v_pad, skew = rest
    window = reach + tile
    scale = (q_ref.shape[1] // heads) ** (-0.5)
    fill_skew(line_ref, skew, heads)
    fill_window(k_ref, k_pad)
    fill_window(v_ref, v_pad)

    def step(index, carry):
        start = pl.multiple_of(index * tile, tile)
        q_all = spread_heads(q_ref[pl.ds(start, tile), :], heads, scale)
        powers, inverse = window_powers(
            q_all, k_pad[pl.ds(start, window), :], skew, seg_q_ref, seg_k_ref, start, heads
        )
        probs = (powers * inverse).astype(bf16)
        part = dot(probs, v_pad[pl.ds(start, window), :], 1, 0)
        mixed[pl.ds(start, tile), :] = collect_heads(part, heads).astype(bf16)
        return carry

    lax.fori_loop(0, q_ref.shape[0] // tile, step, 0)
    rows = out_refs[0].shape[0]
    for r, out_ref in enumerate(out_refs):
        out_ref[...] = mixed[pl.ds(pl.multiple_of((place[1] ^ r) * rows, rows), rows), :]


def attend(place, query, key_rows, value_rows, seg_q, seg_k, line, heads, members, after):
    seq_len, span = query.shape
    window = reach + tile

    def kernel(place_ref, *refs):
        attend_kernel(heads, place_ref, *refs)

    return call(
        kernel,
        "attend",
        [query, key_rows, value_rows, seg_q, seg_k, line],
        [shape((seq_len // members, span), bf16)] * members,
        scratch=[
            pltpu.VMEM((seq_len, span), bf16),
            pltpu.VMEM((seq_len + reach, span), bf16),
            pltpu.VMEM((seq_len + reach, span), bf16),
            pltpu.VMEM((heads * tile, window), f32),
        ],
        scalars=place,
        after=after,
    )


def attend_back_kernel(heads, members, place, *refs):
    q_ref, k_ref, v_ref, seg_q_ref, seg_k_ref, line_ref = refs[:6]
    g_refs = refs[6 : 6 + members]
    dq_ref, dk_ref, dv_ref, line_grad_ref = refs[6 + members : 10 + members]
    grad, k_pad, v_pad, skew, dk_sum, dv_sum, bias_sum = refs[10 + members :]
    window = reach + tile
    scale = (q_ref.shape[1] // heads) ** (-0.5)
    rows = g_refs[0].shape[0]
    fill_skew(line_ref, skew, heads)
    fill_window(k_ref, k_pad)
    fill_window(v_ref, v_pad)
    dk_sum[...] = jnp.zeros_like(dk_sum)
    dv_sum[...] = jnp.zeros_like(dv_sum)
    bias_sum[...] = jnp.zeros_like(bias_sum)
    for r, g_ref in enumerate(g_refs):
        grad[pl.ds(pl.multiple_of((place[1] ^ r) * rows, rows), rows), :] = g_ref[...]

    def step(index, carry):
        start = pl.multiple_of(index * tile, tile)
        keys = k_pad[pl.ds(start, window), :]
        values = v_pad[pl.ds(start, window), :]
        q_all = spread_heads(q_ref[pl.ds(start, tile), :], heads, scale)
        g_all = spread_heads(grad[pl.ds(start, tile), :], heads, 1.0)
        powers, inverse = window_powers(q_all, keys, skew, seg_q_ref, seg_k_ref, start, heads)
        probs = powers * inverse
        dot_grad = dot(g_all, values, 1, 1)
        inner = jnp.sum(probs * dot_grad, axis=-1, keepdims=True)
        score_grad = (probs * (dot_grad - inner)).astype(bf16)
        bias_sum[...] += score_grad.astype(f32)
        part = collect_heads(dot(score_grad, keys, 1, 0), heads) * scale
        dq_ref[pl.ds(start, tile), :] = part.astype(bf16)
        dk_sum[pl.ds(start, window), :] += dot(score_grad, q_all, 0, 0)
        dv_sum[pl.ds(start, window), :] += dot(probs.astype(bf16), g_all, 0, 0)
        return carry

    lax.fori_loop(0, q_ref.shape[0] // tile, step, 0)
    dk_ref[...] = dk_sum[reach:, :].astype(bf16)
    dv_ref[...] = dv_sum[reach:, :].astype(bf16)
    line_grad_ref[...] = jnp.zeros_like(line_grad_ref)
    row = lax.broadcasted_iota(jnp.int32, (tile, tile), 0)
    column = lax.broadcasted_iota(jnp.int32, (tile, tile), 1)
    mirror = (row + column == tile - 1).astype(f32)
    for head in range(heads):
        part = bias_sum[head * tile : (head + 1) * tile, :]
        turned = dot(mirror, part, 1, 0, highest)
        straight = pltpu.roll(turned, window - tile + 1, 1, stride=1, stride_axis=0)
        line_grad_ref[head : head + 1, :] = jnp.sum(straight, axis=0, keepdims=True)


def attend_back(place, query, key_rows, value_rows, seg_q, seg_k, line, grads, heads, after):
    seq_len, span = query.shape
    window = reach + tile

    def kernel(place_ref, *refs):
        attend_back_kernel(heads, len(grads), place_ref, *refs)

    return call(
        kernel,
        "attend_back",
        [query, key_rows, value_rows, seg_q, seg_k, line] + grads,
        [shape((seq_len, span), bf16)] * 3 + [shape((8, window), f32)],
        scratch=[
            pltpu.VMEM((seq_len, span), bf16),
            pltpu.VMEM((seq_len + reach, span), bf16),
            pltpu.VMEM((seq_len + reach, span), bf16),
            pltpu.VMEM((heads * tile, window), f32),
            pltpu.VMEM((seq_len + reach, span), f32),
            pltpu.VMEM((seq_len + reach, span), f32),
            pltpu.VMEM((heads * tile, window), f32),
        ],
        scalars=place,
        after=after,
    )


def pack_weights(w_query, w_key, w_value, w_output):
    part, span = w_query.shape

    def kernel(q_ref, k_ref, v_ref, o_ref, pack_ref):
        for at, ref in enumerate((q_ref, k_ref, v_ref)):
            pack_ref[:, at * span : (at + 1) * span] = ref[...]
        pack_ref[:, 3 * span :] = o_ref[...].astype(f32).T.astype(bf16)

    (pack,) = call(
        kernel, "pack_weights", [w_query, w_key, w_value, w_output], [shape((part, 4 * span), bf16)]
    )
    return pack


def pair_up(pack, far, after):
    part = pack.shape[0]

    def kernel(near_ref, far_ref, both_ref):
        both_ref[:part, :] = near_ref[...]
        both_ref[part:, :] = far_ref[...]

    (both,) = call(
        kernel, "pair_up", [pack, far], [shape((2 * part, pack.shape[1]), bf16)], after=after
    )
    return both


def project(place, token_blocks, pack_blocks, gain, cotangent, span, after):
    rows, width = token_blocks[0].shape
    members = len(token_blocks)
    seq_len = rows * members
    parts = sum(len(held) for _, held in pack_blocks)
    part = width // parts

    def kernel(place_ref, gain_ref, *refs):
        token_refs = refs[:members]
        pack_refs = refs[members : members + len(pack_blocks)]
        (normed_ref, q_ref, k_ref, v_ref, wq_ref, wk_ref, wv_ref, wo_ref, pack) = refs[
            members + len(pack_blocks) :
        ]
        for (_, held), ref in zip(pack_blocks, pack_refs):
            for i, r in enumerate(held):
                at = pl.multiple_of((place_ref[0] ^ r) * part, part) if parts > 1 else 0
                pack[pl.ds(at, part), :] = ref[i * part : (i + 1) * part, :]
        for at, ref in enumerate((wq_ref, wk_ref, wv_ref)):
            ref[...] = pack[:, at * span : (at + 1) * span]
        wo_ref[...] = pack[:, 3 * span :].astype(f32).T.astype(bf16)
        for r, ref in enumerate(token_refs):
            normed, _ = normalize(ref[...].astype(f32), gain_ref[...])
            normed = normed.astype(bf16)
            at = pl.ds(pl.multiple_of((place_ref[1] ^ r) * rows, rows), rows)
            normed_ref[at, :] = normed
            q_ref[at, :] = dot(normed, wq_ref[...], 1, 0).astype(bf16)
            k_ref[at, :] = dot(normed, wk_ref[...], 1, 0).astype(bf16)
            v_ref[at, :] = dot(normed, wv_ref[...], 1, 0).astype(bf16)

    return call(
        kernel,
        "project",
        [gain] + list(token_blocks) + [array for array, _ in pack_blocks],
        [shape((seq_len, width), bf16)]
        + [shape((seq_len, span), bf16)] * 3
        + [shape((width, span), bf16)] * 3
        + [shape((span, width), bf16)],
        scratch=[pltpu.VMEM((width, width), bf16)],
        scalars=place,
        through=[cotangent],
        after=after,
    )


def hot(slots_ref, first, count):
    tokens = slots_ref.shape[1]
    slot = lax.broadcasted_iota(jnp.int32, (count, tokens), 0) + first
    taken = (slot == slots_ref[0:1, :]) | (slot == slots_ref[1:2, :])
    return jnp.where(taken, 1.0, 0.0).astype(bf16)


def to_slots(name, sets, blocks, size, after=()):
    width = sets[0][0].shape[1]

    def kernel(*refs):
        out_refs = refs[2 * len(sets) :]
        for at in range(len(sets)):
            rows_ref, slots_ref = refs[2 * at], refs[2 * at + 1]
            for b, out_ref in enumerate(out_refs):
                part = dot(hot(slots_ref, b * size, size), rows_ref[...], 1, 0)
                out_ref[at * size : (at + 1) * size, :] = part.astype(bf16)

    operands = [item for pair in sets for item in pair]
    return call(
        kernel,
        name,
        operands,
        [shape((size * len(sets), width), bf16)] * blocks,
        after=after,
    )


def from_slots(name, blocks, slots, size, dtypes, after=(), through=(), cost=None):
    count, sets = len(blocks), len(slots)
    width = blocks[0].shape[1]
    rows = slots[0].shape[1]

    def kernel(*refs):
        block_refs, slot_refs, out_refs = refs[:count], refs[count : count + sets], refs[count + sets :]
        for at in range(sets):
            total = None
            for b, ref in enumerate(block_refs):
                held = ref[at * size : (at + 1) * size, :]
                part = dot(hot(slot_refs[at], b * size, size), held, 0, 0)
                total = part if total is None else total + part
            out_refs[at][...] = total.astype(out_refs[at].dtype)

    return call(
        kernel,
        name,
        list(blocks) + list(slots),
        [shape((rows, width), dtype) for dtype in dtypes],
        after=after,
        through=through,
        cost=cost,
    )


def router_softmax(values, w_router, experts):
    logits = dot(values, w_router, 1, 0)
    lane = lax.broadcasted_iota(jnp.int32, logits.shape, 1)
    logits = jnp.where(lane < experts, logits, excluded)
    powers = jnp.exp(logits - jnp.max(logits, axis=-1, keepdims=True))
    return powers / jnp.sum(powers, axis=-1, keepdims=True)


def middle(tokens, mixed, weight_o, gain, w_router, slots, experts, blocks, size, after):
    rows, width = tokens.shape
    members = len(mixed)

    def kernel(*refs):
        token_ref, gain_ref, router_ref, slots_ref = refs[:4]
        mixed_refs, weight_refs = refs[4 : 4 + members], refs[4 + members : 4 + 2 * members]
        hidden_ref, input_ref, probs_ref, *send_refs = refs[4 + 2 * members :]
        hidden = token_ref[...].astype(f32)
        for left, right in zip(mixed_refs, weight_refs):
            hidden = hidden + dot(left[...], right[...], 1, 0)
        hidden_ref[...] = hidden
        normed, _ = normalize(hidden, gain_ref[...])
        normed = normed.astype(bf16)
        input_ref[...] = normed
        for b, ref in enumerate(send_refs):
            ref[...] = dot(hot(slots_ref, b * size, size), normed, 1, 0).astype(bf16)
        probs_ref[...] = router_softmax(normed, router_ref[...], experts)

    return call(
        kernel,
        "middle",
        [tokens, gain, w_router, slots] + mixed + weight_o,
        [shape((rows, width), f32), shape((rows, width), bf16), shape((rows, 128), f32)]
        + [shape((size, width), bf16)] * blocks,
        after=after,
    )


def join_rows(refs):
    return jnp.concatenate([ref[...] for ref in refs], axis=0)


def experts_forward(place, w_in, w_out, w_router, x_blocks, experts, after):
    width, units = w_in.shape
    count, size = len(x_blocks), x_blocks[0].shape[0]
    total, piece, chunk = size * count, 768, 256

    def kernel(me_ref, w_in_ref, w_out_ref, router_ref, *refs):
        x_refs, refs = refs[:count], refs[count + len(after) :]
        active_ref, slope_ref, x_all, result_ref, gates_ref, gated_ref, result_sum = refs

        @pl.when(pl.program_id(0) == 0)
        def _():
            x_all[...] = jnp.concatenate([ref[...] for ref in x_refs], axis=0)
            probs = router_softmax(x_all[...], router_ref[...], experts)
            lane = lax.broadcasted_iota(jnp.int32, probs.shape, 1)
            own = jnp.sum(jnp.where(lane == me_ref[0], probs, 0.0), axis=1, keepdims=True)
            gates_ref[...] = jnp.broadcast_to(own, gates_ref.shape)
            result_sum[...] = jnp.zeros_like(result_sum)

        for c in range(piece // chunk):
            at = slice(c * chunk, (c + 1) * chunk)
            pre_act = dot(x_all[...], w_in_ref[:, at], 1, 0)
            below = 0.5 + 0.5 * lax.erf(pre_act * math.sqrt(0.5))
            bell = jnp.exp(-0.5 * pre_act * pre_act) * (1.0 / math.sqrt(2.0 * math.pi))
            active_ref[:, at] = (pre_act * below).astype(bf16)
            slope_ref[:, at] = (below + pre_act * bell).astype(bf16)
        result_sum[...] += dot(active_ref[...], w_out_ref[...], 1, 0)

        @pl.when(pl.program_id(0) == pl.num_programs(0) - 1)
        def _():
            result = result_sum[...].astype(bf16)
            result_ref[...] = result
            gated_ref[...] = (gates_ref[:, 0:1] * result.astype(f32)).astype(bf16)

    columns = pl.BlockSpec((total, piece), lambda i: (0, i))
    rows = shape((total, width), bf16)
    kept = [rows, rows, shape((total, 128), f32), rows]
    return pl.pallas_call(
        kernel,
        name="experts_forward",
        grid=(units // piece,),
        in_specs=[
            pl.BlockSpec(memory_space=pltpu.SMEM),
            pl.BlockSpec((width, piece), lambda i: (0, i)),
            pl.BlockSpec((piece, width), lambda i: (i, 0)),
            whole(w_router.shape),
        ]
        + [whole(o.shape) for o in x_blocks]
        + [pl.BlockSpec(memory_space=pl.ANY)] * len(after),
        out_specs=[columns] * 2 + [whole(o.shape) for o in kept],
        out_shape=[shape((total, units), bf16)] * 2 + kept,
        scratch_shapes=[pltpu.VMEM((total, width), f32)],
        compiler_params=limit(64),
        cost_estimate=long,
    )(place, w_in, w_out, w_router, *x_blocks, *after)


def experts_backward(place, w_in, w_out, slope, result, gates, g_blocks, size):
    width, units = w_in.shape
    total, piece, chunk = slope.shape[0], 768, 256
    count = len(g_blocks)

    def kernel(me_ref, w_in_ref, w_out_ref, slope_ref, result_ref, gates_ref, *refs):
        g_refs, back_refs = refs[:count], refs[count : 2 * count]
        pre_grad_ref, s_all, back_sum = refs[2 * count :]

        @pl.when(pl.program_id(0) == 0)
        def _():
            back_sum[...] = jnp.zeros_like(back_sum)
            for b, ref in enumerate(g_refs):
                rows = slice(b * size, (b + 1) * size)
                s_all[rows, :] = (gates_ref[rows, 0:1] * ref[...].astype(f32)).astype(bf16)

        for c in range(piece // chunk):
            at = slice(c * chunk, (c + 1) * chunk)
            active_grad = dot(s_all[...], w_out_ref[at, :], 1, 1)
            pre_grad_ref[:, at] = (active_grad * slope_ref[:, at].astype(f32)).astype(bf16)
        back_sum[...] += dot(pre_grad_ref[...], w_in_ref[...], 1, 1)

        @pl.when(pl.program_id(0) == pl.num_programs(0) - 1)
        def _():
            lane = lax.broadcasted_iota(jnp.int32, (size, 128), 1)
            for b, (ref, g_ref) in enumerate(zip(back_refs, g_refs)):
                rows = slice(b * size, (b + 1) * size)
                products = g_ref[...].astype(f32) * result_ref[rows, :].astype(f32)
                gate_grad = jnp.sum(products, axis=1, keepdims=True)
                upper = gate_grad.astype(bf16).astype(f32)
                ref[:, :width] = back_sum[rows, :].astype(bf16)
                ref[:, width:] = jnp.where(
                    lane == me_ref[0],
                    upper,
                    jnp.where(lane == me_ref[0] + 64, gate_grad - upper, 0.0),
                ).astype(bf16)

    by_units = pl.BlockSpec((total, piece), lambda i: (0, i))
    outs = [shape((size, width + 128), bf16)] * count
    flat = pl.pallas_call(
        kernel,
        name="experts_backward",
        grid=(units // piece,),
        in_specs=[
            pl.BlockSpec(memory_space=pltpu.SMEM),
            pl.BlockSpec((width, piece), lambda i: (0, i)),
            pl.BlockSpec((piece, width), lambda i: (i, 0)),
            by_units,
            whole(result.shape),
            whole(gates.shape),
        ]
        + [whole((size, width))] * count,
        out_specs=[whole(o.shape) for o in outs] + [by_units, whole((total, width))],
        out_shape=outs + [shape((total, units), bf16), shape((total, width), bf16)],
        scratch_shapes=[pltpu.VMEM((total, width), f32)],
        compiler_params=limit(64),
        cost_estimate=long,
    )(place, w_in, w_out, slope, result, gates, *g_blocks)
    return list(flat[:count]), flat[count], flat[count + 1]


def run_experts(
    name, place, w_in, w_out, w_router, x_blocks, g_blocks, at_set, before, cost, after
):
    width, units = w_in.shape
    count, size = len(x_blocks), x_blocks[0].shape[0]
    total, piece, chunk = size * count, 512, 256
    experts = before[0]
    held = list(before[1:])
    sets = g_blocks[0].shape[0] // size
    last = at_set == sets - 1

    def kernel(me_ref, w_in_ref, w_out_ref, router_ref, *refs):
        x_refs, refs = refs[:count], refs[count:]
        g_refs, refs = refs[:count], refs[count:]
        held_refs, refs = refs[: len(held)], refs[len(held) + len(after) :]
        back_refs, refs = refs[:count], refs[count:]
        result_refs, refs = refs[:count] if last else refs[:1], refs[count if last else 1 :]
        active_ref, pre_grad_ref, x_all, s_all, gates, result_sum, back_sum = refs

        @pl.when(pl.program_id(0) == 0)
        def _():
            for b in range(count):
                rows = slice(b * size, (b + 1) * size)
                x_all[rows, :] = x_refs[b][...]
            probs = router_softmax(x_all[...], router_ref[...], experts)
            lane = lax.broadcasted_iota(jnp.int32, probs.shape, 1)
            own = jnp.sum(jnp.where(lane == me_ref[0], probs, 0.0), axis=1, keepdims=True)
            gates[...] = jnp.broadcast_to(own, gates.shape)
            for b in range(count):
                rows = slice(b * size, (b + 1) * size)
                grad = g_refs[b][at_set * size : (at_set + 1) * size, :].astype(f32)
                s_all[rows, :] = (gates[rows, 0:1] * grad).astype(bf16)
            result_sum[...] = jnp.zeros_like(result_sum)
            back_sum[...] = jnp.zeros_like(back_sum)

        for c in range(piece // chunk):
            at = slice(c * chunk, (c + 1) * chunk)
            pre_act = dot(x_all[...], w_in_ref[:, at], 1, 0)
            active_grad = dot(s_all[...], w_out_ref[at, :], 1, 1)
            below = 0.5 + 0.5 * lax.erf(pre_act * math.sqrt(0.5))
            bell = jnp.exp(-0.5 * pre_act * pre_act) * (1.0 / math.sqrt(2.0 * math.pi))
            active_ref[:, at] = (pre_act * below).astype(bf16)
            pre_grad_ref[:, at] = (active_grad * (below + pre_act * bell)).astype(bf16)
        result_sum[...] += dot(active_ref[...], w_out_ref[...], 1, 0)
        back_sum[...] += dot(pre_grad_ref[...], w_in_ref[...], 1, 1)

        @pl.when(pl.program_id(0) == pl.num_programs(0) - 1)
        def _():
            lane = lax.broadcasted_iota(jnp.int32, (size, 128), 1)
            for b, (ref, g_ref) in enumerate(zip(back_refs, g_refs)):
                rows = slice(b * size, (b + 1) * size)
                result = result_sum[rows, :].astype(bf16).astype(f32)
                grad = g_ref[at_set * size : (at_set + 1) * size, :].astype(f32)
                gate_grad = jnp.sum(grad * result, axis=1, keepdims=True)
                upper = gate_grad.astype(bf16).astype(f32)
                ref[:, :width] = back_sum[rows, :].astype(bf16)
                ref[:, width:] = jnp.where(
                    lane == me_ref[0],
                    upper,
                    jnp.where(lane == me_ref[0] + 64, gate_grad - upper, 0.0),
                ).astype(bf16)
                gated = (gates[rows, 0:1] * result).astype(bf16)
                if last:
                    for at, other in enumerate(held_refs):
                        result_refs[b][at * size : (at + 1) * size, :] = other[rows, :]
                    result_refs[b][at_set * size : (at_set + 1) * size, :] = gated
                else:
                    result_refs[0][rows, :] = gated

    columns = pl.BlockSpec((total, piece), lambda i: (0, i))
    outs = [shape((size, width + 128), bf16)] * count
    results = [shape((size * sets, width), bf16)] * count if last else [shape((total, width), bf16)]
    rows_out = [shape((total, width), bf16)] * 2
    flat = pl.pallas_call(
        kernel,
        name=name,
        grid=(units // piece,),
        in_specs=[
            pl.BlockSpec(memory_space=pltpu.SMEM),
            pl.BlockSpec((width, piece), lambda i: (0, i)),
            pl.BlockSpec((piece, width), lambda i: (i, 0)),
            whole(w_router.shape),
        ]
        + [whole(o.shape) for o in list(x_blocks) + list(g_blocks) + held]
        + [pl.BlockSpec(memory_space=pl.ANY)] * len(after),
        out_specs=[whole(o.shape) for o in outs + results]
        + [columns] * 2
        + [whole(o.shape) for o in rows_out],
        out_shape=outs + results + [shape((total, units), bf16)] * 2 + rows_out,
        scratch_shapes=[
            pltpu.VMEM((total, 128), f32),
            pltpu.VMEM((total, width), f32),
            pltpu.VMEM((total, width), f32),
        ],
        compiler_params=limit(64),
        cost_estimate=cost,
    )(place, w_in, w_out, w_router, *x_blocks, *g_blocks, *held, *after)
    return list(flat[:count]), list(flat[count:-4]), flat[-4:]


def home(
    own_back,
    far_sum,
    slots,
    hidden,
    probs,
    cotangent,
    gain,
    w_router,
    ffn_input,
    weight_o,
    mixed,
    size,
    experts,
    after,
    through,
):
    rows, width = hidden.shape
    count, members = len(own_back), len(weight_o)
    span = weight_o[0].shape[0]
    far = [] if far_sum is None else [far_sum]

    def kernel(*refs):
        slots_ref, hidden_ref, probs_ref, cot_ref, gain_ref, router_ref, input_ref = refs[:7]
        refs = refs[7:]
        back_refs, refs = refs[:count], refs[count:]
        far_refs, refs = refs[: len(far)], refs[len(far) :]
        weight_refs, mixed_refs, refs = refs[:members], refs[members : 2 * members], refs[2 * members :]
        grad_refs = refs[:members]
        hidden_grad_ref, gain_grad_ref, router_grad_ref, near_ref, base_ref = refs[members:]
        total = None
        for b, ref in enumerate(back_refs):
            part = dot(hot(slots_ref, b * size, size), ref[...], 0, 0)
            total = part if total is None else total + part
        for ref in far_refs:
            total = total + ref[...].astype(f32)
        columns = total[:, width:]
        lane = lax.broadcasted_iota(jnp.int32, columns.shape, 1)
        prob_grad = jnp.where(lane < 64, columns + pltpu.roll(columns, 64, 1), 0.0)
        router_probs = probs_ref[...]
        logit_grad = router_probs * (
            prob_grad - jnp.sum(router_probs * prob_grad, axis=-1, keepdims=True)
        )
        router_grad_ref[...] = dot(logit_grad, input_ref[...].astype(f32), 0, 0, highest)[:experts, :]
        grad = total[:, :width] + dot(logit_grad, router_ref[...].astype(f32), 1, 1, highest)
        hidden_now = hidden_ref[...]
        inverse = lax.rsqrt(jnp.mean(hidden_now * hidden_now, axis=-1, keepdims=True) + eps)
        scaled = grad * gain_ref[...]
        gain_grad_ref[...] = jnp.sum(grad * hidden_now * inverse, axis=0, keepdims=True)
        inner = jnp.mean(scaled * hidden_now, axis=-1, keepdims=True)
        hidden_grad = (
            cot_ref[...].astype(f32)
            + inverse * scaled
            - hidden_now * inverse * inverse * inverse * inner
        )
        hidden_grad_ref[...] = hidden_grad
        attn_grad = hidden_grad.astype(bf16)
        for ref, weight in zip(grad_refs, weight_refs):
            ref[...] = dot(attn_grad, weight[...], 1, 1).astype(bf16)
        for r, (ref, first) in enumerate(
            ((base_ref, 0), (near_ref, 0), (base_ref, span), (near_ref, span))
        ):
            part = dot(mixed_refs[r][...], attn_grad, 0, 0)
            ref[first : first + span, :] = part.astype(ref.dtype)

    return call(
        kernel,
        "home",
        [slots, hidden, probs, cotangent, gain, w_router, ffn_input]
        + list(own_back)
        + far
        + weight_o
        + mixed,
        [shape((rows, span), bf16)] * members
        + [
            shape((rows, width), f32),
            shape((1, width), f32),
            shape((experts, width), f32),
            shape((2 * span, width), bf16),
            shape((2 * span, width), f32),
        ],
        after=after,
        through=through,
    )


def expert_weight_grads(place, rows_in, pre_grads, actives, slot_grads, members):
    sets = len(rows_in)
    total, width = rows_in[0].shape
    piece = pre_grads[0].shape[1] // members

    def kernel(place_ref, *refs):
        x_refs, p_refs, a_refs, s_refs = [refs[i * sets : (i + 1) * sets] for i in range(4)]
        near_ref, base_ref = refs[4 * sets :]
        step = pl.program_id(0)

        def total_of(lefts, rights):
            held = dot(lefts[0][...], rights[0][...], 0, 0)
            for left, right in zip(lefts[1:], rights[1:]):
                held = held + dot(left[...], right[...], 0, 0)
            return held

        @pl.when(step < 2)
        def _():
            near_ref[...] = total_of(x_refs, p_refs).astype(bf16)

        @pl.when((step >= 2) & (step < 4))
        def _():
            base_ref[...] = total_of(x_refs, p_refs)

        @pl.when((step >= 4) & (step < 6))
        def _():
            near_ref[...] = total_of(a_refs, s_refs).astype(bf16)

        @pl.when(step >= 6)
        def _():
            base_ref[...] = total_of(a_refs, s_refs)

    def partner(i):
        return jnp.where(i < 2, 2 * i + 1, 2 * i - 4)

    fixed = pl.BlockSpec((total, width), lambda i, p: (0, 0))
    pre_cut = pl.BlockSpec((total, piece), lambda i, p: (0, p[1] ^ partner(jnp.minimum(i, 3))))
    act_cut = pl.BlockSpec((total, piece), lambda i, p: (0, p[1] ^ partner(jnp.maximum(i - 4, 0))))
    return pl.pallas_call(
        kernel,
        name="expert_weight_grads",
        grid_spec=pltpu.PrefetchScalarGridSpec(
            num_scalar_prefetch=1,
            grid=(8,),
            in_specs=[fixed] * sets + [pre_cut] * sets + [act_cut] * sets + [fixed] * sets,
            out_specs=[
                pl.BlockSpec(
                    (piece, width), lambda i, p: (2 * (i // 4) + jnp.minimum(i % 4, 1), 0)
                ),
                pl.BlockSpec(
                    (piece, width), lambda i, p: (2 * (i // 4) + jnp.maximum(i % 4 - 2, 0), 0)
                ),
            ],
        ),
        out_shape=[shape((4 * piece, width), bf16), shape((4 * piece, width), f32)],
        compiler_params=limit(64),
        cost_estimate=long,
    )(place, *rows_in, *pre_grads, *actives, *slot_grads)


def far_sums(near, base, near_o, base_o, cuts, after):
    size, width = base.shape[0] // 4, base.shape[1]
    span = near_o.shape[0] // 2

    def block(rows, at):
        return pl.BlockSpec((rows, width), lambda *_: (at, 0), pipeline_mode=pl.Buffered(1))

    def kernel(near_in, near_out, base_in, base_out, near_o_ref, base_o_ref, *refs):
        out_refs = refs[len(after) :]
        out_refs[0][:span, :] = (base_o_ref[...] + near_o_ref[...].astype(f32)).astype(bf16)
        starts = [0] + cuts
        for i, ref in enumerate(out_refs):
            low, high = starts[i], starts[i + 1]
            at = span if i == 0 else 0
            for near_ref, base_ref, shift in ((near_in, base_in, 0), (near_out, base_out, size)):
                first, last = max(low, shift), min(high, shift + size)
                if first < last:
                    rows = slice(first - shift, last - shift)
                    held = base_ref[rows, :] + near_ref[rows, :].astype(f32)
                    ref[at + first - low : at + last - low, :] = held.astype(bf16)

    rows = [high - low for low, high in zip([0] + cuts, cuts)]
    rows[0] = rows[0] + span
    return pl.pallas_call(
        kernel,
        name="far_sums",
        grid=(1,),
        in_specs=[block(size, 1), block(size, 3), block(size, 1), block(size, 3)]
        + [block(span, 1), block(span, 1)]
        + [pl.BlockSpec(memory_space=pl.ANY)] * len(after),
        out_specs=[whole((count, width)) for count in rows],
        out_shape=[shape((count, width), bf16) for count in rows],
        compiler_params=limit(64),
        cost_estimate=brief,
    )(near, near, base, base, near_o, base_o, *after)


def input_grads(
    place,
    proj_grads,
    normed,
    weights,
    output_parts,
    gain,
    line_grad,
    bucket_hot,
    ffn_gain_grad,
    router_grad,
    members,
    owners,
    heads,
    buckets_all,
    after,
):
    seq_len, width = normed.shape
    span = weights[0].shape[1]
    rows = seq_len // members
    part = width // owners
    few = owners == 8
    experts = router_grad.shape[0]
    extra = -(-(3 + experts) // 16) * 16

    def kernel(place_ref, *refs):
        dq_ref, dk_ref, dv_ref, normed_ref, wq_ref, wk_ref, wv_ref, gain_ref = refs[:8]
        line_ref, hot_ref, ffn_gain_ref, router_ref = refs[8:12]
        base_o_ref, near_o_ref, far_o_ref = refs[12:15]
        near_ref, base_ref, far_ref, small_ref, *weight_refs, sums = refs[15:]
        for at, ref in enumerate((dq_ref, dk_ref, dv_ref)):
            sums[:, at * span : (at + 1) * span] = dot(normed_ref[...], ref[...], 0, 0)
        output_sum = base_o_ref[...] + near_o_ref[...].astype(f32) + far_o_ref[...].astype(f32)
        sums[:, 3 * span :] = output_sum.T
        if few:
            for r, ref in enumerate(weight_refs):
                for i, far in enumerate((0, 4)):
                    at = pl.multiple_of((place_ref[0] ^ r ^ far) * part, part)
                    ref[i * part : (i + 1) * part, :] = sums[pl.ds(at, part), :].astype(ref.dtype)
        else:
            weight_refs[0][...] = sums[...]
        gain_grad = jnp.zeros((1, width), f32)
        for r, (ref, first) in enumerate(
            ((base_ref, 0), (near_ref, 0), (far_ref, 0), (near_ref, rows))
        ):
            at = pl.ds(pl.multiple_of((place_ref[1] ^ r) * rows, rows), rows)
            grad = (
                dot(dq_ref[at, :], wq_ref[...], 1, 1)
                + dot(dk_ref[at, :], wk_ref[...], 1, 1)
                + dot(dv_ref[at, :], wv_ref[...], 1, 1)
            )
            gain_grad = gain_grad + jnp.sum(
                grad * normed_ref[at, :].astype(f32), axis=0, keepdims=True
            )
            ref[first : first + rows, :] = grad.astype(ref.dtype)
        table = dot(line_ref[...], hot_ref[...], 1, 0, highest)
        bucket = lax.broadcasted_iota(jnp.int32, (128, width), 0)
        lane = lax.broadcasted_iota(jnp.int32, (128, width), 1)
        flat = jnp.zeros((1, width), f32)
        for head in range(heads):
            first = (place_ref[1] * heads + head) * buckets_all
            spread = jnp.where((bucket < buckets_all) & (lane == bucket + first), 1.0, 0.0)
            flat = flat + dot(table[head : head + 1, :], spread, 1, 0, highest)
        small_ref[...] = jnp.zeros_like(small_ref)
        small_ref[0:1, :] = gain_grad / gain_ref[...]
        small_ref[1:2, :] = ffn_gain_ref[...]
        small_ref[2:3, :] = flat
        small_ref[3 : 3 + experts, :] = router_ref[...]
        if few:
            upper, lower = two_halves(small_ref[...])
            small_ref[...] = upper.astype(f32) + lower.astype(f32)
            for ref in weight_refs[1:]:
                ref[2 * part : 2 * part + extra, :] = upper
                ref[2 * part + extra :, :] = lower

    if few:
        weight_outs = [shape((2 * part, 4 * span), f32)]
        weight_outs += [shape((2 * part + 2 * extra, 4 * span), bf16)] * 3
    else:
        weight_outs = [shape((width, 4 * span), f32)]
    return call(
        kernel,
        "input_grads",
        list(proj_grads)
        + [normed]
        + list(weights)
        + [gain, line_grad, bucket_hot, ffn_gain_grad, router_grad]
        + [(part, span) for part in output_parts],
        [
            shape((2 * rows, width), bf16),
            shape((rows, width), f32),
            shape((rows, width), f32),
            shape((extra, width), f32),
        ]
        + weight_outs,
        scratch=[pltpu.VMEM((width, 4 * span), f32)],
        scalars=place,
        after=after,
    )


def add_up(base, near, parts, after):
    size, width = base.shape[0] // 4, base.shape[1]

    def kernel(in_base, in_near, out_base, out_near, *refs):
        part_refs, (in_ref, out_ref) = refs[: len(parts)], refs[-2:]
        first = 0
        for (array, at), ref in zip(parts[:-1], part_refs[:-1]):
            rows = slice(first, first + array.shape[0] - at)
            total = in_base[rows, :] + in_near[rows, :].astype(f32)
            in_ref[rows, :] = total + ref[at:, :].astype(f32)
            first = first + array.shape[0] - at
        total = out_base[...] + out_near[...].astype(f32)
        out_ref[...] = total + part_refs[-1][...].astype(f32)

    def block(at):
        return pl.BlockSpec((size, width), lambda *_: (at, 0), pipeline_mode=pl.Buffered(1))

    specs = [block(0), block(0), block(2), block(2)] + [whole(o.shape) for o, _ in parts]
    return pl.pallas_call(
        kernel,
        name="add_up",
        grid=(1,),
        in_specs=specs + [pl.BlockSpec(memory_space=pl.ANY)] * len(after),
        out_specs=[whole((size, width))] * 2,
        out_shape=[shape((size, width), f32)] * 2,
        compiler_params=limit(64),
        cost_estimate=long,
    )(base, near, base, near, *[array for array, _ in parts], *after)


def two_halves(values):
    upper = values.astype(bf16)
    return upper, (values - upper.astype(f32)).astype(bf16)


def fold_weights(base, arrived, small, after, through):
    part, width, extra = base.shape[0] // 2, base.shape[1], small.shape[0]

    def kernel(base_ref, one_ref, two_ref, three_ref, small_ref, own_ref, far_ref, half_ref):
        refs = (one_ref, two_ref, three_ref)
        total = base_ref[...]
        for ref in refs:
            total = total + ref[: 2 * part, :].astype(f32)
        own_ref[...] = total[:part, :]
        far_ref[:part, :] = total[part:, :].astype(bf16)
        one, two, three = [
            ref[2 * part : 2 * part + extra, :].astype(f32)
            + ref[2 * part + extra :, :].astype(f32)
            for ref in refs
        ]
        upper, lower = two_halves((small_ref[...] + one) + (two + three))
        far_ref[part : part + extra, :] = upper
        far_ref[part + extra :, :] = lower
        half_ref[...] = upper.astype(f32) + lower.astype(f32)

    return call(
        kernel,
        "fold_weights",
        [base] + arrived + [small],
        [
            shape((part, width), f32),
            shape((part + 2 * extra, width), bf16),
            shape((extra, width), f32),
        ],
        after=after,
        through=through,
    )


def split_weights(own, far, small, span, after):
    part, extra = own.shape[0], small.shape[0]

    def kernel(*refs):
        own_ref, small_ref, *far_refs = refs[:-5]
        q_ref, k_ref, v_ref, o_ref, sum_ref = refs[-5:]
        total, sums = own_ref[...], small_ref[...]
        for ref in far_refs:
            total = total + ref[:part, :].astype(f32)
            sums = sums + (
                ref[part : part + extra, :].astype(f32) + ref[part + extra :, :].astype(f32)
            )
        for at, ref in enumerate((q_ref, k_ref, v_ref)):
            ref[...] = total[:, at * span : (at + 1) * span]
        o_ref[...] = total[:, 3 * span :].T
        sum_ref[...] = sums

    return call(
        kernel,
        "split_weights",
        [own, small] + ([] if far is None else [far]),
        [shape((part, span), f32)] * 3
        + [shape((span, part), f32), shape((extra, own.shape[1]), f32)],
        after=after,
    )


def gather_mp(values):
    across = swap(values, "mp", 2)
    return [values, swap(values, "mp", 1), across, swap(across, "mp", 1)]


def sum_over(values, axis):
    step = 1
    while step < lax.axis_size(axis):
        values = values + swap(values, axis, step)
        step = 2 * step
    return values


def all_to_all_dp(values):
    return lax.all_to_all(values, "dp", split_axis=0, concat_axis=0, tiled=True)


def slots_of(routes, place, capacity, experts, limit):
    rows = routes.shape[0]
    expert_ids = jnp.arange(experts, dtype=jnp.int32)[None, :]
    hits = (routes[:, 0:1] == expert_ids) | (routes[:, 1:2] == expert_ids)
    earlier = jnp.arange(rows)[:, None] > jnp.arange(rows)[None, :]
    ranks = jnp.dot(earlier.astype(bf16), hits.astype(bf16), preferred_element_type=f32)
    lines = []
    for k in (0, 1):
        rank = jnp.sum(jnp.where(routes[:, k : k + 1] == expert_ids, ranks, 0.0), axis=1)
        block = routes[:, k] ^ place
        lines.append(jnp.where(block < limit, block * capacity + rank.astype(jnp.int32), -1))
    return jnp.pad(jnp.stack(lines), ((0, 6), (0, 0)), constant_values=-1)


def on_device(
    tokens,
    norm_gain,
    w_query,
    w_key,
    w_value,
    w_output,
    bias_table,
    ffn_gain,
    w_router,
    w_in,
    w_out,
    segments,
    buckets,
    routes,
    cotangent,
):
    rows, width = tokens.shape
    heads = bias_table.shape[1]
    seq_len = buckets.shape[0]
    experts = w_router.shape[1]
    owners, members = lax.axis_size("dp"), lax.axis_size("mp")
    me, member = lax.axis_index("dp"), lax.axis_index("mp")
    place = jnp.stack([me, member]).astype(jnp.int32)
    capacity = 4 * rows // experts
    span = w_query.shape[1]
    window = reach + tile
    few = owners == 8

    token_blocks = gather_mp(tokens)
    pack = pack_weights(w_query, w_key, w_value, w_output)
    if few:
        both = pair_up(pack, swap(pack, "dp", 4), token_blocks[1:3])
        pack_blocks = [(both, (0, 4))] + [(swap(both, "dp", r), (r, r ^ 4)) for r in (1, 2, 3)]
    else:
        pack_blocks = [(lax.all_gather(pack, "dp", axis=0, tiled=True), (0,))]
    gain_one, gain_two = norm_gain.reshape(1, width), ffn_gain.reshape(1, width)
    if few:
        blocks, size = 4, capacity
        slots = [slots_of(routes, me, capacity, experts, 4)]
        slots.append(slots_of(swap(routes, "dp", 4), me, capacity, experts, 4))
    else:
        blocks, size = 1, experts * capacity
        slots = [slots_of(routes, 0, capacity, experts, experts)]

    line_buckets = jnp.pad(jnp.flip(buckets[: reach + 1]), (0, window - reach - 1))
    bucket_hot = (
        line_buckets[:, None] == jnp.arange(128, dtype=jnp.int32)[None, :]
    ).astype(f32)
    buckets_all = bias_table.shape[0]
    table = jnp.pad(bias_table.T, ((0, 8 - heads), (0, 128 - buckets_all)))
    line = jnp.dot(table, bucket_hot.T, precision=highest)
    seg_q = segments.reshape(seq_len, 1)
    seg_k = jnp.pad(segments.reshape(1, seq_len), ((0, 0), (reach, 0)), constant_values=-1)
    router_wide = jnp.pad(w_router, ((0, 0), (0, 128 - experts)))
    ready = slots[:1] + [seg_q, seg_k, router_wide, gain_two]
    normed, query, key_rows, value_rows, weight_q, weight_k, weight_v, w_o, late_cotangent = (
        project(place, token_blocks, pack_blocks, gain_one, cotangent, span, ready)
    )


    if few:
        far_cotangent = swap(late_cotangent, "dp", 4)

    mixed_out = attend(
        place, query, key_rows, value_rows, seg_q, seg_k, line, heads, members, [bucket_hot]
    )
    weight_o = gather_mp(w_o)
    mixed_in = [mixed_out[0]] + [swap(mixed_out[r], "mp", r) for r in range(1, members)]

    hidden, ffn_input, router_probs, *send = middle(
        tokens,
        mixed_in,
        weight_o,
        gain_two,
        router_wide,
        slots[0],
        experts,
        blocks,
        size,
        [far_cotangent] if few else [],
    )
    if few:
        held = to_slots(
            "grads_to_slots",
            [(cotangent, slots[0]), (far_cotangent, slots[1])],
            blocks,
            size,
            after=[ffn_input],
        )
        g_blocks = [held[0]] + [swap(held[r], "dp", r) for r in (1, 2, 3)]
        far_input = swap(ffn_input, "dp", 4)
        own = [send[0]] + [swap(send[r], "dp", r) for r in (1, 2, 3)]
        far = to_slots(
            "far_to_slots", [(far_input, slots[1])], blocks, size, after=g_blocks[1:3]
        )
        far = [far[0]] + [swap(far[r], "dp", r) for r in (1, 2, 3)]
        x_sets = [own, far]
    else:
        held = to_slots("grads_to_slots", [(cotangent, slots[0])], blocks, size)
        g_blocks = [all_to_all_dp(held[0])]
        x_sets = [[all_to_all_dp(send[0])]]

    before = [experts]
    if few:
        active, slope, rows_in, plain, slot_gates, gated = experts_forward(
            place, w_in[0], w_out[0], router_wide, x_sets[0], experts, far[:1]
        )
        before = before + [gated]
    back, result, state = run_experts(
        "run_experts",
        place,
        w_in[0],
        w_out[0],
        router_wide,
        x_sets[-1],
        g_blocks,
        len(x_sets) - 1,
        before,
        brief,
        [],
    )
    kept, backs = [state], [back]
    if few:
        back, pre_grad, slot_grad = experts_backward(
            place, w_in[0], w_out[0], slope, plain, slot_gates, g_blocks, size
        )
        kept = [(active, pre_grad, rows_in, slot_grad)] + kept
        backs = [back] + backs
    actives, pre_grads, arrived, slot_grads = zip(*kept)
    if few:
        own_back, far_back = backs
        far_back = [far_back[0]] + [swap(far_back[r], "dp", r) for r in (1, 2, 3)]
        far_total, *passed = from_slots(
            "back_from_slots", far_back, [slots[1]], size, [bf16], through=own_back[1:]
        )
        far_sum = swap(far_total, "dp", 4)
        own_back = [own_back[0]] + [swap(passed[r - 1], "dp", r) for r in (1, 2, 3)]
        result_in = [result[0]] + [swap(result[r], "dp", r) for r in (1, 2, 3)]
    else:
        own_back, far_sum = [all_to_all_dp(backs[0][0])], None
        result_in = [all_to_all_dp(result[0])]
    near_w, base_w = expert_weight_grads(place, arrived, pre_grads, actives, slot_grads, members)

    homed = home(
        own_back,
        far_sum,
        slots[0],
        hidden,
        router_probs,
        cotangent,
        gain_two,
        router_wide,
        ffn_input,
        weight_o,
        mixed_in,
        size,
        experts,
        [],
        [near_w],
    )
    grad_out, homed = homed[:members], homed[members:]
    hidden_grad, ffn_gain_grad, router_grad, near_o, base_o, near_w = homed
    grad_in = [grad_out[0]] + [swap(grad_out[r], "mp", r) for r in range(1, members)]
    near_o, near_w = swap(near_o, "mp", 1), swap(near_w, "mp", 1)
    piece = w_in.shape[2] // members
    far_first, far_next, far_last = far_sums(
        near_w, base_w, near_o, base_o, [2 * rows, piece, 2 * piece], grad_in[2:]
    )

    *proj_grads, line_grad = attend_back(
        place,
        query,
        key_rows,
        value_rows,
        seg_q,
        seg_k,
        line,
        grad_in,
        heads,
        [far_first],
    )
    far_first = swap(far_first, "mp", 2)
    far_last = swap(far_last, "mp", 2)
    near, base, base_far, small, *weight_sums = input_grads(
        place,
        proj_grads,
        normed,
        (weight_q, weight_k, weight_v),
        (base_o, near_o, far_first),
        gain_one,
        line_grad,
        bucket_hot,
        ffn_gain_grad,
        router_grad,
        members,
        owners,
        heads,
        buckets_all,
        result_in[1:],
    )
    near = swap(near, "mp", 1)
    far_normed = swap((base_far + near[rows:].astype(f32)).astype(bf16), "mp", 2)
    if few:
        arrived_sums = [swap(weight_sums[r], "dp", r) for r in (1, 2, 3)]
        own_sum, far_part, small, far_next = fold_weights(
            weight_sums[0], arrived_sums, small, [near], [far_next]
        )
        far_next = swap(far_next, "mp", 2)
        own_result, far_result = from_slots(
            "result_from_slots", result_in, slots, size, [f32, bf16], after=[own_sum]
        )
        far_result = swap(far_result, "dp", 4)
        w_in_grad, w_out_grad = add_up(
            base_w, near_w, [(far_first, span), (far_next, 0), (far_last, 0)], [own_result]
        )
        *weight_grads, small = split_weights(
            own_sum, swap(far_part, "dp", 4), small, span, [w_in_grad, far_normed]
        )
    else:
        joined_grad = lax.psum_scatter(weight_sums[0], "dp", scatter_dimension=0, tiled=True)
        *weight_grads, small = split_weights(
            joined_grad, None, sum_over(small, "dp"), span, []
        )
        (own_result,) = from_slots("result_from_slots", result_in, slots, size, [f32])
        far_next = swap(far_next, "mp", 2)
        w_in_grad, w_out_grad = add_up(
            base_w, near_w, [(far_first, span), (far_next, 0), (far_last, 0)], []
        )
    small = sum_over(small, "mp")
    normed_grad = base + near[:rows].astype(f32) + far_normed.astype(f32)
    resid = tokens.astype(f32)
    _, inverse_one = normalize(resid, norm_gain)
    scaled = normed_grad * norm_gain
    inner = jnp.mean(scaled * resid, axis=-1, keepdims=True)
    tokens_grad = (
        hidden_grad + inverse_one * scaled - resid * inverse_one * inverse_one * inverse_one * inner
    ).astype(bf16)

    block_out = hidden + own_result
    if few:
        block_out = block_out + far_result.astype(f32)
    block_out = block_out.astype(bf16)
    return (
        block_out,
        tokens_grad,
        small[0],
        *weight_grads,
        small[2, : heads * members * buckets_all].reshape(heads * members, buckets_all).T,
        small[1],
        small[3 : 3 + experts].T,
        w_in_grad[None],
        w_out_grad[None],
    )


def solution(mesh):
    return jax.shard_map(
        on_device,
        mesh=mesh,
        in_specs=(
            P(("dp", "mp"), None),
            P(),
            P("dp", "mp"),
            P("dp", "mp"),
            P("dp", "mp"),
            P("mp", "dp"),
            P(None, "mp"),
            P(),
            P(),
            P("dp", None, None),
            P("dp", None, None),
            P("dp", None),
            P(),
            P(("dp", "mp"), None),
            P(("dp", "mp"), None),
        ),
        out_specs=(
            P(("dp", "mp"), None),
            P(("dp", "mp"), None),
            P(),
            P("dp", "mp"),
            P("dp", "mp"),
            P("dp", "mp"),
            P("mp", "dp"),
            P(),
            P(),
            P(),
            P("dp", None, "mp"),
            P("dp", "mp", None),
        ),
        check_vma=False,
    )
```
